32 devices in a mesh: seq: 8 (over y, x, core), head: 4 (over z).
Axes of the slice: x: 2, y: 2, z: 4, core: 2. Of those that a mesh axis runs over, the one named last changes fastest.
Arguments:
- x_input: bfloat16 [8192, 1024], P('seq'), may hold values from -6 to 6
- seg_ids: int32 [8192], P('seq'), may hold values from 0 to 1, as said below
- cotangent: bfloat16 [8192, 1024], P('seq'), may hold values from -6 to 6
- norm_gain: float32 [2, 1024], replicated, may hold values from 0.5 to 1.5
- w_z: bfloat16 [2, 1024, 2048], P(None, None, 'head'), may hold values from -0.1875 to 0.1875
- w_x: bfloat16 [2, 1024, 2048], P(None, None, 'head'), may hold values from -0.1875 to 0.1875
- w_bc: bfloat16 [2, 1024, 256], replicated, may hold values from -0.1875 to 0.1875
- w_dt: bfloat16 [2, 1024, 32], P(None, None, 'head'), may hold values from -0.1875 to 0.1875
- conv_x: float32 [2, 4, 2048], P(None, None, 'head'), may hold values from -3 to 3
- conv_bc: float32 [2, 4, 256], replicated, may hold values from -3 to 3
- bias_x: float32 [2, 2048], P(None, 'head'), may hold values from -2 to 2
- bias_bc: float32 [2, 256], replicated, may hold values from -2 to 2
- dt_bias: float32 [2, 32], P(None, 'head'), may hold values from -30 to -3
- a_log: float32 [2, 32], P(None, 'head'), may hold values from 0 to 1
- d_skip: float32 [2, 32], P(None, 'head'), may hold values from 0.5 to 1.5
- gate_gain: float32 [2, 2048], P(None, 'head'), may hold values from 0.5 to 1.5
- w_out: bfloat16 [2, 1024, 2048], P(None, None, 'head'), may hold values from -0.125 to 0.125
Outputs:
- block_out: bfloat16 [8192, 1024], P('seq')
- input_grad: float32 [8192, 1024], P('seq')
- grad_norm_gain: float32 [2, 1024], replicated
- grad_w_z: float32 [2, 1024, 2048], P(None, 'seq', 'head')
- grad_w_x: float32 [2, 1024, 2048], P(None, 'seq', 'head')
- grad_w_bc: float32 [2, 1024, 256], P(None, 'seq')
- grad_w_dt: float32 [2, 1024, 32], P(None, 'seq', 'head')
- grad_conv_x: float32 [2, 4, 2048], P(None, None, 'head')
- grad_conv_bc: float32 [2, 4, 256], replicated
- grad_bias_x: float32 [2, 2048], P(None, 'head')
- grad_bias_bc: float32 [2, 256], replicated
- grad_dt_bias: float32 [2, 32], P(None, 'head')
- grad_a_log: float32 [2, 32], P(None, 'head')
- grad_d_skip: float32 [2, 32], P(None, 'head')
- grad_gate_gain: float32 [2, 2048], P(None, 'head')
- grad_w_out: float32 [2, 1024, 2048], P(None, 'seq', 'head')
The draws below stay inside these ranges and needn't reach their ends.
Inputs may be any that keep to these rules, and one draw needn't show every extreme that they name: `seg_ids`: ids start at 0 and each token's id equals the previous token's or is one more. There are exactly 2 documents, each of more than 1280 tokens; no document but the first starts at the first token of a block of 1024 tokens.
All inputs are finite; a program needn't handle non-finite values.
Results may differ from the reference program's by a relative error of at most 0.012.
Values sent between devices are 32-bit elements; how exact they have to be, the bound alone decides.
No kernel may reach another device: no remote copies, remote signals or barrier semaphores. Data moves between devices by JAX's collectives and lax.ppermute only.
A program may use at most 192 MiB of HBM per device.

```python
import jax
import jax.numpy as jnp
from jax import lax

D = 1024
HEADS = 32
HEADDIM = 64
STATE = 128
CONV = 4
GROUP = 256
LAYERS = 2
TOK_DEV = 1024
INNER = 2048
TOKENS = 8192


def draw_seg_ids(key, part):
    key = jax.random.fold_in(key, 11)
    keys = jax.random.split(key, 2)
    doc_count = TOKENS // (4 * TOK_DEV)
    block_pick = jax.random.randint(keys[0], (doc_count,), 0, 3)
    inner_pick = jax.random.randint(keys[1], (doc_count,), TOK_DEV // 4, 3 * TOK_DEV // 4)
    first_tokens = jnp.arange(doc_count) * (4 * TOK_DEV) + block_pick * TOK_DEV + inner_pick
    first_tokens = jnp.where(jnp.arange(doc_count) == 0, 0, first_tokens)
    position = jnp.arange(TOKENS)
    flags = jnp.sum((position[:, None] == first_tokens[None, :]).astype(jnp.int32), axis=1)
    return (jnp.cumsum(flags) - 1).astype(jnp.int32)


def draw_dt_bias(key, part):
    key = jax.random.fold_in(key, 23)
    keys = jax.random.split(key, 3)
    fast_bias = jax.random.uniform(keys[0], (LAYERS, HEADS), jnp.float32, -4.0, -3.0)
    slow_bias = -jnp.log(jnp.float32(TOKENS)) - jax.random.uniform(keys[1], (LAYERS, HEADS), jnp.float32, 1.0, 2.0)
    share = 0.5
    picked = jax.random.uniform(keys[2], (LAYERS, HEADS), jnp.float32) < share
    return jnp.where(picked, fast_bias, slow_bias)


def levels(stream_key, dims, cuts, smallest, largest):
    factor_of, own = 1.0, jax.random.fold_in(stream_key, 6)
    for dim, shards_of in cuts:
        draws = jnp.exp(jax.random.uniform(jax.random.fold_in(own, dim), (shards_of,), jnp.float32, smallest / len(cuts), largest / len(cuts)))
        factor_of = factor_of * jnp.repeat(draws, dims[dim] // shards_of).reshape([-1 if axis == dim else 1 for axis in range(len(dims))])
    return factor_of


def bell_draw(rng, shape, scale, bound, cuts=(), held_as=jnp.bfloat16):
    values = scale * jax.random.normal(rng, shape, jnp.float32)
    if cuts:
        values = values * levels(rng, shape, cuts, -0.22, 0.18)
    return jnp.clip(values, -bound, bound).astype(held_as)


def setup_inputs(seed: int = 0) -> dict:
    splits = jax.random.split(jax.random.key(seed), 18)
    return {
        "x_input": bell_draw(splits[0], (TOKENS, D), 1.0, 6.0, ((0, 8),)),
        "seg_ids": draw_seg_ids(jax.random.fold_in(splits[17], 71), 0),
        "cotangent": bell_draw(splits[2], (TOKENS, D), 1.0, 6.0, ((0, 8),)),
        "norm_gain": jnp.clip(1.0 + 0.1 * jax.random.normal(splits[3], (LAYERS, D), jnp.float32), 0.5, 1.5),
        "w_z": bell_draw(splits[4], (LAYERS, D, INNER), D ** -0.5, 0.1875, ((2, 4),)),
        "w_x": bell_draw(splits[5], (LAYERS, D, INNER), D ** -0.5, 0.1875, ((2, 4),)),
        "w_bc": bell_draw(splits[6], (LAYERS, D, 2 * STATE), D ** -0.5, 0.1875),
        "w_dt": bell_draw(splits[7], (LAYERS, D, HEADS), D ** -0.5, 0.1875, ((2, 4),)),
        "conv_x": bell_draw(splits[8], (LAYERS, CONV, INNER), CONV ** -0.5, 3.0, ((2, 4),), jnp.float32),
        "conv_bc": bell_draw(splits[9], (LAYERS, CONV, 2 * STATE), CONV ** -0.5, 3.0, (), jnp.float32),
        "bias_x": bell_draw(splits[10], (LAYERS, INNER), 0.3, 2.0, ((1, 4),), jnp.float32),
        "bias_bc": bell_draw(splits[11], (LAYERS, 2 * STATE), 0.3, 2.0, (), jnp.float32),
        "dt_bias": draw_dt_bias(jax.random.fold_in(splits[17], 71), 0),
        "a_log": jnp.clip(1.0 * jax.random.uniform(splits[13], (LAYERS, HEADS), jnp.float32) ** levels(splits[13], (LAYERS, HEADS), ((1, 4),), -0.2, 0.2), 0.0, 1.0),
        "d_skip": jnp.clip(0.5 + 1.0 * jax.random.uniform(splits[14], (LAYERS, HEADS), jnp.float32) ** levels(splits[14], (LAYERS, HEADS), ((1, 4),), -0.2, 0.2), 0.5, 1.5),
        "gate_gain": jnp.clip(1.0 + 0.1 * jax.random.normal(splits[15], (LAYERS, INNER), jnp.float32), 0.5, 1.5),
        "w_out": bell_draw(splits[16], (LAYERS, D, INNER), INNER ** -0.5, 0.125, ((2, 4),)),
    }


@jax.custom_vjp
def low(v):
    return lax.optimization_barrier(v.astype(jnp.bfloat16)).astype(jnp.float32)

@jax.custom_vjp
def low_back(v):
    return v

def low_keep(v):
    return (low(v), None)

def low_pass(kept, grad):
    return (grad,)

def back_keep(v):
    return (v, None)

def back_low(kept, grad):
    return (low(grad),)
low.defvjp(low_keep, low_pass)
low_back.defvjp(back_keep, back_low)
epsilon = 1e-05
highest = lax.Precision.HIGHEST

def group_step(state, pieces):
    x_group, b_group, c_group, dt_group, da_group, seg_group, start_group = pieces
    cumulative = jnp.cumsum(da_group, axis=0)
    totals = cumulative[-1]
    position = jnp.arange(GROUP)
    same_run = (seg_group[:, None] == seg_group[None, :]) & (position[:, None] >= position[None, :])
    cum_heads = cumulative.T
    log_gap = cum_heads[:, :, None] - cum_heads[:, None, :]
    decay_mat = jnp.where(same_run[None], jnp.exp(jnp.where(same_run[None], log_gap, 0.0)), 0.0)
    inner_prod = jnp.dot(c_group, b_group.T, precision=highest)
    weights = decay_mat * inner_prod[None] * dt_group.T[:, None, :]
    y_intra = jnp.einsum('hts,shp->thp', weights, x_group, precision=highest)
    alive_mask = (jnp.cumsum(start_group) == 0).astype(jnp.float32)
    entry_decay = jnp.exp(cumulative) * alive_mask[:, None]
    y_inter = entry_decay[:, :, None] * jnp.einsum('tn,hpn->thp', c_group, state, precision=highest)
    end_mask = (seg_group == seg_group[-1]).astype(jnp.float32)
    tail_weight = jnp.exp(totals[None, :] - cumulative) * end_mask[:, None] * dt_group
    contrib = jnp.einsum('sh,shp,sn->hpn', tail_weight, x_group, b_group, precision=highest)
    through = alive_mask[-1] * jnp.exp(totals)
    return (through[:, None, None] * state + contrib, y_intra + y_inter)

def mixer_layer(hidden, seg_ids, starts, params):
    ngain, wz, wx, wbc, wdt, cx, cbc, bx, bbc, dtb, alog, dskip, ggain, wout = params
    inv_rms = lax.rsqrt(lax.optimization_barrier(jnp.mean(hidden * hidden, axis=-1, keepdims=True)) + epsilon)
    normed = low(hidden * inv_rms * ngain[None, :])
    zvalue = low_back(jnp.dot(normed, wz, precision=highest))
    conv_in = low_back(jnp.dot(normed, jnp.concatenate([wx, wbc], axis=1), precision=highest))
    dt_pre = low_back(jnp.dot(normed, wdt, precision=highest))
    kernel = jnp.concatenate([cx, cbc], axis=1)
    offset = jnp.concatenate([bx, bbc])
    padded = jnp.pad(conv_in, ((CONV - 1, 0), (0, 0)))
    seg_pad = jnp.concatenate([jnp.full((CONV - 1,), -1, jnp.int32), seg_ids.astype(jnp.int32)])
    conv_pre = jnp.zeros(conv_in.shape, jnp.float32) + offset[None, :]
    for tap_idx in range(CONV):
        same_doc = (seg_pad[tap_idx:tap_idx + TOKENS] == seg_ids).astype(jnp.float32)
        conv_pre = conv_pre + kernel[tap_idx][None, :] * padded[tap_idx:tap_idx + TOKENS] * same_doc[:, None]
    active = jax.nn.silu(conv_pre)
    xvalue = active[:, :INNER].reshape(TOKENS, HEADS, HEADDIM)
    bvalue = active[:, INNER:INNER + STATE]
    cvalue = active[:, INNER + STATE:]
    dt_value = jax.nn.softplus(dt_pre + dtb[None, :])
    da_value = dt_value * (-jnp.exp(alog))[None, :]
    nchunk = TOKENS // GROUP
    pieces = (xvalue.reshape(nchunk, GROUP, HEADS, HEADDIM), bvalue.reshape(nchunk, GROUP, STATE), cvalue.reshape(nchunk, GROUP, STATE), dt_value.reshape(nchunk, GROUP, HEADS), da_value.reshape(nchunk, GROUP, HEADS), seg_ids.reshape(nchunk, GROUP), starts.reshape(nchunk, GROUP))
    start_state = jnp.zeros((HEADS, HEADDIM, STATE), jnp.float32)
    final_state, y_groups = lax.scan(jax.checkpoint(group_step), start_state, pieces)
    yvalue = y_groups.reshape(TOKENS, HEADS, HEADDIM) + dskip[None, :, None] * xvalue
    gated_out = yvalue.reshape(TOKENS, INNER) * jax.nn.silu(zvalue)
    gate_scale = lax.rsqrt(lax.optimization_barrier(jnp.mean(gated_out * gated_out, axis=-1, keepdims=True)) + epsilon)
    proj = low_back(jnp.dot(low(gated_out * ggain[None, :]), wout.T, precision=highest))
    return hidden + gate_scale * proj

def reference(x_input, seg_ids, cotangent, norm_gain, w_z, w_x, w_bc, w_dt, conv_x, conv_bc, bias_x, bias_bc, dt_bias, a_log, d_skip, gate_gain, w_out):
    starts = jnp.concatenate([jnp.ones((1,), jnp.int32), (seg_ids[1:] != seg_ids[:-1]).astype(jnp.int32)])
    weight_set = tuple((weight_arr.astype(jnp.float32) for weight_arr in (norm_gain, w_z, w_x, w_bc, w_dt, conv_x, conv_bc, bias_x, bias_bc, dt_bias, a_log, d_skip, gate_gain, w_out)))

    def forward(hidden, weight_all):
        for layer_idx in range(LAYERS):
            params = tuple((weight_arr[layer_idx] for weight_arr in weight_all))
            hidden = mixer_layer(hidden, seg_ids, starts, params)
        return hidden
    result, pullback = jax.vjp(forward, x_input.astype(jnp.float32), weight_set)
    grad_in, grads = pullback(cotangent.astype(jnp.float32))
    return (result.astype(jnp.bfloat16), grad_in, grads[0], grads[1], grads[2], grads[3], grads[4], grads[5], grads[6], grads[7], grads[8], grads[9], grads[10], grads[11], grads[12], grads[13])
```

```python
import functools

import jax
import jax.numpy as jnp
from jax import lax
from jax.experimental import pallas as pl
from jax.experimental.pallas import tpu as pltpu
from jax.sharding import PartitionSpec as P

HEADDIM = 64
STATE = 128
CONV = 4
GROUP = 256
LAYERS = 2
INNER = 2048
LANES = 128
ROWS = 8
BC = 2 * STATE

epsilon = 1e-05
highest = lax.Precision.HIGHEST
f32 = jnp.float32
bf16 = jnp.bfloat16


def mm(left, right, dims=((1,), (0,)), precision=None):
    return lax.dot_general(
        left, right, (dims, ((), ())), preferred_element_type=f32, precision=precision
    )


def softplus(value):
    small = jnp.exp(-jnp.abs(value))
    series = small * (1.0 - small * (0.5 - small * (1.0 / 3.0 - small * (0.25 - small * 0.2))))
    return jnp.maximum(value, 0.0) + jnp.where(small < 0.03, series, jnp.log(1.0 + small))


def silu_slope(value, sigma):
    return sigma * (1.0 + value * (1.0 - sigma))


def spread(heads, expand):
    return mm(heads, expand, precision=highest)


def gather_heads(lanes, expand):
    return mm(lanes, expand, ((1,), (1,)), precision=highest)


def in_kernel(
    hid, wall, ngain, taps, bias, dtb, avec, mask, halo, expand, tri,
    normed, zval, cin, cpre, dtp, cum, dtv, xdt, bc, sloc, pref, send,
    state, thru, prev,
):
    step = pl.program_id(0)
    inner = expand.shape[1]

    @pl.when(step == 0)
    def _():
        state[...] = jnp.zeros_like(state)
        thru[...] = jnp.ones_like(thru)
        prev[...] = halo[...]

    h = hid[...].astype(f32)
    inv = lax.rsqrt(jnp.mean(h * h, axis=1, keepdims=True) + epsilon)
    low = (h * inv * ngain[...]).astype(bf16)
    normed[...] = low
    zval[...] = mm(low, wall[:, :inner])
    rows = mm(low, wall[:, inner : 2 * inner + BC])
    pre_dt = mm(low, wall[:, 2 * inner + BC :])
    dtp[...] = pre_dt
    cin[...] = rows
    ext = jnp.concatenate([prev[...], rows], axis=0)
    prev[...] = rows[GROUP - ROWS :]
    total = taps[CONV - 1 : CONV, :] * rows + bias[0:1, :]
    for k in range(CONV - 1):
        first = ROWS - CONV + 1 + k
        total = total + taps[k : k + 1, :] * ext[first : first + GROUP] * mask[:, k : k + 1]
    cpre[...] = total
    act = total * jax.nn.sigmoid(total)
    x = act[:, :inner]
    low_bc = act[:, inner:].astype(bf16)
    bc[...] = low_bc
    dt = softplus(pre_dt + dtb[0:1, :])
    dtv[...] = dt
    run = mm(tri[...], dt * avec[0:1, :], precision=highest)
    cum[...] = run
    last = run[GROUP - 1 : GROUP]
    xdt[...] = (x * spread(dt, expand[...])).astype(bf16)
    tail = jnp.exp(last - run) * mask[:, 4:5] * dt
    contrib = mm(low_bc[:, :STATE], (x * spread(tail, expand[...])).astype(bf16), ((0,), (0,)))
    through = jnp.broadcast_to(jnp.exp(last) * mask[GROUP - 1 : GROUP, 3:4], (ROWS, LANES))
    through = spread(through, expand[...])
    sloc[0] = state[...]
    pref[0] = thru[...]
    state[...] = through[0:1] * state[...] + contrib
    thru[...] = thru[...] * through

    @pl.when(step == pl.num_programs(0) - 1)
    def _():
        send[:STATE] = state[...]
        send[STATE:] = thru[...]


def pair_lanes(value, which):
    lane = lax.broadcasted_iota(jnp.int32, value.shape, 1)
    keep = lane < HEADDIM if which == 0 else lane >= HEADDIM
    return jnp.where(keep, value, jnp.zeros_like(value))


def intra_kernel(cum, xdt, bc, seg, segrow, y):
    inner = xdt.shape[1]
    run = cum[...]
    run_t = run.T
    base = mm(bc[:, STATE:], bc[:, :STATE], ((1,), (1,)))
    t_at = lax.broadcasted_iota(jnp.int32, (GROUP, GROUP), 0)
    s_at = lax.broadcasted_iota(jnp.int32, (GROUP, GROUP), 1)
    same = (seg[:, 0:1] == segrow[0:1, :]) & (t_at >= s_at)
    closed = jnp.where(same, 0.0, -1e30)
    for pair in range(inner // LANES):
        cols = slice(pair * LANES, (pair + 1) * LANES)
        xs = xdt[:, cols]
        parts = []
        for which in range(2):
            head = 2 * pair + which
            decay = jnp.exp(run[:, head : head + 1] - run_t[head : head + 1, :] + closed)
            parts.append(mm((decay * base).astype(bf16), xs))
        lane = lax.broadcasted_iota(jnp.int32, (GROUP, LANES), 1)
        y[:, cols] = jnp.where(lane < HEADDIM, parts[0], parts[1])


def out_kernel(
    yin, cpre, cum, bc, mask, zval, sloc, pref, entry, dskip, ggain, wout, expand, cot,
    y, gate_in, proj, sums,
):
    inner = expand.shape[1]
    pre = cpre[...]
    x = pre * jax.nn.sigmoid(pre)
    full = sloc[0] + pref[0][0:1] * entry[...]
    reach = spread(jnp.exp(cum[...]) * mask[:, 3:4], expand[...])
    value = yin[...] + reach * mm(bc[:, STATE:], full.astype(bf16)) + dskip[0:1, :] * x
    y[...] = value
    z = zval[...]
    gated = value * (z * jax.nn.sigmoid(z))
    low = (gated * ggain[0:1, :]).astype(bf16)
    gate_in[...] = low
    proj[...] = mm(low, wout[...], ((1,), (1,)))
    ones = jnp.ones((ROWS, inner), f32)
    squares = mm(ones, gated * gated, ((1,), (1,)), precision=highest)
    back = mm(cot[...], wout[...])
    dots = mm(ones, low.astype(f32) * back, ((1,), (1,)), precision=highest)
    row = lax.broadcasted_iota(jnp.int32, squares.shape, 0)
    sums[...] = jnp.where(row == 0, squares, dots)


def gate_kernel(
    gh, scale, gsq, y, zval, ggain, wout, cum, bc, mask, expand,
    gproj, dy, dz, gloc, suf, send, acc,
    carry, thru,
):
    step = pl.program_id(0)

    @pl.when(step == 0)
    def _():
        carry[...] = jnp.zeros_like(carry)
        thru[...] = jnp.ones_like(thru)
        acc[...] = jnp.zeros_like(acc)

    gp = (scale[...] * gh[...].astype(f32)).astype(bf16)
    gproj[...] = gp
    ggi = mm(gp, wout[...])
    z = zval[...]
    sigma = jax.nn.sigmoid(z)
    silu = z * sigma
    value = y[...]
    gated = value * silu
    ggated = ggi * ggain[0:1, :] + gated * gsq[...]
    acc[0:1, :] += jnp.sum(ggi * gated, axis=0, keepdims=True)
    low = (ggated * silu).astype(bf16)
    dy[...] = low
    dz[...] = (ggated * value * silu_slope(z, sigma)).astype(bf16)
    run = cum[...]
    last = run[GROUP - 1 : GROUP]
    reach = spread(jnp.exp(run) * mask[:, 3:4], expand[...])
    back = mm(bc[:, STATE:], (reach * low.astype(f32)).astype(bf16), ((0,), (0,)))
    through = jnp.broadcast_to(jnp.exp(last) * mask[GROUP - 1 : GROUP, 3:4], (ROWS, LANES))
    through = spread(through, expand[...])
    gloc[0] = carry[...]
    suf[0] = thru[...]
    carry[...] = back + through[0:1] * carry[...]
    thru[...] = thru[...] * through

    @pl.when(step == pl.num_programs(0) - 1)
    def _():
        send[:STATE] = carry[...]
        send[STATE:] = thru[...]


def intra_back_kernel(cum, xdt, bc, seg, segrow, dy, u, dbc):
    inner = xdt.shape[1]
    run = cum[...]
    run_t = run.T
    base = mm(bc[:, :STATE], bc[:, STATE:], ((1,), (1,)))
    s_at = lax.broadcasted_iota(jnp.int32, (GROUP, GROUP), 0)
    t_at = lax.broadcasted_iota(jnp.int32, (GROUP, GROUP), 1)
    same = (seg[:, 0:1] == segrow[0:1, :]) & (t_at >= s_at)
    closed = jnp.where(same, 0.0, -1e30)
    grad_base = jnp.zeros((GROUP, GROUP), f32)
    for pair in range(inner // LANES):
        cols = slice(pair * LANES, (pair + 1) * LANES)
        xs = xdt[:, cols]
        ds = dy[:, cols]
        parts = []
        for which in range(2):
            head = 2 * pair + which
            decay = jnp.exp(run_t[head : head + 1, :] - run[:, head : head + 1] + closed)
            parts.append(mm((decay * base).astype(bf16), ds))
            grad_base = grad_base + decay * mm(xs, pair_lanes(ds, which), ((1,), (1,)))
        lane = lax.broadcasted_iota(jnp.int32, (GROUP, LANES), 1)
        u[:, cols] = jnp.where(lane < HEADDIM, parts[0], parts[1])
    low = grad_base.astype(bf16)
    dbc[:, :STATE] = mm(low, bc[:, STATE:])
    dbc[:, STATE:] = mm(low, bc[:, :STATE], ((0,), (0,)))


def in_back_kernel(
    uin, dbc, dy, dz, y, cpre, cin, dtp, dtv, cum, xdt, bc, mask, sloc, pref, entry, gloc, suf,
    gout, halo, taps, dtb, avec, dskip, expand, triback,
    gall, last8, rim, gtaps, vecs, dsk,
    nexts,
):
    step = pl.program_id(0)
    inner = expand.shape[1]

    @pl.when(step == 0)
    def _():
        nexts[...] = jnp.zeros_like(nexts)
        gtaps[...] = jnp.zeros_like(gtaps)
        vecs[...] = jnp.zeros_like(vecs)
        dsk[...] = jnp.zeros_like(dsk)

    e = expand[...]
    pre = cpre[...]
    sigma = jax.nn.sigmoid(pre)
    x = (pre * sigma)[:, :inner]
    full = sloc[0] + pref[0][0:1] * entry[...]
    nxt = gloc[0] + suf[0][0:1] * gout[...]
    nxt_low = nxt.astype(bf16)
    run = cum[...]
    last = run[GROUP - 1 : GROUP]
    dt = dtv[...]
    low_dy = dy[...].astype(f32)
    xw = xdt[...].astype(f32)
    tail = spread(jnp.exp(last - run) * mask[:, 4:5], e)
    reach = spread(jnp.exp(run) * mask[:, 3:4], e)
    u_inter = tail * mm(bc[:, :STATE], nxt_low)
    u = uin[...] + u_inter
    dx = spread(dt, e) * u + dskip[0:1, :] * low_dy
    dsk[0:1, :] += jnp.sum(low_dy * x, axis=0, keepdims=True)
    db = dbc[:, :STATE] + mm((tail * xw).astype(bf16), nxt_low, ((1,), (1,)))
    dc = dbc[:, STATE:] + mm((reach * low_dy).astype(bf16), full.astype(bf16), ((1,), (1,)))
    grad_dt = gather_heads(x * u, e)
    y_plain = y[...] - dskip[0:1, :] * x
    grad_cum = gather_heads(low_dy * y_plain - xw * u, e)
    flow = jnp.sum(nxt * full, axis=0, keepdims=True)
    flow = gather_heads(jnp.broadcast_to(flow, (ROWS, inner)), e)[0:1]
    ends = jnp.sum(xw * u_inter, axis=0, keepdims=True)
    ends = gather_heads(jnp.broadcast_to(ends, (ROWS, inner)), e)[0:1]
    grad_tot = mask[GROUP - 1 : GROUP, 3:4] * jnp.exp(last) * flow + ends
    grad_da = mm(triback[...], grad_cum, precision=highest) + grad_tot
    a = avec[0:1, :]
    grad_dtv = grad_dt + grad_da * a
    grad_dtpre = grad_dtv * jax.nn.sigmoid(dtp[...] + dtb[0:1, :])
    vecs[0:1, :] += jnp.sum(grad_da * dt, axis=0, keepdims=True) * a
    vecs[1:2, :] += jnp.sum(grad_dtpre, axis=0, keepdims=True)
    slope = silu_slope(pre, sigma)
    grad_pre = jnp.concatenate([dx, db, dc], axis=1) * slope
    gtaps[4:5, :] += jnp.sum(grad_pre, axis=0, keepdims=True)
    rows = cin[...]
    grad_rows = taps[CONV - 1 : CONV, :] * grad_pre
    gtaps[3:4, :] += jnp.sum(rows * grad_pre, axis=0, keepdims=True)
    masked = []
    for k in range(CONV - 1):
        m = grad_pre * mask[:, k : k + 1]
        masked.append(m[:ROWS])
        ahead = CONV - 1 - k
        shifted = jnp.concatenate([m, nexts[k]], axis=0)[ahead : ahead + GROUP]
        grad_rows = grad_rows + taps[k : k + 1, :] * shifted
        gtaps[k : k + 1, :] += jnp.sum(rows * shifted, axis=0, keepdims=True)
    for k in range(CONV - 1):
        nexts[k] = masked[k]
    gall[:, :inner] = dz[...]
    gall[:, inner : 2 * inner + BC] = grad_rows.astype(bf16)
    gall[:, 2 * inner + BC :] = grad_dtpre.astype(bf16)

    @pl.when(step == 0)
    def _():
        last8[...] = grad_rows[GROUP - ROWS :]

    @pl.when(step == pl.num_programs(0) - 1)
    def _():
        spill = jnp.zeros((ROWS, inner + BC), f32)
        edge = halo[...]
        for k in range(CONV - 1):
            down = ROWS - CONV + 1 + k
            moved = jnp.concatenate([jnp.zeros((ROWS, inner + BC), f32), masked[k]], axis=0)
            moved = moved[ROWS - down : 2 * ROWS - down]
            spill = spill + taps[k : k + 1, :] * moved
            gtaps[k : k + 1, :] += jnp.sum(edge * moved, axis=0, keepdims=True)
        rim[...] = spill


def whole(shape):
    return pl.BlockSpec(shape, lambda c: (0,) * len(shape))


def by_rows(cols, count, reverse=False):
    if reverse:
        return pl.BlockSpec((GROUP, cols), lambda c: (count - 1 - c, 0))
    return pl.BlockSpec((GROUP, cols), lambda c: (c, 0))


def by_group(shape, count, reverse=False):
    if reverse:
        return pl.BlockSpec((1,) + shape, lambda c: (count - 1 - c, 0, 0))
    return pl.BlockSpec((1,) + shape, lambda c: (c, 0, 0))


def by_cols(count):
    return pl.BlockSpec((ROWS, GROUP), lambda c: (0, c))


def call(kernel, count, ins, outs, scratch, flops, name):
    return pl.pallas_call(
        kernel,
        grid=(count,),
        in_specs=[spec for spec, _ in ins],
        out_specs=[spec for spec, _ in outs],
        out_shape=[shape for _, shape in outs],
        scratch_shapes=scratch,
        compiler_params=pltpu.CompilerParams(
            dimension_semantics=("arbitrary",), vmem_limit_bytes=56 * 1024 * 1024
        ),
        cost_estimate=pl.CostEstimate(
            flops=flops, bytes_accessed=8 * 1024 * 1024, transcendentals=0
        ),
        name=name,
    )(*[value for _, value in ins])


def shape(*dims, dtype=f32):
    return jax.ShapeDtypeStruct(dims, dtype)


def shifted(value, axis, steps):
    count = lax.axis_size(axis)
    leading, last = (max(0, -steps), min(count, count - steps))
    return lax.ppermute(value, axis, [(source, source + steps) for source in range(leading, last)])


def chain(part, axis, reverse):
    count = lax.axis_size(axis)
    place = lax.axis_index(axis)
    gathered = lax.all_gather(part, axis)
    decay = gathered[:, STATE]
    source = jnp.arange(count)[:, None, None]
    middle = jnp.arange(count)[None, :, None]
    if reverse:
        between = (middle < source) & (middle > place)
        ahead = jnp.arange(count) > place
    else:
        between = (middle > source) & (middle < place)
        ahead = jnp.arange(count) < place
    weight = jnp.prod(jnp.where(between, decay[None], 1.0), axis=1)
    weight = jnp.where(ahead[:, None], weight, 0.0)
    return jnp.sum(weight[:, None, :] * gathered[:, :STATE], axis=0)


def eight(row):
    return jnp.broadcast_to(row[None, :], (ROWS, row.shape[0]))


def pad_lanes(value):
    return jnp.pad(value, [(0, 0)] * (value.ndim - 1) + [(0, LANES - value.shape[-1])])


def shards(
    x_input,
    seg_ids,
    cotangent,
    norm_gain,
    w_z,
    w_x,
    w_bc,
    w_dt,
    conv_x,
    conv_bc,
    bias_x,
    bias_bc,
    dt_bias,
    a_log,
    d_skip,
    gate_gain,
    w_out,
):
    tok, width = x_input.shape
    inner = w_z.shape[2]
    heads = w_dt.shape[2]
    count = tok // GROUP
    conv_cols = inner + BC
    all_cols = 2 * inner + BC + LANES

    seg = seg_ids.astype(f32)
    edge_seg = shifted(seg[tok - ROWS :], "seq", 1)
    seg_ext = jnp.concatenate([edge_seg, seg])
    before = jnp.concatenate([edge_seg[ROWS - 1 :], seg[GROUP - 1 : tok - 1 : GROUP]])
    after = seg[GROUP - 1 :: GROUP]
    mask = jnp.stack(
        [
            (seg_ext[ROWS - CONV + 1 + k : ROWS - CONV + 1 + k + tok] == seg).astype(f32)
            for k in range(CONV - 1)
        ]
        + [
            (seg == jnp.repeat(before, GROUP)).astype(f32),
            (seg == jnp.repeat(after, GROUP)).astype(f32),
            seg,
            seg,
            seg,
        ],
        axis=1,
    )
    seg_col = seg[:, None]
    seg_row = eight(seg)
    expand = (jnp.arange(LANES)[:, None] == jnp.arange(inner)[None, :] // HEADDIM).astype(f32)
    position = jnp.arange(GROUP)
    tri = (position[:, None] >= position[None, :]).astype(f32)
    triback = (position[:, None] <= position[None, :]).astype(f32)

    matmul_flops = 2 * tok * width
    hidden = x_input
    stored = []
    for layer in range(LAYERS):
        wall = jnp.concatenate(
            [w_z[layer], w_x[layer], w_bc[layer], pad_lanes(w_dt[layer])], axis=1
        )
        taps = jnp.concatenate([conv_x[layer], conv_bc[layer]], axis=1)
        bias = eight(jnp.concatenate([bias_x[layer], bias_bc[layer]]))
        dtb = eight(pad_lanes(dt_bias[layer]))
        avec = eight(pad_lanes(-jnp.exp(a_log[layer])))
        dskip = eight(jnp.repeat(d_skip[layer], HEADDIM))
        ggain = eight(gate_gain[layer])
        ngain = norm_gain[layer][None, :]
        end = hidden[tok - 16 :].astype(f32)
        end = end * lax.rsqrt(jnp.mean(end * end, axis=1, keepdims=True) + epsilon) * ngain
        end = mm(end.astype(bf16), wall[:, inner : 2 * inner + BC])[ROWS:]
        halo = shifted(end, "seq", 1)
        normed, zval, cin, cpre, dtp, cum, dtv, xdt, bc, sloc, pref, send = call(
            in_kernel,
            count,
            [
                (by_rows(width, count), hidden),
                (whole((width, all_cols)), wall),
                (whole((1, width)), ngain),
                (whole((CONV, conv_cols)), taps),
                (whole((ROWS, conv_cols)), bias),
                (whole((ROWS, LANES)), dtb),
                (whole((ROWS, LANES)), avec),
                (by_rows(ROWS, count), mask),
                (whole((ROWS, conv_cols)), halo),
                (whole((LANES, inner)), expand),
                (whole((GROUP, GROUP)), tri),
            ],
            [
                (by_rows(width, count), shape(tok, width, dtype=bf16)),
                (by_rows(inner, count), shape(tok, inner)),
                (by_rows(conv_cols, count), shape(tok, conv_cols)),
                (by_rows(conv_cols, count), shape(tok, conv_cols)),
                (by_rows(LANES, count), shape(tok, LANES)),
                (by_rows(LANES, count), shape(tok, LANES)),
                (by_rows(LANES, count), shape(tok, LANES)),
                (by_rows(inner, count), shape(tok, inner, dtype=bf16)),
                (by_rows(BC, count), shape(tok, BC, dtype=bf16)),
                (by_group((STATE, inner), count), shape(count, STATE, inner)),
                (by_group((ROWS, inner), count), shape(count, ROWS, inner)),
                (whole((STATE + ROWS, inner)), shape(STATE + ROWS, inner)),
            ],
            [
                pltpu.VMEM((STATE, inner), f32),
                pltpu.VMEM((ROWS, inner), f32),
                pltpu.VMEM((ROWS, conv_cols), f32),
            ],
            matmul_flops * all_cols,
            "in_proj_conv",
        )
        (yin,) = call(
            intra_kernel,
            count,
            [
                (by_rows(LANES, count), cum),
                (by_rows(inner, count), xdt),
                (by_rows(BC, count), bc),
                (by_rows(1, count), seg_col),
                (by_cols(count), seg_row),
            ],
            [(by_rows(inner, count), shape(tok, inner))],
            [],
            matmul_flops * 512,
            "ssd_within",
        )
        entry = chain(send, "seq", False)
        y, gate_in, proj, sums = call(
            out_kernel,
            count,
            [
                (by_rows(inner, count), yin),
                (by_rows(inner, count), cpre),
                (by_rows(LANES, count), cum),
                (by_rows(BC, count), bc),
                (by_rows(ROWS, count), mask),
                (by_rows(inner, count), zval),
                (by_group((STATE, inner), count), sloc),
                (by_group((ROWS, inner), count), pref),
                (whole((STATE, inner)), entry),
                (whole((ROWS, inner)), dskip),
                (whole((ROWS, inner)), ggain),
                (whole((width, inner)), w_out[layer]),
                (whole((LANES, inner)), expand),
                (by_rows(width, count), cotangent),
            ],
            [
                (by_rows(inner, count), shape(tok, inner)),
                (by_rows(inner, count), shape(tok, inner, dtype=bf16)),
                (by_rows(width, count), shape(tok, width)),
                (by_cols(count), shape(ROWS, tok)),
            ],
            [],
            matmul_flops * 2 * inner,
            "gate_out_proj",
        )
        sums = lax.psum(sums, "head")
        proj_sum = lax.psum(proj, "head")
        gate_scale = lax.rsqrt(sums[0] / INNER + epsilon)
        stored.append(
            dict(
                hidden=hidden, normed=normed, zval=zval, cin=cin, cpre=cpre, dtp=dtp, cum=cum,
                dtv=dtv, xdt=xdt, bc=bc, sloc=sloc, pref=pref, entry=entry, y=y, gate_in=gate_in,
                proj_sum=proj_sum, gate_scale=gate_scale, dots=sums[1], halo=halo, wall=wall,
                taps=taps, dtb=dtb, avec=avec, dskip=dskip, ggain=ggain,
            )
        )
        hidden = hidden.astype(f32) + gate_scale[:, None] * proj_sum
    final_out = hidden.astype(bf16)

    grad_h = cotangent
    matrices = [None] * LAYERS
    vectors = [None] * LAYERS
    shared = [None] * LAYERS
    for layer in reversed(range(LAYERS)):
        kept = stored[layer]
        gate_scale = kept["gate_scale"]
        if layer == LAYERS - 1:
            grad_scale = kept["dots"]
        else:
            grad_scale = jnp.sum(grad_h * kept["proj_sum"], axis=1)
        gsq = -grad_scale * gate_scale**3 / INNER
        rev = functools.partial(by_rows, count=count, reverse=True)
        rev_group = functools.partial(by_group, count=count, reverse=True)
        gproj, dy, dz, gloc, suf, gsend, acc = call(
            gate_kernel,
            count,
            [
                (rev(width), grad_h),
                (rev(1), gate_scale[:, None]),
                (rev(1), gsq[:, None]),
                (rev(inner), kept["y"]),
                (rev(inner), kept["zval"]),
                (whole((ROWS, inner)), kept["ggain"]),
                (whole((width, inner)), w_out[layer]),
                (rev(LANES), kept["cum"]),
                (rev(BC), kept["bc"]),
                (rev(ROWS), mask),
                (whole((LANES, inner)), expand),
            ],
            [
                (rev(width), shape(tok, width, dtype=bf16)),
                (rev(inner), shape(tok, inner, dtype=bf16)),
                (rev(inner), shape(tok, inner, dtype=bf16)),
                (rev_group((STATE, inner)), shape(count, STATE, inner)),
                (rev_group((ROWS, inner)), shape(count, ROWS, inner)),
                (whole((STATE + ROWS, inner)), shape(STATE + ROWS, inner)),
                (whole((ROWS, inner)), shape(ROWS, inner)),
            ],
            [pltpu.VMEM((STATE, inner), f32), pltpu.VMEM((ROWS, inner), f32)],
            matmul_flops * inner,
            "gate_back",
        )
        u, dbc = call(
            intra_back_kernel,
            count,
            [
                (by_rows(LANES, count), kept["cum"]),
                (by_rows(inner, count), kept["xdt"]),
                (by_rows(BC, count), kept["bc"]),
                (by_rows(1, count), seg_col),
                (by_cols(count), seg_row),
                (by_rows(inner, count), dy),
            ],
            [
                (by_rows(inner, count), shape(tok, inner)),
                (by_rows(BC, count), shape(tok, BC)),
            ],
            [],
            matmul_flops * 1024,
            "ssd_within_back",
        )
        gout = chain(gsend, "seq", True)
        grad_wout = mm(gproj, kept["gate_in"], ((0,), (0,)))
        gall, last8, rim, gtaps, vecs, dsk = call(
            in_back_kernel,
            count,
            [
                (rev(inner), u),
                (rev(BC), dbc),
                (rev(inner), dy),
                (rev(inner), dz),
                (rev(inner), kept["y"]),
                (rev(conv_cols), kept["cpre"]),
                (rev(conv_cols), kept["cin"]),
                (rev(LANES), kept["dtp"]),
                (rev(LANES), kept["dtv"]),
                (rev(LANES), kept["cum"]),
                (rev(inner), kept["xdt"]),
                (rev(BC), kept["bc"]),
                (rev(ROWS), mask),
                (rev_group((STATE, inner)), kept["sloc"]),
                (rev_group((ROWS, inner)), kept["pref"]),
                (whole((STATE, inner)), kept["entry"]),
                (rev_group((STATE, inner)), gloc),
                (rev_group((ROWS, inner)), suf),
                (whole((STATE, inner)), gout),
                (whole((ROWS, conv_cols)), kept["halo"]),
                (whole((CONV, conv_cols)), kept["taps"]),
                (whole((ROWS, LANES)), kept["dtb"]),
                (whole((ROWS, LANES)), kept["avec"]),
                (whole((ROWS, inner)), kept["dskip"]),
                (whole((LANES, inner)), expand),
                (whole((GROUP, GROUP)), triback),
            ],
            [
                (rev(all_cols), shape(tok, all_cols, dtype=bf16)),
                (whole((ROWS, conv_cols)), shape(ROWS, conv_cols)),
                (whole((ROWS, conv_cols)), shape(ROWS, conv_cols)),
                (whole((ROWS, conv_cols)), shape(ROWS, conv_cols)),
                (whole((ROWS, LANES)), shape(ROWS, LANES)),
                (whole((ROWS, inner)), shape(ROWS, inner)),
            ],
            [pltpu.VMEM((CONV - 1, ROWS, conv_cols), f32)],
            matmul_flops * 1024,
            "in_proj_conv_back",
        )
        rim_back = shifted(rim, "seq", -1)
        gall = lax.dynamic_update_slice(
            gall, (last8 + rim_back).astype(bf16), (tok - ROWS, inner)
        )
        grad_normed = lax.psum(mm(gall, kept["wall"], ((1,), (1,))), "head")
        grad_win = mm(kept["normed"], gall, ((0,), (0,)))
        matrices[layer] = (
            lax.psum_scatter(grad_win, "seq", scatter_dimension=0, tiled=True),
            lax.psum_scatter(grad_wout, "seq", scatter_dimension=0, tiled=True),
        )
        hidden_in = kept["hidden"].astype(f32)
        inv = lax.rsqrt(jnp.mean(hidden_in * hidden_in, axis=1, keepdims=True) + epsilon)
        grad_ngain = jnp.sum(grad_normed * hidden_in * inv, axis=0)
        back = grad_normed * norm_gain[layer][None, :]
        grad_h = grad_h.astype(f32) + inv * (
            back - hidden_in * inv * inv * jnp.mean(back * hidden_in, axis=1, keepdims=True)
        )
        vectors[layer] = jnp.concatenate(
            [
                grad_ngain,
                gtaps[: CONV + 1, :inner].reshape(-1),
                acc[0],
                vecs[0],
                vecs[1],
                dsk[0],
            ]
        )
        shared[layer] = gtaps[: CONV + 1, inner:]
    vector = jnp.stack(vectors)
    share = jnp.stack(shared).reshape(LAYERS, -1)
    vector = lax.psum(jnp.concatenate([vector, share], axis=1), "seq")
    share = vector[:, -(CONV + 1) * BC :]
    grad_wbc = jnp.stack([m[0][:, 2 * inner : 2 * inner + BC] for m in matrices])
    share_all = lax.psum(
        jnp.concatenate([grad_wbc.reshape(LAYERS, -1), share], axis=1), "head"
    )
    grad_wbc = share_all[:, : -(CONV + 1) * BC].reshape(grad_wbc.shape)
    share = share_all[:, -(CONV + 1) * BC :].reshape(LAYERS, CONV + 1, BC)
    at = 0
    pieces = []
    for size in (width, CONV * inner, inner, inner, LANES, LANES, inner):
        pieces.append(vector[:, at : at + size])
        at += size
    g_ngain, g_conv, g_bias, g_ggain, g_alog, g_dtb, g_dsk = pieces
    g_win = jnp.stack([m[0] for m in matrices])
    return (
        final_out,
        grad_h,
        g_ngain,
        g_win[:, :, :inner],
        g_win[:, :, inner : 2 * inner],
        grad_wbc,
        g_win[:, :, 2 * inner + BC : 2 * inner + BC + heads],
        g_conv.reshape(LAYERS, CONV, inner),
        share[:, :CONV],
        g_bias,
        share[:, CONV],
        g_dtb[:, :heads],
        g_alog[:, :heads],
        jnp.sum(g_dsk.reshape(LAYERS, heads, HEADDIM), axis=2),
        g_ggain,
        jnp.stack([m[1] for m in matrices]),
    )


def solution(mesh):
    placed = (
        P("seq", None),
        P("seq"),
        P("seq", None),
        P(),
        P(None, None, "head"),
        P(None, None, "head"),
        P(),
        P(None, None, "head"),
        P(None, None, "head"),
        P(),
        P(None, "head"),
        P(),
        P(None, "head"),
        P(None, "head"),
        P(None, "head"),
        P(None, "head"),
        P(None, None, "head"),
    )
    return jax.shard_map(
        shards,
        mesh=mesh,
        in_specs=placed,
        out_specs=(
            P("seq", None),
            P("seq", None),
            P(),
            P(None, "seq", "head"),
            P(None, "seq", "head"),
            P(None, "seq", None),
            P(None, "seq", "head"),
            P(None, None, "head"),
            P(),
            P(None, "head"),
            P(),
            P(None, "head"),
            P(None, "head"),
            P(None, "head"),
            P(None, "head"),
            P(None, "seq", "head"),
        ),
        check_vma=False,
    )
```

```python
import functools

import jax
import jax.numpy as jnp
from jax import lax
from jax.experimental import pallas as pl
from jax.experimental.pallas import tpu as pltpu
from jax.sharding import PartitionSpec as P

HEADDIM = 64
STATE = 128
CONV = 4
GROUP = 256
LAYERS = 2
INNER = 2048
LANES = 128
ROWS = 8
BC = 2 * STATE

epsilon = 1e-05
highest = lax.Precision.HIGHEST
f32 = jnp.float32
bf16 = jnp.bfloat16


def mm(left, right, dims=((1,), (0,)), precision=None):
    return lax.dot_general(
        left, right, (dims, ((), ())), preferred_element_type=f32, precision=precision
    )


def softplus(value):
    small = jnp.exp(-jnp.abs(value))
    series = small * (1.0 - small * (0.5 - small * (1.0 / 3.0 - small * (0.25 - small * 0.2))))
    return jnp.maximum(value, 0.0) + jnp.where(small < 0.03, series, jnp.log(1.0 + small))


def silu_slope(value, sigma):
    return sigma * (1.0 + value * (1.0 - sigma))


def spread(heads, expand):
    return mm(heads, expand, precision=highest)


def gather_heads(lanes, expand):
    return mm(lanes, expand, ((1,), (1,)), precision=highest)


def in_kernel(
    hid, wall, ngain, taps, bias, dtb, avec, mask, halo, expand, tri,
    normed, zval, cin, cpre, dtp, cum, dtv, xdt, bc, sloc, pref, send,
    state, thru, prev,
):
    step = pl.program_id(0)
    inner = expand.shape[1]

    @pl.when(step == 0)
    def _():
        state[...] = jnp.zeros_like(state)
        thru[...] = jnp.ones_like(thru)
        prev[...] = halo[...]

    h = hid[...].astype(f32)
    inv = lax.rsqrt(jnp.mean(h * h, axis=1, keepdims=True) + epsilon)
    low = (h * inv * ngain[...]).astype(bf16)
    normed[...] = low
    zval[...] = mm(low, wall[:, :inner])
    rows = mm(low, wall[:, inner : 2 * inner + BC])
    pre_dt = mm(low, wall[:, 2 * inner + BC :])
    dtp[...] = pre_dt
    cin[...] = rows
    ext = jnp.concatenate([prev[...], rows], axis=0)
    prev[...] = rows[GROUP - ROWS :]
    total = taps[CONV - 1 : CONV, :] * rows + bias[0:1, :]
    for k in range(CONV - 1):
        first = ROWS - CONV + 1 + k
        total = total + taps[k : k + 1, :] * ext[first : first + GROUP] * mask[:, k : k + 1]
    cpre[...] = total
    act = total * jax.nn.sigmoid(total)
    x = act[:, :inner]
    low_bc = act[:, inner:].astype(bf16)
    bc[...] = low_bc
    dt = softplus(pre_dt + dtb[0:1, :])
    dtv[...] = dt
    run = mm(tri[...], dt * avec[0:1, :], precision=highest)
    cum[...] = run
    last = run[GROUP - 1 : GROUP]
    xdt[...] = (x * spread(dt, expand[...])).astype(bf16)
    tail = jnp.exp(last - run) * mask[:, 4:5] * dt
    contrib = mm(low_bc[:, :STATE], (x * spread(tail, expand[...])).astype(bf16), ((0,), (0,)))
    through = jnp.broadcast_to(jnp.exp(last) * mask[GROUP - 1 : GROUP, 3:4], (ROWS, LANES))
    through = spread(through, expand[...])
    sloc[0] = state[...]
    pref[0] = thru[...]
    state[...] = through[0:1] * state[...] + contrib
    thru[...] = thru[...] * through

    @pl.when(step == pl.num_programs(0) - 1)
    def _():
        send[:STATE] = state[...]
        send[STATE:] = thru[...]


def pair_lanes(value, which):
    lane = lax.broadcasted_iota(jnp.int32, value.shape, 1)
    keep = lane < HEADDIM if which == 0 else lane >= HEADDIM
    return jnp.where(keep, value, jnp.zeros_like(value))


def intra_kernel(cum, xdt, bc, seg, segrow, y):
    inner = xdt.shape[1]
    run = cum[...]
    run_t = run.T
    base = mm(bc[:, STATE:], bc[:, :STATE], ((1,), (1,)))
    t_at = lax.broadcasted_iota(jnp.int32, (GROUP, GROUP), 0)
    s_at = lax.broadcasted_iota(jnp.int32, (GROUP, GROUP), 1)
    same = (seg[:, 0:1] == segrow[0:1, :]) & (t_at >= s_at)
    closed = jnp.where(same, 0.0, -1e30)
    for pair in range(inner // LANES):
        cols = slice(pair * LANES, (pair + 1) * LANES)
        xs = xdt[:, cols]
        parts = []
        for which in range(2):
            head = 2 * pair + which
            decay = jnp.exp(run[:, head : head + 1] - run_t[head : head + 1, :] + closed)
            parts.append(mm((decay * base).astype(bf16), xs))
        lane = lax.broadcasted_iota(jnp.int32, (GROUP, LANES), 1)
        y[:, cols] = jnp.where(lane < HEADDIM, parts[0], parts[1])


def out_kernel(
    yin, cpre, cum, bc, mask, zval, sloc, pref, entry, dskip, ggain, wout, expand, cot,
    y, gate_in, proj, sums,
):
    inner = expand.shape[1]
    pre = cpre[...]
    x = pre * jax.nn.sigmoid(pre)
    full = sloc[0] + pref[0][0:1] * entry[...]
    reach = spread(jnp.exp(cum[...]) * mask[:, 3:4], expand[...])
    value = yin[...] + reach * mm(bc[:, STATE:], full.astype(bf16)) + dskip[0:1, :] * x
    y[...] = value
    z = zval[...]
    gated = value * (z * jax.nn.sigmoid(z))
    low = (gated * ggain[0:1, :]).astype(bf16)
    gate_in[...] = low
    proj[...] = mm(low, wout[...], ((1,), (1,)))
    ones = jnp.ones((ROWS, inner), f32)
    squares = mm(ones, gated * gated, ((1,), (1,)), precision=highest)
    back = mm(cot[...].astype(bf16), wout[...])
    dots = mm(ones, low.astype(f32) * back, ((1,), (1,)), precision=highest)
    row = lax.broadcasted_iota(jnp.int32, squares.shape, 0)
    sums[...] = jnp.where(row == 0, squares, dots)


def gate_kernel(
    gh, scale, gsq, y, zval, ggain, wout, cum, bc, mask, expand,
    gproj, dy, dz, gloc, suf, send, acc,
    carry, thru,
):
    step = pl.program_id(0)

    @pl.when(step == 0)
    def _():
        carry[...] = jnp.zeros_like(carry)
        thru[...] = jnp.ones_like(thru)
        acc[...] = jnp.zeros_like(acc)

    gp = (scale[...] * gh[...].astype(f32)).astype(bf16)
    gproj[...] = gp
    ggi = mm(gp, wout[...])
    z = zval[...]
    sigma = jax.nn.sigmoid(z)
    silu = z * sigma
    value = y[...]
    gated = value * silu
    ggated = ggi * ggain[0:1, :] + gated * gsq[...]
    acc[0:1, :] += jnp.sum(ggi * gated, axis=0, keepdims=True)
    low = (ggated * silu).astype(bf16)
    dy[...] = low
    dz[...] = (ggated * value * silu_slope(z, sigma)).astype(bf16)
    run = cum[...]
    last = run[GROUP - 1 : GROUP]
    reach = spread(jnp.exp(run) * mask[:, 3:4], expand[...])
    back = mm(bc[:, STATE:], (reach * low.astype(f32)).astype(bf16), ((0,), (0,)))
    through = jnp.broadcast_to(jnp.exp(last) * mask[GROUP - 1 : GROUP, 3:4], (ROWS, LANES))
    through = spread(through, expand[...])
    gloc[0] = carry[...]
    suf[0] = thru[...]
    carry[...] = back + through[0:1] * carry[...]
    thru[...] = thru[...] * through

    @pl.when(step == pl.num_programs(0) - 1)
    def _():
        send[:STATE] = carry[...]
        send[STATE:] = thru[...]


def intra_back_kernel(cum, xdt, bc, seg, segrow, dy, u, dbc):
    inner = xdt.shape[1]
    run = cum[...]
    run_t = run.T
    base = mm(bc[:, :STATE], bc[:, STATE:], ((1,), (1,)))
    s_at = lax.broadcasted_iota(jnp.int32, (GROUP, GROUP), 0)
    t_at = lax.broadcasted_iota(jnp.int32, (GROUP, GROUP), 1)
    same = (seg[:, 0:1] == segrow[0:1, :]) & (t_at >= s_at)
    closed = jnp.where(same, 0.0, -1e30)
    grad_base = jnp.zeros((GROUP, GROUP), f32)
    for pair in range(inner // LANES):
        cols = slice(pair * LANES, (pair + 1) * LANES)
        xs = xdt[:, cols]
        ds = dy[:, cols]
        parts = []
        for which in range(2):
            head = 2 * pair + which
            decay = jnp.exp(run_t[head : head + 1, :] - run[:, head : head + 1] + closed)
            parts.append(mm((decay * base).astype(bf16), ds))
            grad_base = grad_base + decay * mm(xs, pair_lanes(ds, which), ((1,), (1,)))
        lane = lax.broadcasted_iota(jnp.int32, (GROUP, LANES), 1)
        u[:, cols] = jnp.where(lane < HEADDIM, parts[0], parts[1])
    low = grad_base.astype(bf16)
    dbc[:, :STATE] = mm(low, bc[:, STATE:])
    dbc[:, STATE:] = mm(low, bc[:, :STATE], ((0,), (0,)))


def in_back_kernel(
    uin, dbc, dy, dz, y, cpre, cin, dtp, dtv, cum, xdt, bc, mask, sloc, pref, entry, gloc, suf,
    gout, halo, taps, dtb, avec, dskip, expand, triback,
    gall, last8, rim, gtaps, vecs, dsk,
    nexts,
):
    step = pl.program_id(0)
    inner = expand.shape[1]

    @pl.when(step == 0)
    def _():
        nexts[...] = jnp.zeros_like(nexts)
        gtaps[...] = jnp.zeros_like(gtaps)
        vecs[...] = jnp.zeros_like(vecs)
        dsk[...] = jnp.zeros_like(dsk)

    e = expand[...]
    pre = cpre[...]
    sigma = jax.nn.sigmoid(pre)
    x = (pre * sigma)[:, :inner]
    full = sloc[0] + pref[0][0:1] * entry[...]
    nxt = gloc[0] + suf[0][0:1] * gout[...]
    nxt_low = nxt.astype(bf16)
    run = cum[...]
    last = run[GROUP - 1 : GROUP]
    dt = dtv[...]
    low_dy = dy[...].astype(f32)
    xw = xdt[...].astype(f32)
    tail = spread(jnp.exp(last - run) * mask[:, 4:5], e)
    reach = spread(jnp.exp(run) * mask[:, 3:4], e)
    u_inter = tail * mm(bc[:, :STATE], nxt_low)
    u = uin[...] + u_inter
    dx = spread(dt, e) * u + dskip[0:1, :] * low_dy
    dsk[0:1, :] += jnp.sum(low_dy * x, axis=0, keepdims=True)
    db = dbc[:, :STATE] + mm((tail * xw).astype(bf16), nxt_low, ((1,), (1,)))
    dc = dbc[:, STATE:] + mm((reach * low_dy).astype(bf16), full.astype(bf16), ((1,), (1,)))
    grad_dt = gather_heads(x * u, e)
    y_plain = y[...] - dskip[0:1, :] * x
    grad_cum = gather_heads(low_dy * y_plain - xw * u, e)
    flow = jnp.sum(nxt * full, axis=0, keepdims=True)
    flow = gather_heads(jnp.broadcast_to(flow, (ROWS, inner)), e)[0:1]
    ends = jnp.sum(xw * u_inter, axis=0, keepdims=True)
    ends = gather_heads(jnp.broadcast_to(ends, (ROWS, inner)), e)[0:1]
    grad_tot = mask[GROUP - 1 : GROUP, 3:4] * jnp.exp(last) * flow + ends
    grad_da = mm(triback[...], grad_cum, precision=highest) + grad_tot
    a = avec[0:1, :]
    grad_dtv = grad_dt + grad_da * a
    grad_dtpre = grad_dtv * jax.nn.sigmoid(dtp[...] + dtb[0:1, :])
    vecs[0:1, :] += jnp.sum(grad_da * dt, axis=0, keepdims=True) * a
    vecs[1:2, :] += jnp.sum(grad_dtpre, axis=0, keepdims=True)
    slope = silu_slope(pre, sigma)
    grad_pre = jnp.concatenate([dx, db, dc], axis=1) * slope
    gtaps[4:5, :] += jnp.sum(grad_pre, axis=0, keepdims=True)
    rows = cin[...]
    grad_rows = taps[CONV - 1 : CONV, :] * grad_pre
    gtaps[3:4, :] += jnp.sum(rows * grad_pre, axis=0, keepdims=True)
    masked = []
    for k in range(CONV - 1):
        m = grad_pre * mask[:, k : k + 1]
        masked.append(m[:ROWS])
        ahead = CONV - 1 - k
        shifted = jnp.concatenate([m, nexts[k]], axis=0)[ahead : ahead + GROUP]
        grad_rows = grad_rows + taps[k : k + 1, :] * shifted
        gtaps[k : k + 1, :] += jnp.sum(rows * shifted, axis=0, keepdims=True)
    for k in range(CONV - 1):
        nexts[k] = masked[k]
    gall[:, :inner] = dz[...]
    gall[:, inner : 2 * inner + BC] = grad_rows.astype(bf16)
    gall[:, 2 * inner + BC :] = grad_dtpre.astype(bf16)

    @pl.when(step == 0)
    def _():
        last8[...] = grad_rows[GROUP - ROWS :]

    @pl.when(step == pl.num_programs(0) - 1)
    def _():
        spill = jnp.zeros((ROWS, inner + BC), f32)
        edge = halo[...]
        for k in range(CONV - 1):
            down = ROWS - CONV + 1 + k
            moved = jnp.concatenate([jnp.zeros((ROWS, inner + BC), f32), masked[k]], axis=0)
            moved = moved[ROWS - down : 2 * ROWS - down]
            spill = spill + taps[k : k + 1, :] * moved
            gtaps[k : k + 1, :] += jnp.sum(edge * moved, axis=0, keepdims=True)
        rim[...] = spill


def whole(shape):
    return pl.BlockSpec(shape, lambda c: (0,) * len(shape))


def by_rows(cols, count, reverse=False):
    if reverse:
        return pl.BlockSpec((GROUP, cols), lambda c: (count - 1 - c, 0))
    return pl.BlockSpec((GROUP, cols), lambda c: (c, 0))


def by_group(shape, count, reverse=False):
    if reverse:
        return pl.BlockSpec((1,) + shape, lambda c: (count - 1 - c, 0, 0))
    return pl.BlockSpec((1,) + shape, lambda c: (c, 0, 0))


def by_cols(count):
    return pl.BlockSpec((ROWS, GROUP), lambda c: (0, c))


def call(kernel, count, ins, outs, scratch, flops, name):
    return pl.pallas_call(
        kernel,
        grid=(count,),
        in_specs=[spec for spec, _ in ins],
        out_specs=[spec for spec, _ in outs],
        out_shape=[shape for _, shape in outs],
        scratch_shapes=scratch,
        compiler_params=pltpu.CompilerParams(
            dimension_semantics=("arbitrary",), vmem_limit_bytes=56 * 1024 * 1024
        ),
        cost_estimate=pl.CostEstimate(
            flops=flops, bytes_accessed=8 * 1024 * 1024, transcendentals=0
        ),
        name=name,
    )(*[value for _, value in ins])


def shape(*dims, dtype=f32):
    return jax.ShapeDtypeStruct(dims, dtype)


SWAP = ((0, 1), (1, 0))
CROSS = ((0, 1), (3, 2))
CROSS_BACK = ((1, 0), (2, 3))
CORE_OUT = ((0, 2), (3, 1))
CORE_IN = ((2, 0), (1, 3))
DIAGONAL = ((2, 1), (1, 2))
BOTH = ("core", "zh")
BLOCKS = ("chip", "zh")


def shifted(value, steps):
    count = lax.axis_size(BLOCKS)
    leading, last = (max(0, -steps), min(count, count - steps))
    return lax.ppermute(value, BLOCKS, [(source, source + steps) for source in range(leading, last)])


def chain(part, reverse):
    count = lax.axis_size(BLOCKS)
    place = lax.axis_index(BLOCKS)
    gathered = lax.all_gather(part, BLOCKS)
    decay = gathered[:, STATE]
    source = jnp.arange(count)[:, None, None]
    middle = jnp.arange(count)[None, :, None]
    if reverse:
        between = (middle < source) & (middle > place)
        ahead = jnp.arange(count) > place
    else:
        between = (middle > source) & (middle < place)
        ahead = jnp.arange(count) < place
    weight = jnp.prod(jnp.where(between, decay[None], 1.0), axis=1)
    weight = jnp.where(ahead[:, None], weight, 0.0)
    return jnp.sum(weight[:, None, :] * gathered[:, :STATE], axis=0)


def swap(value, axis):
    return lax.ppermute(value, axis, SWAP)


def total(value, axes):
    for axis in axes:
        count = lax.axis_size(axis)
        step = 1
        while step < count:
            value = value + lax.ppermute(value, axis, [(i, i ^ step) for i in range(count)])
            step *= 2
    return value


def take(value, index, count):
    size = value.shape[0] // count
    return lax.dynamic_slice_in_dim(value, index * size, size)


def ordered(place, mine, theirs):
    return jnp.where(
        place == 0, jnp.concatenate([mine, theirs]), jnp.concatenate([theirs, mine])
    )


def scatter_sum(part):
    core, near = lax.axis_index("core"), lax.axis_index("zl")
    half = take(part, core, 2) + swap(take(part, 1 - core, 2), "core")
    if lax.axis_size("zl") == 2:
        return take(half, near, 2) + swap(take(half, 1 - near, 2), "zl")
    return lax.psum_scatter(half, "zl", scatter_dimension=0, tiled=True)


def own_rows(value):
    core, near = lax.axis_index("core"), lax.axis_index("zl")
    return take(take(value, core, 2), near, lax.axis_size("zl"))


def gather_near(value):
    if lax.axis_size("zl") == 2:
        return ordered(lax.axis_index("zl"), value, swap(value, "zl"))
    return lax.all_gather(value, "zl", tiled=True)


def gather_rows(value):
    half = gather_near(value)
    return ordered(lax.axis_index("core"), half, swap(half, "core"))


def deliver(value):
    core, far = lax.axis_index("core"), lax.axis_index("zh")
    mine = lax.ppermute(value, BOTH, CROSS)
    theirs = lax.ppermute(value, BOTH, DIAGONAL)
    near = lax.ppermute(value, BOTH, CORE_IN)
    held = core == far
    mine = gather_near(jnp.where(held, value, mine))
    theirs = gather_near(jnp.where(held, near, theirs))
    return ordered(core, mine, theirs)


def to_block(value):
    got = lax.ppermute(value, BOTH, CORE_OUT)
    return jnp.where(lax.axis_index("core") == lax.axis_index("zh"), value, got)


def eight(row):
    return jnp.broadcast_to(row[None, :], (ROWS, row.shape[0]))


def pad_lanes(value):
    return jnp.pad(value, [(0, 0)] * (value.ndim - 1) + [(0, LANES - value.shape[-1])])


def weight_kernel(place, own_z, own_x, own_out, bc, dt, *refs):
    parts, (wall, wout) = refs[:-2], refs[-2:]
    block = pl.program_id(0)
    inner = own_z.shape[1]
    wall[:, 2 * inner : 2 * inner + BC] = bc[...]
    wall[:, 2 * inner + BC :] = dt[...].astype(bf16)

    @pl.when(place[1] == 1)
    def _():
        wall[:, :inner] = own_z[...]
        wall[:, inner : 2 * inner] = own_x[...]
        wout[...] = own_out[...]

    for away in range(len(parts)):

        @pl.when((place[1] == 0) & (lax.bitwise_xor(place[0], block) == away))
        def _():
            wall[:, : 2 * inner] = parts[away][:, : 2 * inner].astype(bf16)
            wout[...] = parts[away][:, 2 * inner :].astype(bf16)


def narrow_kernel(wide, narrow):
    narrow[...] = wide[...].astype(bf16)


def narrowed(value):
    rows, cols = value.shape
    return pl.pallas_call(
        narrow_kernel,
        grid=(rows // GROUP,),
        in_specs=[by_rows(cols, 0)],
        out_specs=by_rows(cols, 0),
        out_shape=shape(rows, cols, dtype=bf16),
        name="narrowed",
    )(value)


def gather_weights(own_z, own_x, own_out, bc, dt):
    width, inner = own_z.shape
    chips = lax.axis_size("chip")
    chip = lax.axis_index("chip")
    core, far = lax.axis_index("core"), lax.axis_index("zh")
    size = width // chips
    cut = functools.partial(lax.dynamic_slice_in_dim, start_index=chip * size, slice_size=size)
    piece = jnp.concatenate(
        [cut(own_z).astype(f32), cut(own_x).astype(f32), cut(own_out).astype(f32)], axis=1
    )
    piece = lax.ppermute(piece, ("core", "zh"), CROSS)
    if chips == 4:
        parts = [piece]
        for away in range(1, chips):
            pairs = [
                (4 * c + kind, 4 * (c ^ away) + kind) for c in range(chips) for kind in (1, 2)
            ]
            parts.append(lax.ppermute(piece, ("chip", "core", "zh"), pairs))
        place = jnp.stack([chip, (core == far).astype(jnp.int32)]).astype(jnp.int32)
        blocks = chips
    else:
        parts = [lax.all_gather(piece, "chip", tiled=True)]
        place = jnp.stack([0, (core == far).astype(jnp.int32)]).astype(jnp.int32)
        blocks, size = 1, width
    wall_cols = 2 * inner + BC + LANES

    def rows(cols):
        return pl.BlockSpec((size, cols), lambda c: (c, 0))

    return pl.pallas_call(
        weight_kernel,
        grid=(blocks,),
        in_specs=[pl.BlockSpec(memory_space=pltpu.SMEM)]
        + [rows(inner), rows(inner), rows(inner), rows(BC), rows(LANES)]
        + [whole((size, 3 * inner))] * len(parts),
        out_specs=[rows(wall_cols), rows(inner)],
        out_shape=[shape(width, wall_cols, dtype=bf16), shape(width, inner, dtype=bf16)],
        compiler_params=pltpu.CompilerParams(
            dimension_semantics=("arbitrary",), vmem_limit_bytes=56 * 1024 * 1024
        ),
        name="weights",
    )(place, own_z, own_x, own_out, bc, dt, *parts)


def shards(
    x_input,
    seg_ids,
    cotangent,
    norm_gain,
    w_z,
    w_x,
    w_bc,
    w_dt,
    conv_x,
    conv_bc,
    bias_x,
    bias_bc,
    dt_bias,
    a_log,
    d_skip,
    gate_gain,
    w_out,
):
    tok, width = x_input.shape
    inner = w_z.shape[2]
    core, far = lax.axis_index("core"), lax.axis_index("zh")
    held = core == far
    heads = w_dt.shape[2]
    count = tok // GROUP
    conv_cols = inner + BC
    all_cols = 2 * inner + BC + LANES

    small = jnp.concatenate(
        [
            value.astype(f32).reshape(LAYERS, -1)
            for value in (w_dt, conv_x, bias_x, dt_bias, a_log, d_skip, gate_gain)
        ],
        axis=1,
    )
    small = jnp.where(held, small, lax.ppermute(small, BOTH, CROSS))
    sizes = (width * heads, CONV * inner, inner, heads, heads, heads, inner)
    pieces, at = [], 0
    for size in sizes:
        pieces.append(small[:, at : at + size])
        at += size
    w_dt, conv_x, bias_x, dt_bias, a_log, d_skip, gate_gain = pieces
    w_dt = w_dt.reshape(LAYERS, width, heads)
    conv_x = conv_x.reshape(LAYERS, CONV, inner)
    weights = [
        gather_weights(w_z[layer], w_x[layer], w_out[layer], w_bc[layer], pad_lanes(w_dt[layer]))
        for layer in range(LAYERS)
    ]
    seg = to_block(seg_ids.astype(f32))
    hidden = to_block(x_input.astype(f32))
    cotangent = to_block(cotangent.astype(f32))
    hidden_own = own_rows(hidden)
    edge_seg = shifted(seg[tok - ROWS :], 1)
    seg_ext = jnp.concatenate([edge_seg, seg])
    before = jnp.concatenate([edge_seg[ROWS - 1 :], seg[GROUP - 1 : tok - 1 : GROUP]])
    after = seg[GROUP - 1 :: GROUP]
    mask = jnp.stack(
        [
            (seg_ext[ROWS - CONV + 1 + k : ROWS - CONV + 1 + k + tok] == seg).astype(f32)
            for k in range(CONV - 1)
        ]
        + [
            (seg == jnp.repeat(before, GROUP)).astype(f32),
            (seg == jnp.repeat(after, GROUP)).astype(f32),
            seg,
            seg,
            seg,
        ],
        axis=1,
    )
    seg_col = seg[:, None]
    seg_row = eight(seg)
    expand = (jnp.arange(LANES)[:, None] == jnp.arange(inner)[None, :] // HEADDIM).astype(f32)
    position = jnp.arange(GROUP)
    tri = (position[:, None] >= position[None, :]).astype(f32)
    triback = (position[:, None] <= position[None, :]).astype(f32)

    matmul_flops = 2 * tok * width
    stored = []
    for layer in range(LAYERS):
        wall, wout = weights[layer]
        taps = jnp.concatenate([conv_x[layer], conv_bc[layer]], axis=1)
        bias = eight(jnp.concatenate([bias_x[layer], bias_bc[layer]]))
        dtb = eight(pad_lanes(dt_bias[layer]))
        avec = eight(pad_lanes(-jnp.exp(a_log[layer])))
        dskip = eight(jnp.repeat(d_skip[layer], HEADDIM))
        ggain = eight(gate_gain[layer])
        ngain = norm_gain[layer][None, :]
        end = hidden[tok - 16 :].astype(f32)
        end = end * lax.rsqrt(jnp.mean(end * end, axis=1, keepdims=True) + epsilon) * ngain
        end = mm(end.astype(bf16), wall[:, inner : 2 * inner + BC])[ROWS:]
        halo = shifted(end, 1)
        normed, zval, cin, cpre, dtp, cum, dtv, xdt, bc, sloc, pref, send = call(
            in_kernel,
            count,
            [
                (by_rows(width, count), hidden),
                (whole((width, all_cols)), wall),
                (whole((1, width)), ngain),
                (whole((CONV, conv_cols)), taps),
                (whole((ROWS, conv_cols)), bias),
                (whole((ROWS, LANES)), dtb),
                (whole((ROWS, LANES)), avec),
                (by_rows(ROWS, count), mask),
                (whole((ROWS, conv_cols)), halo),
                (whole((LANES, inner)), expand),
                (whole((GROUP, GROUP)), tri),
            ],
            [
                (by_rows(width, count), shape(tok, width, dtype=bf16)),
                (by_rows(inner, count), shape(tok, inner)),
                (by_rows(conv_cols, count), shape(tok, conv_cols)),
                (by_rows(conv_cols, count), shape(tok, conv_cols)),
                (by_rows(LANES, count), shape(tok, LANES)),
                (by_rows(LANES, count), shape(tok, LANES)),
                (by_rows(LANES, count), shape(tok, LANES)),
                (by_rows(inner, count), shape(tok, inner, dtype=bf16)),
                (by_rows(BC, count), shape(tok, BC, dtype=bf16)),
                (by_group((STATE, inner), count), shape(count, STATE, inner)),
                (by_group((ROWS, inner), count), shape(count, ROWS, inner)),
                (whole((STATE + ROWS, inner)), shape(STATE + ROWS, inner)),
            ],
            [
                pltpu.VMEM((STATE, inner), f32),
                pltpu.VMEM((ROWS, inner), f32),
                pltpu.VMEM((ROWS, conv_cols), f32),
            ],
            matmul_flops * all_cols,
            "in_proj_conv",
        )
        (yin,) = call(
            intra_kernel,
            count,
            [
                (by_rows(LANES, count), cum),
                (by_rows(inner, count), xdt),
                (by_rows(BC, count), bc),
                (by_rows(1, count), seg_col),
                (by_cols(count), seg_row),
            ],
            [(by_rows(inner, count), shape(tok, inner))],
            [],
            matmul_flops * 512,
            "ssd_within",
        )
        entry = chain(send, False)
        y, gate_in, proj, sums = call(
            out_kernel,
            count,
            [
                (by_rows(inner, count), yin),
                (by_rows(inner, count), cpre),
                (by_rows(LANES, count), cum),
                (by_rows(BC, count), bc),
                (by_rows(ROWS, count), mask),
                (by_rows(inner, count), zval),
                (by_group((STATE, inner), count), sloc),
                (by_group((ROWS, inner), count), pref),
                (whole((STATE, inner)), entry),
                (whole((ROWS, inner)), dskip),
                (whole((ROWS, inner)), ggain),
                (whole((width, inner)), wout),
                (whole((LANES, inner)), expand),
                (by_rows(width, count), cotangent),
            ],
            [
                (by_rows(inner, count), shape(tok, inner)),
                (by_rows(inner, count), shape(tok, inner, dtype=bf16)),
                (by_rows(width, count), shape(tok, width)),
                (by_cols(count), shape(ROWS, tok)),
            ],
            [],
            matmul_flops * 2 * inner,
            "gate_out_proj",
        )
        sums = total(sums, ("core", "zl"))
        proj_sum = scatter_sum(proj)
        gate_scale = lax.rsqrt(sums[0] / INNER + epsilon)
        stored.append(
            dict(
                hidden=hidden_own, normed=normed, zval=zval, cin=cin, cpre=cpre, dtp=dtp, cum=cum,
                dtv=dtv, xdt=xdt, bc=bc, sloc=sloc, pref=pref, entry=entry, y=y, gate_in=gate_in,
                proj_sum=proj_sum, gate_scale=gate_scale, dots=sums[1], halo=halo, wall=wall, wout=wout,
                taps=taps, dtb=dtb, avec=avec, dskip=dskip, ggain=ggain,
            )
        )
        hidden_own = hidden_own + own_rows(gate_scale)[:, None] * proj_sum
        if layer < LAYERS - 1:
            hidden = gather_rows(hidden_own)
    final_out = narrowed(deliver(hidden_own))

    grad_h = cotangent
    grad_own = own_rows(cotangent)
    matrices = [None] * LAYERS
    vectors = [None] * LAYERS
    shared = [None] * LAYERS
    for layer in reversed(range(LAYERS)):
        kept = stored[layer]
        gate_scale = kept["gate_scale"]
        if layer == LAYERS - 1:
            grad_scale = kept["dots"]
        else:
            grad_scale = gather_rows(jnp.sum(grad_own * kept["proj_sum"], axis=1))
        gsq = -grad_scale * gate_scale**3 / INNER
        rev = functools.partial(by_rows, count=count, reverse=True)
        rev_group = functools.partial(by_group, count=count, reverse=True)
        gproj, dy, dz, gloc, suf, gsend, acc = call(
            gate_kernel,
            count,
            [
                (rev(width), grad_h),
                (rev(1), gate_scale[:, None]),
                (rev(1), gsq[:, None]),
                (rev(inner), kept["y"]),
                (rev(inner), kept["zval"]),
                (whole((ROWS, inner)), kept["ggain"]),
                (whole((width, inner)), kept["wout"]),
                (rev(LANES), kept["cum"]),
                (rev(BC), kept["bc"]),
                (rev(ROWS), mask),
                (whole((LANES, inner)), expand),
            ],
            [
                (rev(width), shape(tok, width, dtype=bf16)),
                (rev(inner), shape(tok, inner, dtype=bf16)),
                (rev(inner), shape(tok, inner, dtype=bf16)),
                (rev_group((STATE, inner)), shape(count, STATE, inner)),
                (rev_group((ROWS, inner)), shape(count, ROWS, inner)),
                (whole((STATE + ROWS, inner)), shape(STATE + ROWS, inner)),
                (whole((ROWS, inner)), shape(ROWS, inner)),
            ],
            [pltpu.VMEM((STATE, inner), f32), pltpu.VMEM((ROWS, inner), f32)],
            matmul_flops * inner,
            "gate_back",
        )
        u, dbc = call(
            intra_back_kernel,
            count,
            [
                (by_rows(LANES, count), kept["cum"]),
                (by_rows(inner, count), kept["xdt"]),
                (by_rows(BC, count), kept["bc"]),
                (by_rows(1, count), seg_col),
                (by_cols(count), seg_row),
                (by_rows(inner, count), dy),
            ],
            [
                (by_rows(inner, count), shape(tok, inner)),
                (by_rows(BC, count), shape(tok, BC)),
            ],
            [],
            matmul_flops * 1024,
            "ssd_within_back",
        )
        gout = chain(gsend, True)
        grad_wout = mm(gproj, kept["gate_in"], ((0,), (0,)))
        gall, last8, rim, gtaps, vecs, dsk = call(
            in_back_kernel,
            count,
            [
                (rev(inner), u),
                (rev(BC), dbc),
                (rev(inner), dy),
                (rev(inner), dz),
                (rev(inner), kept["y"]),
                (rev(conv_cols), kept["cpre"]),
                (rev(conv_cols), kept["cin"]),
                (rev(LANES), kept["dtp"]),
                (rev(LANES), kept["dtv"]),
                (rev(LANES), kept["cum"]),
                (rev(inner), kept["xdt"]),
                (rev(BC), kept["bc"]),
                (rev(ROWS), mask),
                (rev_group((STATE, inner)), kept["sloc"]),
                (rev_group((ROWS, inner)), kept["pref"]),
                (whole((STATE, inner)), kept["entry"]),
                (rev_group((STATE, inner)), gloc),
                (rev_group((ROWS, inner)), suf),
                (whole((STATE, inner)), gout),
                (whole((ROWS, conv_cols)), kept["halo"]),
                (whole((CONV, conv_cols)), kept["taps"]),
                (whole((ROWS, LANES)), kept["dtb"]),
                (whole((ROWS, LANES)), kept["avec"]),
                (whole((ROWS, inner)), kept["dskip"]),
                (whole((LANES, inner)), expand),
                (whole((GROUP, GROUP)), triback),
            ],
            [
                (rev(all_cols), shape(tok, all_cols, dtype=bf16)),
                (whole((ROWS, conv_cols)), shape(ROWS, conv_cols)),
                (whole((ROWS, conv_cols)), shape(ROWS, conv_cols)),
                (whole((ROWS, conv_cols)), shape(ROWS, conv_cols)),
                (whole((ROWS, LANES)), shape(ROWS, LANES)),
                (whole((ROWS, inner)), shape(ROWS, inner)),
            ],
            [pltpu.VMEM((CONV - 1, ROWS, conv_cols), f32)],
            matmul_flops * 1024,
            "in_proj_conv_back",
        )
        rim_back = shifted(rim, -1)
        gall = lax.dynamic_update_slice(
            gall, (last8 + rim_back).astype(bf16), (tok - ROWS, inner)
        )
        grad_normed = scatter_sum(mm(gall, kept["wall"], ((1,), (1,))))
        grad_win = mm(kept["normed"], gall[:, : 2 * inner + BC], ((0,), (0,)))
        grad_wdt = mm(kept["normed"], gall[:, 2 * inner + BC :], ((0,), (0,)))
        hidden_in = kept["hidden"]
        inv = lax.rsqrt(jnp.mean(hidden_in * hidden_in, axis=1, keepdims=True) + epsilon)
        grad_ngain = jnp.sum(grad_normed * hidden_in * inv, axis=0)
        back = grad_normed * norm_gain[layer][None, :]
        grad_own = grad_own + inv * (
            back - hidden_in * inv * inv * jnp.mean(back * hidden_in, axis=1, keepdims=True)
        )
        if layer > 0:
            grad_h = gather_rows(grad_own)
        grad_win = lax.psum_scatter(grad_win, "chip", scatter_dimension=0, tiled=True)
        grad_wout = lax.psum_scatter(grad_wout, "chip", scatter_dimension=0, tiled=True)
        matrices[layer] = (
            place_rows(grad_win[:, : 2 * inner]),
            place_rows(grad_wout),
            shared_rows(grad_win[:, 2 * inner :]),
        )
        vectors[layer] = jnp.concatenate(
            [
                gtaps[: CONV + 1, :inner].reshape(-1),
                acc[0],
                vecs[0, :heads],
                vecs[1, :heads],
                dsk[0],
                grad_wdt[:, :heads].reshape(-1),
                gtaps[: CONV + 1, inner:].reshape(-1),
                grad_ngain,
            ]
        )
    vector = total(jnp.stack(vectors), ("zh", "chip"))
    other = swap(vector, "core")
    common = (CONV + 1) * BC + width
    by_head = jnp.where(held, vector, other)[:, :-common]
    shared = total((vector + other)[:, -common:], ("zl",))
    g_bc = shared[:, :-width].reshape(LAYERS, CONV + 1, BC)
    g_ngain = shared[:, -width:]
    at = 0
    pieces = []
    for size in (CONV * inner, inner, inner, heads, heads, inner, width * heads):
        pieces.append(by_head[:, at : at + size])
        at += size
    g_conv, g_bias, g_ggain, g_alog, g_dtb, g_dsk, g_wdt = pieces
    g_wdt = g_wdt.reshape(LAYERS, width, heads)
    rows = width // lax.axis_size(("chip", "core"))
    g_wdt = lax.dynamic_slice_in_dim(g_wdt, lax.axis_index(("chip", "core")) * rows, rows, axis=1)
    g_win = jnp.stack([m[0] for m in matrices])
    return (
        final_out,
        deliver(grad_own),
        g_ngain,
        g_win[:, :, :inner],
        g_win[:, :, inner:],
        jnp.stack([m[2] for m in matrices]),
        g_wdt,
        g_conv.reshape(LAYERS, CONV, inner),
        g_bc[:, :CONV],
        g_bias,
        g_bc[:, CONV],
        g_dtb,
        g_alog,
        jnp.sum(g_dsk.reshape(LAYERS, heads, HEADDIM), axis=2),
        g_ggain,
        jnp.stack([m[1] for m in matrices]),
    )


def place_rows(part):
    core, far = lax.axis_index("core"), lax.axis_index("zh")
    full = part + lax.ppermute(part, BOTH, CROSS_BACK)
    sent = lax.ppermute(take(full, 1 - core, 2), BOTH, CORE_OUT)
    return jnp.where(core == far, take(full, core, 2), sent)


def shared_rows(part):
    core = lax.axis_index("core")
    part = take(part, core, 2) + swap(take(part, 1 - core, 2), "core")
    return total(part, ("zl", "zh"))


def solution(mesh):
    seq, head = mesh.devices.shape
    mesh = jax.sharding.Mesh(
        mesh.devices.reshape(seq // 2, 2, 2, head // 2), ("chip", "core", "zh", "zl")
    )
    tokens, columns = ("chip", "core"), ("zh", "zl")
    by_col = P(None, None, columns)
    by_head = P(None, columns)
    both = P(None, tokens, columns)
    placed = (
        P(tokens, None),
        P(tokens),
        P(tokens, None),
        P(),
        by_col,
        by_col,
        P(),
        by_col,
        by_col,
        P(),
        by_head,
        P(),
        by_head,
        by_head,
        by_head,
        by_head,
        by_col,
    )
    return jax.shard_map(
        shards,
        mesh=mesh,
        in_specs=placed,
        out_specs=(
            P(tokens, None),
            P(tokens, None),
            P(),
            both,
            both,
            P(None, tokens, None),
            both,
            by_col,
            P(),
            by_head,
            P(),
            by_head,
            by_head,
            by_head,
            by_head,
            both,
        ),
        check_vma=False,
    )
```

```python
import functools

import jax
import jax.numpy as jnp
from jax import lax
from jax.experimental import pallas as pl
from jax.experimental.pallas import tpu as pltpu
from jax.sharding import PartitionSpec as P

HEADDIM = 64
STATE = 128
CONV = 4
GROUP = 256
LAYERS = 2
INNER = 2048
LANES = 128
ROWS = 8
BC = 2 * STATE

epsilon = 1e-05
highest = lax.Precision.HIGHEST
f32 = jnp.float32
bf16 = jnp.bfloat16


def mm(left, right, dims=((1,), (0,)), precision=None):
    return lax.dot_general(
        left, right, (dims, ((), ())), preferred_element_type=f32, precision=precision
    )


def softplus(value):
    small = jnp.exp(-jnp.abs(value))
    series = small * (1.0 - small * (0.5 - small * (1.0 / 3.0 - small * (0.25 - small * 0.2))))
    return jnp.maximum(value, 0.0) + jnp.where(small < 0.03, series, jnp.log(1.0 + small))


def silu_slope(value, sigma):
    return sigma * (1.0 + value * (1.0 - sigma))


def spread(heads, expand):
    return mm(heads, expand, precision=highest)


def gather_heads(lanes, expand):
    return mm(lanes, expand, ((1,), (1,)), precision=highest)


def pick(place, pieces, held):
    if len(pieces) == 1:
        return pieces[0][...]
    away = lax.bitwise_xor(pl.program_id(0) if held is None else held, place[0])
    value = pieces[3][...]
    for number in range(3):
        value = jnp.where(away == number, pieces[number][...], value)
    return value


def in_kernel(
    place, wall, ngain, taps, bias, dtb, avec, mask, halo, expand, tri, *refs
):
    hid = refs[:-14]
    normed, cin, cpre, dtp, cum, dtv, xdt, bc, sloc, pref, send, state, thru, prev = refs[-14:]
    step = pl.program_id(0)
    inner = expand.shape[1]

    @pl.when(step == 0)
    def _():
        state[...] = jnp.zeros_like(state)
        thru[...] = jnp.ones_like(thru)
        prev[...] = halo[...]

    h = pick(place, hid, None)
    inv = lax.rsqrt(jnp.mean(h * h, axis=1, keepdims=True) + epsilon)
    low = (h * inv * ngain[...]).astype(bf16)
    normed[...] = low
    rows = mm(low, wall[:, : inner + BC])
    pre_dt = mm(low, wall[:, inner + BC :])
    dtp[...] = pre_dt
    cin[...] = rows
    ext = jnp.concatenate([prev[...], rows], axis=0)
    prev[...] = rows[GROUP - ROWS :]
    total = taps[CONV - 1 : CONV, :] * rows + bias[0:1, :]
    for k in range(CONV - 1):
        first = ROWS - CONV + 1 + k
        total = total + taps[k : k + 1, :] * ext[first : first + GROUP] * mask[:, k : k + 1]
    cpre[...] = total
    act = total * jax.nn.sigmoid(total)
    x = act[:, :inner]
    low_bc = act[:, inner:].astype(bf16)
    bc[...] = low_bc
    dt = softplus(pre_dt + dtb[0:1, :])
    dtv[...] = dt
    run = mm(tri[...], dt * avec[0:1, :], precision=highest)
    cum[...] = run
    last = run[GROUP - 1 : GROUP]
    xdt[...] = (x * spread(dt, expand[...])).astype(bf16)
    tail = jnp.exp(last - run) * mask[:, 4:5] * dt
    contrib = mm(low_bc[:, :STATE], (x * spread(tail, expand[...])).astype(bf16), ((0,), (0,)))
    through = jnp.broadcast_to(jnp.exp(last) * mask[GROUP - 1 : GROUP, 3:4], (ROWS, LANES))
    through = spread(through, expand[...])
    sloc[0] = state[...]
    pref[0] = thru[...]
    state[...] = through[0:1] * state[...] + contrib
    thru[...] = thru[...] * through

    @pl.when(step == pl.num_programs(0) - 1)
    def _():
        send[:STATE] = state[...]
        send[STATE:] = thru[...]


def pair_lanes(value, which):
    lane = lax.broadcasted_iota(jnp.int32, value.shape, 1)
    keep = lane < HEADDIM if which == 0 else lane >= HEADDIM
    return jnp.where(keep, value, jnp.zeros_like(value))


def intra_kernel(cum, xdt, bc, seg, segrow, y):
    inner = xdt.shape[1]
    run = cum[...]
    run_t = run.T
    base = mm(bc[:, STATE:], bc[:, :STATE], ((1,), (1,)))
    t_at = lax.broadcasted_iota(jnp.int32, (GROUP, GROUP), 0)
    s_at = lax.broadcasted_iota(jnp.int32, (GROUP, GROUP), 1)
    same = (seg[:, 0:1] == segrow[0:1, :]) & (t_at >= s_at)
    closed = jnp.where(same, 0.0, -1e30)
    for pair in range(inner // LANES):
        cols = slice(pair * LANES, (pair + 1) * LANES)
        xs = xdt[:, cols]
        parts = []
        for which in range(2):
            head = 2 * pair + which
            decay = jnp.exp(run[:, head : head + 1] - run_t[head : head + 1, :] + closed)
            parts.append(mm((decay * base).astype(bf16), xs))
        lane = lax.broadcasted_iota(jnp.int32, (GROUP, LANES), 1)
        y[:, cols] = jnp.where(lane < HEADDIM, parts[0], parts[1])


def out_kernel(
    yin, cpre, cum, bc, mask, zval, sloc, pref, entry, dskip, ggain, wout, expand, *refs
):
    cot, (y, gate_in, proj, sums) = refs[:-4], refs[-4:]
    inner = expand.shape[1]
    pre = cpre[...]
    x = pre * jax.nn.sigmoid(pre)
    full = sloc[0] + pref[0][0:1] * entry[...]
    reach = spread(jnp.exp(cum[...]) * mask[:, 3:4], expand[...])
    value = yin[...] + reach * mm(bc[:, STATE:], full.astype(bf16)) + dskip[0:1, :] * x
    y[...] = value
    z = zval[...]
    gated = value * (z * jax.nn.sigmoid(z))
    low = (gated * ggain[0:1, :]).astype(bf16)
    gate_in[...] = low
    proj[...] = mm(low, wout[...], ((1,), (1,)))
    ones = jnp.ones((ROWS, inner), f32)
    squares = mm(ones, gated * gated, ((1,), (1,)), precision=highest)
    if cot:
        back = mm(cot[0][...].astype(bf16), wout[...])
        dots = mm(ones, low.astype(f32) * back, ((1,), (1,)), precision=highest)
        row = lax.broadcasted_iota(jnp.int32, squares.shape, 0)
        squares = jnp.where(row == 0, squares, dots)
    sums[...] = squares


def gate_kernel(
    place, scale, gsq, y, zval, ggain, wout, cum, bc, mask, expand, *refs
):
    gh = refs[:-9]
    gproj, dy, dz, gloc, suf, send, acc, carry, thru = refs[-9:]
    step = pl.program_id(0)

    @pl.when(step == 0)
    def _():
        carry[...] = jnp.zeros_like(carry)
        thru[...] = jnp.ones_like(thru)
        acc[...] = jnp.zeros_like(acc)

    gp = (scale[...] * pick(place, gh, pl.num_programs(0) - 1 - step)).astype(bf16)
    gproj[...] = gp
    ggi = mm(gp, wout[...])
    z = zval[...]
    sigma = jax.nn.sigmoid(z)
    silu = z * sigma
    value = y[...]
    gated = value * silu
    ggated = ggi * ggain[0:1, :] + gated * gsq[...]
    acc[0:1, :] += jnp.sum(ggi * gated, axis=0, keepdims=True)
    low = (ggated * silu).astype(bf16)
    dy[...] = low
    dz[...] = (ggated * value * silu_slope(z, sigma)).astype(bf16)
    run = cum[...]
    last = run[GROUP - 1 : GROUP]
    reach = spread(jnp.exp(run) * mask[:, 3:4], expand[...])
    back = mm(bc[:, STATE:], (reach * low.astype(f32)).astype(bf16), ((0,), (0,)))
    through = jnp.broadcast_to(jnp.exp(last) * mask[GROUP - 1 : GROUP, 3:4], (ROWS, LANES))
    through = spread(through, expand[...])
    gloc[0] = carry[...]
    suf[0] = thru[...]
    carry[...] = back + through[0:1] * carry[...]
    thru[...] = thru[...] * through

    @pl.when(step == pl.num_programs(0) - 1)
    def _():
        send[:STATE] = carry[...]
        send[STATE:] = thru[...]


def intra_back_kernel(cum, xdt, bc, seg, segrow, dy, u, dbc):
    inner = xdt.shape[1]
    run = cum[...]
    run_t = run.T
    base = mm(bc[:, :STATE], bc[:, STATE:], ((1,), (1,)))
    s_at = lax.broadcasted_iota(jnp.int32, (GROUP, GROUP), 0)
    t_at = lax.broadcasted_iota(jnp.int32, (GROUP, GROUP), 1)
    same = (seg[:, 0:1] == segrow[0:1, :]) & (t_at >= s_at)
    closed = jnp.where(same, 0.0, -1e30)
    grad_base = jnp.zeros((GROUP, GROUP), f32)
    for pair in range(inner // LANES):
        cols = slice(pair * LANES, (pair + 1) * LANES)
        xs = xdt[:, cols]
        ds = dy[:, cols]
        parts = []
        for which in range(2):
            head = 2 * pair + which
            decay = jnp.exp(run_t[head : head + 1, :] - run[:, head : head + 1] + closed)
            parts.append(mm((decay * base).astype(bf16), ds))
            grad_base = grad_base + decay * mm(xs, pair_lanes(ds, which), ((1,), (1,)))
        lane = lax.broadcasted_iota(jnp.int32, (GROUP, LANES), 1)
        u[:, cols] = jnp.where(lane < HEADDIM, parts[0], parts[1])
    low = grad_base.astype(bf16)
    dbc[:, :STATE] = mm(low, bc[:, STATE:])
    dbc[:, STATE:] = mm(low, bc[:, :STATE], ((0,), (0,)))


def in_back_kernel(
    uin, dbc, dy, y, cpre, cin, dtp, dtv, cum, xdt, bc, mask, sloc, pref, entry, gloc, suf,
    gout, halo, taps, dtb, avec, dskip, expand, triback,
    gall, last8, rim, gtaps, vecs, dsk,
    nexts,
):
    step = pl.program_id(0)
    inner = expand.shape[1]

    @pl.when(step == 0)
    def _():
        nexts[...] = jnp.zeros_like(nexts)
        gtaps[...] = jnp.zeros_like(gtaps)
        vecs[...] = jnp.zeros_like(vecs)
        dsk[...] = jnp.zeros_like(dsk)

    e = expand[...]
    pre = cpre[...]
    sigma = jax.nn.sigmoid(pre)
    x = (pre * sigma)[:, :inner]
    full = sloc[0] + pref[0][0:1] * entry[...]
    nxt = gloc[0] + suf[0][0:1] * gout[...]
    nxt_low = nxt.astype(bf16)
    run = cum[...]
    last = run[GROUP - 1 : GROUP]
    dt = dtv[...]
    low_dy = dy[...].astype(f32)
    xw = xdt[...].astype(f32)
    tail = spread(jnp.exp(last - run) * mask[:, 4:5], e)
    reach = spread(jnp.exp(run) * mask[:, 3:4], e)
    u_inter = tail * mm(bc[:, :STATE], nxt_low)
    u = uin[...] + u_inter
    dx = spread(dt, e) * u + dskip[0:1, :] * low_dy
    dsk[0:1, :] += jnp.sum(low_dy * x, axis=0, keepdims=True)
    db = dbc[:, :STATE] + mm((tail * xw).astype(bf16), nxt_low, ((1,), (1,)))
    dc = dbc[:, STATE:] + mm((reach * low_dy).astype(bf16), full.astype(bf16), ((1,), (1,)))
    grad_dt = gather_heads(x * u, e)
    y_plain = y[...] - dskip[0:1, :] * x
    grad_cum = gather_heads(low_dy * y_plain - xw * u, e)
    flow = jnp.sum(nxt * full, axis=0, keepdims=True)
    flow = gather_heads(jnp.broadcast_to(flow, (ROWS, inner)), e)[0:1]
    ends = jnp.sum(xw * u_inter, axis=0, keepdims=True)
    ends = gather_heads(jnp.broadcast_to(ends, (ROWS, inner)), e)[0:1]
    grad_tot = mask[GROUP - 1 : GROUP, 3:4] * jnp.exp(last) * flow + ends
    grad_da = mm(triback[...], grad_cum, precision=highest) + grad_tot
    a = avec[0:1, :]
    grad_dtv = grad_dt + grad_da * a
    grad_dtpre = grad_dtv * jax.nn.sigmoid(dtp[...] + dtb[0:1, :])
    vecs[0:1, :] += jnp.sum(grad_da * dt, axis=0, keepdims=True) * a
    vecs[1:2, :] += jnp.sum(grad_dtpre, axis=0, keepdims=True)
    slope = silu_slope(pre, sigma)
    grad_pre = jnp.concatenate([dx, db, dc], axis=1) * slope
    gtaps[4:5, :] += jnp.sum(grad_pre, axis=0, keepdims=True)
    rows = cin[...]
    grad_rows = taps[CONV - 1 : CONV, :] * grad_pre
    gtaps[3:4, :] += jnp.sum(rows * grad_pre, axis=0, keepdims=True)
    masked = []
    for k in range(CONV - 1):
        m = grad_pre * mask[:, k : k + 1]
        masked.append(m[:ROWS])
        ahead = CONV - 1 - k
        shifted = jnp.concatenate([m, nexts[k]], axis=0)[ahead : ahead + GROUP]
        grad_rows = grad_rows + taps[k : k + 1, :] * shifted
        gtaps[k : k + 1, :] += jnp.sum(rows * shifted, axis=0, keepdims=True)
    for k in range(CONV - 1):
        nexts[k] = masked[k]
    gall[:, : inner + BC] = grad_rows.astype(bf16)
    gall[:, inner + BC :] = grad_dtpre.astype(bf16)

    @pl.when(step == 0)
    def _():
        last8[...] = grad_rows[GROUP - ROWS :]

    @pl.when(step == pl.num_programs(0) - 1)
    def _():
        spill = jnp.zeros((ROWS, inner + BC), f32)
        edge = halo[...]
        for k in range(CONV - 1):
            down = ROWS - CONV + 1 + k
            moved = jnp.concatenate([jnp.zeros((ROWS, inner + BC), f32), masked[k]], axis=0)
            moved = moved[ROWS - down : 2 * ROWS - down]
            spill = spill + taps[k : k + 1, :] * moved
            gtaps[k : k + 1, :] += jnp.sum(edge * moved, axis=0, keepdims=True)
        rim[...] = spill


def whole(shape):
    return pl.BlockSpec(shape, lambda c: (0,) * len(shape))


def by_rows(cols, count, reverse=False):
    if reverse:
        return pl.BlockSpec((GROUP, cols), lambda c: (count - 1 - c, 0))
    return pl.BlockSpec((GROUP, cols), lambda c: (c, 0))


def by_group(shape, count, reverse=False):
    if reverse:
        return pl.BlockSpec((1,) + shape, lambda c: (count - 1 - c, 0, 0))
    return pl.BlockSpec((1,) + shape, lambda c: (c, 0, 0))


def by_piece(pieces, count, reverse=False):
    if len(pieces) == 1:
        return [(by_rows(pieces[0].shape[1], count, reverse), pieces[0])]
    return [(whole(piece.shape), piece) for piece in pieces]


def by_cols(count):
    return pl.BlockSpec((ROWS, GROUP), lambda c: (0, c))


def call(kernel, count, ins, outs, scratch, flops, name):
    return pl.pallas_call(
        kernel,
        grid=(count,),
        in_specs=[spec for spec, _ in ins],
        out_specs=[spec for spec, _ in outs],
        out_shape=[shape for _, shape in outs],
        scratch_shapes=scratch,
        compiler_params=pltpu.CompilerParams(
            dimension_semantics=("arbitrary",), vmem_limit_bytes=56 * 1024 * 1024
        ),
        cost_estimate=pl.CostEstimate(
            flops=flops, bytes_accessed=8 * 1024 * 1024, transcendentals=0
        ),
        name=name,
    )(*[value for _, value in ins])


def shape(*dims, dtype=f32):
    return jax.ShapeDtypeStruct(dims, dtype)


SWAP = ((0, 1), (1, 0))
CROSS = ((0, 1), (3, 2))
CROSS_BACK = ((1, 0), (2, 3))
CORE_OUT = ((0, 2), (3, 1))
CORE_IN = ((2, 0), (1, 3))
DIAGONAL = ((2, 1), (1, 2))
BOTH = ("core", "zh")
BLOCKS = ("chip", "zh")


def shifted(value, steps):
    count = lax.axis_size(BLOCKS)
    leading, last = (max(0, -steps), min(count, count - steps))
    return lax.ppermute(value, BLOCKS, [(source, source + steps) for source in range(leading, last)])


def chain(part, reverse):
    count = lax.axis_size(BLOCKS)
    place = lax.axis_index(BLOCKS)
    state, decay = part[:STATE], part[STATE : STATE + 1]
    entry, reach = jnp.zeros_like(state), jnp.ones_like(decay)
    step = 1
    while step < count:
        got = lax.ppermute(part, BLOCKS, [(i, i ^ step) for i in range(count)])
        got_state, got_decay = got[:STATE], got[STATE : STATE + 1]
        later = ((place & step) == 0) if reverse else ((place & step) != 0)
        entry = jnp.where(later, entry + reach * got_state, entry)
        reach = jnp.where(later, reach * got_decay, reach)
        state = jnp.where(later, state + decay * got_state, got_state + got_decay * state)
        decay = decay * got_decay
        part = jnp.concatenate([state, jnp.broadcast_to(decay, (ROWS, decay.shape[1]))])
        step *= 2
    return entry


def swap(value, axis):
    return lax.ppermute(value, axis, SWAP)


def total(value, axes):
    for axis in axes:
        count = lax.axis_size(axis)
        step = 1
        while step < count:
            value = value + lax.ppermute(value, axis, [(i, i ^ step) for i in range(count)])
            step *= 2
    return value


def take(value, index, count):
    size = value.shape[0] // count
    return lax.dynamic_slice_in_dim(value, index * size, size)


def ordered(place, mine, theirs):
    return jnp.where(
        place == 0, jnp.concatenate([mine, theirs]), jnp.concatenate([theirs, mine])
    )


def behind(value, *marks):
    return lax.optimization_barrier((value, *marks))[0]


def scatter_sum(part, first=(), second=(), third=()):
    core, near = lax.axis_index("core"), lax.axis_index("zl")
    part = behind(part, *first)
    half = take(part, core, 2) + behind(swap(take(part, 1 - core, 2), "core"), *second)
    if lax.axis_size("zl") == 2:
        return take(half, near, 2) + behind(swap(take(half, 1 - near, 2), "zl"), *third)
    return lax.psum_scatter(half, "zl", scatter_dimension=0, tiled=True)


def own_rows(value):
    core, near = lax.axis_index("core"), lax.axis_index("zl")
    return take(take(value, core, 2), near, lax.axis_size("zl"))


def gather_near(value):
    if lax.axis_size("zl") == 2:
        return ordered(lax.axis_index("zl"), value, swap(value, "zl"))
    return lax.all_gather(value, "zl", tiled=True)


def gather_rows(value):
    half = gather_near(value)
    return ordered(lax.axis_index("core"), half, swap(half, "core"))


def own_place():
    return 2 * lax.axis_index("core") + lax.axis_index("zl")


def gather_pieces(value):
    if lax.axis_size("zl") != 2 or value.shape[0] != GROUP:
        return [gather_rows(value)]
    near = swap(value, "zl")
    return [value, near, swap(value, "core"), swap(near, "core")]


def place_kernel(place, value, mine, near, theirs, value_s, mine_s, near_s, theirs_s, out):
    away = lax.bitwise_xor(pl.program_id(0), place[0])
    pairs = ((value, mine), (value_s, mine_s), (near, theirs), (near_s, theirs_s))
    for number, (here, there) in enumerate(pairs):

        @pl.when((away == number) & (place[1] == 1))
        def _():
            out[...] = here[...].astype(out.dtype)

        @pl.when((away == number) & (place[1] == 0))
        def _():
            out[...] = there[...].astype(out.dtype)


def deliver(value, dtype, first=(), second=(), third=()):
    core, far = lax.axis_index("core"), lax.axis_index("zh")
    held = core == far
    value = behind(value, *first)
    mine = lax.ppermute(value, BOTH, CROSS)
    theirs = lax.ppermute(value, BOTH, DIAGONAL)
    near = lax.ppermute(value, BOTH, CORE_IN)
    if lax.axis_size("zl") != 2 or value.shape[0] != GROUP:
        mine = gather_near(jnp.where(held, value, mine))
        theirs = gather_near(jnp.where(held, near, theirs))
        full = ordered(core, mine, theirs)
        return narrowed(full) if dtype == bf16 else full
    axes = ("core", "zh", "zl")
    here = [(2 * kind + i, 2 * kind + 1 - i) for kind in (0, 3) for i in range(2)]
    there = [(2 * kind + i, 2 * kind + 1 - i) for kind in (1, 2) for i in range(2)]
    value_s = lax.ppermute(value, axes, here)
    near_s = lax.ppermute(near, axes, here)
    mine, theirs = behind(mine, *second), behind(theirs, *second)
    mine_s = lax.ppermute(mine, axes, there)
    theirs_s = lax.ppermute(theirs, axes, there)
    place = jnp.stack([own_place(), held.astype(jnp.int32)]).astype(jnp.int32)
    width = value.shape[1]
    parts = (value, mine, near, theirs, value_s, mine_s, near_s, behind(theirs_s, *third))
    return pl.pallas_call(
        place_kernel,
        grid=(4,),
        in_specs=[pl.BlockSpec(memory_space=pltpu.SMEM)] + [whole((GROUP, width))] * 8,
        out_specs=by_rows(width, 4),
        out_shape=shape(4 * GROUP, width, dtype=dtype),
        compiler_params=pltpu.CompilerParams(
            dimension_semantics=("arbitrary",), vmem_limit_bytes=40 * 1024 * 1024
        ),
        name="place",
    )(place, *parts)


def to_block(value):
    got = lax.ppermute(value, BOTH, CORE_OUT)
    return jnp.where(lax.axis_index("core") == lax.axis_index("zh"), value, got)


def eight(row):
    return jnp.broadcast_to(row[None, :], (ROWS, row.shape[0]))


def pad_lanes(value):
    return jnp.pad(value, [(0, 0)] * (value.ndim - 1) + [(0, LANES - value.shape[-1])])


def weight_kernel(place, own, *refs):
    parts, out = refs[:-1], refs[-1]
    block = pl.program_id(0)
    cols = own.shape[1]

    @pl.when(place[1] == 1)
    def _():
        out[:, :cols] = own[...]

    for away in range(len(parts) if out.shape[1] == cols else len(parts) - 2):

        @pl.when((place[1] == 0) & (lax.bitwise_xor(place[0], block) == away))
        def _():
            out[:, :cols] = parts[away][...].astype(bf16)

    if out.shape[1] > cols:
        out[:, cols : cols + BC] = parts[-2][...]
        out[:, cols + BC :] = parts[-1][...].astype(bf16)


def narrow_kernel(wide, narrow):
    narrow[...] = wide[...].astype(bf16)


def narrowed(value):
    rows, cols = value.shape
    return pl.pallas_call(
        narrow_kernel,
        grid=(rows // GROUP,),
        in_specs=[by_rows(cols, 0)],
        out_specs=by_rows(cols, 0),
        out_shape=shape(rows, cols, dtype=bf16),
        name="narrowed",
    )(value)


def gather_weights(own, more=(), first=(), second=()):
    width, cols = own.shape
    chips = lax.axis_size("chip")
    chip = lax.axis_index("chip")
    held = (lax.axis_index("core") == lax.axis_index("zh")).astype(jnp.int32)
    size = width // chips
    piece = lax.dynamic_slice_in_dim(behind(own, *first), chip * size, size).astype(f32)
    piece = behind(lax.ppermute(piece, BOTH, CROSS), *second)
    if chips == 4:
        parts = [piece]
        for away in range(1, chips):
            pairs = [
                (4 * c + kind, 4 * (c ^ away) + kind) for c in range(chips) for kind in (1, 2)
            ]
            parts.append(lax.ppermute(piece, ("chip", "core", "zh"), pairs))
        place = jnp.stack([chip, held]).astype(jnp.int32)
        blocks = chips
    else:
        parts = [lax.all_gather(piece, "chip", tiled=True)]
        place = jnp.stack([0, held]).astype(jnp.int32)
        blocks, size = 1, width
    all_cols = cols + sum(value.shape[1] for value in more)

    def rows(cols):
        return pl.BlockSpec((size, cols), lambda c: (c, 0))

    return pl.pallas_call(
        weight_kernel,
        grid=(blocks,),
        in_specs=[pl.BlockSpec(memory_space=pltpu.SMEM), rows(cols)]
        + [whole((size, cols))] * len(parts)
        + [rows(value.shape[1]) for value in more],
        out_specs=rows(all_cols),
        out_shape=shape(width, all_cols, dtype=bf16),
        compiler_params=pltpu.CompilerParams(
            dimension_semantics=("arbitrary",), vmem_limit_bytes=40 * 1024 * 1024
        ),
        name="weights",
    )(place, own, *parts, *more)


def shards(
    x_input,
    seg_ids,
    cotangent,
    norm_gain,
    w_z,
    w_x,
    w_bc,
    w_dt,
    conv_x,
    conv_bc,
    bias_x,
    bias_bc,
    dt_bias,
    a_log,
    d_skip,
    gate_gain,
    w_out,
):
    tok, width = x_input.shape
    inner = w_z.shape[2]
    core, far = lax.axis_index("core"), lax.axis_index("zh")
    held = core == far
    heads = w_dt.shape[2]
    count = tok // GROUP
    conv_cols = inner + BC
    all_cols = inner + BC + LANES

    dt_own = w_dt.astype(f32).reshape(LAYERS, width * heads // LANES, LANES)
    dt_sent = lax.ppermute(dt_own, BOTH, CROSS)
    dt_all = pad_lanes(jnp.where(held, dt_own, dt_sent).reshape(LAYERS, width, heads))
    wall = gather_weights(w_x[0], (w_bc[0], dt_all[0]))
    hidden = to_block(x_input.astype(f32))
    seg = to_block(seg_ids.astype(f32))
    small = jnp.concatenate(
        [
            value.reshape(LAYERS, -1)
            for value in (conv_x, bias_x, dt_bias, a_log, d_skip, gate_gain)
        ],
        axis=1,
    )
    small = jnp.where(held, small, lax.ppermute(small, BOTH, CROSS))
    sizes = (CONV * inner, inner, heads, heads, heads, inner)
    pieces, at = [], 0
    for size in sizes:
        pieces.append(small[:, at : at + size])
        at += size
    conv_x, bias_x, dt_bias, a_log, d_skip, gate_gain = pieces
    conv_x = conv_x.reshape(LAYERS, CONV, inner)
    hidden_own = own_rows(hidden)
    hidden = [hidden]
    place = jnp.stack([own_place(), own_place()]).astype(jnp.int32)
    smem = pl.BlockSpec(memory_space=pltpu.SMEM)
    edge_seg = shifted(seg[tok - ROWS :], 1)
    seg_ext = jnp.concatenate([edge_seg, seg])
    before = jnp.concatenate([edge_seg[ROWS - 1 :], seg[GROUP - 1 : tok - 1 : GROUP]])
    after = seg[GROUP - 1 :: GROUP]
    mask = jnp.stack(
        [
            (seg_ext[ROWS - CONV + 1 + k : ROWS - CONV + 1 + k + tok] == seg).astype(f32)
            for k in range(CONV - 1)
        ]
        + [
            (seg == jnp.repeat(before, GROUP)).astype(f32),
            (seg == jnp.repeat(after, GROUP)).astype(f32),
            seg,
            seg,
            seg,
        ],
        axis=1,
    )
    seg_col = seg[:, None]
    seg_row = eight(seg)
    expand = (jnp.arange(LANES)[:, None] == jnp.arange(inner)[None, :] // HEADDIM).astype(f32)
    position = jnp.arange(GROUP)
    tri = (position[:, None] >= position[None, :]).astype(f32)
    triback = (position[:, None] <= position[None, :]).astype(f32)

    matmul_flops = 2 * tok * width
    stored = []
    for layer in range(LAYERS):
        if layer > 0:
            wall = next_wall
        taps = jnp.concatenate([conv_x[layer], conv_bc[layer]], axis=1)
        bias = eight(jnp.concatenate([bias_x[layer], bias_bc[layer]]))
        dtb = eight(pad_lanes(dt_bias[layer]))
        avec = eight(pad_lanes(-jnp.exp(a_log[layer])))
        dskip = eight(jnp.repeat(d_skip[layer], HEADDIM))
        ggain = eight(gate_gain[layer])
        ngain = norm_gain[layer][None, :]
        if len(hidden) == 1:
            end = hidden[0][tok - 16 :]
        else:
            ends = jnp.stack([piece[GROUP - 16 :] for piece in hidden])
            end = lax.dynamic_index_in_dim(ends, 3 ^ own_place(), 0, False)
        end = end * lax.rsqrt(jnp.mean(end * end, axis=1, keepdims=True) + epsilon) * ngain
        end = mm(end.astype(bf16), wall[:, : inner + BC])[ROWS:]
        halo = shifted(end, 1)
        normed, cin, cpre, dtp, cum, dtv, xdt, bc, sloc, pref, send = call(
            in_kernel,
            count,
            [
                (smem, place),
                (whole((width, all_cols)), wall),
                (whole((1, width)), ngain),
                (whole((CONV, conv_cols)), taps),
                (whole((ROWS, conv_cols)), bias),
                (whole((ROWS, LANES)), dtb),
                (whole((ROWS, LANES)), avec),
                (by_rows(ROWS, count), mask),
                (whole((ROWS, conv_cols)), halo),
                (whole((LANES, inner)), expand),
                (whole((GROUP, GROUP)), tri),
            ]
            + by_piece(hidden, count),
            [
                (by_rows(width, count), shape(tok, width, dtype=bf16)),
                (by_rows(conv_cols, count), shape(tok, conv_cols)),
                (by_rows(conv_cols, count), shape(tok, conv_cols)),
                (by_rows(LANES, count), shape(tok, LANES)),
                (by_rows(LANES, count), shape(tok, LANES)),
                (by_rows(LANES, count), shape(tok, LANES)),
                (by_rows(inner, count), shape(tok, inner, dtype=bf16)),
                (by_rows(BC, count), shape(tok, BC, dtype=bf16)),
                (by_group((STATE, inner), count), shape(count, STATE, inner)),
                (by_group((ROWS, inner), count), shape(count, ROWS, inner)),
                (whole((STATE + ROWS, inner)), shape(STATE + ROWS, inner)),
            ],
            [
                pltpu.VMEM((STATE, inner), f32),
                pltpu.VMEM((ROWS, inner), f32),
                pltpu.VMEM((ROWS, conv_cols), f32),
            ],
            matmul_flops * all_cols,
            "in_proj_conv",
        )
        if layer == 0:
            wz = gather_weights(w_z[0], first=(wall,))
            wout = gather_weights(w_out[0], first=(wall,))
            cotangent = to_block(behind(cotangent.astype(f32), wall))
            next_wall = gather_weights(w_x[1], (w_bc[1], dt_all[1]), (send,))
            next_wz = gather_weights(w_z[1], first=(send,))
            next_wout = gather_weights(w_out[1], first=(send,))
        else:
            wz, wout = next_wz, next_wout
        zval = mm(normed, wz)
        (yin,) = call(
            intra_kernel,
            count,
            [
                (by_rows(LANES, count), cum),
                (by_rows(inner, count), xdt),
                (by_rows(BC, count), bc),
                (by_rows(1, count), seg_col),
                (by_cols(count), seg_row),
            ],
            [(by_rows(inner, count), shape(tok, inner))],
            [],
            matmul_flops * 512,
            "ssd_within",
        )
        entry = chain(send, False)
        y, gate_in, proj, sums = call(
            out_kernel,
            count,
            [
                (by_rows(inner, count), yin),
                (by_rows(inner, count), cpre),
                (by_rows(LANES, count), cum),
                (by_rows(BC, count), bc),
                (by_rows(ROWS, count), mask),
                (by_rows(inner, count), zval),
                (by_group((STATE, inner), count), sloc),
                (by_group((ROWS, inner), count), pref),
                (whole((STATE, inner)), entry),
                (whole((ROWS, inner)), dskip),
                (whole((ROWS, inner)), ggain),
                (whole((width, inner)), wout),
                (whole((LANES, inner)), expand),
            ]
            + ([(by_rows(width, count), cotangent)] if layer == LAYERS - 1 else []),
            [
                (by_rows(inner, count), shape(tok, inner)),
                (by_rows(inner, count), shape(tok, inner, dtype=bf16)),
                (by_rows(width, count), shape(tok, width)),
                (by_cols(count), shape(ROWS, tok)),
            ],
            [],
            matmul_flops * 2 * inner,
            "gate_out_proj",
        )
        sums = total(sums, ("core", "zl"))
        gate_scale = lax.rsqrt(sums[0] / INNER + epsilon)
        stored.append(
            dict(
                hidden=hidden_own, normed=normed, zval=zval, cin=cin, cpre=cpre, dtp=dtp, cum=cum,
                dtv=dtv, xdt=xdt, bc=bc, sloc=sloc, pref=pref, entry=entry, y=y, gate_in=gate_in,
                proj=proj, gate_scale=gate_scale, dots=sums[1], halo=halo, wall=wall, wz=wz, wout=wout,
                taps=taps, dtb=dtb, avec=avec, dskip=dskip, ggain=ggain,
            )
        )
        if layer < LAYERS - 1:
            proj_sum = scatter_sum(proj)
            stored[layer]["proj_sum"] = proj_sum
            hidden_own = hidden_own + own_rows(gate_scale)[:, None] * proj_sum
            hidden = gather_pieces(hidden_own)

    grad_h = [cotangent]
    grad_own = own_rows(cotangent)
    matrices = [None] * LAYERS
    vectors = [None] * LAYERS
    shared = [None] * LAYERS
    for layer in reversed(range(LAYERS)):
        kept = stored[layer]
        gate_scale = kept["gate_scale"]
        if layer == LAYERS - 1:
            grad_scale = kept["dots"]
        else:
            grad_scale = gather_rows(jnp.sum(grad_own * kept["proj_sum"], axis=1))
        gsq = -grad_scale * gate_scale**3 / INNER
        rev = functools.partial(by_rows, count=count, reverse=True)
        rev_group = functools.partial(by_group, count=count, reverse=True)
        gproj, dy, dz, gloc, suf, gsend, acc = call(
            gate_kernel,
            count,
            [
                (smem, place),
                (rev(1), gate_scale[:, None]),
                (rev(1), gsq[:, None]),
                (rev(inner), kept["y"]),
                (rev(inner), kept["zval"]),
                (whole((ROWS, inner)), kept["ggain"]),
                (whole((width, inner)), kept["wout"]),
                (rev(LANES), kept["cum"]),
                (rev(BC), kept["bc"]),
                (rev(ROWS), mask),
                (whole((LANES, inner)), expand),
            ]
            + by_piece(grad_h, count, True),
            [
                (rev(width), shape(tok, width, dtype=bf16)),
                (rev(inner), shape(tok, inner, dtype=bf16)),
                (rev(inner), shape(tok, inner, dtype=bf16)),
                (rev_group((STATE, inner)), shape(count, STATE, inner)),
                (rev_group((ROWS, inner)), shape(count, ROWS, inner)),
                (whole((STATE + ROWS, inner)), shape(STATE + ROWS, inner)),
                (whole((ROWS, inner)), shape(ROWS, inner)),
            ],
            [pltpu.VMEM((STATE, inner), f32), pltpu.VMEM((ROWS, inner), f32)],
            matmul_flops * inner,
            "gate_back",
        )
        u, dbc = call(
            intra_back_kernel,
            count,
            [
                (by_rows(LANES, count), kept["cum"]),
                (by_rows(inner, count), kept["xdt"]),
                (by_rows(BC, count), kept["bc"]),
                (by_rows(1, count), seg_col),
                (by_cols(count), seg_row),
                (by_rows(inner, count), dy),
            ],
            [
                (by_rows(inner, count), shape(tok, inner)),
                (by_rows(BC, count), shape(tok, BC)),
            ],
            [],
            matmul_flops * 1024,
            "ssd_within_back",
        )
        gout = chain(gsend, True)
        grad_wout = mm(gproj, kept["gate_in"], ((0,), (0,)))
        grad_wz = mm(kept["normed"], dz, ((0,), (0,)))
        partial_z = mm(dz, kept["wz"], ((1,), (1,)))
        gall, last8, rim, gtaps, vecs, dsk = call(
            in_back_kernel,
            count,
            [
                (rev(inner), u),
                (rev(BC), dbc),
                (rev(inner), dy),
                (rev(inner), kept["y"]),
                (rev(conv_cols), kept["cpre"]),
                (rev(conv_cols), kept["cin"]),
                (rev(LANES), kept["dtp"]),
                (rev(LANES), kept["dtv"]),
                (rev(LANES), kept["cum"]),
                (rev(inner), kept["xdt"]),
                (rev(BC), kept["bc"]),
                (rev(ROWS), mask),
                (rev_group((STATE, inner)), kept["sloc"]),
                (rev_group((ROWS, inner)), kept["pref"]),
                (whole((STATE, inner)), kept["entry"]),
                (rev_group((STATE, inner)), gloc),
                (rev_group((ROWS, inner)), suf),
                (whole((STATE, inner)), gout),
                (whole((ROWS, conv_cols)), kept["halo"]),
                (whole((CONV, conv_cols)), kept["taps"]),
                (whole((ROWS, LANES)), kept["dtb"]),
                (whole((ROWS, LANES)), kept["avec"]),
                (whole((ROWS, inner)), kept["dskip"]),
                (whole((LANES, inner)), expand),
                (whole((GROUP, GROUP)), triback),
            ],
            [
                (rev(all_cols), shape(tok, all_cols, dtype=bf16)),
                (whole((ROWS, conv_cols)), shape(ROWS, conv_cols)),
                (whole((ROWS, conv_cols)), shape(ROWS, conv_cols)),
                (whole((ROWS, conv_cols)), shape(ROWS, conv_cols)),
                (whole((ROWS, LANES)), shape(ROWS, LANES)),
                (whole((ROWS, inner)), shape(ROWS, inner)),
            ],
            [pltpu.VMEM((CONV - 1, ROWS, conv_cols), f32)],
            matmul_flops * 1024,
            "in_proj_conv_back",
        )
        rim_back = shifted(rim, -1)
        gall = lax.dynamic_update_slice(
            gall, (last8 + rim_back).astype(bf16), (tok - ROWS, 0)
        )
        partial = partial_z + mm(gall, kept["wall"], ((1,), (1,)))
        grad_normed = scatter_sum(partial)
        late = behind(gall, partial)
        grad_win = mm(kept["normed"], late[:, : inner + BC], ((0,), (0,)))
        grad_wdt = mm(kept["normed"], late[:, inner + BC :], ((0,), (0,)))
        hidden_in = kept["hidden"]
        inv = lax.rsqrt(jnp.mean(hidden_in * hidden_in, axis=1, keepdims=True) + epsilon)
        grad_ngain = jnp.sum(grad_normed * hidden_in * inv, axis=0)
        back = grad_normed * norm_gain[layer][None, :]
        grad_own = grad_own + inv * (
            back - hidden_in * inv * inv * jnp.mean(back * hidden_in, axis=1, keepdims=True)
        )
        if layer > 0:
            grad_h = gather_pieces(grad_own)
        matrices[layer] = [
            lax.psum_scatter(value, "chip", scatter_dimension=0, tiled=True)
            for value in (grad_wout, grad_wz, grad_win)
        ]
        if layer == LAYERS - 1:
            last_sum = scatter_sum(kept["proj"], (dy,), (u,), (gall,))
            hidden_own = hidden_own + own_rows(gate_scale)[:, None] * last_sum
        else:
            marks = ((dy,), (u,), (partial,))
            final_out = deliver(hidden_own, bf16, *marks)
            input_grad = deliver(grad_own, f32)
            matrices[1] = [behind(value, u) for value in matrices[1]]
            matrices[0] = [behind(value, grad_own) for value in matrices[0]]
            for number, (g_out, g_z, g_in) in enumerate(matrices):
                matrices[number] = (
                    place_rows(g_out),
                    place_rows(g_z),
                    place_rows(g_in[:, :inner]),
                    shared_rows(g_in[:, inner:]),
                )
        vectors[layer] = jnp.concatenate(
            [
                gtaps[: CONV + 1, :inner].reshape(-1),
                acc[0],
                vecs[0, :heads],
                vecs[1, :heads],
                dsk[0],
                grad_wdt[:, :heads].reshape(-1),
                gtaps[: CONV + 1, inner:].reshape(-1),
                grad_ngain,
            ]
        )
    vector = total(jnp.stack(vectors), ("zh", "chip"))
    other = swap(vector, "core")
    common = (CONV + 1) * BC + width
    by_head = jnp.where(held, vector, other)[:, :-common]
    shared = total((vector + other)[:, -common:], ("zl",))
    g_bc = shared[:, :-width].reshape(LAYERS, CONV + 1, BC)
    g_ngain = shared[:, -width:]
    at = 0
    pieces = []
    for size in (CONV * inner, inner, inner, heads, heads, inner, width * heads):
        pieces.append(by_head[:, at : at + size])
        at += size
    g_conv, g_bias, g_ggain, g_alog, g_dtb, g_dsk, g_wdt = pieces
    g_wdt = g_wdt.reshape(LAYERS, width, heads)
    rows = width // lax.axis_size(("chip", "core"))
    g_wdt = lax.dynamic_slice_in_dim(g_wdt, lax.axis_index(("chip", "core")) * rows, rows, axis=1)
    return (
        final_out,
        input_grad,
        g_ngain,
        jnp.stack([m[1] for m in matrices]),
        jnp.stack([m[2] for m in matrices]),
        jnp.stack([m[3] for m in matrices]),
        g_wdt,
        g_conv.reshape(LAYERS, CONV, inner),
        g_bc[:, :CONV],
        g_bias,
        g_bc[:, CONV],
        g_dtb,
        g_alog,
        jnp.sum(g_dsk.reshape(LAYERS, heads, HEADDIM), axis=2),
        g_ggain,
        jnp.stack([m[0] for m in matrices]),
    )


def place_rows(part):
    core, far = lax.axis_index("core"), lax.axis_index("zh")
    full = part + lax.ppermute(part, BOTH, CROSS_BACK)
    sent = lax.ppermute(take(full, 1 - core, 2), BOTH, CORE_OUT)
    return jnp.where(core == far, take(full, core, 2), sent)


def shared_rows(part):
    core = lax.axis_index("core")
    part = take(part, core, 2) + swap(take(part, 1 - core, 2), "core")
    return total(part, ("zl", "zh"))


def solution(mesh):
    seq, head = mesh.devices.shape
    mesh = jax.sharding.Mesh(
        mesh.devices.reshape(seq // 2, 2, 2, head // 2), ("chip", "core", "zh", "zl")
    )
    tokens, columns = ("chip", "core"), ("zh", "zl")
    by_col = P(None, None, columns)
    by_head = P(None, columns)
    both = P(None, tokens, columns)
    placed = (
        P(tokens, None),
        P(tokens),
        P(tokens, None),
        P(),
        by_col,
        by_col,
        P(),
        by_col,
        by_col,
        P(),
        by_head,
        P(),
        by_head,
        by_head,
        by_head,
        by_head,
        by_col,
    )
    return jax.shard_map(
        shards,
        mesh=mesh,
        in_specs=placed,
        out_specs=(
            P(tokens, None),
            P(tokens, None),
            P(),
            both,
            both,
            P(None, tokens, None),
            both,
            by_col,
            P(),
            by_head,
            P(),
            by_head,
            by_head,
            by_head,
            by_head,
            both,
        ),
        check_vma=False,
    )
```

```python
import functools

import jax
import jax.numpy as jnp
from jax import lax
from jax.experimental import pallas as pl
from jax.experimental.pallas import tpu as pltpu
from jax.sharding import PartitionSpec as P

HEADDIM = 64
STATE = 128
CONV = 4
GROUP = 256
LAYERS = 2
INNER = 2048
LANES = 128
ROWS = 8
BC = 2 * STATE

epsilon = 1e-05
highest = lax.Precision.HIGHEST
f32 = jnp.float32
bf16 = jnp.bfloat16


def mm(left, right, dims=((1,), (0,)), precision=None):
    return lax.dot_general(
        left, right, (dims, ((), ())), preferred_element_type=f32, precision=precision
    )


def softplus(value):
    small = jnp.exp(-jnp.abs(value))
    series = small * (1.0 - small * (0.5 - small * (1.0 / 3.0 - small * (0.25 - small * 0.2))))
    return jnp.maximum(value, 0.0) + jnp.where(small < 0.03, series, jnp.log(1.0 + small))


def silu_slope(value, sigma):
    return sigma * (1.0 + value * (1.0 - sigma))


def spread(heads, expand):
    return mm(heads, expand, precision=highest)


def gather_heads(lanes, expand):
    return mm(lanes, expand, ((1,), (1,)), precision=highest)


def pick(place, pieces, held):
    if len(pieces) == 1:
        return pieces[0][...]
    away = lax.bitwise_xor(pl.program_id(0) if held is None else held, place[0])
    value = pieces[3][...]
    for number in range(3):
        value = jnp.where(away == number, pieces[number][...], value)
    return value


def in_kernel(
    place, wall, ngain, taps, bias, dtb, avec, mask, halo, expand, tri, *refs
):
    hid = refs[:-14]
    normed, cin, cpre, dtp, cum, dtv, xdt, bc, sloc, pref, send, state, thru, prev = refs[-14:]
    step = pl.program_id(0)
    inner = expand.shape[1]

    @pl.when(step == 0)
    def _():
        state[...] = jnp.zeros_like(state)
        thru[...] = jnp.ones_like(thru)
        prev[...] = halo[...]

    h = pick(place, hid, None)
    inv = lax.rsqrt(jnp.mean(h * h, axis=1, keepdims=True) + epsilon)
    low = (h * inv * ngain[...]).astype(bf16)
    normed[...] = low
    rows = mm(low, wall[:, : inner + BC])
    pre_dt = mm(low, wall[:, inner + BC :])
    dtp[...] = pre_dt
    cin[...] = rows
    ext = jnp.concatenate([prev[...], rows], axis=0)
    prev[...] = rows[GROUP - ROWS :]
    total = taps[CONV - 1 : CONV, :] * rows + bias[0:1, :]
    for k in range(CONV - 1):
        first = ROWS - CONV + 1 + k
        total = total + taps[k : k + 1, :] * ext[first : first + GROUP] * mask[:, k : k + 1]
    cpre[...] = total
    act = total * jax.nn.sigmoid(total)
    x = act[:, :inner]
    low_bc = act[:, inner:].astype(bf16)
    bc[...] = low_bc
    dt = softplus(pre_dt + dtb[0:1, :])
    dtv[...] = dt
    run = mm(tri[...], dt * avec[0:1, :], precision=highest)
    cum[...] = run
    last = run[GROUP - 1 : GROUP]
    xdt[...] = (x * spread(dt, expand[...])).astype(bf16)
    tail = jnp.exp(last - run) * mask[:, 4:5] * dt
    contrib = mm(low_bc[:, :STATE], (x * spread(tail, expand[...])).astype(bf16), ((0,), (0,)))
    through = jnp.broadcast_to(jnp.exp(last) * mask[GROUP - 1 : GROUP, 3:4], (ROWS, LANES))
    through = spread(through, expand[...])
    sloc[0] = state[...]
    pref[0] = thru[...]
    state[...] = through[0:1] * state[...] + contrib
    thru[...] = thru[...] * through

    @pl.when(step == pl.num_programs(0) - 1)
    def _():
        send[:STATE] = state[...]
        send[STATE:] = thru[...]


def pair_lanes(value, which):
    lane = lax.broadcasted_iota(jnp.int32, value.shape, 1)
    keep = lane < HEADDIM if which == 0 else lane >= HEADDIM
    return jnp.where(keep, value, jnp.zeros_like(value))


def intra_kernel(cum, xdt, bc, seg, segrow, y):
    inner = xdt.shape[1]
    run = cum[...]
    run_t = run.T
    base = mm(bc[:, STATE:], bc[:, :STATE], ((1,), (1,)))
    t_at = lax.broadcasted_iota(jnp.int32, (GROUP, GROUP), 0)
    s_at = lax.broadcasted_iota(jnp.int32, (GROUP, GROUP), 1)
    same = (seg[:, 0:1] == segrow[0:1, :]) & (t_at >= s_at)
    closed = jnp.where(same, 0.0, -1e30)
    for pair in range(inner // LANES):
        cols = slice(pair * LANES, (pair + 1) * LANES)
        xs = xdt[:, cols]
        parts = []
        for which in range(2):
            head = 2 * pair + which
            decay = jnp.exp(run[:, head : head + 1] - run_t[head : head + 1, :] + closed)
            parts.append(mm((decay * base).astype(bf16), xs))
        lane = lax.broadcasted_iota(jnp.int32, (GROUP, LANES), 1)
        y[:, cols] = jnp.where(lane < HEADDIM, parts[0], parts[1])


def out_kernel(
    yin, cpre, cum, bc, mask, zval, sloc, pref, entry, dskip, ggain, wout, expand, *refs
):
    cot, (y, gate_in, proj, sums) = refs[:-4], refs[-4:]
    inner = expand.shape[1]
    pre = cpre[...]
    x = pre * jax.nn.sigmoid(pre)
    full = sloc[0] + pref[0][0:1] * entry[...]
    reach = spread(jnp.exp(cum[...]) * mask[:, 3:4], expand[...])
    value = yin[...] + reach * mm(bc[:, STATE:], full.astype(bf16)) + dskip[0:1, :] * x
    y[...] = value
    z = zval[...]
    gated = value * (z * jax.nn.sigmoid(z))
    low = (gated * ggain[0:1, :]).astype(bf16)
    gate_in[...] = low
    proj[...] = mm(low, wout[...], ((1,), (1,)))
    ones = jnp.ones((ROWS, inner), f32)
    squares = mm(ones, gated * gated, ((1,), (1,)), precision=highest)
    if cot:
        back = mm(cot[0][...].astype(bf16), wout[...])
        dots = mm(ones, low.astype(f32) * back, ((1,), (1,)), precision=highest)
        row = lax.broadcasted_iota(jnp.int32, squares.shape, 0)
        squares = jnp.where(row == 0, squares, dots)
    sums[...] = squares


def gate_kernel(
    place, scale, gsq, y, zval, ggain, wout, cum, bc, mask, expand, *refs
):
    gh = refs[:-9]
    gproj, dy, dz, gloc, suf, send, acc, carry, thru = refs[-9:]
    step = pl.program_id(0)

    @pl.when(step == 0)
    def _():
        carry[...] = jnp.zeros_like(carry)
        thru[...] = jnp.ones_like(thru)
        acc[...] = jnp.zeros_like(acc)

    gp = (scale[...] * pick(place, gh, pl.num_programs(0) - 1 - step)).astype(bf16)
    gproj[...] = gp
    ggi = mm(gp, wout[...])
    z = zval[...]
    sigma = jax.nn.sigmoid(z)
    silu = z * sigma
    value = y[...]
    gated = value * silu
    ggated = ggi * ggain[0:1, :] + gated * gsq[...]
    acc[0:1, :] += jnp.sum(ggi * gated, axis=0, keepdims=True)
    low = (ggated * silu).astype(bf16)
    dy[...] = low
    dz[...] = (ggated * value * silu_slope(z, sigma)).astype(bf16)
    run = cum[...]
    last = run[GROUP - 1 : GROUP]
    reach = spread(jnp.exp(run) * mask[:, 3:4], expand[...])
    back = mm(bc[:, STATE:], (reach * low.astype(f32)).astype(bf16), ((0,), (0,)))
    through = jnp.broadcast_to(jnp.exp(last) * mask[GROUP - 1 : GROUP, 3:4], (ROWS, LANES))
    through = spread(through, expand[...])
    gloc[0] = carry[...]
    suf[0] = thru[...]
    carry[...] = back + through[0:1] * carry[...]
    thru[...] = thru[...] * through

    @pl.when(step == pl.num_programs(0) - 1)
    def _():
        send[:STATE] = carry[...]
        send[STATE:] = thru[...]


def intra_back_kernel(cum, xdt, bc, seg, segrow, dy, u, dbc):
    inner = xdt.shape[1]
    run = cum[...]
    run_t = run.T
    base = mm(bc[:, :STATE], bc[:, STATE:], ((1,), (1,)))
    s_at = lax.broadcasted_iota(jnp.int32, (GROUP, GROUP), 0)
    t_at = lax.broadcasted_iota(jnp.int32, (GROUP, GROUP), 1)
    same = (seg[:, 0:1] == segrow[0:1, :]) & (t_at >= s_at)
    closed = jnp.where(same, 0.0, -1e30)
    grad_base = jnp.zeros((GROUP, GROUP), f32)
    for pair in range(inner // LANES):
        cols = slice(pair * LANES, (pair + 1) * LANES)
        xs = xdt[:, cols]
        ds = dy[:, cols]
        parts = []
        for which in range(2):
            head = 2 * pair + which
            decay = jnp.exp(run_t[head : head + 1, :] - run[:, head : head + 1] + closed)
            parts.append(mm((decay * base).astype(bf16), ds))
            grad_base = grad_base + decay * mm(xs, pair_lanes(ds, which), ((1,), (1,)))
        lane = lax.broadcasted_iota(jnp.int32, (GROUP, LANES), 1)
        u[:, cols] = jnp.where(lane < HEADDIM, parts[0], parts[1])
    low = grad_base.astype(bf16)
    dbc[:, :STATE] = mm(low, bc[:, STATE:])
    dbc[:, STATE:] = mm(low, bc[:, :STATE], ((0,), (0,)))


def in_back_kernel(
    uin, dbc, dy, y, cpre, cin, dtp, dtv, cum, xdt, bc, mask, sloc, pref, entry, gloc, suf,
    gout, halo, taps, dtb, avec, dskip, expand, triback,
    gall, last8, rim, gtaps, vecs, dsk,
    nexts,
):
    step = pl.program_id(0)
    inner = expand.shape[1]

    @pl.when(step == 0)
    def _():
        nexts[...] = jnp.zeros_like(nexts)
        gtaps[...] = jnp.zeros_like(gtaps)
        vecs[...] = jnp.zeros_like(vecs)
        dsk[...] = jnp.zeros_like(dsk)

    e = expand[...]
    pre = cpre[...]
    sigma = jax.nn.sigmoid(pre)
    x = (pre * sigma)[:, :inner]
    full = sloc[0] + pref[0][0:1] * entry[...]
    nxt = gloc[0] + suf[0][0:1] * gout[...]
    nxt_low = nxt.astype(bf16)
    run = cum[...]
    last = run[GROUP - 1 : GROUP]
    dt = dtv[...]
    low_dy = dy[...].astype(f32)
    xw = xdt[...].astype(f32)
    tail = spread(jnp.exp(last - run) * mask[:, 4:5], e)
    reach = spread(jnp.exp(run) * mask[:, 3:4], e)
    u_inter = tail * mm(bc[:, :STATE], nxt_low)
    u = uin[...] + u_inter
    dx = spread(dt, e) * u + dskip[0:1, :] * low_dy
    dsk[0:1, :] += jnp.sum(low_dy * x, axis=0, keepdims=True)
    db = dbc[:, :STATE] + mm((tail * xw).astype(bf16), nxt_low, ((1,), (1,)))
    dc = dbc[:, STATE:] + mm((reach * low_dy).astype(bf16), full.astype(bf16), ((1,), (1,)))
    grad_dt = gather_heads(x * u, e)
    y_plain = y[...] - dskip[0:1, :] * x
    grad_cum = gather_heads(low_dy * y_plain - xw * u, e)
    flow = jnp.sum(nxt * full, axis=0, keepdims=True)
    flow = gather_heads(jnp.broadcast_to(flow, (ROWS, inner)), e)[0:1]
    ends = jnp.sum(xw * u_inter, axis=0, keepdims=True)
    ends = gather_heads(jnp.broadcast_to(ends, (ROWS, inner)), e)[0:1]
    grad_tot = mask[GROUP - 1 : GROUP, 3:4] * jnp.exp(last) * flow + ends
    grad_da = mm(triback[...], grad_cum, precision=highest) + grad_tot
    a = avec[0:1, :]
    grad_dtv = grad_dt + grad_da * a
    grad_dtpre = grad_dtv * jax.nn.sigmoid(dtp[...] + dtb[0:1, :])
    vecs[0:1, :] += jnp.sum(grad_da * dt, axis=0, keepdims=True) * a
    vecs[1:2, :] += jnp.sum(grad_dtpre, axis=0, keepdims=True)
    slope = silu_slope(pre, sigma)
    grad_pre = jnp.concatenate([dx, db, dc], axis=1) * slope
    gtaps[4:5, :] += jnp.sum(grad_pre, axis=0, keepdims=True)
    rows = cin[...]
    grad_rows = taps[CONV - 1 : CONV, :] * grad_pre
    gtaps[3:4, :] += jnp.sum(rows * grad_pre, axis=0, keepdims=True)
    masked = []
    for k in range(CONV - 1):
        m = grad_pre * mask[:, k : k + 1]
        masked.append(m[:ROWS])
        ahead = CONV - 1 - k
        shifted = jnp.concatenate([m, nexts[k]], axis=0)[ahead : ahead + GROUP]
        grad_rows = grad_rows + taps[k : k + 1, :] * shifted
        gtaps[k : k + 1, :] += jnp.sum(rows * shifted, axis=0, keepdims=True)
    for k in range(CONV - 1):
        nexts[k] = masked[k]
    gall[:, : inner + BC] = grad_rows.astype(bf16)
    gall[:, inner + BC :] = grad_dtpre.astype(bf16)

    @pl.when(step == 0)
    def _():
        last8[...] = grad_rows[GROUP - ROWS :]

    @pl.when(step == pl.num_programs(0) - 1)
    def _():
        spill = jnp.zeros((ROWS, inner + BC), f32)
        edge = halo[...]
        for k in range(CONV - 1):
            down = ROWS - CONV + 1 + k
            moved = jnp.concatenate([jnp.zeros((ROWS, inner + BC), f32), masked[k]], axis=0)
            moved = moved[ROWS - down : 2 * ROWS - down]
            spill = spill + taps[k : k + 1, :] * moved
            gtaps[k : k + 1, :] += jnp.sum(edge * moved, axis=0, keepdims=True)
        rim[...] = spill


def whole(shape):
    return pl.BlockSpec(shape, lambda c: (0,) * len(shape))


def by_rows(cols, count, reverse=False):
    if reverse:
        return pl.BlockSpec((GROUP, cols), lambda c: (count - 1 - c, 0))
    return pl.BlockSpec((GROUP, cols), lambda c: (c, 0))


def by_group(shape, count, reverse=False):
    if reverse:
        return pl.BlockSpec((1,) + shape, lambda c: (count - 1 - c, 0, 0))
    return pl.BlockSpec((1,) + shape, lambda c: (c, 0, 0))


def by_piece(pieces, count, reverse=False):
    if len(pieces) == 1:
        return [(by_rows(pieces[0].shape[1], count, reverse), pieces[0])]
    return [(whole(piece.shape), piece) for piece in pieces]


def by_cols(count):
    return pl.BlockSpec((ROWS, GROUP), lambda c: (0, c))


def call(kernel, count, ins, outs, scratch, flops, name):
    return pl.pallas_call(
        kernel,
        grid=(count,),
        in_specs=[spec for spec, _ in ins],
        out_specs=[spec for spec, _ in outs],
        out_shape=[shape for _, shape in outs],
        scratch_shapes=scratch,
        compiler_params=pltpu.CompilerParams(
            dimension_semantics=("arbitrary",), vmem_limit_bytes=56 * 1024 * 1024
        ),
        cost_estimate=pl.CostEstimate(
            flops=flops, bytes_accessed=8 * 1024 * 1024, transcendentals=0
        ),
        name=name,
    )(*[value for _, value in ins])


def shape(*dims, dtype=f32):
    return jax.ShapeDtypeStruct(dims, dtype)


SWAP = ((0, 1), (1, 0))
CROSS = ((0, 1), (3, 2))
CROSS_BACK = ((1, 0), (2, 3))
CORE_OUT = ((0, 2), (3, 1))
CORE_IN = ((2, 0), (1, 3))
DIAGONAL = ((2, 1), (1, 2))
BOTH = ("core", "zh")
BLOCKS = ("chip", "zh")


def shifted(value, steps):
    count = lax.axis_size(BLOCKS)
    leading, last = (max(0, -steps), min(count, count - steps))
    return lax.ppermute(value, BLOCKS, [(source, source + steps) for source in range(leading, last)])


def chain(part, reverse):
    count = lax.axis_size(BLOCKS)
    place = lax.axis_index(BLOCKS)
    state, decay = part[:STATE], part[STATE : STATE + 1]
    entry, reach = jnp.zeros_like(state), jnp.ones_like(decay)
    step = 1
    while step < count:
        got = lax.ppermute(part, BLOCKS, [(i, i ^ step) for i in range(count)])
        got_state, got_decay = got[:STATE], got[STATE : STATE + 1]
        later = ((place & step) == 0) if reverse else ((place & step) != 0)
        entry = jnp.where(later, entry + reach * got_state, entry)
        reach = jnp.where(later, reach * got_decay, reach)
        state = jnp.where(later, state + decay * got_state, got_state + got_decay * state)
        decay = decay * got_decay
        part = jnp.concatenate([state, jnp.broadcast_to(decay, (ROWS, decay.shape[1]))])
        step *= 2
    return entry


def swap(value, axis):
    return lax.ppermute(value, axis, SWAP)


def total(value, axes):
    for axis in axes:
        count = lax.axis_size(axis)
        step = 1
        while step < count:
            value = value + lax.ppermute(value, axis, [(i, i ^ step) for i in range(count)])
            step *= 2
    return value


def take(value, index, count):
    size = value.shape[0] // count
    return lax.dynamic_slice_in_dim(value, index * size, size)


def ordered(place, mine, theirs):
    return jnp.where(
        place == 0, jnp.concatenate([mine, theirs]), jnp.concatenate([theirs, mine])
    )


def behind(value, *marks):
    return lax.optimization_barrier((value, *marks))[0]


def scatter_sum(part, mark=()):
    core, near = lax.axis_index("core"), lax.axis_index("zl")
    half = take(part, core, 2) + behind(swap(take(part, 1 - core, 2), "core"), *mark)
    if lax.axis_size("zl") == 2:
        return take(half, near, 2) + swap(take(half, 1 - near, 2), "zl")
    return lax.psum_scatter(half, "zl", scatter_dimension=0, tiled=True)


def own_rows(value):
    core, near = lax.axis_index("core"), lax.axis_index("zl")
    return take(take(value, core, 2), near, lax.axis_size("zl"))


def gather_near(value):
    if lax.axis_size("zl") == 2:
        return ordered(lax.axis_index("zl"), value, swap(value, "zl"))
    return lax.all_gather(value, "zl", tiled=True)


def gather_rows(value):
    half = gather_near(value)
    return ordered(lax.axis_index("core"), half, swap(half, "core"))


def own_place():
    return 2 * lax.axis_index("core") + lax.axis_index("zl")


def gather_pieces(value):
    if lax.axis_size("zl") != 2 or value.shape[0] != GROUP:
        return [gather_rows(value)]
    near = swap(value, "zl")
    return [value, near, swap(value, "core"), swap(near, "core")]


def place_kernel(place, value, mine, near, theirs, value_s, mine_s, near_s, theirs_s, out):
    away = lax.bitwise_xor(pl.program_id(0), place[0])
    pairs = ((value, mine), (value_s, mine_s), (near, theirs), (near_s, theirs_s))
    for number, (here, there) in enumerate(pairs):

        @pl.when((away == number) & (place[1] == 1))
        def _():
            out[...] = here[...].astype(out.dtype)

        @pl.when((away == number) & (place[1] == 0))
        def _():
            out[...] = there[...].astype(out.dtype)


def cross_over(value):
    return [lax.ppermute(value, BOTH, pairs) for pairs in (CROSS, DIAGONAL, CORE_IN)]


def deliver(value, mine, theirs, near, dtype):
    core, far = lax.axis_index("core"), lax.axis_index("zh")
    held = core == far
    if lax.axis_size("zl") != 2 or value.shape[0] != GROUP:
        mine = gather_near(jnp.where(held, value, mine))
        theirs = gather_near(jnp.where(held, near, theirs))
        full = ordered(core, mine, theirs)
        return narrowed(full) if dtype == bf16 else full
    axes = ("core", "zh", "zl")
    here = [(2 * kind + i, 2 * kind + 1 - i) for kind in (0, 3) for i in range(2)]
    there = [(2 * kind + i, 2 * kind + 1 - i) for kind in (1, 2) for i in range(2)]
    value_s = lax.ppermute(value, axes, here)
    near_s = lax.ppermute(near, axes, here)
    mine_s = lax.ppermute(mine, axes, there)
    theirs_s = lax.ppermute(theirs, axes, there)
    place = jnp.stack([own_place(), held.astype(jnp.int32)]).astype(jnp.int32)
    width = value.shape[1]
    parts = (value, mine, near, theirs, value_s, mine_s, near_s, theirs_s)
    return pl.pallas_call(
        place_kernel,
        grid=(4,),
        in_specs=[pl.BlockSpec(memory_space=pltpu.SMEM)] + [whole((GROUP, width))] * 8,
        out_specs=by_rows(width, 4),
        out_shape=shape(4 * GROUP, width, dtype=dtype),
        compiler_params=pltpu.CompilerParams(
            dimension_semantics=("arbitrary",), vmem_limit_bytes=40 * 1024 * 1024
        ),
        name="place",
    )(place, *parts)


def to_block(value):
    got = lax.ppermute(value, BOTH, CORE_OUT)
    return jnp.where(lax.axis_index("core") == lax.axis_index("zh"), value, got)


def eight(row):
    return jnp.broadcast_to(row[None, :], (ROWS, row.shape[0]))


def pad_lanes(value):
    return jnp.pad(value, [(0, 0)] * (value.ndim - 1) + [(0, LANES - value.shape[-1])])


def weight_kernel(count, extra, place, *refs):
    own, rest = refs[:count], refs[count:]
    outs, rest = rest[-count:], rest[:-count]
    parts, more = (rest[:-2], rest[-2:]) if extra else (rest, ())
    block = pl.program_id(0)
    at = 0
    for source, out in zip(own, outs):
        cols = source.shape[1]

        @pl.when(place[1] == 1)
        def _():
            out[:, :cols] = source[...]

        for away, part in enumerate(parts):

            @pl.when((place[1] == 0) & (lax.bitwise_xor(place[0], block) == away))
            def _():
                out[:, :cols] = part[:, at : at + cols].astype(bf16)

        at += cols
    if more:
        cols = own[0].shape[1]
        outs[0][:, cols : cols + BC] = more[0][...]
        outs[0][:, cols + BC :] = more[1][...].astype(bf16)


def narrow_kernel(wide, narrow):
    narrow[...] = wide[...].astype(bf16)


def narrowed(value):
    rows, cols = value.shape
    return pl.pallas_call(
        narrow_kernel,
        grid=(rows // GROUP,),
        in_specs=[by_rows(cols, 0)],
        out_specs=by_rows(cols, 0),
        out_shape=shape(rows, cols, dtype=bf16),
        name="narrowed",
    )(value)


def gather_weights(own, more=(), first=(), second=(), third=()):
    width = own[0].shape[0]
    chips = lax.axis_size("chip")
    chip = lax.axis_index("chip")
    held = (lax.axis_index("core") == lax.axis_index("zh")).astype(jnp.int32)
    size = width // chips
    piece = jnp.concatenate(
        [
            lax.dynamic_slice_in_dim(value, chip * size, size).astype(f32)
            for value in behind(own, *first)
        ],
        axis=1,
    )
    piece = behind(lax.ppermute(piece, BOTH, CROSS), *second)
    if chips == 4:
        parts = [piece]
        for away in range(1, chips):
            pairs = [
                (4 * c + kind, 4 * (c ^ away) + kind) for c in range(chips) for kind in (1, 2)
            ]
            parts.append(lax.ppermute(piece, ("chip", "core", "zh"), pairs))
        place = jnp.stack([chip, held]).astype(jnp.int32)
        blocks = chips
    else:
        parts = [lax.all_gather(piece, "chip", tiled=True)]
        place = jnp.stack([0, held]).astype(jnp.int32)
        blocks, size = 1, width
    parts = behind(parts, *third)
    out_cols = [value.shape[1] for value in own]
    out_cols[0] += sum(value.shape[1] for value in more)

    def rows(cols):
        return pl.BlockSpec((size, cols), lambda c: (c, 0))

    return pl.pallas_call(
        functools.partial(weight_kernel, len(own), bool(more)),
        grid=(blocks,),
        in_specs=[pl.BlockSpec(memory_space=pltpu.SMEM)]
        + [rows(value.shape[1]) for value in own]
        + [whole(piece.shape if chips == 4 else parts[0].shape)] * len(parts)
        + [rows(value.shape[1]) for value in more],
        out_specs=[rows(cols) for cols in out_cols],
        out_shape=[shape(width, cols, dtype=bf16) for cols in out_cols],
        compiler_params=pltpu.CompilerParams(
            dimension_semantics=("arbitrary",), vmem_limit_bytes=40 * 1024 * 1024
        ),
        name="weights",
    )(place, *own, *parts, *more)


def shards(
    x_input,
    seg_ids,
    cotangent,
    norm_gain,
    w_z,
    w_x,
    w_bc,
    w_dt,
    conv_x,
    conv_bc,
    bias_x,
    bias_bc,
    dt_bias,
    a_log,
    d_skip,
    gate_gain,
    w_out,
):
    tok, width = x_input.shape
    inner = w_z.shape[2]
    core, far = lax.axis_index("core"), lax.axis_index("zh")
    held = core == far
    heads = w_dt.shape[2]
    count = tok // GROUP
    conv_cols = inner + BC
    all_cols = inner + BC + LANES

    dt_own = w_dt.astype(f32).reshape(LAYERS, width * heads // LANES, LANES)
    dt_sent = lax.ppermute(dt_own, BOTH, CROSS)
    dt_all = pad_lanes(jnp.where(held, dt_own, dt_sent).reshape(LAYERS, width, heads))
    (wall,) = gather_weights([w_x[0]], (w_bc[0], dt_all[0]))
    hidden = to_block(x_input.astype(f32))
    cotangent = to_block(behind(cotangent.astype(f32), hidden))
    seg = to_block(seg_ids.astype(f32))
    small = jnp.concatenate(
        [
            value.reshape(LAYERS, -1)
            for value in (conv_x, bias_x, dt_bias, a_log, d_skip, gate_gain)
        ],
        axis=1,
    )
    small = jnp.where(held, small, lax.ppermute(small, BOTH, CROSS))
    sizes = (CONV * inner, inner, heads, heads, heads, inner)
    pieces, at = [], 0
    for size in sizes:
        pieces.append(small[:, at : at + size])
        at += size
    conv_x, bias_x, dt_bias, a_log, d_skip, gate_gain = pieces
    conv_x = conv_x.reshape(LAYERS, CONV, inner)
    hidden_own = own_rows(hidden)
    hidden = [hidden]
    place = jnp.stack([own_place(), own_place()]).astype(jnp.int32)
    smem = pl.BlockSpec(memory_space=pltpu.SMEM)
    edge_seg = shifted(seg[tok - ROWS :], 1)
    seg_ext = jnp.concatenate([edge_seg, seg])
    before = jnp.concatenate([edge_seg[ROWS - 1 :], seg[GROUP - 1 : tok - 1 : GROUP]])
    after = seg[GROUP - 1 :: GROUP]
    mask = jnp.stack(
        [
            (seg_ext[ROWS - CONV + 1 + k : ROWS - CONV + 1 + k + tok] == seg).astype(f32)
            for k in range(CONV - 1)
        ]
        + [
            (seg == jnp.repeat(before, GROUP)).astype(f32),
            (seg == jnp.repeat(after, GROUP)).astype(f32),
            seg,
            seg,
            seg,
        ],
        axis=1,
    )
    seg_col = seg[:, None]
    seg_row = eight(seg)
    expand = (jnp.arange(LANES)[:, None] == jnp.arange(inner)[None, :] // HEADDIM).astype(f32)
    position = jnp.arange(GROUP)
    tri = (position[:, None] >= position[None, :]).astype(f32)
    triback = (position[:, None] <= position[None, :]).astype(f32)

    matmul_flops = 2 * tok * width
    stored = []
    for layer in range(LAYERS):
        if layer > 0:
            wall = next_wall
        taps = jnp.concatenate([conv_x[layer], conv_bc[layer]], axis=1)
        bias = eight(jnp.concatenate([bias_x[layer], bias_bc[layer]]))
        dtb = eight(pad_lanes(dt_bias[layer]))
        avec = eight(pad_lanes(-jnp.exp(a_log[layer])))
        dskip = eight(jnp.repeat(d_skip[layer], HEADDIM))
        ggain = eight(gate_gain[layer])
        ngain = norm_gain[layer][None, :]
        if len(hidden) == 1:
            end = hidden[0][tok - 16 :]
        else:
            ends = jnp.stack([piece[GROUP - 16 :] for piece in hidden])
            end = lax.dynamic_index_in_dim(ends, 3 ^ own_place(), 0, False)
        end = end * lax.rsqrt(jnp.mean(end * end, axis=1, keepdims=True) + epsilon) * ngain
        end = mm(end.astype(bf16), wall[:, : inner + BC])[ROWS:]
        halo = shifted(end, 1)
        normed, cin, cpre, dtp, cum, dtv, xdt, bc, sloc, pref, send = call(
            in_kernel,
            count,
            [
                (smem, place),
                (whole((width, all_cols)), wall),
                (whole((1, width)), ngain),
                (whole((CONV, conv_cols)), taps),
                (whole((ROWS, conv_cols)), bias),
                (whole((ROWS, LANES)), dtb),
                (whole((ROWS, LANES)), avec),
                (by_rows(ROWS, count), mask),
                (whole((ROWS, conv_cols)), halo),
                (whole((LANES, inner)), expand),
                (whole((GROUP, GROUP)), tri),
            ]
            + by_piece(hidden, count),
            [
                (by_rows(width, count), shape(tok, width, dtype=bf16)),
                (by_rows(conv_cols, count), shape(tok, conv_cols)),
                (by_rows(conv_cols, count), shape(tok, conv_cols)),
                (by_rows(LANES, count), shape(tok, LANES)),
                (by_rows(LANES, count), shape(tok, LANES)),
                (by_rows(LANES, count), shape(tok, LANES)),
                (by_rows(inner, count), shape(tok, inner, dtype=bf16)),
                (by_rows(BC, count), shape(tok, BC, dtype=bf16)),
                (by_group((STATE, inner), count), shape(count, STATE, inner)),
                (by_group((ROWS, inner), count), shape(count, ROWS, inner)),
                (whole((STATE + ROWS, inner)), shape(STATE + ROWS, inner)),
            ],
            [
                pltpu.VMEM((STATE, inner), f32),
                pltpu.VMEM((ROWS, inner), f32),
                pltpu.VMEM((ROWS, conv_cols), f32),
            ],
            matmul_flops * all_cols,
            "in_proj_conv",
        )
        if layer == 0:
            wz, wout = gather_weights(
                [w_z[0], w_out[0]], first=(hidden[0],), second=(wall,), third=(send,)
            )
        else:
            wz, wout = next_wz, next_wout
        zval = mm(normed, wz)
        (yin,) = call(
            intra_kernel,
            count,
            [
                (by_rows(LANES, count), cum),
                (by_rows(inner, count), xdt),
                (by_rows(BC, count), bc),
                (by_rows(1, count), seg_col),
                (by_cols(count), seg_row),
            ],
            [(by_rows(inner, count), shape(tok, inner))],
            [],
            matmul_flops * 512,
            "ssd_within",
        )
        entry = chain(send, False)
        y, gate_in, proj, sums = call(
            out_kernel,
            count,
            [
                (by_rows(inner, count), yin),
                (by_rows(inner, count), cpre),
                (by_rows(LANES, count), cum),
                (by_rows(BC, count), bc),
                (by_rows(ROWS, count), mask),
                (by_rows(inner, count), zval),
                (by_group((STATE, inner), count), sloc),
                (by_group((ROWS, inner), count), pref),
                (whole((STATE, inner)), entry),
                (whole((ROWS, inner)), dskip),
                (whole((ROWS, inner)), ggain),
                (whole((width, inner)), wout),
                (whole((LANES, inner)), expand),
            ]
            + ([(by_rows(width, count), cotangent)] if layer == LAYERS - 1 else []),
            [
                (by_rows(inner, count), shape(tok, inner)),
                (by_rows(inner, count), shape(tok, inner, dtype=bf16)),
                (by_rows(width, count), shape(tok, width)),
                (by_cols(count), shape(ROWS, tok)),
            ],
            [],
            matmul_flops * 2 * inner,
            "gate_out_proj",
        )
        sums = total(sums, ("core", "zl"))
        gate_scale = lax.rsqrt(sums[0] / INNER + epsilon)
        stored.append(
            dict(
                hidden=hidden_own, normed=normed, zval=zval, cin=cin, cpre=cpre, dtp=dtp, cum=cum,
                dtv=dtv, xdt=xdt, bc=bc, sloc=sloc, pref=pref, entry=entry, y=y, gate_in=gate_in,
                proj=proj, gate_scale=gate_scale, dots=sums[1], halo=halo, wall=wall, wz=wz, wout=wout,
                taps=taps, dtb=dtb, avec=avec, dskip=dskip, ggain=ggain,
            )
        )
        if layer < LAYERS - 1:
            next_wall, next_wz, next_wout = gather_weights(
                [w_x[1], w_z[1], w_out[1]],
                (w_bc[1], dt_all[1]),
                first=(yin,),
                second=(proj,),
                third=(gate_scale,),
            )
            proj_sum = scatter_sum(proj)
            stored[layer]["proj_sum"] = proj_sum
            hidden_own = hidden_own + own_rows(gate_scale)[:, None] * proj_sum
            hidden = gather_pieces(hidden_own)

    grad_h = [cotangent]
    grad_own = own_rows(cotangent)
    matrices = [None] * LAYERS
    vectors = [None] * LAYERS
    shared = [None] * LAYERS
    for layer in reversed(range(LAYERS)):
        kept = stored[layer]
        gate_scale = kept["gate_scale"]
        if layer == LAYERS - 1:
            grad_scale = kept["dots"]
        else:
            grad_scale = gather_rows(jnp.sum(grad_own * kept["proj_sum"], axis=1))
        gsq = -grad_scale * gate_scale**3 / INNER
        rev = functools.partial(by_rows, count=count, reverse=True)
        rev_group = functools.partial(by_group, count=count, reverse=True)
        gproj, dy, dz, gloc, suf, gsend, acc = call(
            gate_kernel,
            count,
            [
                (smem, place),
                (rev(1), gate_scale[:, None]),
                (rev(1), gsq[:, None]),
                (rev(inner), kept["y"]),
                (rev(inner), kept["zval"]),
                (whole((ROWS, inner)), kept["ggain"]),
                (whole((width, inner)), kept["wout"]),
                (rev(LANES), kept["cum"]),
                (rev(BC), kept["bc"]),
                (rev(ROWS), mask),
                (whole((LANES, inner)), expand),
            ]
            + by_piece(grad_h, count, True),
            [
                (rev(width), shape(tok, width, dtype=bf16)),
                (rev(inner), shape(tok, inner, dtype=bf16)),
                (rev(inner), shape(tok, inner, dtype=bf16)),
                (rev_group((STATE, inner)), shape(count, STATE, inner)),
                (rev_group((ROWS, inner)), shape(count, ROWS, inner)),
                (whole((STATE + ROWS, inner)), shape(STATE + ROWS, inner)),
                (whole((ROWS, inner)), shape(ROWS, inner)),
            ],
            [pltpu.VMEM((STATE, inner), f32), pltpu.VMEM((ROWS, inner), f32)],
            matmul_flops * inner,
            "gate_back",
        )
        u, dbc = call(
            intra_back_kernel,
            count,
            [
                (by_rows(LANES, count), kept["cum"]),
                (by_rows(inner, count), kept["xdt"]),
                (by_rows(BC, count), kept["bc"]),
                (by_rows(1, count), seg_col),
                (by_cols(count), seg_row),
                (by_rows(inner, count), dy),
            ],
            [
                (by_rows(inner, count), shape(tok, inner)),
                (by_rows(BC, count), shape(tok, BC)),
            ],
            [],
            matmul_flops * 1024,
            "ssd_within_back",
        )
        gout = chain(gsend, True)
        if layer == LAYERS - 1:
            last_sum = scatter_sum(kept["proj"], (dy,))
            hidden_own = hidden_own + own_rows(gate_scale)[:, None] * last_sum
            u = behind(u, hidden_own)
        else:
            out_parts = cross_over(behind(hidden_own, gout))
            first_sums = join_halves(behind(matrices[LAYERS - 1], dy))
        grad_wout = mm(gproj, kept["gate_in"], ((0,), (0,)))
        grad_wz = mm(kept["normed"], dz, ((0,), (0,)))
        partial_z = mm(dz, kept["wz"], ((1,), (1,)))
        gall, last8, rim, gtaps, vecs, dsk = call(
            in_back_kernel,
            count,
            [
                (rev(inner), u),
                (rev(BC), dbc),
                (rev(inner), dy),
                (rev(inner), kept["y"]),
                (rev(conv_cols), kept["cpre"]),
                (rev(conv_cols), kept["cin"]),
                (rev(LANES), kept["dtp"]),
                (rev(LANES), kept["dtv"]),
                (rev(LANES), kept["cum"]),
                (rev(inner), kept["xdt"]),
                (rev(BC), kept["bc"]),
                (rev(ROWS), mask),
                (rev_group((STATE, inner)), kept["sloc"]),
                (rev_group((ROWS, inner)), kept["pref"]),
                (whole((STATE, inner)), kept["entry"]),
                (rev_group((STATE, inner)), gloc),
                (rev_group((ROWS, inner)), suf),
                (whole((STATE, inner)), gout),
                (whole((ROWS, conv_cols)), kept["halo"]),
                (whole((CONV, conv_cols)), kept["taps"]),
                (whole((ROWS, LANES)), kept["dtb"]),
                (whole((ROWS, LANES)), kept["avec"]),
                (whole((ROWS, inner)), kept["dskip"]),
                (whole((LANES, inner)), expand),
                (whole((GROUP, GROUP)), triback),
            ],
            [
                (rev(all_cols), shape(tok, all_cols, dtype=bf16)),
                (whole((ROWS, conv_cols)), shape(ROWS, conv_cols)),
                (whole((ROWS, conv_cols)), shape(ROWS, conv_cols)),
                (whole((ROWS, conv_cols)), shape(ROWS, conv_cols)),
                (whole((ROWS, LANES)), shape(ROWS, LANES)),
                (whole((ROWS, inner)), shape(ROWS, inner)),
            ],
            [pltpu.VMEM((CONV - 1, ROWS, conv_cols), f32)],
            matmul_flops * 1024,
            "in_proj_conv_back",
        )
        rim_back = shifted(rim, -1)
        if layer == 0:
            last8 = behind(last8, first_sums)
        gall = lax.dynamic_update_slice(
            gall, (last8 + rim_back).astype(bf16), (tok - ROWS, 0)
        )
        partial = partial_z + mm(gall, kept["wall"], ((1,), (1,)))
        grad_normed = scatter_sum(partial)
        if layer == 0:
            grad_normed = behind(grad_normed, *out_parts)
        late = behind(gall, partial)
        grad_win = mm(kept["normed"], late[:, : inner + BC], ((0,), (0,)))
        grad_wdt = mm(kept["normed"], late[:, inner + BC :], ((0,), (0,)))
        hidden_in = kept["hidden"]
        inv = lax.rsqrt(jnp.mean(hidden_in * hidden_in, axis=1, keepdims=True) + epsilon)
        grad_ngain = jnp.sum(grad_normed * hidden_in * inv, axis=0)
        back = grad_normed * norm_gain[layer][None, :]
        grad_own = grad_own + inv * (
            back - hidden_in * inv * inv * jnp.mean(back * hidden_in, axis=1, keepdims=True)
        )
        if layer > 0:
            grad_h = gather_pieces(grad_own)
        matrices[layer] = [
            lax.psum_scatter(value, "chip", scatter_dimension=0, tiled=True)
            for value in (grad_wout, grad_wz, grad_win)
        ]
        vectors[layer] = jnp.concatenate(
            [
                gtaps[: CONV + 1, :inner].reshape(-1),
                acc[0],
                vecs[0, :heads],
                vecs[1, :heads],
                dsk[0],
                grad_wdt[:, :heads].reshape(-1),
                gtaps[: CONV + 1, inner:].reshape(-1),
                grad_ngain,
            ]
        )
    grad_parts = cross_over(grad_own)
    near = grad_parts[2]
    early = join_halves(behind(matrices[0][:2], near))
    vector = total(behind(jnp.stack(vectors), near), ("zh", "chip"))
    final_out = deliver(hidden_own, *out_parts, bf16)
    input_grad = deliver(grad_own, *grad_parts, f32)
    late = join_halves(matrices[0][2:])
    g_cols = [place_rows(early, late), place_rows(first_sums)]
    grad_wbc = shared_rows(
        jnp.stack([matrices[layer][2][:, inner:] for layer in range(LAYERS)], axis=1)
    )
    other = swap(vector, "core")
    common = (CONV + 1) * BC + width
    by_head = jnp.where(held, vector, other)[:, :-common]
    shared = total((vector + other)[:, -common:], ("zl",))
    g_bc = shared[:, :-width].reshape(LAYERS, CONV + 1, BC)
    g_ngain = shared[:, -width:]
    at = 0
    pieces = []
    for size in (CONV * inner, inner, inner, heads, heads, inner, width * heads):
        pieces.append(by_head[:, at : at + size])
        at += size
    g_conv, g_bias, g_ggain, g_alog, g_dtb, g_dsk, g_wdt = pieces
    g_wdt = g_wdt.reshape(LAYERS, width, heads)
    rows = width // lax.axis_size(("chip", "core"))
    g_wdt = lax.dynamic_slice_in_dim(g_wdt, lax.axis_index(("chip", "core")) * rows, rows, axis=1)
    return (
        final_out,
        input_grad,
        g_ngain,
        jnp.stack([g[:, inner : 2 * inner] for g in g_cols]),
        jnp.stack([g[:, 2 * inner :] for g in g_cols]),
        jnp.stack([grad_wbc[:, layer] for layer in range(LAYERS)]),
        g_wdt,
        g_conv.reshape(LAYERS, CONV, inner),
        g_bc[:, :CONV],
        g_bias,
        g_bc[:, CONV],
        g_dtb,
        g_alog,
        jnp.sum(g_dsk.reshape(LAYERS, heads, HEADDIM), axis=2),
        g_ggain,
        jnp.stack([g[:, :inner] for g in g_cols]),
    )


def join_halves(parts):
    inner = parts[0].shape[1]
    part = jnp.concatenate([value[:, :inner] for value in parts], axis=1)
    if len(parts) == 1:
        part = part[:, : inner - BC]
    return part + lax.ppermute(part, BOTH, CROSS_BACK)


def place_rows(*parts):
    core, far = lax.axis_index("core"), lax.axis_index("zh")
    sent = [lax.ppermute(take(full, 1 - core, 2), BOTH, CORE_OUT) for full in parts]
    rows = [
        jnp.where(core == far, take(full, core, 2), got) for full, got in zip(parts, sent)
    ]
    return jnp.concatenate(rows, axis=1)


def shared_rows(part):
    core = lax.axis_index("core")
    part = take(part, core, 2) + swap(take(part, 1 - core, 2), "core")
    return total(part, ("zl", "zh"))


def solution(mesh):
    seq, head = mesh.devices.shape
    mesh = jax.sharding.Mesh(
        mesh.devices.reshape(seq // 2, 2, 2, head // 2), ("chip", "core", "zh", "zl")
    )
    tokens, columns = ("chip", "core"), ("zh", "zl")
    by_col = P(None, None, columns)
    by_head = P(None, columns)
    both = P(None, tokens, columns)
    placed = (
        P(tokens, None),
        P(tokens),
        P(tokens, None),
        P(),
        by_col,
        by_col,
        P(),
        by_col,
        by_col,
        P(),
        by_head,
        P(),
        by_head,
        by_head,
        by_head,
        by_head,
        by_col,
    )
    return jax.shard_map(
        shards,
        mesh=mesh,
        in_specs=placed,
        out_specs=(
            P(tokens, None),
            P(tokens, None),
            P(),
            both,
            both,
            P(None, tokens, None),
            both,
            by_col,
            P(),
            by_head,
            P(),
            by_head,
            by_head,
            by_head,
            by_head,
            both,
        ),
        check_vma=False,
    )
```

```python
import functools

import jax
import jax.numpy as jnp
from jax import lax
from jax.experimental import pallas as pl
from jax.experimental.pallas import tpu as pltpu
from jax.sharding import PartitionSpec as P

HEADDIM = 64
STATE = 128
CONV = 4
GROUP = 256
LAYERS = 2
INNER = 2048
LANES = 128
ROWS = 8
BC = 2 * STATE

epsilon = 1e-05
highest = lax.Precision.HIGHEST
f32 = jnp.float32
bf16 = jnp.bfloat16


def mm(left, right, dims=((1,), (0,)), precision=None):
    return lax.dot_general(
        left, right, (dims, ((), ())), preferred_element_type=f32, precision=precision
    )


def softplus(value):
    small = jnp.exp(-jnp.abs(value))
    series = small * (1.0 - small * (0.5 - small * (1.0 / 3.0 - small * (0.25 - small * 0.2))))
    return jnp.maximum(value, 0.0) + jnp.where(small < 0.03, series, jnp.log(1.0 + small))


def silu_slope(value, sigma):
    return sigma * (1.0 + value * (1.0 - sigma))


def spread(heads, expand):
    return mm(heads, expand, precision=highest)


def gather_heads(lanes, expand):
    return mm(lanes, expand, ((1,), (1,)), precision=highest)


def pick(place, pieces, held):
    if len(pieces) == 1:
        return pieces[0][...]
    away = lax.bitwise_xor(pl.program_id(0) if held is None else held, place[0])
    value = pieces[3][...]
    for number in range(3):
        value = jnp.where(away == number, pieces[number][...], value)
    return value


def in_kernel(
    place, wall, ngain, taps, bias, dtb, avec, mask, halo, expand, tri, *refs
):
    hid = refs[:-14]
    normed, cin, cpre, dtp, cum, dtv, xdt, bc, sloc, pref, send, state, thru, prev = refs[-14:]
    step = pl.program_id(0)
    inner = expand.shape[1]

    @pl.when(step == 0)
    def _():
        state[...] = jnp.zeros_like(state)
        thru[...] = jnp.ones_like(thru)
        prev[...] = halo[...]

    h = pick(place, hid, None)
    inv = lax.rsqrt(jnp.mean(h * h, axis=1, keepdims=True) + epsilon)
    low = (h * inv * ngain[...]).astype(bf16)
    normed[...] = low
    rows = mm(low, wall[:, : inner + BC])
    pre_dt = mm(low, wall[:, inner + BC :])
    dtp[...] = pre_dt
    cin[...] = rows
    ext = jnp.concatenate([prev[...], rows], axis=0)
    prev[...] = rows[GROUP - ROWS :]
    total = taps[CONV - 1 : CONV, :] * rows + bias[0:1, :]
    for k in range(CONV - 1):
        first = ROWS - CONV + 1 + k
        total = total + taps[k : k + 1, :] * ext[first : first + GROUP] * mask[:, k : k + 1]
    cpre[...] = total
    act = total * jax.nn.sigmoid(total)
    x = act[:, :inner]
    low_bc = act[:, inner:].astype(bf16)
    bc[...] = low_bc
    dt = softplus(pre_dt + dtb[0:1, :])
    dtv[...] = dt
    run = mm(tri[...], dt * avec[0:1, :], precision=highest)
    cum[...] = run
    last = run[GROUP - 1 : GROUP]
    xdt[...] = (x * spread(dt, expand[...])).astype(bf16)
    tail = jnp.exp(last - run) * mask[:, 4:5] * dt
    contrib = mm(low_bc[:, :STATE], (x * spread(tail, expand[...])).astype(bf16), ((0,), (0,)))
    through = jnp.broadcast_to(jnp.exp(last) * mask[GROUP - 1 : GROUP, 3:4], (ROWS, LANES))
    through = spread(through, expand[...])
    sloc[0] = state[...]
    pref[0] = thru[...]
    state[...] = through[0:1] * state[...] + contrib
    thru[...] = thru[...] * through

    @pl.when(step == pl.num_programs(0) - 1)
    def _():
        send[:STATE] = state[...]
        send[STATE:] = thru[...]


def pair_lanes(value, which):
    lane = lax.broadcasted_iota(jnp.int32, value.shape, 1)
    keep = lane < HEADDIM if which == 0 else lane >= HEADDIM
    return jnp.where(keep, value, jnp.zeros_like(value))


def intra_kernel(cum, xdt, bc, seg, segrow, y):
    inner = xdt.shape[1]
    run = cum[...]
    run_t = run.T
    base = mm(bc[:, STATE:], bc[:, :STATE], ((1,), (1,)))
    t_at = lax.broadcasted_iota(jnp.int32, (GROUP, GROUP), 0)
    s_at = lax.broadcasted_iota(jnp.int32, (GROUP, GROUP), 1)
    same = (seg[:, 0:1] == segrow[0:1, :]) & (t_at >= s_at)
    closed = jnp.where(same, 0.0, -1e30)
    for pair in range(inner // LANES):
        cols = slice(pair * LANES, (pair + 1) * LANES)
        xs = xdt[:, cols]
        parts = []
        for which in range(2):
            head = 2 * pair + which
            decay = jnp.exp(run[:, head : head + 1] - run_t[head : head + 1, :] + closed)
            parts.append(mm((decay * base).astype(bf16), xs))
        lane = lax.broadcasted_iota(jnp.int32, (GROUP, LANES), 1)
        y[:, cols] = jnp.where(lane < HEADDIM, parts[0], parts[1])


def out_kernel(
    yin, cpre, cum, bc, mask, zval, sloc, pref, entry, dskip, ggain, wout, expand, *refs
):
    cot, (y, gate_in, proj, sums) = refs[:-4], refs[-4:]
    inner = expand.shape[1]
    pre = cpre[...]
    x = pre * jax.nn.sigmoid(pre)
    full = sloc[0] + pref[0][0:1] * entry[...]
    reach = spread(jnp.exp(cum[...]) * mask[:, 3:4], expand[...])
    value = yin[...] + reach * mm(bc[:, STATE:], full.astype(bf16)) + dskip[0:1, :] * x
    y[...] = value
    z = zval[...]
    gated = value * (z * jax.nn.sigmoid(z))
    low = (gated * ggain[0:1, :]).astype(bf16)
    gate_in[...] = low
    proj[...] = mm(low, wout[...], ((1,), (1,)))
    ones = jnp.ones((ROWS, inner), f32)
    squares = mm(ones, gated * gated, ((1,), (1,)), precision=highest)
    if cot:
        back = mm(cot[0][...].astype(bf16), wout[...])
        dots = mm(ones, low.astype(f32) * back, ((1,), (1,)), precision=highest)
        row = lax.broadcasted_iota(jnp.int32, squares.shape, 0)
        squares = jnp.where(row == 0, squares, dots)
    sums[...] = squares


def gate_kernel(
    place, scale, gsq, y, zval, ggain, wout, cum, bc, mask, expand, *refs
):
    gh = refs[:-9]
    gproj, dy, dz, gloc, suf, send, acc, carry, thru = refs[-9:]
    step = pl.program_id(0)

    @pl.when(step == 0)
    def _():
        carry[...] = jnp.zeros_like(carry)
        thru[...] = jnp.ones_like(thru)
        acc[...] = jnp.zeros_like(acc)

    gp = (scale[...] * pick(place, gh, pl.num_programs(0) - 1 - step)).astype(bf16)
    gproj[...] = gp
    ggi = mm(gp, wout[...])
    z = zval[...]
    sigma = jax.nn.sigmoid(z)
    silu = z * sigma
    value = y[...]
    gated = value * silu
    ggated = ggi * ggain[0:1, :] + gated * gsq[...]
    acc[0:1, :] += jnp.sum(ggi * gated, axis=0, keepdims=True)
    low = (ggated * silu).astype(bf16)
    dy[...] = low
    dz[...] = (ggated * value * silu_slope(z, sigma)).astype(bf16)
    run = cum[...]
    last = run[GROUP - 1 : GROUP]
    reach = spread(jnp.exp(run) * mask[:, 3:4], expand[...])
    back = mm(bc[:, STATE:], (reach * low.astype(f32)).astype(bf16), ((0,), (0,)))
    through = jnp.broadcast_to(jnp.exp(last) * mask[GROUP - 1 : GROUP, 3:4], (ROWS, LANES))
    through = spread(through, expand[...])
    gloc[0] = carry[...]
    suf[0] = thru[...]
    carry[...] = back + through[0:1] * carry[...]
    thru[...] = thru[...] * through

    @pl.when(step == pl.num_programs(0) - 1)
    def _():
        send[:STATE] = carry[...]
        send[STATE:] = thru[...]


def intra_back_kernel(cum, xdt, bc, seg, segrow, dy, u, dbc):
    inner = xdt.shape[1]
    run = cum[...]
    run_t = run.T
    base = mm(bc[:, :STATE], bc[:, STATE:], ((1,), (1,)))
    s_at = lax.broadcasted_iota(jnp.int32, (GROUP, GROUP), 0)
    t_at = lax.broadcasted_iota(jnp.int32, (GROUP, GROUP), 1)
    same = (seg[:, 0:1] == segrow[0:1, :]) & (t_at >= s_at)
    closed = jnp.where(same, 0.0, -1e30)
    grad_base = jnp.zeros((GROUP, GROUP), f32)
    for pair in range(inner // LANES):
        cols = slice(pair * LANES, (pair + 1) * LANES)
        xs = xdt[:, cols]
        ds = dy[:, cols]
        parts = []
        for which in range(2):
            head = 2 * pair + which
            decay = jnp.exp(run_t[head : head + 1, :] - run[:, head : head + 1] + closed)
            parts.append(mm((decay * base).astype(bf16), ds))
            grad_base = grad_base + decay * mm(xs, pair_lanes(ds, which), ((1,), (1,)))
        lane = lax.broadcasted_iota(jnp.int32, (GROUP, LANES), 1)
        u[:, cols] = jnp.where(lane < HEADDIM, parts[0], parts[1])
    low = grad_base.astype(bf16)
    dbc[:, :STATE] = mm(low, bc[:, STATE:])
    dbc[:, STATE:] = mm(low, bc[:, :STATE], ((0,), (0,)))


def in_back_kernel(
    uin, dbc, dy, y, cpre, cin, dtp, dtv, cum, xdt, bc, mask, sloc, pref, entry, gloc, suf,
    gout, halo, taps, dtb, avec, dskip, expand, triback,
    gall, last8, rim, gtaps, vecs, dsk,
    nexts,
):
    step = pl.program_id(0)
    inner = expand.shape[1]

    @pl.when(step == 0)
    def _():
        nexts[...] = jnp.zeros_like(nexts)
        gtaps[...] = jnp.zeros_like(gtaps)
        vecs[...] = jnp.zeros_like(vecs)
        dsk[...] = jnp.zeros_like(dsk)

    e = expand[...]
    pre = cpre[...]
    sigma = jax.nn.sigmoid(pre)
    x = (pre * sigma)[:, :inner]
    full = sloc[0] + pref[0][0:1] * entry[...]
    nxt = gloc[0] + suf[0][0:1] * gout[...]
    nxt_low = nxt.astype(bf16)
    run = cum[...]
    last = run[GROUP - 1 : GROUP]
    dt = dtv[...]
    low_dy = dy[...].astype(f32)
    xw = xdt[...].astype(f32)
    tail = spread(jnp.exp(last - run) * mask[:, 4:5], e)
    reach = spread(jnp.exp(run) * mask[:, 3:4], e)
    u_inter = tail * mm(bc[:, :STATE], nxt_low)
    u = uin[...] + u_inter
    dx = spread(dt, e) * u + dskip[0:1, :] * low_dy
    dsk[0:1, :] += jnp.sum(low_dy * x, axis=0, keepdims=True)
    db = dbc[:, :STATE] + mm((tail * xw).astype(bf16), nxt_low, ((1,), (1,)))
    dc = dbc[:, STATE:] + mm((reach * low_dy).astype(bf16), full.astype(bf16), ((1,), (1,)))
    grad_dt = gather_heads(x * u, e)
    y_plain = y[...] - dskip[0:1, :] * x
    grad_cum = gather_heads(low_dy * y_plain - xw * u, e)
    flow = jnp.sum(nxt * full, axis=0, keepdims=True)
    flow = gather_heads(jnp.broadcast_to(flow, (ROWS, inner)), e)[0:1]
    ends = jnp.sum(xw * u_inter, axis=0, keepdims=True)
    ends = gather_heads(jnp.broadcast_to(ends, (ROWS, inner)), e)[0:1]
    grad_tot = mask[GROUP - 1 : GROUP, 3:4] * jnp.exp(last) * flow + ends
    grad_da = mm(triback[...], grad_cum, precision=highest) + grad_tot
    a = avec[0:1, :]
    grad_dtv = grad_dt + grad_da * a
    grad_dtpre = grad_dtv * jax.nn.sigmoid(dtp[...] + dtb[0:1, :])
    vecs[0:1, :] += jnp.sum(grad_da * dt, axis=0, keepdims=True) * a
    vecs[1:2, :] += jnp.sum(grad_dtpre, axis=0, keepdims=True)
    slope = silu_slope(pre, sigma)
    grad_pre = jnp.concatenate([dx, db, dc], axis=1) * slope
    gtaps[4:5, :] += jnp.sum(grad_pre, axis=0, keepdims=True)
    rows = cin[...]
    grad_rows = taps[CONV - 1 : CONV, :] * grad_pre
    gtaps[3:4, :] += jnp.sum(rows * grad_pre, axis=0, keepdims=True)
    masked = []
    for k in range(CONV - 1):
        m = grad_pre * mask[:, k : k + 1]
        masked.append(m[:ROWS])
        ahead = CONV - 1 - k
        shifted = jnp.concatenate([m, nexts[k]], axis=0)[ahead : ahead + GROUP]
        grad_rows = grad_rows + taps[k : k + 1, :] * shifted
        gtaps[k : k + 1, :] += jnp.sum(rows * shifted, axis=0, keepdims=True)
    for k in range(CONV - 1):
        nexts[k] = masked[k]
    gall[:, : inner + BC] = grad_rows.astype(bf16)
    gall[:, inner + BC :] = grad_dtpre.astype(bf16)

    @pl.when(step == 0)
    def _():
        last8[...] = grad_rows[GROUP - ROWS :]

    @pl.when(step == pl.num_programs(0) - 1)
    def _():
        spill = jnp.zeros((ROWS, inner + BC), f32)
        edge = halo[...]
        for k in range(CONV - 1):
            down = ROWS - CONV + 1 + k
            moved = jnp.concatenate([jnp.zeros((ROWS, inner + BC), f32), masked[k]], axis=0)
            moved = moved[ROWS - down : 2 * ROWS - down]
            spill = spill + taps[k : k + 1, :] * moved
            gtaps[k : k + 1, :] += jnp.sum(edge * moved, axis=0, keepdims=True)
        rim[...] = spill


def whole(shape):
    return pl.BlockSpec(shape, lambda c: (0,) * len(shape))


def by_rows(cols, count, reverse=False):
    if reverse:
        return pl.BlockSpec((GROUP, cols), lambda c: (count - 1 - c, 0))
    return pl.BlockSpec((GROUP, cols), lambda c: (c, 0))


def by_group(shape, count, reverse=False):
    if reverse:
        return pl.BlockSpec((1,) + shape, lambda c: (count - 1 - c, 0, 0))
    return pl.BlockSpec((1,) + shape, lambda c: (c, 0, 0))


def by_piece(pieces, count, reverse=False):
    if len(pieces) == 1:
        return [(by_rows(pieces[0].shape[1], count, reverse), pieces[0])]
    return [(whole(piece.shape), piece) for piece in pieces]


def by_cols(count):
    return pl.BlockSpec((ROWS, GROUP), lambda c: (0, c))


def call(kernel, count, ins, outs, scratch, micros, name):
    return pl.pallas_call(
        kernel,
        grid=(count,),
        in_specs=[spec for spec, _ in ins],
        out_specs=[spec for spec, _ in outs],
        out_shape=[shape for _, shape in outs],
        scratch_shapes=scratch,
        compiler_params=pltpu.CompilerParams(
            dimension_semantics=("arbitrary",), vmem_limit_bytes=56 * 1024 * 1024
        ),
        cost_estimate=pl.CostEstimate(
            flops=micros * 1_150_000_000, bytes_accessed=1024 * 1024, transcendentals=0
        ),
        name=name,
    )(*[value for _, value in ins])


def shape(*dims, dtype=f32):
    return jax.ShapeDtypeStruct(dims, dtype)


SWAP = ((0, 1), (1, 0))
CROSS = ((0, 1), (3, 2))
CROSS_BACK = ((1, 0), (2, 3))
CORE_OUT = ((0, 2), (3, 1))
CORE_IN = ((2, 0), (1, 3))
DIAGONAL = ((2, 1), (1, 2))
BOTH = ("core", "zh")
BLOCKS = ("chip", "zh")


def shifted(value, steps):
    count = lax.axis_size(BLOCKS)
    leading, last = (max(0, -steps), min(count, count - steps))
    return lax.ppermute(value, BLOCKS, [(source, source + steps) for source in range(leading, last)])


def chain(part, reverse):
    count = lax.axis_size(BLOCKS)
    place = lax.axis_index(BLOCKS)
    state, decay = part[:STATE], part[STATE : STATE + 1]
    entry, reach = jnp.zeros_like(state), jnp.ones_like(decay)
    step = 1
    while step < count:
        got = lax.ppermute(part, BLOCKS, [(i, i ^ step) for i in range(count)])
        got_state, got_decay = got[:STATE], got[STATE : STATE + 1]
        later = ((place & step) == 0) if reverse else ((place & step) != 0)
        entry = jnp.where(later, entry + reach * got_state, entry)
        reach = jnp.where(later, reach * got_decay, reach)
        state = jnp.where(later, state + decay * got_state, got_state + got_decay * state)
        decay = decay * got_decay
        part = jnp.concatenate([state, jnp.broadcast_to(decay, (ROWS, decay.shape[1]))])
        step *= 2
    return entry


def swap(value, axis):
    return lax.ppermute(value, axis, SWAP)


def total(value, axes):
    for axis in axes:
        count = lax.axis_size(axis)
        step = 1
        while step < count:
            value = value + lax.ppermute(value, axis, [(i, i ^ step) for i in range(count)])
            step *= 2
    return value


def take(value, index, count):
    size = value.shape[0] // count
    return lax.dynamic_slice_in_dim(value, index * size, size)


def ordered(place, mine, theirs):
    return jnp.where(
        place == 0, jnp.concatenate([mine, theirs]), jnp.concatenate([theirs, mine])
    )


def behind(value, *marks):
    return lax.optimization_barrier((value, *marks))[0]


def scatter_sum(part, mark=()):
    core, near = lax.axis_index("core"), lax.axis_index("zl")
    half = take(part, core, 2) + behind(swap(take(part, 1 - core, 2), "core"), *mark)
    if lax.axis_size("zl") == 2:
        return take(half, near, 2) + swap(take(half, 1 - near, 2), "zl")
    return lax.psum_scatter(half, "zl", scatter_dimension=0, tiled=True)


def own_rows(value):
    core, near = lax.axis_index("core"), lax.axis_index("zl")
    return take(take(value, core, 2), near, lax.axis_size("zl"))


def gather_near(value):
    if lax.axis_size("zl") == 2:
        return ordered(lax.axis_index("zl"), value, swap(value, "zl"))
    return lax.all_gather(value, "zl", tiled=True)


def gather_rows(value):
    half = gather_near(value)
    return ordered(lax.axis_index("core"), half, swap(half, "core"))


def own_place():
    return 2 * lax.axis_index("core") + lax.axis_index("zl")


def gather_pieces(value):
    if lax.axis_size("zl") != 2 or value.shape[0] != GROUP:
        return [gather_rows(value)]
    near = swap(value, "zl")
    return [value, near, swap(value, "core"), swap(near, "core")]


def place_kernel(place, value, mine, near, theirs, value_s, mine_s, near_s, theirs_s, out):
    away = lax.bitwise_xor(pl.program_id(0), place[0])
    pairs = ((value, mine), (value_s, mine_s), (near, theirs), (near_s, theirs_s))
    for number, (here, there) in enumerate(pairs):

        @pl.when((away == number) & (place[1] == 1))
        def _():
            out[...] = here[...].astype(out.dtype)

        @pl.when((away == number) & (place[1] == 0))
        def _():
            out[...] = there[...].astype(out.dtype)


def cross_over(value):
    return [lax.ppermute(value, BOTH, pairs) for pairs in (CROSS, DIAGONAL, CORE_IN)]


def deliver(value, mine, theirs, near, dtype):
    core, far = lax.axis_index("core"), lax.axis_index("zh")
    held = core == far
    if lax.axis_size("zl") != 2 or value.shape[0] != GROUP:
        mine = gather_near(jnp.where(held, value, mine))
        theirs = gather_near(jnp.where(held, near, theirs))
        full = ordered(core, mine, theirs)
        return narrowed(full) if dtype == bf16 else full
    axes = ("core", "zh", "zl")
    here = [(2 * kind + i, 2 * kind + 1 - i) for kind in (0, 3) for i in range(2)]
    there = [(2 * kind + i, 2 * kind + 1 - i) for kind in (1, 2) for i in range(2)]
    value_s = lax.ppermute(value, axes, here)
    near_s = lax.ppermute(near, axes, here)
    mine_s = lax.ppermute(mine, axes, there)
    theirs_s = lax.ppermute(theirs, axes, there)
    place = jnp.stack([own_place(), held.astype(jnp.int32)]).astype(jnp.int32)
    width = value.shape[1]
    parts = (value, mine, near, theirs, value_s, mine_s, near_s, theirs_s)
    return pl.pallas_call(
        place_kernel,
        grid=(4,),
        in_specs=[pl.BlockSpec(memory_space=pltpu.SMEM)] + [whole((GROUP, width))] * 8,
        out_specs=by_rows(width, 4),
        out_shape=shape(4 * GROUP, width, dtype=dtype),
        compiler_params=pltpu.CompilerParams(
            dimension_semantics=("arbitrary",), vmem_limit_bytes=40 * 1024 * 1024
        ),
        name="place",
    )(place, *parts)


def to_block(value):
    got = lax.ppermute(value, BOTH, CORE_OUT)
    return jnp.where(lax.axis_index("core") == lax.axis_index("zh"), value, got)


def eight(row):
    return jnp.broadcast_to(row[None, :], (ROWS, row.shape[0]))


def pad_lanes(value):
    return jnp.pad(value, [(0, 0)] * (value.ndim - 1) + [(0, LANES - value.shape[-1])])


def weight_kernel(count, extra, place, *refs):
    own, rest = refs[:count], refs[count:]
    outs, rest = rest[-count:], rest[:-count]
    parts, more = (rest[:-2], rest[-2:]) if extra else (rest, ())
    block = pl.program_id(0)
    at = 0
    for source, out in zip(own, outs):
        cols = source.shape[1]

        @pl.when(place[1] == 1)
        def _():
            out[:, :cols] = source[...]

        for away, part in enumerate(parts):

            @pl.when((place[1] == 0) & (lax.bitwise_xor(place[0], block) == away))
            def _():
                out[:, :cols] = part[:, at : at + cols].astype(bf16)

        at += cols
    if more:
        cols = own[0].shape[1]
        outs[0][:, cols : cols + BC] = more[0][...]
        outs[0][:, cols + BC :] = more[1][...].astype(bf16)


def narrow_kernel(wide, narrow):
    narrow[...] = wide[...].astype(bf16)


def narrowed(value):
    rows, cols = value.shape
    return pl.pallas_call(
        narrow_kernel,
        grid=(rows // GROUP,),
        in_specs=[by_rows(cols, 0)],
        out_specs=by_rows(cols, 0),
        out_shape=shape(rows, cols, dtype=bf16),
        name="narrowed",
    )(value)


def weights_over(own, *marks):
    chips = lax.axis_size("chip")
    piece = jnp.concatenate(
        [take(value, lax.axis_index("chip"), chips).astype(f32) for value in behind(own, *marks)],
        axis=1,
    )
    return lax.ppermute(piece, BOTH, CROSS)


def gather_weights(piece, own, more=(), third=()):
    width = own[0].shape[0]
    chips = lax.axis_size("chip")
    chip = lax.axis_index("chip")
    held = (lax.axis_index("core") == lax.axis_index("zh")).astype(jnp.int32)
    size = width // chips
    if chips == 4:
        parts = [piece]
        for away in range(1, chips):
            pairs = [
                (4 * c + kind, 4 * (c ^ away) + kind) for c in range(chips) for kind in (1, 2)
            ]
            parts.append(lax.ppermute(piece, ("chip", "core", "zh"), pairs))
        place = jnp.stack([chip, held]).astype(jnp.int32)
        blocks = chips
    else:
        parts = [lax.all_gather(piece, "chip", tiled=True)]
        place = jnp.stack([0, held]).astype(jnp.int32)
        blocks, size = 1, width
    parts = behind(parts, *third)
    out_cols = [value.shape[1] for value in own]
    out_cols[0] += sum(value.shape[1] for value in more)

    def rows(cols):
        return pl.BlockSpec((size, cols), lambda c: (c, 0))

    return pl.pallas_call(
        functools.partial(weight_kernel, len(own), bool(more)),
        grid=(blocks,),
        in_specs=[pl.BlockSpec(memory_space=pltpu.SMEM)]
        + [rows(value.shape[1]) for value in own]
        + [whole(piece.shape if chips == 4 else parts[0].shape)] * len(parts)
        + [rows(value.shape[1]) for value in more],
        out_specs=[rows(cols) for cols in out_cols],
        out_shape=[shape(width, cols, dtype=bf16) for cols in out_cols],
        compiler_params=pltpu.CompilerParams(
            dimension_semantics=("arbitrary",), vmem_limit_bytes=40 * 1024 * 1024
        ),
        name="weights",
    )(place, *own, *parts, *more)


def shards(
    x_input,
    seg_ids,
    cotangent,
    norm_gain,
    w_z,
    w_x,
    w_bc,
    w_dt,
    conv_x,
    conv_bc,
    bias_x,
    bias_bc,
    dt_bias,
    a_log,
    d_skip,
    gate_gain,
    w_out,
):
    tok, width = x_input.shape
    inner = w_z.shape[2]
    core, far = lax.axis_index("core"), lax.axis_index("zh")
    held = core == far
    heads = w_dt.shape[2]
    count = tok // GROUP
    conv_cols = inner + BC
    all_cols = inner + BC + LANES

    dt_own = w_dt.astype(f32).reshape(LAYERS, width * heads // LANES, LANES)
    dt_sent = lax.ppermute(dt_own, BOTH, CROSS)
    dt_all = pad_lanes(jnp.where(held, dt_own, dt_sent).reshape(LAYERS, width, heads))
    hidden = to_block(x_input.astype(f32))
    first_x = weights_over([w_x[0]])
    first_rest = weights_over([w_z[0], w_out[0]], dt_sent)
    second_all = weights_over([w_x[1], w_z[1], w_out[1]], hidden)
    (wall,) = gather_weights(first_x, [w_x[0]], (w_bc[0], dt_all[0]))
    cotangent = to_block(behind(cotangent.astype(f32), hidden))
    hidden = behind(hidden, first_rest, cotangent)
    seg = to_block(seg_ids.astype(f32))
    small = jnp.concatenate(
        [
            value.reshape(LAYERS, -1)
            for value in (conv_x, bias_x, dt_bias, a_log, d_skip, gate_gain)
        ],
        axis=1,
    )
    small = jnp.where(held, small, lax.ppermute(small, BOTH, CROSS))
    sizes = (CONV * inner, inner, heads, heads, heads, inner)
    pieces, at = [], 0
    for size in sizes:
        pieces.append(small[:, at : at + size])
        at += size
    conv_x, bias_x, dt_bias, a_log, d_skip, gate_gain = pieces
    conv_x = conv_x.reshape(LAYERS, CONV, inner)
    hidden_own = own_rows(hidden)
    hidden_block = hidden
    hidden = [hidden]
    place = jnp.stack([own_place(), own_place()]).astype(jnp.int32)
    smem = pl.BlockSpec(memory_space=pltpu.SMEM)
    edge_seg = shifted(seg[tok - ROWS :], 1)
    seg_ext = jnp.concatenate([edge_seg, seg])
    before = jnp.concatenate([edge_seg[ROWS - 1 :], seg[GROUP - 1 : tok - 1 : GROUP]])
    after = seg[GROUP - 1 :: GROUP]
    mask = jnp.stack(
        [
            (seg_ext[ROWS - CONV + 1 + k : ROWS - CONV + 1 + k + tok] == seg).astype(f32)
            for k in range(CONV - 1)
        ]
        + [
            (seg == jnp.repeat(before, GROUP)).astype(f32),
            (seg == jnp.repeat(after, GROUP)).astype(f32),
            seg,
            seg,
            seg,
        ],
        axis=1,
    )
    seg_col = seg[:, None]
    seg_row = eight(seg)
    expand = (jnp.arange(LANES)[:, None] == jnp.arange(inner)[None, :] // HEADDIM).astype(f32)
    position = jnp.arange(GROUP)
    tri = (position[:, None] >= position[None, :]).astype(f32)
    triback = (position[:, None] <= position[None, :]).astype(f32)

    stored = []
    for layer in range(LAYERS):
        if layer > 0:
            wall = next_wall
        taps = jnp.concatenate([conv_x[layer], conv_bc[layer]], axis=1)
        bias = eight(jnp.concatenate([bias_x[layer], bias_bc[layer]]))
        dtb = eight(pad_lanes(dt_bias[layer]))
        avec = eight(pad_lanes(-jnp.exp(a_log[layer])))
        dskip = eight(jnp.repeat(d_skip[layer], HEADDIM))
        ggain = eight(gate_gain[layer])
        ngain = norm_gain[layer][None, :]
        if len(hidden) == 1:
            end = hidden[0][tok - 16 :]
        else:
            ends = jnp.stack([piece[GROUP - 16 :] for piece in hidden])
            end = lax.dynamic_index_in_dim(ends, 3 ^ own_place(), 0, False)
        end = end * lax.rsqrt(jnp.mean(end * end, axis=1, keepdims=True) + epsilon) * ngain
        end = mm(end.astype(bf16), wall[:, : inner + BC])[ROWS:]
        halo = shifted(end, 1)
        normed, cin, cpre, dtp, cum, dtv, xdt, bc, sloc, pref, send = call(
            in_kernel,
            count,
            [
                (smem, place),
                (whole((width, all_cols)), wall),
                (whole((1, width)), ngain),
                (whole((CONV, conv_cols)), taps),
                (whole((ROWS, conv_cols)), bias),
                (whole((ROWS, LANES)), dtb),
                (whole((ROWS, LANES)), avec),
                (by_rows(ROWS, count), mask),
                (whole((ROWS, conv_cols)), halo),
                (whole((LANES, inner)), expand),
                (whole((GROUP, GROUP)), tri),
            ]
            + by_piece(hidden, count),
            [
                (by_rows(width, count), shape(tok, width, dtype=bf16)),
                (by_rows(conv_cols, count), shape(tok, conv_cols)),
                (by_rows(conv_cols, count), shape(tok, conv_cols)),
                (by_rows(LANES, count), shape(tok, LANES)),
                (by_rows(LANES, count), shape(tok, LANES)),
                (by_rows(LANES, count), shape(tok, LANES)),
                (by_rows(inner, count), shape(tok, inner, dtype=bf16)),
                (by_rows(BC, count), shape(tok, BC, dtype=bf16)),
                (by_group((STATE, inner), count), shape(count, STATE, inner)),
                (by_group((ROWS, inner), count), shape(count, ROWS, inner)),
                (whole((STATE + ROWS, inner)), shape(STATE + ROWS, inner)),
            ],
            [
                pltpu.VMEM((STATE, inner), f32),
                pltpu.VMEM((ROWS, inner), f32),
                pltpu.VMEM((ROWS, conv_cols), f32),
            ],
            16,
            "in_proj_conv",
        )
        if layer == 0:
            wz, wout = gather_weights(
                behind(first_rest, wall), [w_z[0], w_out[0]], third=(send,)
            )
            send = behind(send, second_all)
        else:
            wz, wout = next_wz, next_wout
        zval = mm(normed, wz)
        (yin,) = call(
            intra_kernel,
            count,
            [
                (by_rows(LANES, count), cum),
                (by_rows(inner, count), xdt),
                (by_rows(BC, count), bc),
                (by_rows(1, count), seg_col),
                (by_cols(count), seg_row),
            ],
            [(by_rows(inner, count), shape(tok, inner))],
            [],
            6,
            "ssd_within",
        )
        entry = chain(send, False)
        y, gate_in, proj, sums = call(
            out_kernel,
            count,
            [
                (by_rows(inner, count), yin),
                (by_rows(inner, count), cpre),
                (by_rows(LANES, count), cum),
                (by_rows(BC, count), bc),
                (by_rows(ROWS, count), mask),
                (by_rows(inner, count), zval),
                (by_group((STATE, inner), count), sloc),
                (by_group((ROWS, inner), count), pref),
                (whole((STATE, inner)), entry),
                (whole((ROWS, inner)), dskip),
                (whole((ROWS, inner)), ggain),
                (whole((width, inner)), wout),
                (whole((LANES, inner)), expand),
            ]
            + ([(by_rows(width, count), cotangent)] if layer == LAYERS - 1 else []),
            [
                (by_rows(inner, count), shape(tok, inner)),
                (by_rows(inner, count), shape(tok, inner, dtype=bf16)),
                (by_rows(width, count), shape(tok, width)),
                (by_cols(count), shape(ROWS, tok)),
            ],
            [],
            12,
            "gate_out_proj",
        )
        sums = total(sums, ("core", "zl"))
        gate_scale = lax.rsqrt(sums[0] / INNER + epsilon)
        stored.append(
            dict(
                hidden=hidden_own, normed=normed, zval=zval, cin=cin, cpre=cpre, dtp=dtp, cum=cum,
                dtv=dtv, xdt=xdt, bc=bc, sloc=sloc, pref=pref, entry=entry, y=y, gate_in=gate_in,
                proj=proj, gate_scale=gate_scale, dots=sums[1], halo=halo, wall=wall, wz=wz, wout=wout,
                taps=taps, dtb=dtb, avec=avec, dskip=dskip, ggain=ggain,
            )
        )
        if layer < LAYERS - 1:
            next_wall, next_wz, next_wout = gather_weights(
                behind(second_all, entry),
                [w_x[1], w_z[1], w_out[1]],
                (w_bc[1], dt_all[1]),
                third=(gate_scale,),
            )
            proj_sum = scatter_sum(proj)
            stored[layer]["proj_sum"] = proj_sum
            hidden_own = hidden_own + own_rows(gate_scale)[:, None] * proj_sum
            hidden = gather_pieces(hidden_own)

    grad_h = [cotangent]
    grad_own = own_rows(cotangent)
    matrices = [None] * LAYERS
    vectors = [None] * LAYERS
    shared = [None] * LAYERS
    for layer in reversed(range(LAYERS)):
        kept = stored[layer]
        gate_scale = kept["gate_scale"]
        if layer == LAYERS - 1:
            grad_scale = kept["dots"]
        else:
            grad_scale = gather_rows(jnp.sum(grad_own * kept["proj_sum"], axis=1))
        gsq = -grad_scale * gate_scale**3 / INNER
        rev = functools.partial(by_rows, count=count, reverse=True)
        rev_group = functools.partial(by_group, count=count, reverse=True)
        gproj, dy, dz, gloc, suf, gsend, acc = call(
            gate_kernel,
            count,
            [
                (smem, place),
                (rev(1), gate_scale[:, None]),
                (rev(1), gsq[:, None]),
                (rev(inner), kept["y"]),
                (rev(inner), kept["zval"]),
                (whole((ROWS, inner)), kept["ggain"]),
                (whole((width, inner)), kept["wout"]),
                (rev(LANES), kept["cum"]),
                (rev(BC), kept["bc"]),
                (rev(ROWS), mask),
                (whole((LANES, inner)), expand),
            ]
            + by_piece(grad_h, count, True),
            [
                (rev(width), shape(tok, width, dtype=bf16)),
                (rev(inner), shape(tok, inner, dtype=bf16)),
                (rev(inner), shape(tok, inner, dtype=bf16)),
                (rev_group((STATE, inner)), shape(count, STATE, inner)),
                (rev_group((ROWS, inner)), shape(count, ROWS, inner)),
                (whole((STATE + ROWS, inner)), shape(STATE + ROWS, inner)),
                (whole((ROWS, inner)), shape(ROWS, inner)),
            ],
            [pltpu.VMEM((STATE, inner), f32), pltpu.VMEM((ROWS, inner), f32)],
            10,
            "gate_back",
        )
        if layer == 0:
            out_parts = cross_over(behind(hidden_own, *grad_h))
            dy = behind(dy, *out_parts)
        u, dbc = call(
            intra_back_kernel,
            count,
            [
                (by_rows(LANES, count), kept["cum"]),
                (by_rows(inner, count), kept["xdt"]),
                (by_rows(BC, count), kept["bc"]),
                (by_rows(1, count), seg_col),
                (by_cols(count), seg_row),
                (by_rows(inner, count), dy),
            ],
            [
                (by_rows(inner, count), shape(tok, inner)),
                (by_rows(BC, count), shape(tok, BC)),
            ],
            [],
            8,
            "ssd_within_back",
        )
        gout = chain(gsend, True)
        if layer == LAYERS - 1:
            last_sum = scatter_sum(kept["proj"], (dy,))
            hidden_own = hidden_own + own_rows(gate_scale)[:, None] * last_sum
            u = behind(u, hidden_own)
        else:
            first_sums = join_halves(behind(matrices[LAYERS - 1], u))
        grad_wout = mm(gproj, kept["gate_in"], ((0,), (0,)))
        grad_wz = mm(kept["normed"], dz, ((0,), (0,)))
        partial_z = mm(dz, kept["wz"], ((1,), (1,)))
        gall, last8, rim, gtaps, vecs, dsk = call(
            in_back_kernel,
            count,
            [
                (rev(inner), u),
                (rev(BC), dbc),
                (rev(inner), dy),
                (rev(inner), kept["y"]),
                (rev(conv_cols), kept["cpre"]),
                (rev(conv_cols), kept["cin"]),
                (rev(LANES), kept["dtp"]),
                (rev(LANES), kept["dtv"]),
                (rev(LANES), kept["cum"]),
                (rev(inner), kept["xdt"]),
                (rev(BC), kept["bc"]),
                (rev(ROWS), mask),
                (rev_group((STATE, inner)), kept["sloc"]),
                (rev_group((ROWS, inner)), kept["pref"]),
                (whole((STATE, inner)), kept["entry"]),
                (rev_group((STATE, inner)), gloc),
                (rev_group((ROWS, inner)), suf),
                (whole((STATE, inner)), gout),
                (whole((ROWS, conv_cols)), kept["halo"]),
                (whole((CONV, conv_cols)), kept["taps"]),
                (whole((ROWS, LANES)), kept["dtb"]),
                (whole((ROWS, LANES)), kept["avec"]),
                (whole((ROWS, inner)), kept["dskip"]),
                (whole((LANES, inner)), expand),
                (whole((GROUP, GROUP)), triback),
            ],
            [
                (rev(all_cols), shape(tok, all_cols, dtype=bf16)),
                (whole((ROWS, conv_cols)), shape(ROWS, conv_cols)),
                (whole((ROWS, conv_cols)), shape(ROWS, conv_cols)),
                (whole((ROWS, conv_cols)), shape(ROWS, conv_cols)),
                (whole((ROWS, LANES)), shape(ROWS, LANES)),
                (whole((ROWS, inner)), shape(ROWS, inner)),
            ],
            [pltpu.VMEM((CONV - 1, ROWS, conv_cols), f32)],
            20,
            "in_proj_conv_back",
        )
        rim_back = shifted(rim, -1)
        if layer == 0:
            last8 = behind(last8, first_sums)
        gall = lax.dynamic_update_slice(
            gall, (last8 + rim_back).astype(bf16), (tok - ROWS, 0)
        )
        partial = partial_z + mm(gall, kept["wall"], ((1,), (1,)))
        grad_normed = scatter_sum(partial)
        late = behind(gall, partial)
        grad_win = mm(kept["normed"], late[:, : inner + BC], ((0,), (0,)))
        grad_wdt = mm(kept["normed"], late[:, inner + BC :], ((0,), (0,)))
        hidden_in = kept["hidden"]
        inv = lax.rsqrt(jnp.mean(hidden_in * hidden_in, axis=1, keepdims=True) + epsilon)
        if layer == 0:
            full = hidden_block
            grad_ngain = jnp.sum(
                partial
                * (full * lax.rsqrt(jnp.mean(full * full, axis=1, keepdims=True) + epsilon)),
                axis=0,
            )
        else:
            grad_ngain = jnp.sum(grad_normed * hidden_in * inv, axis=0)
        back = grad_normed * norm_gain[layer][None, :]
        grad_own = grad_own + inv * (
            back - hidden_in * inv * inv * jnp.mean(back * hidden_in, axis=1, keepdims=True)
        )
        if layer > 0:
            grad_h = gather_pieces(grad_own)
        matrices[layer] = [
            lax.psum_scatter(value, "chip", scatter_dimension=0, tiled=True)
            for value in (grad_wout, grad_wz, grad_win)
        ]
        vectors[layer] = jnp.concatenate(
            [
                gtaps[: CONV + 1, :inner].reshape(-1),
                acc[0],
                vecs[0, :heads],
                vecs[1, :heads],
                dsk[0],
                grad_wdt[:, :heads].reshape(-1),
                gtaps[: CONV + 1, inner:].reshape(-1),
                grad_ngain,
            ]
        )
    vector = total(jnp.stack(vectors), ("chip", "zh"))
    grad_parts = cross_over(grad_own)
    near = grad_parts[2]
    input_grad = deliver(grad_own, *grad_parts, f32)
    final_out = deliver(hidden_own, *out_parts, bf16)
    early = join_halves(behind(matrices[0][:2], near))
    late = join_halves(matrices[0][2:])
    g_cols = [place_rows(early, late), place_rows(first_sums)]
    grad_wbc = shared_rows(
        jnp.stack([matrices[layer][2][:, inner:] for layer in range(LAYERS)], axis=1)
    )
    other = swap(vector, "core")
    common = (CONV + 1) * BC + width
    by_head = jnp.where(held, vector, other)[:, :-common]
    shared = total((vector + other)[:, -common:], ("zl",))
    g_bc = shared[:, :-width].reshape(LAYERS, CONV + 1, BC)
    g_ngain = shared[:, -width:]
    at = 0
    pieces = []
    for size in (CONV * inner, inner, inner, heads, heads, inner, width * heads):
        pieces.append(by_head[:, at : at + size])
        at += size
    g_conv, g_bias, g_ggain, g_alog, g_dtb, g_dsk, g_wdt = pieces
    g_wdt = g_wdt.reshape(LAYERS, width, heads)
    rows = width // lax.axis_size(("chip", "core"))
    g_wdt = lax.dynamic_slice_in_dim(g_wdt, lax.axis_index(("chip", "core")) * rows, rows, axis=1)
    return (
        final_out,
        input_grad,
        g_ngain,
        jnp.stack([g[:, inner : 2 * inner] for g in g_cols]),
        jnp.stack([g[:, 2 * inner :] for g in g_cols]),
        jnp.stack([grad_wbc[:, layer] for layer in range(LAYERS)]),
        g_wdt,
        g_conv.reshape(LAYERS, CONV, inner),
        g_bc[:, :CONV],
        g_bias,
        g_bc[:, CONV],
        g_dtb,
        g_alog,
        jnp.sum(g_dsk.reshape(LAYERS, heads, HEADDIM), axis=2),
        g_ggain,
        jnp.stack([g[:, :inner] for g in g_cols]),
    )


def join_halves(parts):
    inner = parts[0].shape[1]
    part = jnp.concatenate([value[:, :inner] for value in parts], axis=1)
    if len(parts) == 1:
        part = part[:, : inner - BC]
    return part + lax.ppermute(part, BOTH, CROSS_BACK)


def place_rows(*parts):
    core, far = lax.axis_index("core"), lax.axis_index("zh")
    sent = [lax.ppermute(take(full, 1 - core, 2), BOTH, CORE_OUT) for full in parts]
    rows = [
        jnp.where(core == far, take(full, core, 2), got) for full, got in zip(parts, sent)
    ]
    return jnp.concatenate(rows, axis=1)


def shared_rows(part):
    core = lax.axis_index("core")
    part = take(part, core, 2) + swap(take(part, 1 - core, 2), "core")
    return total(part, ("zl", "zh"))


def solution(mesh):
    seq, head = mesh.devices.shape
    mesh = jax.sharding.Mesh(
        mesh.devices.reshape(seq // 2, 2, 2, head // 2), ("chip", "core", "zh", "zl")
    )
    tokens, columns = ("chip", "core"), ("zh", "zl")
    by_col = P(None, None, columns)
    by_head = P(None, columns)
    both = P(None, tokens, columns)
    placed = (
        P(tokens, None),
        P(tokens),
        P(tokens, None),
        P(),
        by_col,
        by_col,
        P(),
        by_col,
        by_col,
        P(),
        by_head,
        P(),
        by_head,
        by_head,
        by_head,
        by_head,
        by_col,
    )
    return jax.shard_map(
        shards,
        mesh=mesh,
        in_specs=placed,
        out_specs=(
            P(tokens, None),
            P(tokens, None),
            P(),
            both,
            both,
            P(None, tokens, None),
            both,
            by_col,
            P(),
            by_head,
            P(),
            by_head,
            by_head,
            by_head,
            by_head,
            both,
        ),
        check_vma=False,
    )
```

```python
import functools

import jax
import jax.numpy as jnp
from jax import lax
from jax.experimental import pallas as pl
from jax.experimental.pallas import tpu as pltpu
from jax.sharding import PartitionSpec as P

HEADDIM = 64
STATE = 128
CONV = 4
GROUP = 256
LAYERS = 2
INNER = 2048
LANES = 128
ROWS = 8
BC = 2 * STATE

epsilon = 1e-05
highest = lax.Precision.HIGHEST
f32 = jnp.float32
bf16 = jnp.bfloat16


def mm(left, right, dims=((1,), (0,)), precision=None):
    return lax.dot_general(
        left, right, (dims, ((), ())), preferred_element_type=f32, precision=precision
    )


def softplus(value):
    small = jnp.exp(-jnp.abs(value))
    series = small * (1.0 - small * (0.5 - small * (1.0 / 3.0 - small * (0.25 - small * 0.2))))
    return jnp.maximum(value, 0.0) + jnp.where(small < 0.03, series, jnp.log(1.0 + small))


def silu_slope(value, sigma):
    return sigma * (1.0 + value * (1.0 - sigma))


def spread(heads, expand):
    return mm(heads, expand, precision=highest)


def gather_heads(lanes, expand):
    return mm(lanes, expand, ((1,), (1,)), precision=highest)


def pick(place, pieces, held):
    if len(pieces) == 1:
        return pieces[0][...]
    away = lax.bitwise_xor(pl.program_id(0) if held is None else held, place[0])
    value = pieces[3][...]
    for number in range(3):
        value = jnp.where(away == number, pieces[number][...], value)
    return value


def in_kernel(
    place, wall, ngain, taps, bias, dtb, avec, mask, halo, expand, tri, *refs
):
    hid = refs[:-14]
    normed, cin, cpre, dtp, cum, dtv, xdt, bc, sloc, pref, send, state, thru, prev = refs[-14:]
    step = pl.program_id(0)
    inner = expand.shape[1]

    @pl.when(step == 0)
    def _():
        state[...] = jnp.zeros_like(state)
        thru[...] = jnp.ones_like(thru)
        prev[...] = halo[...]

    h = pick(place, hid, None)
    inv = lax.rsqrt(jnp.mean(h * h, axis=1, keepdims=True) + epsilon)
    low = (h * inv * ngain[...]).astype(bf16)
    normed[...] = low
    rows = mm(low, wall[:, : inner + BC])
    pre_dt = mm(low, wall[:, inner + BC :])
    dtp[...] = pre_dt
    cin[...] = rows
    ext = jnp.concatenate([prev[...], rows], axis=0)
    prev[...] = rows[GROUP - ROWS :]
    total = taps[CONV - 1 : CONV, :] * rows + bias[0:1, :]
    for k in range(CONV - 1):
        first = ROWS - CONV + 1 + k
        total = total + taps[k : k + 1, :] * ext[first : first + GROUP] * mask[:, k : k + 1]
    cpre[...] = total
    act = total * jax.nn.sigmoid(total)
    x = act[:, :inner]
    low_bc = act[:, inner:].astype(bf16)
    bc[...] = low_bc
    dt = softplus(pre_dt + dtb[0:1, :])
    dtv[...] = dt
    run = mm(tri[...], dt * avec[0:1, :], precision=highest)
    cum[...] = run
    last = run[GROUP - 1 : GROUP]
    xdt[...] = (x * spread(dt, expand[...])).astype(bf16)
    tail = jnp.exp(last - run) * mask[:, 4:5] * dt
    contrib = mm(low_bc[:, :STATE], (x * spread(tail, expand[...])).astype(bf16), ((0,), (0,)))
    through = jnp.broadcast_to(jnp.exp(last) * mask[GROUP - 1 : GROUP, 3:4], (ROWS, LANES))
    through = spread(through, expand[...])
    sloc[0] = state[...]
    pref[0] = thru[...]
    state[...] = through[0:1] * state[...] + contrib
    thru[...] = thru[...] * through

    @pl.when(step == pl.num_programs(0) - 1)
    def _():
        send[:STATE] = state[...]
        send[STATE:] = thru[...]


def pair_lanes(value, which):
    lane = lax.broadcasted_iota(jnp.int32, value.shape, 1)
    keep = lane < HEADDIM if which == 0 else lane >= HEADDIM
    return jnp.where(keep, value, jnp.zeros_like(value))


def intra_kernel(cum, xdt, bc, seg, segrow, y):
    inner = xdt.shape[1]
    run = cum[...]
    run_t = run.T
    base = mm(bc[:, STATE:], bc[:, :STATE], ((1,), (1,)))
    t_at = lax.broadcasted_iota(jnp.int32, (GROUP, GROUP), 0)
    s_at = lax.broadcasted_iota(jnp.int32, (GROUP, GROUP), 1)
    same = (seg[:, 0:1] == segrow[0:1, :]) & (t_at >= s_at)
    closed = jnp.where(same, 0.0, -1e30)
    for pair in range(inner // LANES):
        cols = slice(pair * LANES, (pair + 1) * LANES)
        xs = xdt[:, cols]
        parts = []
        for which in range(2):
            head = 2 * pair + which
            decay = jnp.exp(run[:, head : head + 1] - run_t[head : head + 1, :] + closed)
            parts.append(mm((decay * base).astype(bf16), xs))
        lane = lax.broadcasted_iota(jnp.int32, (GROUP, LANES), 1)
        y[:, cols] = jnp.where(lane < HEADDIM, parts[0], parts[1])


def out_kernel(
    yin, cpre, cum, bc, mask, zval, sloc, pref, entry, dskip, ggain, wout, expand, *refs
):
    cot, (y, gate_in, proj, sums) = refs[:-4], refs[-4:]
    inner = expand.shape[1]
    pre = cpre[...]
    x = pre * jax.nn.sigmoid(pre)
    full = sloc[0] + pref[0][0:1] * entry[...]
    reach = spread(jnp.exp(cum[...]) * mask[:, 3:4], expand[...])
    value = yin[...] + reach * mm(bc[:, STATE:], full.astype(bf16)) + dskip[0:1, :] * x
    y[...] = value
    z = zval[...]
    gated = value * (z * jax.nn.sigmoid(z))
    low = (gated * ggain[0:1, :]).astype(bf16)
    gate_in[...] = low
    proj[...] = mm(low, wout[...], ((1,), (1,)))
    ones = jnp.ones((ROWS, inner), f32)
    squares = mm(ones, gated * gated, ((1,), (1,)), precision=highest)
    if cot:
        back = mm(cot[0][...].astype(bf16), wout[...])
        dots = mm(ones, low.astype(f32) * back, ((1,), (1,)), precision=highest)
        row = lax.broadcasted_iota(jnp.int32, squares.shape, 0)
        squares = jnp.where(row == 0, squares, dots)
    sums[...] = squares


def gate_kernel(
    place, scale, gsq, y, zval, ggain, wout, cum, bc, mask, expand, *refs
):
    gh = refs[:-9]
    gproj, dy, dz, gloc, suf, send, acc, carry, thru = refs[-9:]
    step = pl.program_id(0)

    @pl.when(step == 0)
    def _():
        carry[...] = jnp.zeros_like(carry)
        thru[...] = jnp.ones_like(thru)
        acc[...] = jnp.zeros_like(acc)

    gp = (scale[...] * pick(place, gh, pl.num_programs(0) - 1 - step)).astype(bf16)
    gproj[...] = gp
    ggi = mm(gp, wout[...])
    z = zval[...]
    sigma = jax.nn.sigmoid(z)
    silu = z * sigma
    value = y[...]
    gated = value * silu
    ggated = ggi * ggain[0:1, :] + gated * gsq[...]
    acc[0:1, :] += jnp.sum(ggi * gated, axis=0, keepdims=True)
    low = (ggated * silu).astype(bf16)
    dy[...] = low
    dz[...] = (ggated * value * silu_slope(z, sigma)).astype(bf16)
    run = cum[...]
    last = run[GROUP - 1 : GROUP]
    reach = spread(jnp.exp(run) * mask[:, 3:4], expand[...])
    back = mm(bc[:, STATE:], (reach * low.astype(f32)).astype(bf16), ((0,), (0,)))
    through = jnp.broadcast_to(jnp.exp(last) * mask[GROUP - 1 : GROUP, 3:4], (ROWS, LANES))
    through = spread(through, expand[...])
    gloc[0] = carry[...]
    suf[0] = thru[...]
    carry[...] = back + through[0:1] * carry[...]
    thru[...] = thru[...] * through

    @pl.when(step == pl.num_programs(0) - 1)
    def _():
        send[:STATE] = carry[...]
        send[STATE:] = thru[...]


def intra_back_kernel(cum, xdt, bc, seg, segrow, dy, u, dbc):
    inner = xdt.shape[1]
    run = cum[...]
    run_t = run.T
    base = mm(bc[:, :STATE], bc[:, STATE:], ((1,), (1,)))
    s_at = lax.broadcasted_iota(jnp.int32, (GROUP, GROUP), 0)
    t_at = lax.broadcasted_iota(jnp.int32, (GROUP, GROUP), 1)
    same = (seg[:, 0:1] == segrow[0:1, :]) & (t_at >= s_at)
    closed = jnp.where(same, 0.0, -1e30)
    grad_base = jnp.zeros((GROUP, GROUP), f32)
    for pair in range(inner // LANES):
        cols = slice(pair * LANES, (pair + 1) * LANES)
        xs = xdt[:, cols]
        ds = dy[:, cols]
        parts = []
        for which in range(2):
            head = 2 * pair + which
            decay = jnp.exp(run_t[head : head + 1, :] - run[:, head : head + 1] + closed)
            parts.append(mm((decay * base).astype(bf16), ds))
            grad_base = grad_base + decay * mm(xs, pair_lanes(ds, which), ((1,), (1,)))
        lane = lax.broadcasted_iota(jnp.int32, (GROUP, LANES), 1)
        u[:, cols] = jnp.where(lane < HEADDIM, parts[0], parts[1])
    low = grad_base.astype(bf16)
    dbc[:, :STATE] = mm(low, bc[:, STATE:])
    dbc[:, STATE:] = mm(low, bc[:, :STATE], ((0,), (0,)))


def in_back_kernel(
    uin, dbc, dy, y, cpre, cin, dtp, dtv, cum, xdt, bc, mask, sloc, pref, entry, gloc, suf,
    gout, halo, taps, dtb, avec, dskip, expand, triback,
    gall, last8, rim, gtaps, vecs, dsk,
    nexts,
):
    step = pl.program_id(0)
    inner = expand.shape[1]

    @pl.when(step == 0)
    def _():
        nexts[...] = jnp.zeros_like(nexts)
        gtaps[...] = jnp.zeros_like(gtaps)
        vecs[...] = jnp.zeros_like(vecs)
        dsk[...] = jnp.zeros_like(dsk)

    e = expand[...]
    pre = cpre[...]
    sigma = jax.nn.sigmoid(pre)
    x = (pre * sigma)[:, :inner]
    full = sloc[0] + pref[0][0:1] * entry[...]
    nxt = gloc[0] + suf[0][0:1] * gout[...]
    nxt_low = nxt.astype(bf16)
    run = cum[...]
    last = run[GROUP - 1 : GROUP]
    dt = dtv[...]
    low_dy = dy[...].astype(f32)
    xw = xdt[...].astype(f32)
    tail = spread(jnp.exp(last - run) * mask[:, 4:5], e)
    reach = spread(jnp.exp(run) * mask[:, 3:4], e)
    u_inter = tail * mm(bc[:, :STATE], nxt_low)
    u = uin[...] + u_inter
    dx = spread(dt, e) * u + dskip[0:1, :] * low_dy
    dsk[0:1, :] += jnp.sum(low_dy * x, axis=0, keepdims=True)
    db = dbc[:, :STATE] + mm((tail * xw).astype(bf16), nxt_low, ((1,), (1,)))
    dc = dbc[:, STATE:] + mm((reach * low_dy).astype(bf16), full.astype(bf16), ((1,), (1,)))
    grad_dt = gather_heads(x * u, e)
    y_plain = y[...] - dskip[0:1, :] * x
    grad_cum = gather_heads(low_dy * y_plain - xw * u, e)
    flow = jnp.sum(nxt * full, axis=0, keepdims=True)
    flow = gather_heads(jnp.broadcast_to(flow, (ROWS, inner)), e)[0:1]
    ends = jnp.sum(xw * u_inter, axis=0, keepdims=True)
    ends = gather_heads(jnp.broadcast_to(ends, (ROWS, inner)), e)[0:1]
    grad_tot = mask[GROUP - 1 : GROUP, 3:4] * jnp.exp(last) * flow + ends
    grad_da = mm(triback[...], grad_cum, precision=highest) + grad_tot
    a = avec[0:1, :]
    grad_dtv = grad_dt + grad_da * a
    grad_dtpre = grad_dtv * jax.nn.sigmoid(dtp[...] + dtb[0:1, :])
    vecs[0:1, :] += jnp.sum(grad_da * dt, axis=0, keepdims=True) * a
    vecs[1:2, :] += jnp.sum(grad_dtpre, axis=0, keepdims=True)
    slope = silu_slope(pre, sigma)
    grad_pre = jnp.concatenate([dx, db, dc], axis=1) * slope
    gtaps[4:5, :] += jnp.sum(grad_pre, axis=0, keepdims=True)
    rows = cin[...]
    grad_rows = taps[CONV - 1 : CONV, :] * grad_pre
    gtaps[3:4, :] += jnp.sum(rows * grad_pre, axis=0, keepdims=True)
    masked = []
    for k in range(CONV - 1):
        m = grad_pre * mask[:, k : k + 1]
        masked.append(m[:ROWS])
        ahead = CONV - 1 - k
        shifted = jnp.concatenate([m, nexts[k]], axis=0)[ahead : ahead + GROUP]
        grad_rows = grad_rows + taps[k : k + 1, :] * shifted
        gtaps[k : k + 1, :] += jnp.sum(rows * shifted, axis=0, keepdims=True)
    for k in range(CONV - 1):
        nexts[k] = masked[k]
    gall[:, : inner + BC] = grad_rows.astype(bf16)
    gall[:, inner + BC :] = grad_dtpre.astype(bf16)

    @pl.when(step == 0)
    def _():
        last8[...] = grad_rows[GROUP - ROWS :]

    @pl.when(step == pl.num_programs(0) - 1)
    def _():
        spill = jnp.zeros((ROWS, inner + BC), f32)
        edge = halo[...]
        for k in range(CONV - 1):
            down = ROWS - CONV + 1 + k
            moved = jnp.concatenate([jnp.zeros((ROWS, inner + BC), f32), masked[k]], axis=0)
            moved = moved[ROWS - down : 2 * ROWS - down]
            spill = spill + taps[k : k + 1, :] * moved
            gtaps[k : k + 1, :] += jnp.sum(edge * moved, axis=0, keepdims=True)
        rim[...] = spill


def whole(shape):
    return pl.BlockSpec(shape, lambda c: (0,) * len(shape))


def by_rows(cols, count, reverse=False):
    if reverse:
        return pl.BlockSpec((GROUP, cols), lambda c: (count - 1 - c, 0))
    return pl.BlockSpec((GROUP, cols), lambda c: (c, 0))


def by_group(shape, count, reverse=False):
    if reverse:
        return pl.BlockSpec((1,) + shape, lambda c: (count - 1 - c, 0, 0))
    return pl.BlockSpec((1,) + shape, lambda c: (c, 0, 0))


def by_piece(pieces, count, reverse=False):
    if len(pieces) == 1:
        return [(by_rows(pieces[0].shape[1], count, reverse), pieces[0])]
    return [(whole(piece.shape), piece) for piece in pieces]


def by_cols(count):
    return pl.BlockSpec((ROWS, GROUP), lambda c: (0, c))


def call(kernel, count, ins, outs, scratch, micros, name):
    return pl.pallas_call(
        kernel,
        grid=(count,),
        in_specs=[spec for spec, _ in ins],
        out_specs=[spec for spec, _ in outs],
        out_shape=[shape for _, shape in outs],
        scratch_shapes=scratch,
        compiler_params=pltpu.CompilerParams(
            dimension_semantics=("arbitrary",), vmem_limit_bytes=56 * 1024 * 1024
        ),
        cost_estimate=pl.CostEstimate(
            flops=micros * 1_150_000_000, bytes_accessed=1024 * 1024, transcendentals=0
        ),
        name=name,
    )(*[value for _, value in ins])


def shape(*dims, dtype=f32):
    return jax.ShapeDtypeStruct(dims, dtype)


SWAP = ((0, 1), (1, 0))
CROSS = ((0, 1), (3, 2))
CROSS_BACK = ((1, 0), (2, 3))
CORE_OUT = ((0, 2), (3, 1))
CORE_IN = ((2, 0), (1, 3))
DIAGONAL = ((2, 1), (1, 2))
BOTH = ("core", "zh")
BLOCKS = ("chip", "zh")


def shifted(value, steps):
    count = lax.axis_size(BLOCKS)
    leading, last = (max(0, -steps), min(count, count - steps))
    return lax.ppermute(value, BLOCKS, [(source, source + steps) for source in range(leading, last)])


def chain(part, reverse):
    count = lax.axis_size(BLOCKS)
    place = lax.axis_index(BLOCKS)
    state, decay = part[:STATE], part[STATE : STATE + 1]
    entry, reach = jnp.zeros_like(state), jnp.ones_like(decay)
    step = 1
    while step < count:
        got = lax.ppermute(part, BLOCKS, [(i, i ^ step) for i in range(count)])
        got_state, got_decay = got[:STATE], got[STATE : STATE + 1]
        later = ((place & step) == 0) if reverse else ((place & step) != 0)
        entry = jnp.where(later, entry + reach * got_state, entry)
        reach = jnp.where(later, reach * got_decay, reach)
        state = jnp.where(later, state + decay * got_state, got_state + got_decay * state)
        decay = decay * got_decay
        part = jnp.concatenate([state, jnp.broadcast_to(decay, (ROWS, decay.shape[1]))])
        step *= 2
    return entry


def swap(value, axis):
    return lax.ppermute(value, axis, SWAP)


def total(value, axes):
    for axis in axes:
        count = lax.axis_size(axis)
        step = 1
        while step < count:
            value = value + lax.ppermute(value, axis, [(i, i ^ step) for i in range(count)])
            step *= 2
    return value


def take(value, index, count):
    size = value.shape[0] // count
    return lax.dynamic_slice_in_dim(value, index * size, size)


def ordered(place, mine, theirs):
    return jnp.where(
        place == 0, jnp.concatenate([mine, theirs]), jnp.concatenate([theirs, mine])
    )


def behind(value, *marks):
    return lax.optimization_barrier((value, *marks))[0]


def scatter_sum(part, mark=(), stages=None):
    core, near = lax.axis_index("core"), lax.axis_index("zl")
    half = take(part, core, 2) + behind(swap(take(part, 1 - core, 2), "core"), *mark)
    if stages is not None:
        stages.append(half)
    if lax.axis_size("zl") == 2:
        return take(half, near, 2) + swap(take(half, 1 - near, 2), "zl")
    return lax.psum_scatter(half, "zl", scatter_dimension=0, tiled=True)


def own_rows(value):
    core, near = lax.axis_index("core"), lax.axis_index("zl")
    return take(take(value, core, 2), near, lax.axis_size("zl"))


def gather_near(value):
    if lax.axis_size("zl") == 2:
        return ordered(lax.axis_index("zl"), value, swap(value, "zl"))
    return lax.all_gather(value, "zl", tiled=True)


def gather_rows(value):
    half = gather_near(value)
    return ordered(lax.axis_index("core"), half, swap(half, "core"))


def own_place():
    return 2 * lax.axis_index("core") + lax.axis_index("zl")


def gather_pieces(value):
    if lax.axis_size("zl") != 2 or value.shape[0] != GROUP:
        return [gather_rows(value)]
    near = swap(value, "zl")
    return [value, near, swap(value, "core"), swap(near, "core")]


def place_kernel(place, value, mine, near, theirs, value_s, mine_s, near_s, theirs_s, out):
    away = lax.bitwise_xor(pl.program_id(0), place[0])
    pairs = ((value, mine), (value_s, mine_s), (near, theirs), (near_s, theirs_s))
    for number, (here, there) in enumerate(pairs):

        @pl.when((away == number) & (place[1] == 1))
        def _():
            out[...] = here[...].astype(out.dtype)

        @pl.when((away == number) & (place[1] == 0))
        def _():
            out[...] = there[...].astype(out.dtype)


def cross_over(value):
    return [lax.ppermute(value, BOTH, pairs) for pairs in (CROSS, DIAGONAL, CORE_IN)]


def near_swap(value):
    if lax.axis_size("zl") != 2 or value.shape[0] != GROUP:
        return None
    here = [(2 * kind + i, 2 * kind + 1 - i) for kind in (0, 3) for i in range(2)]
    return lax.ppermute(value, ("core", "zh", "zl"), here)


def near_swaps(value, mine, theirs, near, value_s=None):
    if lax.axis_size("zl") != 2 or value.shape[0] != GROUP:
        return None
    axes = ("core", "zh", "zl")
    there = [(2 * kind + i, 2 * kind + 1 - i) for kind in (1, 2) for i in range(2)]
    return (
        near_swap(value) if value_s is None else value_s,
        lax.ppermute(mine, axes, there),
        lax.ppermute(theirs, axes, there),
        near_swap(near),
    )


def deliver(value, mine, theirs, near, dtype, swaps=None, mark=()):
    core, far = lax.axis_index("core"), lax.axis_index("zh")
    held = core == far
    if lax.axis_size("zl") != 2 or value.shape[0] != GROUP:
        mine = gather_near(jnp.where(held, value, mine))
        theirs = gather_near(jnp.where(held, near, theirs))
        full = ordered(core, mine, theirs)
        return narrowed(full) if dtype == bf16 else full
    if swaps is None:
        swaps = near_swaps(value, mine, theirs, near)
    value_s, mine_s, theirs_s, near_s = swaps
    place = jnp.stack([own_place(), held.astype(jnp.int32)]).astype(jnp.int32)
    width = value.shape[1]
    parts = behind((value, mine, near, theirs, value_s, mine_s, near_s, theirs_s), *mark)
    return pl.pallas_call(
        place_kernel,
        grid=(4,),
        in_specs=[pl.BlockSpec(memory_space=pltpu.SMEM)] + [whole((GROUP, width))] * 8,
        out_specs=by_rows(width, 4),
        out_shape=shape(4 * GROUP, width, dtype=dtype),
        compiler_params=pltpu.CompilerParams(
            dimension_semantics=("arbitrary",), vmem_limit_bytes=40 * 1024 * 1024
        ),
        name="place",
    )(place, *parts)


def to_block(value):
    got = lax.ppermute(value, BOTH, CORE_OUT)
    return jnp.where(lax.axis_index("core") == lax.axis_index("zh"), value, got)


def eight(row):
    return jnp.broadcast_to(row[None, :], (ROWS, row.shape[0]))


def pad_lanes(value):
    return jnp.pad(value, [(0, 0)] * (value.ndim - 1) + [(0, LANES - value.shape[-1])])


def weight_kernel(count, extra, place, *refs):
    own, rest = refs[:count], refs[count:]
    outs, rest = rest[-count:], rest[:-count]
    parts, more = (rest[:-2], rest[-2:]) if extra else (rest, ())
    block = pl.program_id(0)
    at = 0
    for source, out in zip(own, outs):
        cols = source.shape[1]

        @pl.when(place[1] == 1)
        def _():
            out[:, :cols] = source[...]

        for away, part in enumerate(parts):

            @pl.when((place[1] == 0) & (lax.bitwise_xor(place[0], block) == away))
            def _():
                out[:, :cols] = part[:, at : at + cols].astype(bf16)

        at += cols
    if more:
        cols = own[0].shape[1]
        outs[0][:, cols : cols + BC] = more[0][...]
        outs[0][:, cols + BC :] = more[1][...].astype(bf16)


def narrow_kernel(wide, narrow):
    narrow[...] = wide[...].astype(bf16)


def narrowed(value):
    rows, cols = value.shape
    return pl.pallas_call(
        narrow_kernel,
        grid=(rows // GROUP,),
        in_specs=[by_rows(cols, 0)],
        out_specs=by_rows(cols, 0),
        out_shape=shape(rows, cols, dtype=bf16),
        name="narrowed",
    )(value)


def weights_over(own, *marks):
    chips = lax.axis_size("chip")
    piece = jnp.concatenate(
        [take(value, lax.axis_index("chip"), chips).astype(f32) for value in behind(own, *marks)],
        axis=1,
    )
    return lax.ppermute(piece, BOTH, CROSS)


def gather_weights(piece, own, more=(), third=()):
    width = own[0].shape[0]
    chips = lax.axis_size("chip")
    chip = lax.axis_index("chip")
    held = (lax.axis_index("core") == lax.axis_index("zh")).astype(jnp.int32)
    size = width // chips
    if chips == 4:
        parts = [piece]
        for away in range(1, chips):
            pairs = [
                (4 * c + kind, 4 * (c ^ away) + kind) for c in range(chips) for kind in (1, 2)
            ]
            parts.append(lax.ppermute(piece, ("chip", "core", "zh"), pairs))
        place = jnp.stack([chip, held]).astype(jnp.int32)
        blocks = chips
    else:
        parts = [lax.all_gather(piece, "chip", tiled=True)]
        place = jnp.stack([0, held]).astype(jnp.int32)
        blocks, size = 1, width
    parts = behind(parts, *third)
    out_cols = [value.shape[1] for value in own]
    out_cols[0] += sum(value.shape[1] for value in more)

    def rows(cols):
        return pl.BlockSpec((size, cols), lambda c: (c, 0))

    return pl.pallas_call(
        functools.partial(weight_kernel, len(own), bool(more)),
        grid=(blocks,),
        in_specs=[pl.BlockSpec(memory_space=pltpu.SMEM)]
        + [rows(value.shape[1]) for value in own]
        + [whole(piece.shape if chips == 4 else parts[0].shape)] * len(parts)
        + [rows(value.shape[1]) for value in more],
        out_specs=[rows(cols) for cols in out_cols],
        out_shape=[shape(width, cols, dtype=bf16) for cols in out_cols],
        compiler_params=pltpu.CompilerParams(
            dimension_semantics=("arbitrary",), vmem_limit_bytes=40 * 1024 * 1024
        ),
        name="weights",
    )(place, *own, *parts, *more)


def shards(
    x_input,
    seg_ids,
    cotangent,
    norm_gain,
    w_z,
    w_x,
    w_bc,
    w_dt,
    conv_x,
    conv_bc,
    bias_x,
    bias_bc,
    dt_bias,
    a_log,
    d_skip,
    gate_gain,
    w_out,
):
    tok, width = x_input.shape
    inner = w_z.shape[2]
    core, far = lax.axis_index("core"), lax.axis_index("zh")
    held = core == far
    heads = w_dt.shape[2]
    count = tok // GROUP
    conv_cols = inner + BC
    all_cols = inner + BC + LANES

    dt_own = w_dt.astype(f32).reshape(LAYERS, width * heads // LANES, LANES)
    dt_sent = lax.ppermute(dt_own, BOTH, CROSS)
    dt_all = pad_lanes(jnp.where(held, dt_own, dt_sent).reshape(LAYERS, width, heads))
    hidden = to_block(x_input.astype(f32))
    first_x = weights_over([w_x[0]])
    first_rest = weights_over([w_z[0], w_out[0]], dt_sent)
    second_all = weights_over([w_x[1], w_z[1], w_out[1]], dt_sent)
    first_x, first_rest, second_all = behind((first_x, first_rest, second_all))
    (wall,) = gather_weights(first_x, [w_x[0]], (w_bc[0], dt_all[0]))
    seg = to_block(seg_ids.astype(f32))
    small = jnp.concatenate(
        [
            value.reshape(LAYERS, -1)
            for value in (conv_x, bias_x, dt_bias, a_log, d_skip, gate_gain)
        ],
        axis=1,
    )
    small = jnp.where(held, small, lax.ppermute(small, BOTH, CROSS))
    sizes = (CONV * inner, inner, heads, heads, heads, inner)
    pieces, at = [], 0
    for size in sizes:
        pieces.append(small[:, at : at + size])
        at += size
    conv_x, bias_x, dt_bias, a_log, d_skip, gate_gain = pieces
    conv_x = conv_x.reshape(LAYERS, CONV, inner)
    hidden_own = own_rows(hidden)
    hidden_block = hidden
    hidden = [hidden]
    place = jnp.stack([own_place(), own_place()]).astype(jnp.int32)
    smem = pl.BlockSpec(memory_space=pltpu.SMEM)
    edge_seg = shifted(seg[tok - ROWS :], 1)
    seg_ext = jnp.concatenate([edge_seg, seg])
    before = jnp.concatenate([edge_seg[ROWS - 1 :], seg[GROUP - 1 : tok - 1 : GROUP]])
    after = seg[GROUP - 1 :: GROUP]
    mask = jnp.stack(
        [
            (seg_ext[ROWS - CONV + 1 + k : ROWS - CONV + 1 + k + tok] == seg).astype(f32)
            for k in range(CONV - 1)
        ]
        + [
            (seg == jnp.repeat(before, GROUP)).astype(f32),
            (seg == jnp.repeat(after, GROUP)).astype(f32),
            seg,
            seg,
            seg,
        ],
        axis=1,
    )
    seg_col = seg[:, None]
    seg_row = eight(seg)
    expand = (jnp.arange(LANES)[:, None] == jnp.arange(inner)[None, :] // HEADDIM).astype(f32)
    position = jnp.arange(GROUP)
    tri = (position[:, None] >= position[None, :]).astype(f32)
    triback = (position[:, None] <= position[None, :]).astype(f32)

    stored = []
    for layer in range(LAYERS):
        if layer > 0:
            wall = next_wall
        taps = jnp.concatenate([conv_x[layer], conv_bc[layer]], axis=1)
        bias = eight(jnp.concatenate([bias_x[layer], bias_bc[layer]]))
        dtb = eight(pad_lanes(dt_bias[layer]))
        avec = eight(pad_lanes(-jnp.exp(a_log[layer])))
        dskip = eight(jnp.repeat(d_skip[layer], HEADDIM))
        ggain = eight(gate_gain[layer])
        ngain = norm_gain[layer][None, :]
        if len(hidden) == 1:
            end = hidden[0][tok - 16 :]
        else:
            ends = jnp.stack([piece[GROUP - 16 :] for piece in hidden])
            end = lax.dynamic_index_in_dim(ends, 3 ^ own_place(), 0, False)
        end = end * lax.rsqrt(jnp.mean(end * end, axis=1, keepdims=True) + epsilon) * ngain
        end = mm(end.astype(bf16), wall[:, : inner + BC])[ROWS:]
        halo = shifted(end, 1)
        normed, cin, cpre, dtp, cum, dtv, xdt, bc, sloc, pref, send = call(
            in_kernel,
            count,
            [
                (smem, place),
                (whole((width, all_cols)), wall),
                (whole((1, width)), ngain),
                (whole((CONV, conv_cols)), taps),
                (whole((ROWS, conv_cols)), bias),
                (whole((ROWS, LANES)), dtb),
                (whole((ROWS, LANES)), avec),
                (by_rows(ROWS, count), mask),
                (whole((ROWS, conv_cols)), halo),
                (whole((LANES, inner)), expand),
                (whole((GROUP, GROUP)), tri),
            ]
            + by_piece(hidden, count),
            [
                (by_rows(width, count), shape(tok, width, dtype=bf16)),
                (by_rows(conv_cols, count), shape(tok, conv_cols)),
                (by_rows(conv_cols, count), shape(tok, conv_cols)),
                (by_rows(LANES, count), shape(tok, LANES)),
                (by_rows(LANES, count), shape(tok, LANES)),
                (by_rows(LANES, count), shape(tok, LANES)),
                (by_rows(inner, count), shape(tok, inner, dtype=bf16)),
                (by_rows(BC, count), shape(tok, BC, dtype=bf16)),
                (by_group((STATE, inner), count), shape(count, STATE, inner)),
                (by_group((ROWS, inner), count), shape(count, ROWS, inner)),
                (whole((STATE + ROWS, inner)), shape(STATE + ROWS, inner)),
            ],
            [
                pltpu.VMEM((STATE, inner), f32),
                pltpu.VMEM((ROWS, inner), f32),
                pltpu.VMEM((ROWS, conv_cols), f32),
            ],
            16,
            "in_proj_conv",
        )
        if layer == 0:
            wz, wout = gather_weights(
                behind(first_rest, wall), [w_z[0], w_out[0]], third=(send,)
            )
            cotangent = to_block(behind(cotangent, send).astype(f32))
        else:
            wz, wout = next_wz, next_wout
        zval = mm(normed, wz)
        (yin,) = call(
            intra_kernel,
            count,
            [
                (by_rows(LANES, count), cum),
                (by_rows(inner, count), xdt),
                (by_rows(BC, count), bc),
                (by_rows(1, count), seg_col),
                (by_cols(count), seg_row),
            ],
            [(by_rows(inner, count), shape(tok, inner))],
            [],
            6,
            "ssd_within",
        )
        entry = chain(send, False)
        y, gate_in, proj, sums = call(
            out_kernel,
            count,
            [
                (by_rows(inner, count), yin),
                (by_rows(inner, count), cpre),
                (by_rows(LANES, count), cum),
                (by_rows(BC, count), bc),
                (by_rows(ROWS, count), mask),
                (by_rows(inner, count), zval),
                (by_group((STATE, inner), count), sloc),
                (by_group((ROWS, inner), count), pref),
                (whole((STATE, inner)), entry),
                (whole((ROWS, inner)), dskip),
                (whole((ROWS, inner)), ggain),
                (whole((width, inner)), wout),
                (whole((LANES, inner)), expand),
            ]
            + ([(by_rows(width, count), cotangent)] if layer == LAYERS - 1 else []),
            [
                (by_rows(inner, count), shape(tok, inner)),
                (by_rows(inner, count), shape(tok, inner, dtype=bf16)),
                (by_rows(width, count), shape(tok, width)),
                (by_cols(count), shape(ROWS, tok)),
            ],
            [],
            12,
            "gate_out_proj",
        )
        sums = total(sums, ("core", "zl"))
        gate_scale = lax.rsqrt(sums[0] / INNER + epsilon)
        stored.append(
            dict(
                hidden=hidden_own, normed=normed, zval=zval, cin=cin, cpre=cpre, dtp=dtp, cum=cum,
                dtv=dtv, xdt=xdt, bc=bc, sloc=sloc, pref=pref, entry=entry, y=y, gate_in=gate_in,
                proj=proj, gate_scale=gate_scale, dots=sums[1], halo=halo, wall=wall, wz=wz, wout=wout,
                taps=taps, dtb=dtb, avec=avec, dskip=dskip, ggain=ggain,
            )
        )
        if layer < LAYERS - 1:
            next_wall, next_wz, next_wout = gather_weights(
                behind(second_all, entry),
                [w_x[1], w_z[1], w_out[1]],
                (w_bc[1], dt_all[1]),
                third=(gate_scale,),
            )
            proj_sum = scatter_sum(proj)
            stored[layer]["proj_sum"] = proj_sum
            hidden_own = hidden_own + own_rows(gate_scale)[:, None] * proj_sum
            hidden = gather_pieces(hidden_own)

    grad_h = [cotangent]
    grad_own = own_rows(cotangent)
    matrices = [None] * LAYERS
    vectors = [None] * LAYERS
    shared = [None] * LAYERS
    for layer in reversed(range(LAYERS)):
        kept = stored[layer]
        gate_scale = kept["gate_scale"]
        if layer == LAYERS - 1:
            grad_scale = kept["dots"]
        else:
            grad_scale = gather_rows(jnp.sum(grad_own * kept["proj_sum"], axis=1))
        gsq = -grad_scale * gate_scale**3 / INNER
        rev = functools.partial(by_rows, count=count, reverse=True)
        rev_group = functools.partial(by_group, count=count, reverse=True)
        gproj, dy, dz, gloc, suf, gsend, acc = call(
            gate_kernel,
            count,
            [
                (smem, place),
                (rev(1), gate_scale[:, None]),
                (rev(1), gsq[:, None]),
                (rev(inner), kept["y"]),
                (rev(inner), kept["zval"]),
                (whole((ROWS, inner)), kept["ggain"]),
                (whole((width, inner)), kept["wout"]),
                (rev(LANES), kept["cum"]),
                (rev(BC), kept["bc"]),
                (rev(ROWS), mask),
                (whole((LANES, inner)), expand),
            ]
            + by_piece(grad_h, count, True),
            [
                (rev(width), shape(tok, width, dtype=bf16)),
                (rev(inner), shape(tok, inner, dtype=bf16)),
                (rev(inner), shape(tok, inner, dtype=bf16)),
                (rev_group((STATE, inner)), shape(count, STATE, inner)),
                (rev_group((ROWS, inner)), shape(count, ROWS, inner)),
                (whole((STATE + ROWS, inner)), shape(STATE + ROWS, inner)),
                (whole((ROWS, inner)), shape(ROWS, inner)),
            ],
            [pltpu.VMEM((STATE, inner), f32), pltpu.VMEM((ROWS, inner), f32)],
            10,
            "gate_back",
        )
        u, dbc = call(
            intra_back_kernel,
            count,
            [
                (by_rows(LANES, count), kept["cum"]),
                (by_rows(inner, count), kept["xdt"]),
                (by_rows(BC, count), kept["bc"]),
                (by_rows(1, count), seg_col),
                (by_cols(count), seg_row),
                (by_rows(inner, count), dy),
            ],
            [
                (by_rows(inner, count), shape(tok, inner)),
                (by_rows(BC, count), shape(tok, BC)),
            ],
            [],
            8,
            "ssd_within_back",
        )
        gout = chain(gsend, True)
        if layer == LAYERS - 1:
            last_sum = scatter_sum(kept["proj"], (dy,))
            hidden_own = hidden_own + own_rows(gate_scale)[:, None] * last_sum
            u = behind(u, hidden_own)
            out_parts = cross_over(hidden_own)
        else:
            out_swaps = near_swaps(behind(hidden_own, dy), *out_parts)
            g_out, g_z, _, g_x = behind(matrices[LAYERS - 1], u)
            first_sums = join_halves([g_out, g_z, g_x])
        grad_wout = mm(gproj, kept["gate_in"], ((0,), (0,)))
        grad_wz = mm(kept["normed"], dz, ((0,), (0,)))
        partial_z = mm(dz, kept["wz"], ((1,), (1,)))
        u = behind(u, grad_wout, grad_wz, partial_z)
        matrices[layer] = [
            lax.psum_scatter(value, "chip", scatter_dimension=0, tiled=True)
            for value in (grad_wout, grad_wz)
        ]
        gall, last8, rim, gtaps, vecs, dsk = call(
            in_back_kernel,
            count,
            [
                (rev(inner), u),
                (rev(BC), dbc),
                (rev(inner), dy),
                (rev(inner), kept["y"]),
                (rev(conv_cols), kept["cpre"]),
                (rev(conv_cols), kept["cin"]),
                (rev(LANES), kept["dtp"]),
                (rev(LANES), kept["dtv"]),
                (rev(LANES), kept["cum"]),
                (rev(inner), kept["xdt"]),
                (rev(BC), kept["bc"]),
                (rev(ROWS), mask),
                (rev_group((STATE, inner)), kept["sloc"]),
                (rev_group((ROWS, inner)), kept["pref"]),
                (whole((STATE, inner)), kept["entry"]),
                (rev_group((STATE, inner)), gloc),
                (rev_group((ROWS, inner)), suf),
                (whole((STATE, inner)), gout),
                (whole((ROWS, conv_cols)), kept["halo"]),
                (whole((CONV, conv_cols)), kept["taps"]),
                (whole((ROWS, LANES)), kept["dtb"]),
                (whole((ROWS, LANES)), kept["avec"]),
                (whole((ROWS, inner)), kept["dskip"]),
                (whole((LANES, inner)), expand),
                (whole((GROUP, GROUP)), triback),
            ],
            [
                (rev(all_cols), shape(tok, all_cols, dtype=bf16)),
                (whole((ROWS, conv_cols)), shape(ROWS, conv_cols)),
                (whole((ROWS, conv_cols)), shape(ROWS, conv_cols)),
                (whole((ROWS, conv_cols)), shape(ROWS, conv_cols)),
                (whole((ROWS, LANES)), shape(ROWS, LANES)),
                (whole((ROWS, inner)), shape(ROWS, inner)),
            ],
            [pltpu.VMEM((CONV - 1, ROWS, conv_cols), f32)],
            20,
            "in_proj_conv_back",
        )
        rim_back = shifted(rim, -1)
        if layer == 0:
            last8 = behind(last8, first_sums, *(out_swaps or ()))
        else:
            last8 = behind(last8, out_parts[0], out_parts[2])
        gall = lax.dynamic_update_slice(
            gall, (last8 + rim_back).astype(bf16), (tok - ROWS, 0)
        )
        partial = partial_z + mm(gall, kept["wall"], ((1,), (1,)))
        if layer > 0:
            partial = behind(partial, *out_parts)
        stages = []
        grad_normed = scatter_sum(partial, stages=stages)
        late = behind(gall, *stages)
        partial = behind(partial, *stages)
        grad_wbc = mm(kept["normed"], late[:, inner : inner + BC], ((0,), (0,)))
        grad_wdt = mm(kept["normed"], late[:, inner + BC :], ((0,), (0,)))
        grad_win = mm(kept["normed"], behind(late, grad_wbc, grad_wdt)[:, :inner], ((0,), (0,)))
        hidden_in = kept["hidden"]
        inv = lax.rsqrt(jnp.mean(hidden_in * hidden_in, axis=1, keepdims=True) + epsilon)
        if layer == 0:
            full = hidden_block
            grad_ngain = jnp.sum(
                partial
                * (full * lax.rsqrt(jnp.mean(full * full, axis=1, keepdims=True) + epsilon)),
                axis=0,
            )
        else:
            grad_ngain = jnp.sum(grad_normed * hidden_in * inv, axis=0)
        back = grad_normed * norm_gain[layer][None, :]
        grad_own = grad_own + inv * (
            back - hidden_in * inv * inv * jnp.mean(back * hidden_in, axis=1, keepdims=True)
        )
        if layer > 0:
            grad_h = gather_pieces(grad_own)
        matrices[layer] += [
            lax.psum_scatter(value, "chip", scatter_dimension=0, tiled=True)
            for value in (grad_wbc, grad_win)
        ]
        vectors[layer] = jnp.concatenate(
            [
                gtaps[: CONV + 1, :inner].reshape(-1),
                acc[0],
                vecs[0, :heads],
                vecs[1, :heads],
                dsk[0],
                grad_wdt[:, :heads].reshape(-1),
                gtaps[: CONV + 1, inner:].reshape(-1),
                grad_ngain,
            ]
        )
    vector = total(jnp.stack(vectors), ("zh", "chip"))
    other = swap(vector, "core")
    common = (CONV + 1) * BC + width
    shared = total((vector + other)[:, -common:], ("zl",))
    grad_wbc = half_rows(jnp.stack([matrices[1][2], matrices[0][2]], axis=1)[:, ::-1])
    grad_parts = cross_over(grad_own)
    own_s = near_swap(grad_own)
    grad_parts, own_s, shared, grad_wbc = behind((grad_parts, own_s, shared, grad_wbc))
    mark = grad_parts[0]
    input_grad = deliver(grad_own, *grad_parts, f32, near_swaps(grad_own, *grad_parts, own_s))
    final_out = deliver(hidden_own, *out_parts, bf16, out_swaps, (mark,))
    grad_wbc = total(grad_wbc, ("zh",))
    g_out, g_z, g_x = behind((matrices[0][0], matrices[0][1], matrices[0][3]), mark)
    early, late = join_halves([g_out, g_z]), join_halves([g_x])
    g_cols = [place_rows(early, late), place_rows(behind(first_sums, mark))]
    by_head = jnp.where(held, vector, other)[:, :-common]
    g_bc = shared[:, :-width].reshape(LAYERS, CONV + 1, BC)
    g_ngain = shared[:, -width:]
    at = 0
    pieces = []
    for size in (CONV * inner, inner, inner, heads, heads, inner, width * heads):
        pieces.append(by_head[:, at : at + size])
        at += size
    g_conv, g_bias, g_ggain, g_alog, g_dtb, g_dsk, g_wdt = pieces
    g_wdt = g_wdt.reshape(LAYERS, width, heads)
    rows = width // lax.axis_size(("chip", "core"))
    g_wdt = lax.dynamic_slice_in_dim(g_wdt, lax.axis_index(("chip", "core")) * rows, rows, axis=1)
    return (
        final_out,
        input_grad,
        g_ngain,
        jnp.stack([g[:, inner : 2 * inner] for g in g_cols]),
        jnp.stack([g[:, 2 * inner :] for g in g_cols]),
        jnp.stack([grad_wbc[:, layer] for layer in range(LAYERS)]),
        g_wdt,
        g_conv.reshape(LAYERS, CONV, inner),
        g_bc[:, :CONV],
        g_bias,
        g_bc[:, CONV],
        g_dtb,
        g_alog,
        jnp.sum(g_dsk.reshape(LAYERS, heads, HEADDIM), axis=2),
        g_ggain,
        jnp.stack([g[:, :inner] for g in g_cols]),
    )


def join_halves(parts):
    part = jnp.concatenate(parts, axis=1)
    return part + lax.ppermute(part, BOTH, CROSS_BACK)


def place_rows(*parts):
    core, far = lax.axis_index("core"), lax.axis_index("zh")
    sent = [lax.ppermute(take(full, 1 - core, 2), BOTH, CORE_OUT) for full in parts]
    rows = [
        jnp.where(core == far, take(full, core, 2), got) for full, got in zip(parts, sent)
    ]
    return jnp.concatenate(rows, axis=1)


def half_rows(part):
    core = lax.axis_index("core")
    part = take(part, core, 2) + swap(take(part, 1 - core, 2), "core")
    return total(part, ("zl",))


def solution(mesh):
    seq, head = mesh.devices.shape
    mesh = jax.sharding.Mesh(
        mesh.devices.reshape(seq // 2, 2, 2, head // 2), ("chip", "core", "zh", "zl")
    )
    tokens, columns = ("chip", "core"), ("zh", "zl")
    by_col = P(None, None, columns)
    by_head = P(None, columns)
    both = P(None, tokens, columns)
    placed = (
        P(tokens, None),
        P(tokens),
        P(tokens, None),
        P(),
        by_col,
        by_col,
        P(),
        by_col,
        by_col,
        P(),
        by_head,
        P(),
        by_head,
        by_head,
        by_head,
        by_head,
        by_col,
    )
    return jax.shard_map(
        shards,
        mesh=mesh,
        in_specs=placed,
        out_specs=(
            P(tokens, None),
            P(tokens, None),
            P(),
            both,
            both,
            P(None, tokens, None),
            both,
            by_col,
            P(),
            by_head,
            P(),
            by_head,
            by_head,
            by_head,
            by_head,
            both,
        ),
        check_vma=False,
    )
```

```python
import functools

import jax
import jax.numpy as jnp
from jax import lax
from jax.experimental import pallas as pl
from jax.experimental.pallas import tpu as pltpu
from jax.sharding import PartitionSpec as P

HEADDIM = 64
STATE = 128
CONV = 4
GROUP = 256
LAYERS = 2
INNER = 2048
LANES = 128
ROWS = 8
BC = 2 * STATE

epsilon = 1e-05
highest = lax.Precision.HIGHEST
f32 = jnp.float32
bf16 = jnp.bfloat16


def mm(left, right, dims=((1,), (0,)), precision=None):
    return lax.dot_general(
        left, right, (dims, ((), ())), preferred_element_type=f32, precision=precision
    )


def softplus(value):
    small = jnp.exp(-jnp.abs(value))
    series = small * (1.0 - small * (0.5 - small * (1.0 / 3.0 - small * (0.25 - small * 0.2))))
    return jnp.maximum(value, 0.0) + jnp.where(small < 0.03, series, jnp.log(1.0 + small))


def silu_slope(value, sigma):
    return sigma * (1.0 + value * (1.0 - sigma))


def spread(heads, expand):
    return mm(heads, expand, precision=highest)


def gather_heads(lanes, expand):
    return mm(lanes, expand, ((1,), (1,)), precision=highest)


def pick(place, pieces, held):
    if len(pieces) == 1:
        return pieces[0][...]
    away = lax.bitwise_xor(pl.program_id(0) if held is None else held, place[0])
    value = pieces[3][...]
    for number in range(3):
        value = jnp.where(away == number, pieces[number][...], value)
    return value


def in_kernel(
    place, wall, ngain, taps, bias, dtb, avec, mask, halo, expand, tri, *refs
):
    hid = refs[:-14]
    normed, cin, cpre, dtp, cum, dtv, xdt, bc, sloc, pref, send, state, thru, prev = refs[-14:]
    step = pl.program_id(0)
    inner = expand.shape[1]

    @pl.when(step == 0)
    def _():
        state[...] = jnp.zeros_like(state)
        thru[...] = jnp.ones_like(thru)
        prev[...] = halo[...]

    h = pick(place, hid, None)
    inv = lax.rsqrt(jnp.mean(h * h, axis=1, keepdims=True) + epsilon)
    low = (h * inv * ngain[...]).astype(bf16)
    normed[...] = low
    rows = mm(low, wall[:, : inner + BC])
    pre_dt = mm(low, wall[:, inner + BC :])
    dtp[...] = pre_dt
    cin[...] = rows
    ext = jnp.concatenate([prev[...], rows], axis=0)
    prev[...] = rows[GROUP - ROWS :]
    total = taps[CONV - 1 : CONV, :] * rows + bias[0:1, :]
    for k in range(CONV - 1):
        first = ROWS - CONV + 1 + k
        total = total + taps[k : k + 1, :] * ext[first : first + GROUP] * mask[:, k : k + 1]
    cpre[...] = total
    act = total * jax.nn.sigmoid(total)
    x = act[:, :inner]
    low_bc = act[:, inner:].astype(bf16)
    bc[...] = low_bc
    dt = softplus(pre_dt + dtb[0:1, :])
    dtv[...] = dt
    run = mm(tri[...], dt * avec[0:1, :], precision=highest)
    cum[...] = run
    last = run[GROUP - 1 : GROUP]
    xdt[...] = (x * spread(dt, expand[...])).astype(bf16)
    tail = jnp.exp(last - run) * mask[:, 4:5] * dt
    contrib = mm(low_bc[:, :STATE], (x * spread(tail, expand[...])).astype(bf16), ((0,), (0,)))
    through = jnp.broadcast_to(jnp.exp(last) * mask[GROUP - 1 : GROUP, 3:4], (ROWS, LANES))
    through = spread(through, expand[...])
    sloc[0] = state[...]
    pref[0] = thru[...]
    state[...] = through[0:1] * state[...] + contrib
    thru[...] = thru[...] * through

    @pl.when(step == pl.num_programs(0) - 1)
    def _():
        send[:STATE] = state[...]
        send[STATE:] = thru[...]


def pair_lanes(value, which):
    lane = lax.broadcasted_iota(jnp.int32, value.shape, 1)
    keep = lane < HEADDIM if which == 0 else lane >= HEADDIM
    return jnp.where(keep, value, jnp.zeros_like(value))


def intra_kernel(cum, xdt, bc, seg, segrow, y):
    inner = xdt.shape[1]
    run = cum[...]
    run_t = run.T
    base = mm(bc[:, STATE:], bc[:, :STATE], ((1,), (1,)))
    t_at = lax.broadcasted_iota(jnp.int32, (GROUP, GROUP), 0)
    s_at = lax.broadcasted_iota(jnp.int32, (GROUP, GROUP), 1)
    same = (seg[:, 0:1] == segrow[0:1, :]) & (t_at >= s_at)
    closed = jnp.where(same, 0.0, -1e30)
    for pair in range(inner // LANES):
        cols = slice(pair * LANES, (pair + 1) * LANES)
        xs = xdt[:, cols]
        parts = []
        for which in range(2):
            head = 2 * pair + which
            decay = jnp.exp(run[:, head : head + 1] - run_t[head : head + 1, :] + closed)
            parts.append(mm((decay * base).astype(bf16), xs))
        lane = lax.broadcasted_iota(jnp.int32, (GROUP, LANES), 1)
        y[:, cols] = jnp.where(lane < HEADDIM, parts[0], parts[1])


def out_kernel(
    yin, cpre, cum, bc, mask, zval, sloc, pref, entry, dskip, ggain, wout, expand, *refs
):
    cot, (y, gate_in, proj, sums) = refs[:-4], refs[-4:]
    inner = expand.shape[1]
    pre = cpre[...]
    x = pre * jax.nn.sigmoid(pre)
    full = sloc[0] + pref[0][0:1] * entry[...]
    reach = spread(jnp.exp(cum[...]) * mask[:, 3:4], expand[...])
    value = yin[...] + reach * mm(bc[:, STATE:], full.astype(bf16)) + dskip[0:1, :] * x
    y[...] = value
    z = zval[...]
    gated = value * (z * jax.nn.sigmoid(z))
    low = (gated * ggain[0:1, :]).astype(bf16)
    gate_in[...] = low
    proj[...] = mm(low, wout[...], ((1,), (1,)))
    ones = jnp.ones((ROWS, inner), f32)
    squares = mm(ones, gated * gated, ((1,), (1,)), precision=highest)
    if cot:
        back = mm(cot[0][...].astype(bf16), wout[...])
        dots = mm(ones, low.astype(f32) * back, ((1,), (1,)), precision=highest)
        row = lax.broadcasted_iota(jnp.int32, squares.shape, 0)
        squares = jnp.where(row == 0, squares, dots)
    sums[...] = squares


def gate_kernel(
    place, scale, gsq, y, zval, ggain, wout, cum, bc, mask, expand, *refs
):
    gh = refs[:-9]
    gproj, dy, dz, gloc, suf, send, acc, carry, thru = refs[-9:]
    step = pl.program_id(0)

    @pl.when(step == 0)
    def _():
        carry[...] = jnp.zeros_like(carry)
        thru[...] = jnp.ones_like(thru)
        acc[...] = jnp.zeros_like(acc)

    gp = (scale[...] * pick(place, gh, pl.num_programs(0) - 1 - step)).astype(bf16)
    gproj[...] = gp
    ggi = mm(gp, wout[...])
    z = zval[...]
    sigma = jax.nn.sigmoid(z)
    silu = z * sigma
    value = y[...]
    gated = value * silu
    ggated = ggi * ggain[0:1, :] + gated * gsq[...]
    acc[0:1, :] += jnp.sum(ggi * gated, axis=0, keepdims=True)
    low = (ggated * silu).astype(bf16)
    dy[...] = low
    dz[...] = (ggated * value * silu_slope(z, sigma)).astype(bf16)
    run = cum[...]
    last = run[GROUP - 1 : GROUP]
    reach = spread(jnp.exp(run) * mask[:, 3:4], expand[...])
    back = mm(bc[:, STATE:], (reach * low.astype(f32)).astype(bf16), ((0,), (0,)))
    through = jnp.broadcast_to(jnp.exp(last) * mask[GROUP - 1 : GROUP, 3:4], (ROWS, LANES))
    through = spread(through, expand[...])
    gloc[0] = carry[...]
    suf[0] = thru[...]
    carry[...] = back + through[0:1] * carry[...]
    thru[...] = thru[...] * through

    @pl.when(step == pl.num_programs(0) - 1)
    def _():
        send[:STATE] = carry[...]
        send[STATE:] = thru[...]


def intra_back_kernel(cum, xdt, bc, seg, segrow, dy, u, dbc):
    inner = xdt.shape[1]
    run = cum[...]
    run_t = run.T
    base = mm(bc[:, :STATE], bc[:, STATE:], ((1,), (1,)))
    s_at = lax.broadcasted_iota(jnp.int32, (GROUP, GROUP), 0)
    t_at = lax.broadcasted_iota(jnp.int32, (GROUP, GROUP), 1)
    same = (seg[:, 0:1] == segrow[0:1, :]) & (t_at >= s_at)
    closed = jnp.where(same, 0.0, -1e30)
    grad_base = jnp.zeros((GROUP, GROUP), f32)
    for pair in range(inner // LANES):
        cols = slice(pair * LANES, (pair + 1) * LANES)
        xs = xdt[:, cols]
        ds = dy[:, cols]
        parts = []
        for which in range(2):
            head = 2 * pair + which
            decay = jnp.exp(run_t[head : head + 1, :] - run[:, head : head + 1] + closed)
            parts.append(mm((decay * base).astype(bf16), ds))
            grad_base = grad_base + decay * mm(xs, pair_lanes(ds, which), ((1,), (1,)))
        lane = lax.broadcasted_iota(jnp.int32, (GROUP, LANES), 1)
        u[:, cols] = jnp.where(lane < HEADDIM, parts[0], parts[1])
    low = grad_base.astype(bf16)
    dbc[:, :STATE] = mm(low, bc[:, STATE:])
    dbc[:, STATE:] = mm(low, bc[:, :STATE], ((0,), (0,)))


def in_back_kernel(
    uin, dbc, dy, y, cpre, cin, dtp, dtv, cum, xdt, bc, mask, sloc, pref, entry, gloc, suf,
    gout, halo, taps, dtb, avec, dskip, expand, triback,
    gall, last8, rim, gtaps, vecs, dsk,
    nexts,
):
    step = pl.program_id(0)
    inner = expand.shape[1]

    @pl.when(step == 0)
    def _():
        nexts[...] = jnp.zeros_like(nexts)
        gtaps[...] = jnp.zeros_like(gtaps)
        vecs[...] = jnp.zeros_like(vecs)
        dsk[...] = jnp.zeros_like(dsk)

    e = expand[...]
    pre = cpre[...]
    sigma = jax.nn.sigmoid(pre)
    x = (pre * sigma)[:, :inner]
    full = sloc[0] + pref[0][0:1] * entry[...]
    nxt = gloc[0] + suf[0][0:1] * gout[...]
    nxt_low = nxt.astype(bf16)
    run = cum[...]
    last = run[GROUP - 1 : GROUP]
    dt = dtv[...]
    low_dy = dy[...].astype(f32)
    xw = xdt[...].astype(f32)
    tail = spread(jnp.exp(last - run) * mask[:, 4:5], e)
    reach = spread(jnp.exp(run) * mask[:, 3:4], e)
    u_inter = tail * mm(bc[:, :STATE], nxt_low)
    u = uin[...] + u_inter
    dx = spread(dt, e) * u + dskip[0:1, :] * low_dy
    dsk[0:1, :] += jnp.sum(low_dy * x, axis=0, keepdims=True)
    db = dbc[:, :STATE] + mm((tail * xw).astype(bf16), nxt_low, ((1,), (1,)))
    dc = dbc[:, STATE:] + mm((reach * low_dy).astype(bf16), full.astype(bf16), ((1,), (1,)))
    grad_dt = gather_heads(x * u, e)
    y_plain = y[...] - dskip[0:1, :] * x
    grad_cum = gather_heads(low_dy * y_plain - xw * u, e)
    flow = jnp.sum(nxt * full, axis=0, keepdims=True)
    flow = gather_heads(jnp.broadcast_to(flow, (ROWS, inner)), e)[0:1]
    ends = jnp.sum(xw * u_inter, axis=0, keepdims=True)
    ends = gather_heads(jnp.broadcast_to(ends, (ROWS, inner)), e)[0:1]
    grad_tot = mask[GROUP - 1 : GROUP, 3:4] * jnp.exp(last) * flow + ends
    grad_da = mm(triback[...], grad_cum, precision=highest) + grad_tot
    a = avec[0:1, :]
    grad_dtv = grad_dt + grad_da * a
    grad_dtpre = grad_dtv * jax.nn.sigmoid(dtp[...] + dtb[0:1, :])
    vecs[0:1, :] += jnp.sum(grad_da * dt, axis=0, keepdims=True) * a
    vecs[1:2, :] += jnp.sum(grad_dtpre, axis=0, keepdims=True)
    slope = silu_slope(pre, sigma)
    grad_pre = jnp.concatenate([dx, db, dc], axis=1) * slope
    gtaps[4:5, :] += jnp.sum(grad_pre, axis=0, keepdims=True)
    rows = cin[...]
    grad_rows = taps[CONV - 1 : CONV, :] * grad_pre
    gtaps[3:4, :] += jnp.sum(rows * grad_pre, axis=0, keepdims=True)
    masked = []
    for k in range(CONV - 1):
        m = grad_pre * mask[:, k : k + 1]
        masked.append(m[:ROWS])
        ahead = CONV - 1 - k
        shifted = jnp.concatenate([m, nexts[k]], axis=0)[ahead : ahead + GROUP]
        grad_rows = grad_rows + taps[k : k + 1, :] * shifted
        gtaps[k : k + 1, :] += jnp.sum(rows * shifted, axis=0, keepdims=True)
    for k in range(CONV - 1):
        nexts[k] = masked[k]
    gall[:, : inner + BC] = grad_rows.astype(bf16)
    gall[:, inner + BC :] = grad_dtpre.astype(bf16)

    @pl.when(step == 0)
    def _():
        last8[...] = grad_rows[GROUP - ROWS :]

    @pl.when(step == pl.num_programs(0) - 1)
    def _():
        spill = jnp.zeros((ROWS, inner + BC), f32)
        edge = halo[...]
        for k in range(CONV - 1):
            down = ROWS - CONV + 1 + k
            moved = jnp.concatenate([jnp.zeros((ROWS, inner + BC), f32), masked[k]], axis=0)
            moved = moved[ROWS - down : 2 * ROWS - down]
            spill = spill + taps[k : k + 1, :] * moved
            gtaps[k : k + 1, :] += jnp.sum(edge * moved, axis=0, keepdims=True)
        rim[...] = spill


def whole(shape):
    return pl.BlockSpec(shape, lambda c: (0,) * len(shape))


def by_rows(cols, count, reverse=False):
    if reverse:
        return pl.BlockSpec((GROUP, cols), lambda c: (count - 1 - c, 0))
    return pl.BlockSpec((GROUP, cols), lambda c: (c, 0))


def by_group(shape, count, reverse=False):
    if reverse:
        return pl.BlockSpec((1,) + shape, lambda c: (count - 1 - c, 0, 0))
    return pl.BlockSpec((1,) + shape, lambda c: (c, 0, 0))


def by_piece(pieces, count, reverse=False):
    if len(pieces) == 1:
        return [(by_rows(pieces[0].shape[1], count, reverse), pieces[0])]
    return [(whole(piece.shape), piece) for piece in pieces]


def by_cols(count):
    return pl.BlockSpec((ROWS, GROUP), lambda c: (0, c))


def call(kernel, count, ins, outs, scratch, micros, name):
    return pl.pallas_call(
        kernel,
        grid=(count,),
        in_specs=[spec for spec, _ in ins],
        out_specs=[spec for spec, _ in outs],
        out_shape=[shape for _, shape in outs],
        scratch_shapes=scratch,
        compiler_params=pltpu.CompilerParams(
            dimension_semantics=("arbitrary",), vmem_limit_bytes=56 * 1024 * 1024
        ),
        cost_estimate=pl.CostEstimate(
            flops=micros * 1_150_000_000, bytes_accessed=1024 * 1024, transcendentals=0
        ),
        name=name,
    )(*[value for _, value in ins])


def shape(*dims, dtype=f32):
    return jax.ShapeDtypeStruct(dims, dtype)


SWAP = ((0, 1), (1, 0))
CROSS = ((0, 1), (3, 2))
CROSS_BACK = ((1, 0), (2, 3))
CORE_OUT = ((0, 2), (3, 1))
CORE_IN = ((2, 0), (1, 3))
DIAGONAL = ((2, 1), (1, 2))
BOTH = ("core", "zh")
BLOCKS = ("chip", "zh")


def shifted(value, steps):
    count = lax.axis_size(BLOCKS)
    leading, last = (max(0, -steps), min(count, count - steps))
    return lax.ppermute(value, BLOCKS, [(source, source + steps) for source in range(leading, last)])


def chain(part, reverse, stages):
    count = lax.axis_size(BLOCKS)
    place = lax.axis_index(BLOCKS)
    state, decay = part[:STATE], part[STATE : STATE + 1]
    entry, reach = jnp.zeros_like(state), jnp.ones_like(decay)
    step = 1
    while step < count:
        got = lax.ppermute(part, BLOCKS, [(i, i ^ step) for i in range(count)])
        got_state, got_decay = got[:STATE], got[STATE : STATE + 1]
        later = ((place & step) == 0) if reverse else ((place & step) != 0)
        stages.append(got)
        entry = jnp.where(later, entry + reach * got_state, entry)
        reach = jnp.where(later, reach * got_decay, reach)
        state = jnp.where(later, state + decay * got_state, got_state + got_decay * state)
        decay = decay * got_decay
        part = jnp.concatenate([state, jnp.broadcast_to(decay, (ROWS, decay.shape[1]))])
        step *= 2
    return entry


def swap(value, axis):
    return lax.ppermute(value, axis, SWAP)


def total(value, axes):
    for axis in axes:
        count = lax.axis_size(axis)
        step = 1
        while step < count:
            value = value + lax.ppermute(value, axis, [(i, i ^ step) for i in range(count)])
            step *= 2
    return value


def take(value, index, count):
    size = value.shape[0] // count
    return lax.dynamic_slice_in_dim(value, index * size, size)


def ordered(place, mine, theirs):
    return jnp.where(
        place == 0, jnp.concatenate([mine, theirs]), jnp.concatenate([theirs, mine])
    )


def behind(value, *marks):
    return lax.optimization_barrier((value, *marks))[0]


def scatter_sum(part, mark=()):
    core, near = lax.axis_index("core"), lax.axis_index("zl")
    half = take(part, core, 2) + behind(swap(take(part, 1 - core, 2), "core"), *mark)
    if lax.axis_size("zl") == 2:
        return take(half, near, 2) + swap(take(half, 1 - near, 2), "zl")
    return lax.psum_scatter(half, "zl", scatter_dimension=0, tiled=True)


def own_rows(value):
    core, near = lax.axis_index("core"), lax.axis_index("zl")
    return take(take(value, core, 2), near, lax.axis_size("zl"))


def gather_near(value):
    if lax.axis_size("zl") == 2:
        return ordered(lax.axis_index("zl"), value, swap(value, "zl"))
    return lax.all_gather(value, "zl", tiled=True)


def gather_rows(value):
    half = gather_near(value)
    return ordered(lax.axis_index("core"), half, swap(half, "core"))


def own_place():
    return 2 * lax.axis_index("core") + lax.axis_index("zl")


def gather_pieces(value):
    if lax.axis_size("zl") != 2 or value.shape[0] != GROUP:
        return [gather_rows(value)]
    near = swap(value, "zl")
    return [value, near, swap(value, "core"), swap(near, "core")]


def place_kernel(place, value, mine, near, theirs, value_s, mine_s, near_s, theirs_s, out):
    away = lax.bitwise_xor(pl.program_id(0), place[0])
    pairs = ((value, mine), (value_s, mine_s), (near, theirs), (near_s, theirs_s))
    for number, (here, there) in enumerate(pairs):

        @pl.when((away == number) & (place[1] == 1))
        def _():
            out[...] = here[...].astype(out.dtype)

        @pl.when((away == number) & (place[1] == 0))
        def _():
            out[...] = there[...].astype(out.dtype)


def cross_over(value):
    return [lax.ppermute(value, BOTH, pairs) for pairs in (CROSS, DIAGONAL, CORE_IN)]


def near_swap(value):
    if lax.axis_size("zl") != 2 or value.shape[0] != GROUP:
        return None
    here = [(2 * kind + i, 2 * kind + 1 - i) for kind in (0, 3) for i in range(2)]
    return lax.ppermute(value, ("core", "zh", "zl"), here)


def near_swaps(value, mine, theirs, near, value_s=None):
    if lax.axis_size("zl") != 2 or value.shape[0] != GROUP:
        return None
    axes = ("core", "zh", "zl")
    there = [(2 * kind + i, 2 * kind + 1 - i) for kind in (1, 2) for i in range(2)]
    return (
        near_swap(value) if value_s is None else value_s,
        lax.ppermute(mine, axes, there),
        lax.ppermute(theirs, axes, there),
        near_swap(near),
    )


def deliver(value, mine, theirs, near, dtype, swaps=None, mark=()):
    core, far = lax.axis_index("core"), lax.axis_index("zh")
    held = core == far
    if lax.axis_size("zl") != 2 or value.shape[0] != GROUP:
        mine = gather_near(jnp.where(held, value, mine))
        theirs = gather_near(jnp.where(held, near, theirs))
        full = ordered(core, mine, theirs)
        return narrowed(full) if dtype == bf16 else full
    if swaps is None:
        swaps = near_swaps(value, mine, theirs, near)
    value_s, mine_s, theirs_s, near_s = swaps
    place = jnp.stack([own_place(), held.astype(jnp.int32)]).astype(jnp.int32)
    width = value.shape[1]
    parts = behind((value, mine, near, theirs, value_s, mine_s, near_s, theirs_s), *mark)
    return pl.pallas_call(
        place_kernel,
        grid=(4,),
        in_specs=[pl.BlockSpec(memory_space=pltpu.SMEM)] + [whole((GROUP, width))] * 8,
        out_specs=by_rows(width, 4),
        out_shape=shape(4 * GROUP, width, dtype=dtype),
        compiler_params=pltpu.CompilerParams(
            dimension_semantics=("arbitrary",), vmem_limit_bytes=40 * 1024 * 1024
        ),
        name="place",
    )(place, *parts)


def to_block(value):
    got = lax.ppermute(value, BOTH, CORE_OUT)
    return jnp.where(lax.axis_index("core") == lax.axis_index("zh"), value, got)


def eight(row):
    return jnp.broadcast_to(row[None, :], (ROWS, row.shape[0]))


def pad_lanes(value):
    return jnp.pad(value, [(0, 0)] * (value.ndim - 1) + [(0, LANES - value.shape[-1])])


def weight_kernel(count, extra, place, *refs):
    own, rest = refs[:count], refs[count:]
    outs, rest = rest[-count:], rest[:-count]
    parts, more = (rest[:-2], rest[-2:]) if extra else (rest, ())
    block = pl.program_id(0)
    at = 0
    for source, out in zip(own, outs):
        cols = source.shape[1]

        @pl.when(place[1] == 1)
        def _():
            out[:, :cols] = source[...]

        for away, part in enumerate(parts):

            @pl.when((place[1] == 0) & (lax.bitwise_xor(place[0], block) == away))
            def _():
                out[:, :cols] = part[:, at : at + cols].astype(bf16)

        at += cols
    if more:
        cols = own[0].shape[1]
        outs[0][:, cols : cols + BC] = more[0][...]
        outs[0][:, cols + BC :] = more[1][...].astype(bf16)


def narrow_kernel(wide, narrow):
    narrow[...] = wide[...].astype(bf16)


def narrowed(value):
    rows, cols = value.shape
    return pl.pallas_call(
        narrow_kernel,
        grid=(rows // GROUP,),
        in_specs=[by_rows(cols, 0)],
        out_specs=by_rows(cols, 0),
        out_shape=shape(rows, cols, dtype=bf16),
        name="narrowed",
    )(value)


def weights_over(own, *marks):
    chips = lax.axis_size("chip")
    piece = jnp.concatenate(
        [take(value, lax.axis_index("chip"), chips).astype(f32) for value in behind(own, *marks)],
        axis=1,
    )
    return lax.ppermute(piece, BOTH, CROSS)


def gather_weights(piece, own, more=(), third=()):
    width = own[0].shape[0]
    chips = lax.axis_size("chip")
    chip = lax.axis_index("chip")
    held = (lax.axis_index("core") == lax.axis_index("zh")).astype(jnp.int32)
    size = width // chips
    if chips == 4:
        parts = [piece]
        for away in range(1, chips):
            pairs = [
                (4 * c + kind, 4 * (c ^ away) + kind) for c in range(chips) for kind in (1, 2)
            ]
            parts.append(lax.ppermute(piece, ("chip", "core", "zh"), pairs))
        place = jnp.stack([chip, held]).astype(jnp.int32)
        blocks = chips
    else:
        parts = [lax.all_gather(piece, "chip", tiled=True)]
        place = jnp.stack([0, held]).astype(jnp.int32)
        blocks, size = 1, width
    parts = behind(parts, *third)
    out_cols = [value.shape[1] for value in own]
    out_cols[0] += sum(value.shape[1] for value in more)

    def rows(cols):
        return pl.BlockSpec((size, cols), lambda c: (c, 0))

    return pl.pallas_call(
        functools.partial(weight_kernel, len(own), bool(more)),
        grid=(blocks,),
        in_specs=[pl.BlockSpec(memory_space=pltpu.SMEM)]
        + [rows(value.shape[1]) for value in own]
        + [whole(piece.shape if chips == 4 else parts[0].shape)] * len(parts)
        + [rows(value.shape[1]) for value in more],
        out_specs=[rows(cols) for cols in out_cols],
        out_shape=[shape(width, cols, dtype=bf16) for cols in out_cols],
        compiler_params=pltpu.CompilerParams(
            dimension_semantics=("arbitrary",), vmem_limit_bytes=40 * 1024 * 1024
        ),
        name="weights",
    )(place, *own, *parts, *more)


def shards(
    x_input,
    seg_ids,
    cotangent,
    norm_gain,
    w_z,
    w_x,
    w_bc,
    w_dt,
    conv_x,
    conv_bc,
    bias_x,
    bias_bc,
    dt_bias,
    a_log,
    d_skip,
    gate_gain,
    w_out,
):
    tok, width = x_input.shape
    inner = w_z.shape[2]
    core, far = lax.axis_index("core"), lax.axis_index("zh")
    held = core == far
    heads = w_dt.shape[2]
    count = tok // GROUP
    conv_cols = inner + BC
    all_cols = inner + BC + LANES

    dt_own = w_dt.astype(f32).reshape(LAYERS, width * heads // LANES, LANES)
    dt_sent = lax.ppermute(dt_own, BOTH, CROSS)
    dt_all = pad_lanes(jnp.where(held, dt_own, dt_sent).reshape(LAYERS, width, heads))
    first_x = weights_over([w_x[0]])
    hidden = to_block(x_input.astype(f32))
    first_rest = weights_over([w_z[0], w_out[0]], first_x)
    (wall,) = gather_weights(first_x, [w_x[0]], (w_bc[0], dt_all[0]), (first_rest,))
    seg = to_block(seg_ids.astype(f32))
    small = jnp.concatenate(
        [
            value.reshape(LAYERS, -1)
            for value in (conv_x, bias_x, dt_bias, a_log, d_skip, gate_gain)
        ],
        axis=1,
    )
    small = jnp.where(held, small, lax.ppermute(small, BOTH, CROSS))
    sizes = (CONV * inner, inner, heads, heads, heads, inner)
    pieces, at = [], 0
    for size in sizes:
        pieces.append(small[:, at : at + size])
        at += size
    conv_x, bias_x, dt_bias, a_log, d_skip, gate_gain = pieces
    conv_x = conv_x.reshape(LAYERS, CONV, inner)
    hidden_own = own_rows(hidden)
    hidden_block = hidden
    hidden = [hidden]
    place = jnp.stack([own_place(), own_place()]).astype(jnp.int32)
    smem = pl.BlockSpec(memory_space=pltpu.SMEM)
    edge_seg = shifted(seg[tok - ROWS :], 1)
    seg_ext = jnp.concatenate([edge_seg, seg])
    before = jnp.concatenate([edge_seg[ROWS - 1 :], seg[GROUP - 1 : tok - 1 : GROUP]])
    after = seg[GROUP - 1 :: GROUP]
    mask = jnp.stack(
        [
            (seg_ext[ROWS - CONV + 1 + k : ROWS - CONV + 1 + k + tok] == seg).astype(f32)
            for k in range(CONV - 1)
        ]
        + [
            (seg == jnp.repeat(before, GROUP)).astype(f32),
            (seg == jnp.repeat(after, GROUP)).astype(f32),
            seg,
            seg,
            seg,
        ],
        axis=1,
    )
    seg_col = seg[:, None]
    seg_row = eight(seg)
    expand = (jnp.arange(LANES)[:, None] == jnp.arange(inner)[None, :] // HEADDIM).astype(f32)
    position = jnp.arange(GROUP)
    tri = (position[:, None] >= position[None, :]).astype(f32)
    triback = (position[:, None] <= position[None, :]).astype(f32)

    stored = []
    for layer in range(LAYERS):
        if layer > 0:
            wall = next_wall
        taps = jnp.concatenate([conv_x[layer], conv_bc[layer]], axis=1)
        bias = eight(jnp.concatenate([bias_x[layer], bias_bc[layer]]))
        dtb = eight(pad_lanes(dt_bias[layer]))
        avec = eight(pad_lanes(-jnp.exp(a_log[layer])))
        dskip = eight(jnp.repeat(d_skip[layer], HEADDIM))
        ggain = eight(gate_gain[layer])
        ngain = norm_gain[layer][None, :]
        if len(hidden) == 1:
            end = hidden[0][tok - 16 :]
        else:
            ends = jnp.stack([piece[GROUP - 16 :] for piece in hidden])
            end = lax.dynamic_index_in_dim(ends, 3 ^ own_place(), 0, False)
        end = end * lax.rsqrt(jnp.mean(end * end, axis=1, keepdims=True) + epsilon) * ngain
        end = mm(end.astype(bf16), wall[:, : inner + BC])[ROWS:]
        halo = shifted(end, 1)
        normed, cin, cpre, dtp, cum, dtv, xdt, bc, sloc, pref, send = call(
            in_kernel,
            count,
            [
                (smem, place),
                (whole((width, all_cols)), wall),
                (whole((1, width)), ngain),
                (whole((CONV, conv_cols)), taps),
                (whole((ROWS, conv_cols)), bias),
                (whole((ROWS, LANES)), dtb),
                (whole((ROWS, LANES)), avec),
                (by_rows(ROWS, count), mask),
                (whole((ROWS, conv_cols)), halo),
                (whole((LANES, inner)), expand),
                (whole((GROUP, GROUP)), tri),
            ]
            + by_piece(hidden, count),
            [
                (by_rows(width, count), shape(tok, width, dtype=bf16)),
                (by_rows(conv_cols, count), shape(tok, conv_cols)),
                (by_rows(conv_cols, count), shape(tok, conv_cols)),
                (by_rows(LANES, count), shape(tok, LANES)),
                (by_rows(LANES, count), shape(tok, LANES)),
                (by_rows(LANES, count), shape(tok, LANES)),
                (by_rows(inner, count), shape(tok, inner, dtype=bf16)),
                (by_rows(BC, count), shape(tok, BC, dtype=bf16)),
                (by_group((STATE, inner), count), shape(count, STATE, inner)),
                (by_group((ROWS, inner), count), shape(count, ROWS, inner)),
                (whole((STATE + ROWS, inner)), shape(STATE + ROWS, inner)),
            ],
            [
                pltpu.VMEM((STATE, inner), f32),
                pltpu.VMEM((ROWS, inner), f32),
                pltpu.VMEM((ROWS, conv_cols), f32),
            ],
            16,
            "in_proj_conv",
        )
        if layer == 0:
            wz, wout = gather_weights(
                behind(first_rest, wall), [w_z[0], w_out[0]], third=(send,)
            )
            cotangent = behind(cotangent, send).astype(f32)
            cot_sent = lax.ppermute(cotangent, BOTH, CORE_OUT)
        else:
            wz, wout = next_wz, next_wout
        zval = mm(normed, wz)
        (yin,) = call(
            intra_kernel,
            count,
            [
                (by_rows(LANES, count), cum),
                (by_rows(inner, count), xdt),
                (by_rows(BC, count), bc),
                (by_rows(1, count), seg_col),
                (by_cols(count), seg_row),
            ],
            [(by_rows(inner, count), shape(tok, inner))],
            [],
            6,
            "ssd_within",
        )
        stages = []
        entry = chain(send, False, stages)
        if layer == 0:
            second_all = weights_over([w_x[1], w_z[1], w_out[1]], stages[0])
            entry = behind(entry, second_all, cot_sent)
            cotangent = jnp.where(held, cotangent, cot_sent)
        y, gate_in, proj, sums = call(
            out_kernel,
            count,
            [
                (by_rows(inner, count), yin),
                (by_rows(inner, count), cpre),
                (by_rows(LANES, count), cum),
                (by_rows(BC, count), bc),
                (by_rows(ROWS, count), mask),
                (by_rows(inner, count), zval),
                (by_group((STATE, inner), count), sloc),
                (by_group((ROWS, inner), count), pref),
                (whole((STATE, inner)), entry),
                (whole((ROWS, inner)), dskip),
                (whole((ROWS, inner)), ggain),
                (whole((width, inner)), wout),
                (whole((LANES, inner)), expand),
            ]
            + ([(by_rows(width, count), cotangent)] if layer == LAYERS - 1 else []),
            [
                (by_rows(inner, count), shape(tok, inner)),
                (by_rows(inner, count), shape(tok, inner, dtype=bf16)),
                (by_rows(width, count), shape(tok, width)),
                (by_cols(count), shape(ROWS, tok)),
            ],
            [],
            12,
            "gate_out_proj",
        )
        sums = total(sums, ("core", "zl"))
        gate_scale = lax.rsqrt(sums[0] / INNER + epsilon)
        stored.append(
            dict(
                hidden=hidden_own, normed=normed, zval=zval, cin=cin, cpre=cpre, dtp=dtp, cum=cum,
                dtv=dtv, xdt=xdt, bc=bc, sloc=sloc, pref=pref, entry=entry, y=y, gate_in=gate_in,
                proj=proj, gate_scale=gate_scale, dots=sums[1], halo=halo, wall=wall, wz=wz, wout=wout,
                taps=taps, dtb=dtb, avec=avec, dskip=dskip, ggain=ggain,
            )
        )
        if layer < LAYERS - 1:
            proj_sum = scatter_sum(proj)
            stored[layer]["proj_sum"] = proj_sum
            hidden_own = hidden_own + own_rows(gate_scale)[:, None] * proj_sum
            next_wall, next_wz, next_wout = gather_weights(
                behind(second_all, proj),
                [w_x[1], w_z[1], w_out[1]],
                (w_bc[1], dt_all[1]),
                third=(hidden_own,),
            )
            hidden = gather_pieces(hidden_own)

    grad_h = [cotangent]
    grad_own = own_rows(cotangent)
    matrices = [None] * LAYERS
    vectors = [None] * LAYERS
    shared = [None] * LAYERS
    for layer in reversed(range(LAYERS)):
        kept = stored[layer]
        gate_scale = kept["gate_scale"]
        if layer == LAYERS - 1:
            grad_scale = kept["dots"]
        else:
            grad_scale = gather_rows(jnp.sum(grad_own * kept["proj_sum"], axis=1))
        gsq = -grad_scale * gate_scale**3 / INNER
        rev = functools.partial(by_rows, count=count, reverse=True)
        rev_group = functools.partial(by_group, count=count, reverse=True)
        gproj, dy, dz, gloc, suf, gsend, acc = call(
            gate_kernel,
            count,
            [
                (smem, place),
                (rev(1), gate_scale[:, None]),
                (rev(1), gsq[:, None]),
                (rev(inner), kept["y"]),
                (rev(inner), kept["zval"]),
                (whole((ROWS, inner)), kept["ggain"]),
                (whole((width, inner)), kept["wout"]),
                (rev(LANES), kept["cum"]),
                (rev(BC), kept["bc"]),
                (rev(ROWS), mask),
                (whole((LANES, inner)), expand),
            ]
            + by_piece(grad_h, count, True),
            [
                (rev(width), shape(tok, width, dtype=bf16)),
                (rev(inner), shape(tok, inner, dtype=bf16)),
                (rev(inner), shape(tok, inner, dtype=bf16)),
                (rev_group((STATE, inner)), shape(count, STATE, inner)),
                (rev_group((ROWS, inner)), shape(count, ROWS, inner)),
                (whole((STATE + ROWS, inner)), shape(STATE + ROWS, inner)),
                (whole((ROWS, inner)), shape(ROWS, inner)),
            ],
            [pltpu.VMEM((STATE, inner), f32), pltpu.VMEM((ROWS, inner), f32)],
            10,
            "gate_back",
        )
        if layer == LAYERS - 1:
            last_sum = scatter_sum(kept["proj"], (gate_scale,))
            hidden_own = hidden_own + own_rows(gate_scale)[:, None] * last_sum
            dz, gproj = behind((dz, gproj), hidden_own)
        u, dbc = call(
            intra_back_kernel,
            count,
            [
                (by_rows(LANES, count), kept["cum"]),
                (by_rows(inner, count), kept["xdt"]),
                (by_rows(BC, count), kept["bc"]),
                (by_rows(1, count), seg_col),
                (by_cols(count), seg_row),
                (by_rows(inner, count), dy),
            ],
            [
                (by_rows(inner, count), shape(tok, inner)),
                (by_rows(BC, count), shape(tok, BC)),
            ],
            [],
            8,
            "ssd_within_back",
        )
        stages = []
        gout = chain(gsend, True, stages)
        round_one = stages[0]
        if layer == LAYERS - 1:
            out_parts = cross_over(hidden_own)
            u = behind(u, hidden_own)
        else:
            out_swaps = near_swaps(*behind((hidden_own, *out_parts), round_one))
            first_sums = join_halves(behind(matrices[1][:, : 3 * inner], round_one))
        grad_wout = mm(gproj, kept["gate_in"], ((0,), (0,)))
        grad_wz = mm(kept["normed"], dz, ((0,), (0,)))
        partial_z = mm(dz, kept["wz"], ((1,), (1,)))
        u = behind(u, grad_wout, grad_wz, partial_z)
        gall, last8, rim, gtaps, vecs, dsk = call(
            in_back_kernel,
            count,
            [
                (rev(inner), u),
                (rev(BC), dbc),
                (rev(inner), dy),
                (rev(inner), kept["y"]),
                (rev(conv_cols), kept["cpre"]),
                (rev(conv_cols), kept["cin"]),
                (rev(LANES), kept["dtp"]),
                (rev(LANES), kept["dtv"]),
                (rev(LANES), kept["cum"]),
                (rev(inner), kept["xdt"]),
                (rev(BC), kept["bc"]),
                (rev(ROWS), mask),
                (rev_group((STATE, inner)), kept["sloc"]),
                (rev_group((ROWS, inner)), kept["pref"]),
                (whole((STATE, inner)), kept["entry"]),
                (rev_group((STATE, inner)), gloc),
                (rev_group((ROWS, inner)), suf),
                (whole((STATE, inner)), gout),
                (whole((ROWS, conv_cols)), kept["halo"]),
                (whole((CONV, conv_cols)), kept["taps"]),
                (whole((ROWS, LANES)), kept["dtb"]),
                (whole((ROWS, LANES)), kept["avec"]),
                (whole((ROWS, inner)), kept["dskip"]),
                (whole((LANES, inner)), expand),
                (whole((GROUP, GROUP)), triback),
            ],
            [
                (rev(all_cols), shape(tok, all_cols, dtype=bf16)),
                (whole((ROWS, conv_cols)), shape(ROWS, conv_cols)),
                (whole((ROWS, conv_cols)), shape(ROWS, conv_cols)),
                (whole((ROWS, conv_cols)), shape(ROWS, conv_cols)),
                (whole((ROWS, LANES)), shape(ROWS, LANES)),
                (whole((ROWS, inner)), shape(ROWS, inner)),
            ],
            [pltpu.VMEM((CONV - 1, ROWS, conv_cols), f32)],
            20,
            "in_proj_conv_back",
        )
        rim_back = shifted(rim, -1)
        if layer == 0:
            last8 = behind(last8, first_sums, *(out_swaps or ()))
        else:
            last8 = behind(last8, *out_parts)
        gall = lax.dynamic_update_slice(
            gall, (last8 + rim_back).astype(bf16), (tok - ROWS, 0)
        )
        partial = partial_z + mm(gall, kept["wall"], ((1,), (1,)))
        grad_normed = scatter_sum(partial)
        late = behind(gall, partial)
        grad_wbc = mm(kept["normed"], late[:, inner : inner + BC], ((0,), (0,)))
        grad_win = mm(kept["normed"], behind(late, grad_wbc)[:, :inner], ((0,), (0,)))
        partial = behind(partial, grad_normed)
        late = behind(gall, grad_normed)
        grad_wdt = mm(kept["normed"], late[:, inner + BC :], ((0,), (0,)))
        hidden_in = kept["hidden"]
        inv = lax.rsqrt(jnp.mean(hidden_in * hidden_in, axis=1, keepdims=True) + epsilon)
        if layer == 0:
            full = hidden_block
            grad_ngain = jnp.sum(
                partial
                * (full * lax.rsqrt(jnp.mean(full * full, axis=1, keepdims=True) + epsilon)),
                axis=0,
            )
        else:
            grad_ngain = jnp.sum(grad_normed * hidden_in * inv, axis=0)
        back = grad_normed * norm_gain[layer][None, :]
        grad_own = grad_own + inv * (
            back - hidden_in * inv * inv * jnp.mean(back * hidden_in, axis=1, keepdims=True)
        )
        if layer > 0:
            grad_h = gather_pieces(grad_own)
        matrices[layer] = lax.psum_scatter(
            jnp.concatenate([grad_wout, grad_wz, grad_win, grad_wbc], axis=1),
            "chip",
            scatter_dimension=0,
            tiled=True,
        )
        vectors[layer] = jnp.concatenate(
            [
                gtaps[: CONV + 1, :inner].reshape(-1),
                acc[0],
                vecs[0, :heads],
                vecs[1, :heads],
                dsk[0],
                grad_wdt[:, :heads].reshape(-1),
                gtaps[: CONV + 1, inner:].reshape(-1),
                grad_ngain,
            ]
        )
    vector = total(jnp.stack(vectors), ("chip",))
    grad_parts = cross_over(grad_own)
    own_s = near_swap(grad_own)
    grad_parts, own_s, vector, _ = behind((grad_parts, own_s, vector, grad_win))
    mark = grad_parts[0]
    grad_swaps = near_swaps(grad_own, *grad_parts, own_s)
    input_grad = deliver(grad_own, *grad_parts, f32, grad_swaps)
    final_out = deliver(hidden_own, *out_parts, bf16, out_swaps, (mark,))
    g_last = behind(matrices[0], *(grad_swaps or (mark,)))
    last_sums = join_halves(g_last[:, : 3 * inner])
    grad_wbc = jnp.stack([g_last[:, 3 * inner :], matrices[1][:, 3 * inner :]], axis=1)
    grad_wbc = total(half_rows(grad_wbc), ("zh",))
    g_cols = [place_rows(last_sums), place_rows(behind(first_sums, mark))]
    vector = total(vector, ("zh",))
    other = swap(vector, "core")
    common = (CONV + 1) * BC + width
    shared = total((vector + other)[:, -common:], ("zl",))
    by_head = jnp.where(held, vector, other)[:, :-common]
    g_bc = shared[:, :-width].reshape(LAYERS, CONV + 1, BC)
    g_ngain = shared[:, -width:]
    at = 0
    pieces = []
    for size in (CONV * inner, inner, inner, heads, heads, inner, width * heads):
        pieces.append(by_head[:, at : at + size])
        at += size
    g_conv, g_bias, g_ggain, g_alog, g_dtb, g_dsk, g_wdt = pieces
    g_wdt = g_wdt.reshape(LAYERS, width, heads)
    rows = width // lax.axis_size(("chip", "core"))
    g_wdt = lax.dynamic_slice_in_dim(g_wdt, lax.axis_index(("chip", "core")) * rows, rows, axis=1)
    return (
        final_out,
        input_grad,
        g_ngain,
        jnp.stack([g[:, inner : 2 * inner] for g in g_cols]),
        jnp.stack([g[:, 2 * inner :] for g in g_cols]),
        jnp.stack([grad_wbc[:, layer] for layer in range(LAYERS)]),
        g_wdt,
        g_conv.reshape(LAYERS, CONV, inner),
        g_bc[:, :CONV],
        g_bias,
        g_bc[:, CONV],
        g_dtb,
        g_alog,
        jnp.sum(g_dsk.reshape(LAYERS, heads, HEADDIM), axis=2),
        g_ggain,
        jnp.stack([g[:, :inner] for g in g_cols]),
    )


def join_halves(part):
    return part + lax.ppermute(part, BOTH, CROSS_BACK)


def place_rows(full):
    core, far = lax.axis_index("core"), lax.axis_index("zh")
    sent = lax.ppermute(take(full, 1 - core, 2), BOTH, CORE_OUT)
    return jnp.where(core == far, take(full, core, 2), sent)


def half_rows(part):
    core = lax.axis_index("core")
    part = take(part, core, 2) + swap(take(part, 1 - core, 2), "core")
    return total(part, ("zl",))


def solution(mesh):
    seq, head = mesh.devices.shape
    mesh = jax.sharding.Mesh(
        mesh.devices.reshape(seq // 2, 2, 2, head // 2), ("chip", "core", "zh", "zl")
    )
    tokens, columns = ("chip", "core"), ("zh", "zl")
    by_col = P(None, None, columns)
    by_head = P(None, columns)
    both = P(None, tokens, columns)
    placed = (
        P(tokens, None),
        P(tokens),
        P(tokens, None),
        P(),
        by_col,
        by_col,
        P(),
        by_col,
        by_col,
        P(),
        by_head,
        P(),
        by_head,
        by_head,
        by_head,
        by_head,
        by_col,
    )
    return jax.shard_map(
        shards,
        mesh=mesh,
        in_specs=placed,
        out_specs=(
            P(tokens, None),
            P(tokens, None),
            P(),
            both,
            both,
            P(None, tokens, None),
            both,
            by_col,
            P(),
            by_head,
            P(),
            by_head,
            by_head,
            by_head,
            by_head,
            both,
        ),
        check_vma=False,
    )
```

```python
import functools

import jax
import jax.numpy as jnp
from jax import lax
from jax.experimental import pallas as pl
from jax.experimental.pallas import tpu as pltpu
from jax.sharding import PartitionSpec as P

HEADDIM = 64
STATE = 128
CONV = 4
GROUP = 256
LAYERS = 2
INNER = 2048
LANES = 128
ROWS = 8
BC = 2 * STATE

epsilon = 1e-05
highest = lax.Precision.HIGHEST
f32 = jnp.float32
bf16 = jnp.bfloat16


def mm(left, right, dims=((1,), (0,)), precision=None):
    return lax.dot_general(
        left, right, (dims, ((), ())), preferred_element_type=f32, precision=precision
    )


def softplus(value):
    small = jnp.exp(-jnp.abs(value))
    series = small * (1.0 - small * (0.5 - small * (1.0 / 3.0 - small * (0.25 - small * 0.2))))
    return jnp.maximum(value, 0.0) + jnp.where(small < 0.03, series, jnp.log(1.0 + small))


def silu_slope(value, sigma):
    return sigma * (1.0 + value * (1.0 - sigma))


def spread(heads, expand):
    return mm(heads, expand, precision=highest)


def gather_heads(lanes, expand):
    return mm(lanes, expand, ((1,), (1,)), precision=highest)


def pick(place, pieces, held):
    if len(pieces) == 1:
        return pieces[0][...]
    away = lax.bitwise_xor(pl.program_id(0) if held is None else held, place[0])
    value = pieces[3][...]
    for number in range(3):
        value = jnp.where(away == number, pieces[number][...], value)
    return value


def in_kernel(
    place, wall, ngain, taps, bias, dtb, avec, mask, halo, expand, tri, *refs
):
    hid = refs[:-14]
    normed, cin, cpre, dtp, cum, dtv, xdt, bc, sloc, pref, send, state, thru, prev = refs[-14:]
    step = pl.program_id(0)
    inner = expand.shape[1]

    @pl.when(step == 0)
    def _():
        state[...] = jnp.zeros_like(state)
        thru[...] = jnp.ones_like(thru)
        prev[...] = halo[...]

    h = pick(place, hid, None)
    inv = lax.rsqrt(jnp.mean(h * h, axis=1, keepdims=True) + epsilon)
    low = (h * inv * ngain[...]).astype(bf16)
    normed[...] = low
    rows = mm(low, wall[:, : inner + BC])
    pre_dt = mm(low, wall[:, inner + BC :])
    dtp[...] = pre_dt
    cin[...] = rows
    ext = jnp.concatenate([prev[...], rows], axis=0)
    prev[...] = rows[GROUP - ROWS :]
    total = taps[CONV - 1 : CONV, :] * rows + bias[0:1, :]
    for k in range(CONV - 1):
        first = ROWS - CONV + 1 + k
        total = total + taps[k : k + 1, :] * ext[first : first + GROUP] * mask[:, k : k + 1]
    cpre[...] = total
    act = total * jax.nn.sigmoid(total)
    x = act[:, :inner]
    low_bc = act[:, inner:].astype(bf16)
    bc[...] = low_bc
    dt = softplus(pre_dt + dtb[0:1, :])
    dtv[...] = dt
    run = mm(tri[...], dt * avec[0:1, :], precision=highest)
    cum[...] = run
    last = run[GROUP - 1 : GROUP]
    xdt[...] = (x * spread(dt, expand[...])).astype(bf16)
    tail = jnp.exp(last - run) * mask[:, 4:5] * dt
    contrib = mm(low_bc[:, :STATE], (x * spread(tail, expand[...])).astype(bf16), ((0,), (0,)))
    through = jnp.broadcast_to(jnp.exp(last) * mask[GROUP - 1 : GROUP, 3:4], (ROWS, LANES))
    through = spread(through, expand[...])
    sloc[0] = state[...]
    pref[0] = thru[...]
    state[...] = through[0:1] * state[...] + contrib
    thru[...] = thru[...] * through

    @pl.when(step == pl.num_programs(0) - 1)
    def _():
        send[:STATE] = state[...]
        send[STATE:] = thru[...]


def pair_lanes(value, which):
    lane = lax.broadcasted_iota(jnp.int32, value.shape, 1)
    keep = lane < HEADDIM if which == 0 else lane >= HEADDIM
    return jnp.where(keep, value, jnp.zeros_like(value))


def intra_kernel(cum, xdt, bc, seg, segrow, y):
    inner = xdt.shape[1]
    run = cum[...]
    run_t = run.T
    base = mm(bc[:, STATE:], bc[:, :STATE], ((1,), (1,)))
    t_at = lax.broadcasted_iota(jnp.int32, (GROUP, GROUP), 0)
    s_at = lax.broadcasted_iota(jnp.int32, (GROUP, GROUP), 1)
    same = (seg[:, 0:1] == segrow[0:1, :]) & (t_at >= s_at)
    closed = jnp.where(same, 0.0, -1e30)
    for pair in range(inner // LANES):
        cols = slice(pair * LANES, (pair + 1) * LANES)
        xs = xdt[:, cols]
        parts = []
        for which in range(2):
            head = 2 * pair + which
            decay = jnp.exp(run[:, head : head + 1] - run_t[head : head + 1, :] + closed)
            parts.append(mm((decay * base).astype(bf16), xs))
        lane = lax.broadcasted_iota(jnp.int32, (GROUP, LANES), 1)
        y[:, cols] = jnp.where(lane < HEADDIM, parts[0], parts[1])


def out_kernel(
    yin, cpre, cum, bc, mask, zval, sloc, pref, entry, dskip, ggain, wout, expand, *refs
):
    cot, (y, gate_in, proj, sums) = refs[:-4], refs[-4:]
    inner = expand.shape[1]
    pre = cpre[...]
    x = pre * jax.nn.sigmoid(pre)
    full = sloc[0] + pref[0][0:1] * entry[...]
    reach = spread(jnp.exp(cum[...]) * mask[:, 3:4], expand[...])
    value = yin[...] + reach * mm(bc[:, STATE:], full.astype(bf16)) + dskip[0:1, :] * x
    y[...] = value
    z = zval[...]
    gated = value * (z * jax.nn.sigmoid(z))
    low = (gated * ggain[0:1, :]).astype(bf16)
    gate_in[...] = low
    proj[...] = mm(low, wout[...], ((1,), (1,)))
    ones = jnp.ones((ROWS, inner), f32)
    squares = mm(ones, gated * gated, ((1,), (1,)), precision=highest)
    if cot:
        back = mm(cot[0][...].astype(bf16), wout[...])
        dots = mm(ones, low.astype(f32) * back, ((1,), (1,)), precision=highest)
        row = lax.broadcasted_iota(jnp.int32, squares.shape, 0)
        squares = jnp.where(row == 0, squares, dots)
    sums[...] = squares


def gate_kernel(
    place, scale, gsq, y, zval, ggain, wout, cum, bc, mask, expand, *refs
):
    gh = refs[:-9]
    gproj, dy, dz, gloc, suf, send, acc, carry, thru = refs[-9:]
    step = pl.program_id(0)

    @pl.when(step == 0)
    def _():
        carry[...] = jnp.zeros_like(carry)
        thru[...] = jnp.ones_like(thru)
        acc[...] = jnp.zeros_like(acc)

    gp = (scale[...] * pick(place, gh, pl.num_programs(0) - 1 - step)).astype(bf16)
    gproj[...] = gp
    ggi = mm(gp, wout[...])
    z = zval[...]
    sigma = jax.nn.sigmoid(z)
    silu = z * sigma
    value = y[...]
    gated = value * silu
    ggated = ggi * ggain[0:1, :] + gated * gsq[...]
    acc[0:1, :] += jnp.sum(ggi * gated, axis=0, keepdims=True)
    low = (ggated * silu).astype(bf16)
    dy[...] = low
    dz[...] = (ggated * value * silu_slope(z, sigma)).astype(bf16)
    run = cum[...]
    last = run[GROUP - 1 : GROUP]
    reach = spread(jnp.exp(run) * mask[:, 3:4], expand[...])
    back = mm(bc[:, STATE:], (reach * low.astype(f32)).astype(bf16), ((0,), (0,)))
    through = jnp.broadcast_to(jnp.exp(last) * mask[GROUP - 1 : GROUP, 3:4], (ROWS, LANES))
    through = spread(through, expand[...])
    gloc[0] = carry[...]
    suf[0] = thru[...]
    carry[...] = back + through[0:1] * carry[...]
    thru[...] = thru[...] * through

    @pl.when(step == pl.num_programs(0) - 1)
    def _():
        send[:STATE] = carry[...]
        send[STATE:] = thru[...]


def intra_back_kernel(cum, xdt, bc, seg, segrow, dy, dz, wz, u, dbc, part):
    inner = xdt.shape[1]
    run = cum[...]
    run_t = run.T
    base = mm(bc[:, :STATE], bc[:, STATE:], ((1,), (1,)))
    s_at = lax.broadcasted_iota(jnp.int32, (GROUP, GROUP), 0)
    t_at = lax.broadcasted_iota(jnp.int32, (GROUP, GROUP), 1)
    same = (seg[:, 0:1] == segrow[0:1, :]) & (t_at >= s_at)
    closed = jnp.where(same, 0.0, -1e30)
    grad_base = jnp.zeros((GROUP, GROUP), f32)
    for pair in range(inner // LANES):
        cols = slice(pair * LANES, (pair + 1) * LANES)
        xs = xdt[:, cols]
        ds = dy[:, cols]
        parts = []
        for which in range(2):
            head = 2 * pair + which
            decay = jnp.exp(run_t[head : head + 1, :] - run[:, head : head + 1] + closed)
            parts.append(mm((decay * base).astype(bf16), ds))
            grad_base = grad_base + decay * mm(xs, pair_lanes(ds, which), ((1,), (1,)))
        lane = lax.broadcasted_iota(jnp.int32, (GROUP, LANES), 1)
        u[:, cols] = jnp.where(lane < HEADDIM, parts[0], parts[1])
    part[...] = mm(dz[...], wz[...], ((1,), (1,)))
    low = grad_base.astype(bf16)
    dbc[:, :STATE] = mm(low, bc[:, STATE:])
    dbc[:, STATE:] = mm(low, bc[:, :STATE], ((0,), (0,)))


def in_back_kernel(
    uin, dbc, dy, y, cpre, cin, dtp, dtv, cum, xdt, bc, mask, sloc, pref, entry, gloc, suf,
    gout, halo, taps, dtb, avec, dskip, expand, triback,
    gall, last8, rim, gtaps, vecs, dsk,
    nexts,
):
    step = pl.program_id(0)
    inner = expand.shape[1]

    @pl.when(step == 0)
    def _():
        nexts[...] = jnp.zeros_like(nexts)
        gtaps[...] = jnp.zeros_like(gtaps)
        vecs[...] = jnp.zeros_like(vecs)
        dsk[...] = jnp.zeros_like(dsk)

    e = expand[...]
    pre = cpre[...]
    sigma = jax.nn.sigmoid(pre)
    x = (pre * sigma)[:, :inner]
    full = sloc[0] + pref[0][0:1] * entry[...]
    nxt = gloc[0] + suf[0][0:1] * gout[...]
    nxt_low = nxt.astype(bf16)
    run = cum[...]
    last = run[GROUP - 1 : GROUP]
    dt = dtv[...]
    low_dy = dy[...].astype(f32)
    xw = xdt[...].astype(f32)
    tail = spread(jnp.exp(last - run) * mask[:, 4:5], e)
    reach = spread(jnp.exp(run) * mask[:, 3:4], e)
    u_inter = tail * mm(bc[:, :STATE], nxt_low)
    u = uin[...] + u_inter
    dx = spread(dt, e) * u + dskip[0:1, :] * low_dy
    dsk[0:1, :] += jnp.sum(low_dy * x, axis=0, keepdims=True)
    db = dbc[:, :STATE] + mm((tail * xw).astype(bf16), nxt_low, ((1,), (1,)))
    dc = dbc[:, STATE:] + mm((reach * low_dy).astype(bf16), full.astype(bf16), ((1,), (1,)))
    grad_dt = gather_heads(x * u, e)
    y_plain = y[...] - dskip[0:1, :] * x
    grad_cum = gather_heads(low_dy * y_plain - xw * u, e)
    flow = jnp.sum(nxt * full, axis=0, keepdims=True)
    flow = gather_heads(jnp.broadcast_to(flow, (ROWS, inner)), e)[0:1]
    ends = jnp.sum(xw * u_inter, axis=0, keepdims=True)
    ends = gather_heads(jnp.broadcast_to(ends, (ROWS, inner)), e)[0:1]
    grad_tot = mask[GROUP - 1 : GROUP, 3:4] * jnp.exp(last) * flow + ends
    grad_da = mm(triback[...], grad_cum, precision=highest) + grad_tot
    a = avec[0:1, :]
    grad_dtv = grad_dt + grad_da * a
    grad_dtpre = grad_dtv * jax.nn.sigmoid(dtp[...] + dtb[0:1, :])
    vecs[0:1, :] += jnp.sum(grad_da * dt, axis=0, keepdims=True) * a
    vecs[1:2, :] += jnp.sum(grad_dtpre, axis=0, keepdims=True)
    slope = silu_slope(pre, sigma)
    grad_pre = jnp.concatenate([dx, db, dc], axis=1) * slope
    gtaps[4:5, :] += jnp.sum(grad_pre, axis=0, keepdims=True)
    rows = cin[...]
    grad_rows = taps[CONV - 1 : CONV, :] * grad_pre
    gtaps[3:4, :] += jnp.sum(rows * grad_pre, axis=0, keepdims=True)
    masked = []
    for k in range(CONV - 1):
        m = grad_pre * mask[:, k : k + 1]
        masked.append(m[:ROWS])
        ahead = CONV - 1 - k
        shifted = jnp.concatenate([m, nexts[k]], axis=0)[ahead : ahead + GROUP]
        grad_rows = grad_rows + taps[k : k + 1, :] * shifted
        gtaps[k : k + 1, :] += jnp.sum(rows * shifted, axis=0, keepdims=True)
    for k in range(CONV - 1):
        nexts[k] = masked[k]
    gall[:, : inner + BC] = grad_rows.astype(bf16)
    gall[:, inner + BC :] = grad_dtpre.astype(bf16)

    @pl.when(step == 0)
    def _():
        last8[...] = grad_rows[GROUP - ROWS :]

    @pl.when(step == pl.num_programs(0) - 1)
    def _():
        spill = jnp.zeros((ROWS, inner + BC), f32)
        edge = halo[...]
        for k in range(CONV - 1):
            down = ROWS - CONV + 1 + k
            moved = jnp.concatenate([jnp.zeros((ROWS, inner + BC), f32), masked[k]], axis=0)
            moved = moved[ROWS - down : 2 * ROWS - down]
            spill = spill + taps[k : k + 1, :] * moved
            gtaps[k : k + 1, :] += jnp.sum(edge * moved, axis=0, keepdims=True)
        rim[...] = spill


def whole(shape):
    return pl.BlockSpec(shape, lambda c: (0,) * len(shape))


def by_rows(cols, count, reverse=False):
    if reverse:
        return pl.BlockSpec((GROUP, cols), lambda c: (count - 1 - c, 0))
    return pl.BlockSpec((GROUP, cols), lambda c: (c, 0))


def by_group(shape, count, reverse=False):
    if reverse:
        return pl.BlockSpec((1,) + shape, lambda c: (count - 1 - c, 0, 0))
    return pl.BlockSpec((1,) + shape, lambda c: (c, 0, 0))


def by_piece(pieces, count, reverse=False):
    if len(pieces) == 1:
        return [(by_rows(pieces[0].shape[1], count, reverse), pieces[0])]
    return [(whole(piece.shape), piece) for piece in pieces]


def by_cols(count):
    return pl.BlockSpec((ROWS, GROUP), lambda c: (0, c))


def call(kernel, count, ins, outs, scratch, micros, name):
    return pl.pallas_call(
        kernel,
        grid=(count,),
        in_specs=[spec for spec, _ in ins],
        out_specs=[spec for spec, _ in outs],
        out_shape=[shape for _, shape in outs],
        scratch_shapes=scratch,
        compiler_params=pltpu.CompilerParams(
            dimension_semantics=("arbitrary",), vmem_limit_bytes=56 * 1024 * 1024
        ),
        cost_estimate=pl.CostEstimate(
            flops=micros * 1_150_000_000, bytes_accessed=1024 * 1024, transcendentals=0
        ),
        name=name,
    )(*[value for _, value in ins])


def shape(*dims, dtype=f32):
    return jax.ShapeDtypeStruct(dims, dtype)


SWAP = ((0, 1), (1, 0))
CROSS = ((0, 1), (3, 2))
CROSS_BACK = ((1, 0), (2, 3))
CORE_OUT = ((0, 2), (3, 1))
CORE_IN = ((2, 0), (1, 3))
DIAGONAL = ((2, 1), (1, 2))
BOTH = ("core", "zh")
BLOCKS = ("chip", "zh")


def shifted(value, steps):
    count = lax.axis_size(BLOCKS)
    leading, last = (max(0, -steps), min(count, count - steps))
    return lax.ppermute(value, BLOCKS, [(source, source + steps) for source in range(leading, last)])


def chain(part, reverse, stages):
    count = lax.axis_size(BLOCKS)
    place = lax.axis_index(BLOCKS)
    state, decay = part[:STATE], part[STATE : STATE + 1]
    entry, reach = jnp.zeros_like(state), jnp.ones_like(decay)
    step = 1
    while step < count:
        got = lax.ppermute(part, BLOCKS, [(i, i ^ step) for i in range(count)])
        got_state, got_decay = got[:STATE], got[STATE : STATE + 1]
        later = ((place & step) == 0) if reverse else ((place & step) != 0)
        stages.append(got)
        entry = jnp.where(later, entry + reach * got_state, entry)
        reach = jnp.where(later, reach * got_decay, reach)
        state = jnp.where(later, state + decay * got_state, got_state + got_decay * state)
        decay = decay * got_decay
        part = jnp.concatenate([state, jnp.broadcast_to(decay, (ROWS, decay.shape[1]))])
        step *= 2
    return entry


def swap(value, axis):
    return lax.ppermute(value, axis, SWAP)


def total(value, axes):
    for axis in axes:
        count = lax.axis_size(axis)
        step = 1
        while step < count:
            value = value + lax.ppermute(value, axis, [(i, i ^ step) for i in range(count)])
            step *= 2
    return value


def take(value, index, count):
    size = value.shape[0] // count
    return lax.dynamic_slice_in_dim(value, index * size, size)


def ordered(place, mine, theirs):
    return jnp.where(
        place == 0, jnp.concatenate([mine, theirs]), jnp.concatenate([theirs, mine])
    )


def behind(value, *marks):
    return lax.optimization_barrier((value, *marks))[0]


def scatter_sum(part, mark=()):
    core, near = lax.axis_index("core"), lax.axis_index("zl")
    half = take(part, core, 2) + behind(swap(take(part, 1 - core, 2), "core"), *mark)
    if lax.axis_size("zl") == 2:
        return take(half, near, 2) + swap(take(half, 1 - near, 2), "zl")
    return lax.psum_scatter(half, "zl", scatter_dimension=0, tiled=True)


def own_rows(value):
    core, near = lax.axis_index("core"), lax.axis_index("zl")
    return take(take(value, core, 2), near, lax.axis_size("zl"))


def gather_near(value):
    if lax.axis_size("zl") == 2:
        return ordered(lax.axis_index("zl"), value, swap(value, "zl"))
    return lax.all_gather(value, "zl", tiled=True)


def gather_rows(value):
    half = gather_near(value)
    return ordered(lax.axis_index("core"), half, swap(half, "core"))


def own_place():
    return 2 * lax.axis_index("core") + lax.axis_index("zl")


def gather_pieces(value):
    if lax.axis_size("zl") != 2 or value.shape[0] != GROUP:
        return [gather_rows(value)]
    near = swap(value, "zl")
    return [value, near, swap(value, "core"), swap(near, "core")]


def place_kernel(place, value, mine, near, theirs, value_s, mine_s, near_s, theirs_s, out):
    away = lax.bitwise_xor(pl.program_id(0), place[0])
    pairs = ((value, mine), (value_s, mine_s), (near, theirs), (near_s, theirs_s))
    for number, (here, there) in enumerate(pairs):

        @pl.when((away == number) & (place[1] == 1))
        def _():
            out[...] = here[...].astype(out.dtype)

        @pl.when((away == number) & (place[1] == 0))
        def _():
            out[...] = there[...].astype(out.dtype)


def cross_over(value):
    return [lax.ppermute(value, BOTH, pairs) for pairs in (CROSS, DIAGONAL, CORE_IN)]


def near_swap(value):
    if lax.axis_size("zl") != 2 or value.shape[0] != GROUP:
        return None
    here = [(2 * kind + i, 2 * kind + 1 - i) for kind in (0, 3) for i in range(2)]
    return lax.ppermute(value, ("core", "zh", "zl"), here)


def near_swaps(value, mine, theirs, near, value_s=None, near_s=None):
    if lax.axis_size("zl") != 2 or value.shape[0] != GROUP:
        return None
    axes = ("core", "zh", "zl")
    there = [(2 * kind + i, 2 * kind + 1 - i) for kind in (1, 2) for i in range(2)]
    return (
        near_swap(value) if value_s is None else value_s,
        lax.ppermute(mine, axes, there),
        lax.ppermute(theirs, axes, there),
        near_swap(near) if near_s is None else near_s,
    )


def deliver(value, mine, theirs, near, dtype, swaps=None, mark=()):
    core, far = lax.axis_index("core"), lax.axis_index("zh")
    held = core == far
    if lax.axis_size("zl") != 2 or value.shape[0] != GROUP:
        mine = gather_near(jnp.where(held, value, mine))
        theirs = gather_near(jnp.where(held, near, theirs))
        full = ordered(core, mine, theirs)
        return narrowed(full) if dtype == bf16 else full
    if swaps is None:
        swaps = near_swaps(value, mine, theirs, near)
    value_s, mine_s, theirs_s, near_s = swaps
    place = jnp.stack([own_place(), held.astype(jnp.int32)]).astype(jnp.int32)
    width = value.shape[1]
    parts = behind((value, mine, near, theirs, value_s, mine_s, near_s, theirs_s), *mark)
    return pl.pallas_call(
        place_kernel,
        grid=(4,),
        in_specs=[pl.BlockSpec(memory_space=pltpu.SMEM)] + [whole((GROUP, width))] * 8,
        out_specs=by_rows(width, 4),
        out_shape=shape(4 * GROUP, width, dtype=dtype),
        compiler_params=pltpu.CompilerParams(
            dimension_semantics=("arbitrary",), vmem_limit_bytes=40 * 1024 * 1024
        ),
        name="place",
    )(place, *parts)


def to_block(value):
    got = lax.ppermute(value, BOTH, CORE_OUT)
    return jnp.where(lax.axis_index("core") == lax.axis_index("zh"), value, got)


def eight(row):
    return jnp.broadcast_to(row[None, :], (ROWS, row.shape[0]))


def pad_lanes(value):
    return jnp.pad(value, [(0, 0)] * (value.ndim - 1) + [(0, LANES - value.shape[-1])])


def weight_kernel(count, extra, place, *refs):
    own, rest = refs[:count], refs[count:]
    outs, rest = rest[-count:], rest[:-count]
    parts, more = (rest[:-2], rest[-2:]) if extra else (rest, ())
    block = pl.program_id(0)
    at = 0
    for source, out in zip(own, outs):
        cols = source.shape[1]

        @pl.when(place[1] == 1)
        def _():
            out[:, :cols] = source[...]

        for away, part in enumerate(parts):

            @pl.when((place[1] == 0) & (lax.bitwise_xor(place[0], block) == away))
            def _():
                out[:, :cols] = part[:, at : at + cols].astype(bf16)

        at += cols
    if more:
        cols = own[0].shape[1]
        outs[0][:, cols : cols + BC] = more[0][...]
        outs[0][:, cols + BC :] = more[1][...].astype(bf16)


def narrow_kernel(wide, narrow):
    narrow[...] = wide[...].astype(bf16)


def narrowed(value):
    rows, cols = value.shape
    return pl.pallas_call(
        narrow_kernel,
        grid=(rows // GROUP,),
        in_specs=[by_rows(cols, 0)],
        out_specs=by_rows(cols, 0),
        out_shape=shape(rows, cols, dtype=bf16),
        name="narrowed",
    )(value)


def weights_over(own, *marks):
    chips = lax.axis_size("chip")
    piece = jnp.concatenate(
        [take(value, lax.axis_index("chip"), chips).astype(f32) for value in behind(own, *marks)],
        axis=1,
    )
    return lax.ppermute(piece, BOTH, CROSS)


def gather_weights(piece, own, more=(), third=()):
    width = own[0].shape[0]
    chips = lax.axis_size("chip")
    chip = lax.axis_index("chip")
    held = (lax.axis_index("core") == lax.axis_index("zh")).astype(jnp.int32)
    size = width // chips
    if chips == 4:
        parts = [piece]
        for away in range(1, chips):
            pairs = [
                (4 * c + kind, 4 * (c ^ away) + kind) for c in range(chips) for kind in (1, 2)
            ]
            parts.append(lax.ppermute(piece, ("chip", "core", "zh"), pairs))
        place = jnp.stack([chip, held]).astype(jnp.int32)
        blocks = chips
    else:
        parts = [lax.all_gather(piece, "chip", tiled=True)]
        place = jnp.stack([0, held]).astype(jnp.int32)
        blocks, size = 1, width
    parts = behind(parts, *third)
    out_cols = [value.shape[1] for value in own]
    out_cols[0] += sum(value.shape[1] for value in more)

    def rows(cols):
        return pl.BlockSpec((size, cols), lambda c: (c, 0))

    return pl.pallas_call(
        functools.partial(weight_kernel, len(own), bool(more)),
        grid=(blocks,),
        in_specs=[pl.BlockSpec(memory_space=pltpu.SMEM)]
        + [rows(value.shape[1]) for value in own]
        + [whole(piece.shape if chips == 4 else parts[0].shape)] * len(parts)
        + [rows(value.shape[1]) for value in more],
        out_specs=[rows(cols) for cols in out_cols],
        out_shape=[shape(width, cols, dtype=bf16) for cols in out_cols],
        compiler_params=pltpu.CompilerParams(
            dimension_semantics=("arbitrary",), vmem_limit_bytes=40 * 1024 * 1024
        ),
        name="weights",
    )(place, *own, *parts, *more)


def shards(
    x_input,
    seg_ids,
    cotangent,
    norm_gain,
    w_z,
    w_x,
    w_bc,
    w_dt,
    conv_x,
    conv_bc,
    bias_x,
    bias_bc,
    dt_bias,
    a_log,
    d_skip,
    gate_gain,
    w_out,
):
    tok, width = x_input.shape
    inner = w_z.shape[2]
    core, far = lax.axis_index("core"), lax.axis_index("zh")
    held = core == far
    heads = w_dt.shape[2]
    count = tok // GROUP
    conv_cols = inner + BC
    all_cols = inner + BC + LANES

    dt_own = w_dt.astype(f32).reshape(LAYERS, width * heads // LANES, LANES)
    dt_sent = lax.ppermute(dt_own, BOTH, CROSS)
    dt_all = pad_lanes(jnp.where(held, dt_own, dt_sent).reshape(LAYERS, width, heads))
    first_x = weights_over([w_x[0]])
    hidden = to_block(x_input.astype(f32))
    first_rest = weights_over([w_z[0], w_out[0]], first_x)
    (wall,) = gather_weights(first_x, [w_x[0]], (w_bc[0], dt_all[0]), (first_rest,))
    seg = to_block(seg_ids.astype(f32))
    small = jnp.concatenate(
        [
            value.reshape(LAYERS, -1)
            for value in (conv_x, bias_x, dt_bias, a_log, d_skip, gate_gain)
        ],
        axis=1,
    )
    small = jnp.where(held, small, lax.ppermute(small, BOTH, CROSS))
    sizes = (CONV * inner, inner, heads, heads, heads, inner)
    pieces, at = [], 0
    for size in sizes:
        pieces.append(small[:, at : at + size])
        at += size
    conv_x, bias_x, dt_bias, a_log, d_skip, gate_gain = pieces
    conv_x = conv_x.reshape(LAYERS, CONV, inner)
    hidden_own = own_rows(hidden)
    hidden_block = hidden
    hidden = [hidden]
    place = jnp.stack([own_place(), own_place()]).astype(jnp.int32)
    smem = pl.BlockSpec(memory_space=pltpu.SMEM)
    edge_seg = shifted(seg[tok - ROWS :], 1)
    seg_ext = jnp.concatenate([edge_seg, seg])
    before = jnp.concatenate([edge_seg[ROWS - 1 :], seg[GROUP - 1 : tok - 1 : GROUP]])
    after = seg[GROUP - 1 :: GROUP]
    mask = jnp.stack(
        [
            (seg_ext[ROWS - CONV + 1 + k : ROWS - CONV + 1 + k + tok] == seg).astype(f32)
            for k in range(CONV - 1)
        ]
        + [
            (seg == jnp.repeat(before, GROUP)).astype(f32),
            (seg == jnp.repeat(after, GROUP)).astype(f32),
            seg,
            seg,
            seg,
        ],
        axis=1,
    )
    seg_col = seg[:, None]
    seg_row = eight(seg)
    expand = (jnp.arange(LANES)[:, None] == jnp.arange(inner)[None, :] // HEADDIM).astype(f32)
    position = jnp.arange(GROUP)
    tri = (position[:, None] >= position[None, :]).astype(f32)
    triback = (position[:, None] <= position[None, :]).astype(f32)

    stored = []
    for layer in range(LAYERS):
        if layer > 0:
            wall = next_wall
        taps = jnp.concatenate([conv_x[layer], conv_bc[layer]], axis=1)
        bias = eight(jnp.concatenate([bias_x[layer], bias_bc[layer]]))
        dtb = eight(pad_lanes(dt_bias[layer]))
        avec = eight(pad_lanes(-jnp.exp(a_log[layer])))
        dskip = eight(jnp.repeat(d_skip[layer], HEADDIM))
        ggain = eight(gate_gain[layer])
        ngain = norm_gain[layer][None, :]
        if len(hidden) == 1:
            end = hidden[0][tok - 16 :]
        else:
            ends = jnp.stack([piece[GROUP - 16 :] for piece in hidden])
            end = lax.dynamic_index_in_dim(ends, 3 ^ own_place(), 0, False)
        end = end * lax.rsqrt(jnp.mean(end * end, axis=1, keepdims=True) + epsilon) * ngain
        end = mm(end.astype(bf16), wall[:, : inner + BC])[ROWS:]
        halo = shifted(end, 1)
        normed, cin, cpre, dtp, cum, dtv, xdt, bc, sloc, pref, send = call(
            in_kernel,
            count,
            [
                (smem, place),
                (whole((width, all_cols)), wall),
                (whole((1, width)), ngain),
                (whole((CONV, conv_cols)), taps),
                (whole((ROWS, conv_cols)), bias),
                (whole((ROWS, LANES)), dtb),
                (whole((ROWS, LANES)), avec),
                (by_rows(ROWS, count), mask),
                (whole((ROWS, conv_cols)), halo),
                (whole((LANES, inner)), expand),
                (whole((GROUP, GROUP)), tri),
            ]
            + by_piece(hidden, count),
            [
                (by_rows(width, count), shape(tok, width, dtype=bf16)),
                (by_rows(conv_cols, count), shape(tok, conv_cols)),
                (by_rows(conv_cols, count), shape(tok, conv_cols)),
                (by_rows(LANES, count), shape(tok, LANES)),
                (by_rows(LANES, count), shape(tok, LANES)),
                (by_rows(LANES, count), shape(tok, LANES)),
                (by_rows(inner, count), shape(tok, inner, dtype=bf16)),
                (by_rows(BC, count), shape(tok, BC, dtype=bf16)),
                (by_group((STATE, inner), count), shape(count, STATE, inner)),
                (by_group((ROWS, inner), count), shape(count, ROWS, inner)),
                (whole((STATE + ROWS, inner)), shape(STATE + ROWS, inner)),
            ],
            [
                pltpu.VMEM((STATE, inner), f32),
                pltpu.VMEM((ROWS, inner), f32),
                pltpu.VMEM((ROWS, conv_cols), f32),
            ],
            16,
            "in_proj_conv",
        )
        if layer == 0:
            wz, wout = gather_weights(
                behind(first_rest, wall), [w_z[0], w_out[0]], third=(send,)
            )
            cotangent = behind(cotangent, send).astype(f32)
            cot_sent = lax.ppermute(cotangent, BOTH, CORE_OUT)
        else:
            wz, wout = next_wz, next_wout
        zval = mm(normed, wz)
        (yin,) = call(
            intra_kernel,
            count,
            [
                (by_rows(LANES, count), cum),
                (by_rows(inner, count), xdt),
                (by_rows(BC, count), bc),
                (by_rows(1, count), seg_col),
                (by_cols(count), seg_row),
            ],
            [(by_rows(inner, count), shape(tok, inner))],
            [],
            6,
            "ssd_within",
        )
        stages = []
        entry = chain(send, False, stages)
        if layer == 0:
            second_all = weights_over([w_x[1], w_z[1], w_out[1]], stages[0])
            entry = behind(entry, second_all, cot_sent)
            cotangent = jnp.where(held, cotangent, cot_sent)
        y, gate_in, proj, sums = call(
            out_kernel,
            count,
            [
                (by_rows(inner, count), yin),
                (by_rows(inner, count), cpre),
                (by_rows(LANES, count), cum),
                (by_rows(BC, count), bc),
                (by_rows(ROWS, count), mask),
                (by_rows(inner, count), zval),
                (by_group((STATE, inner), count), sloc),
                (by_group((ROWS, inner), count), pref),
                (whole((STATE, inner)), entry),
                (whole((ROWS, inner)), dskip),
                (whole((ROWS, inner)), ggain),
                (whole((width, inner)), wout),
                (whole((LANES, inner)), expand),
            ]
            + ([(by_rows(width, count), cotangent)] if layer == LAYERS - 1 else []),
            [
                (by_rows(inner, count), shape(tok, inner)),
                (by_rows(inner, count), shape(tok, inner, dtype=bf16)),
                (by_rows(width, count), shape(tok, width)),
                (by_cols(count), shape(ROWS, tok)),
            ],
            [],
            12,
            "gate_out_proj",
        )
        sums = total(sums, ("core", "zl"))
        gate_scale = lax.rsqrt(sums[0] / INNER + epsilon)
        stored.append(
            dict(
                hidden=hidden_own, normed=normed, zval=zval, cin=cin, cpre=cpre, dtp=dtp, cum=cum,
                dtv=dtv, xdt=xdt, bc=bc, sloc=sloc, pref=pref, entry=entry, y=y, gate_in=gate_in,
                proj=proj, gate_scale=gate_scale, dots=sums[1], halo=halo, wall=wall, wz=wz, wout=wout,
                taps=taps, dtb=dtb, avec=avec, dskip=dskip, ggain=ggain,
            )
        )
        if layer < LAYERS - 1:
            proj_sum = scatter_sum(proj)
            stored[layer]["proj_sum"] = proj_sum
            hidden_own = hidden_own + own_rows(gate_scale)[:, None] * proj_sum
            next_wall, next_wz, next_wout = gather_weights(
                behind(second_all, proj),
                [w_x[1], w_z[1], w_out[1]],
                (w_bc[1], dt_all[1]),
                third=(hidden_own,),
            )
            hidden = gather_pieces(hidden_own)

    grad_h = [cotangent]
    grad_own = own_rows(cotangent)
    matrices = [None] * LAYERS
    vectors = [None] * LAYERS
    shared = [None] * LAYERS
    for layer in reversed(range(LAYERS)):
        kept = stored[layer]
        gate_scale = kept["gate_scale"]
        if layer == LAYERS - 1:
            grad_scale = kept["dots"]
        else:
            grad_scale = gather_rows(jnp.sum(grad_own * kept["proj_sum"], axis=1))
        gsq = -grad_scale * gate_scale**3 / INNER
        rev = functools.partial(by_rows, count=count, reverse=True)
        rev_group = functools.partial(by_group, count=count, reverse=True)
        gproj, dy, dz, gloc, suf, gsend, acc = call(
            gate_kernel,
            count,
            [
                (smem, place),
                (rev(1), gate_scale[:, None]),
                (rev(1), gsq[:, None]),
                (rev(inner), kept["y"]),
                (rev(inner), kept["zval"]),
                (whole((ROWS, inner)), kept["ggain"]),
                (whole((width, inner)), kept["wout"]),
                (rev(LANES), kept["cum"]),
                (rev(BC), kept["bc"]),
                (rev(ROWS), mask),
                (whole((LANES, inner)), expand),
            ]
            + by_piece(grad_h, count, True),
            [
                (rev(width), shape(tok, width, dtype=bf16)),
                (rev(inner), shape(tok, inner, dtype=bf16)),
                (rev(inner), shape(tok, inner, dtype=bf16)),
                (rev_group((STATE, inner)), shape(count, STATE, inner)),
                (rev_group((ROWS, inner)), shape(count, ROWS, inner)),
                (whole((STATE + ROWS, inner)), shape(STATE + ROWS, inner)),
                (whole((ROWS, inner)), shape(ROWS, inner)),
            ],
            [pltpu.VMEM((STATE, inner), f32), pltpu.VMEM((ROWS, inner), f32)],
            10,
            "gate_back",
        )
        if layer == LAYERS - 1:
            last_sum = scatter_sum(kept["proj"], (gate_scale,))
            hidden_own = hidden_own + own_rows(gate_scale)[:, None] * last_sum
            dy = behind(dy, hidden_own)
            out_parts = cross_over(hidden_own)
            out_held = (near_swap(hidden_own), near_swap(out_parts[2]))
        u, dbc, partial_z = call(
            intra_back_kernel,
            count,
            [
                (by_rows(LANES, count), kept["cum"]),
                (by_rows(inner, count), kept["xdt"]),
                (by_rows(BC, count), kept["bc"]),
                (by_rows(1, count), seg_col),
                (by_cols(count), seg_row),
                (by_rows(inner, count), dy),
                (by_rows(inner, count), dz),
                (whole((width, inner)), kept["wz"]),
            ],
            [
                (by_rows(inner, count), shape(tok, inner)),
                (by_rows(BC, count), shape(tok, BC)),
                (by_rows(width, count), shape(tok, width)),
            ],
            [],
            8,
            "ssd_within_back",
        )
        stages = []
        gout = chain(gsend, True, stages)
        round_one = stages[0]
        if layer == 0:
            out_swaps = near_swaps(hidden_own, *behind(out_parts, round_one), *out_held)
        grad_wout = mm(gproj, kept["gate_in"], ((0,), (0,)))
        grad_wz = mm(kept["normed"], dz, ((0,), (0,)))
        u = behind(u, grad_wout, grad_wz)
        gall, last8, rim, gtaps, vecs, dsk = call(
            in_back_kernel,
            count,
            [
                (rev(inner), u),
                (rev(BC), dbc),
                (rev(inner), dy),
                (rev(inner), kept["y"]),
                (rev(conv_cols), kept["cpre"]),
                (rev(conv_cols), kept["cin"]),
                (rev(LANES), kept["dtp"]),
                (rev(LANES), kept["dtv"]),
                (rev(LANES), kept["cum"]),
                (rev(inner), kept["xdt"]),
                (rev(BC), kept["bc"]),
                (rev(ROWS), mask),
                (rev_group((STATE, inner)), kept["sloc"]),
                (rev_group((ROWS, inner)), kept["pref"]),
                (whole((STATE, inner)), kept["entry"]),
                (rev_group((STATE, inner)), gloc),
                (rev_group((ROWS, inner)), suf),
                (whole((STATE, inner)), gout),
                (whole((ROWS, conv_cols)), kept["halo"]),
                (whole((CONV, conv_cols)), kept["taps"]),
                (whole((ROWS, LANES)), kept["dtb"]),
                (whole((ROWS, LANES)), kept["avec"]),
                (whole((ROWS, inner)), kept["dskip"]),
                (whole((LANES, inner)), expand),
                (whole((GROUP, GROUP)), triback),
            ],
            [
                (rev(all_cols), shape(tok, all_cols, dtype=bf16)),
                (whole((ROWS, conv_cols)), shape(ROWS, conv_cols)),
                (whole((ROWS, conv_cols)), shape(ROWS, conv_cols)),
                (whole((ROWS, conv_cols)), shape(ROWS, conv_cols)),
                (whole((ROWS, LANES)), shape(ROWS, LANES)),
                (whole((ROWS, inner)), shape(ROWS, inner)),
            ],
            [pltpu.VMEM((CONV - 1, ROWS, conv_cols), f32)],
            20,
            "in_proj_conv_back",
        )
        rim_back = shifted(rim, -1)
        if layer == 0:
            last8 = behind(last8, matrices[1], *(out_swaps or ()))
        else:
            last8 = behind(last8, *out_parts, *(out_held if out_held[0] is not None else ()))
        gall = lax.dynamic_update_slice(
            gall, (last8 + rim_back).astype(bf16), (tok - ROWS, 0)
        )
        partial = partial_z + mm(gall, kept["wall"], ((1,), (1,)))
        grad_normed = scatter_sum(partial)
        late = behind(gall, partial)
        grad_wbc = mm(kept["normed"], late[:, inner : inner + BC], ((0,), (0,)))
        grad_win = mm(kept["normed"], behind(late, grad_wbc)[:, :inner], ((0,), (0,)))
        if layer == 0:
            grad_own = input_gradient(grad_own, grad_normed, kept["hidden"], norm_gain[layer])
            grad_parts = cross_over(grad_own)
            own_s = near_swap(grad_own)
            late, partial = behind((gall, partial), grad_parts[2])
            grad_parts, own_s, _ = behind((grad_parts, own_s, grad_win))
            mark = grad_parts[0]
            grad_swaps = near_swaps(grad_own, *grad_parts, own_s)
        grad_wdt = mm(kept["normed"], late[:, inner + BC :], ((0,), (0,)))
        hidden_in = kept["hidden"]
        inv = lax.rsqrt(jnp.mean(hidden_in * hidden_in, axis=1, keepdims=True) + epsilon)
        if layer == 0:
            full = hidden_block
            grad_ngain = jnp.sum(
                partial
                * (full * lax.rsqrt(jnp.mean(full * full, axis=1, keepdims=True) + epsilon)),
                axis=0,
            )
        else:
            grad_ngain = jnp.sum(grad_normed * hidden_in * inv, axis=0)
        if layer > 0:
            grad_own = input_gradient(grad_own, grad_normed, hidden_in, norm_gain[layer])
            grad_h = gather_pieces(grad_own)
        matrices[layer] = lax.psum_scatter(
            jnp.concatenate([grad_wout, grad_wz, grad_win, grad_wbc], axis=1),
            "chip",
            scatter_dimension=0,
            tiled=True,
        )
        vectors[layer] = jnp.concatenate(
            [
                gtaps[: CONV + 1, :inner].reshape(-1),
                acc[0],
                vecs[0, :heads],
                vecs[1, :heads],
                dsk[0],
                grad_wdt[:, :heads].reshape(-1),
                gtaps[: CONV + 1, inner:].reshape(-1),
                grad_ngain,
            ]
        )
    vector = total(behind(jnp.stack(vectors), mark), ("chip",))
    input_grad = deliver(grad_own, *grad_parts, f32, grad_swaps)
    final_out = deliver(hidden_own, *out_parts, bf16, out_swaps, (mark,))
    g_last = behind(matrices[0], *(grad_swaps or (mark,)))
    last_sums = join_halves(g_last[:, : 3 * inner])
    grad_wbc = jnp.stack([g_last[:, 3 * inner :], matrices[1][:, 3 * inner :]], axis=1)
    grad_wbc = total(half_rows(grad_wbc), ("zh",))
    first_sums = join_halves(behind(matrices[1][:, : 3 * inner], mark))
    g_cols = [place_rows(last_sums), place_rows(first_sums)]
    vector = total(behind(vector, first_sums, *(grad_swaps or (mark,))), ("zh",))
    other = swap(vector, "core")
    common = (CONV + 1) * BC + width
    shared = total((vector + other)[:, -common:], ("zl",))
    by_head = jnp.where(held, vector, other)[:, :-common]
    g_bc = shared[:, :-width].reshape(LAYERS, CONV + 1, BC)
    g_ngain = shared[:, -width:]
    at = 0
    pieces = []
    for size in (CONV * inner, inner, inner, heads, heads, inner, width * heads):
        pieces.append(by_head[:, at : at + size])
        at += size
    g_conv, g_bias, g_ggain, g_alog, g_dtb, g_dsk, g_wdt = pieces
    g_wdt = g_wdt.reshape(LAYERS, width, heads)
    rows = width // lax.axis_size(("chip", "core"))
    g_wdt = lax.dynamic_slice_in_dim(g_wdt, lax.axis_index(("chip", "core")) * rows, rows, axis=1)
    return (
        final_out,
        input_grad,
        g_ngain,
        jnp.stack([g[:, inner : 2 * inner] for g in g_cols]),
        jnp.stack([g[:, 2 * inner :] for g in g_cols]),
        jnp.stack([grad_wbc[:, layer] for layer in range(LAYERS)]),
        g_wdt,
        g_conv.reshape(LAYERS, CONV, inner),
        g_bc[:, :CONV],
        g_bias,
        g_bc[:, CONV],
        g_dtb,
        g_alog,
        jnp.sum(g_dsk.reshape(LAYERS, heads, HEADDIM), axis=2),
        g_ggain,
        jnp.stack([g[:, :inner] for g in g_cols]),
    )


def join_halves(part):
    return part + lax.ppermute(part, BOTH, CROSS_BACK)


def input_gradient(grad_out, grad_normed, hidden, gain):
    inv = lax.rsqrt(jnp.mean(hidden * hidden, axis=1, keepdims=True) + epsilon)
    back = grad_normed * gain[None, :]
    return grad_out + inv * (
        back - hidden * inv * inv * jnp.mean(back * hidden, axis=1, keepdims=True)
    )


def place_rows(full):
    core, far = lax.axis_index("core"), lax.axis_index("zh")
    sent = lax.ppermute(take(full, 1 - core, 2), BOTH, CORE_OUT)
    return jnp.where(core == far, take(full, core, 2), sent)


def half_rows(part):
    core = lax.axis_index("core")
    part = take(part, core, 2) + swap(take(part, 1 - core, 2), "core")
    return total(part, ("zl",))


def solution(mesh):
    seq, head = mesh.devices.shape
    mesh = jax.sharding.Mesh(
        mesh.devices.reshape(seq // 2, 2, 2, head // 2), ("chip", "core", "zh", "zl")
    )
    tokens, columns = ("chip", "core"), ("zh", "zl")
    by_col = P(None, None, columns)
    by_head = P(None, columns)
    both = P(None, tokens, columns)
    placed = (
        P(tokens, None),
        P(tokens),
        P(tokens, None),
        P(),
        by_col,
        by_col,
        P(),
        by_col,
        by_col,
        P(),
        by_head,
        P(),
        by_head,
        by_head,
        by_head,
        by_head,
        by_col,
    )
    return jax.shard_map(
        shards,
        mesh=mesh,
        in_specs=placed,
        out_specs=(
            P(tokens, None),
            P(tokens, None),
            P(),
            both,
            both,
            P(None, tokens, None),
            both,
            by_col,
            P(),
            by_head,
            P(),
            by_head,
            by_head,
            by_head,
            by_head,
            both,
        ),
        check_vma=False,
    )
```

```python
import functools

import jax
import jax.numpy as jnp
from jax import lax
from jax.experimental import pallas as pl
from jax.experimental.pallas import tpu as pltpu
from jax.sharding import PartitionSpec as P

HEADDIM = 64
STATE = 128
CONV = 4
GROUP = 256
LAYERS = 2
INNER = 2048
LANES = 128
ROWS = 8
BC = 2 * STATE

epsilon = 1e-05
highest = lax.Precision.HIGHEST
f32 = jnp.float32
bf16 = jnp.bfloat16


def mm(left, right, dims=((1,), (0,)), precision=None):
    return lax.dot_general(
        left, right, (dims, ((), ())), preferred_element_type=f32, precision=precision
    )


def softplus(value):
    small = jnp.exp(-jnp.abs(value))
    series = small * (1.0 - small * (0.5 - small * (1.0 / 3.0 - small * (0.25 - small * 0.2))))
    return jnp.maximum(value, 0.0) + jnp.where(small < 0.03, series, jnp.log(1.0 + small))


def silu_slope(value, sigma):
    return sigma * (1.0 + value * (1.0 - sigma))


def spread(heads, expand):
    return mm(heads, expand, precision=highest)


def gather_heads(lanes, expand):
    return mm(lanes, expand, ((1,), (1,)), precision=highest)


def pick(place, pieces, held):
    if len(pieces) == 1:
        return pieces[0][...]
    away = lax.bitwise_xor(pl.program_id(0) if held is None else held, place[0])
    value = pieces[3][...]
    for number in range(3):
        value = jnp.where(away == number, pieces[number][...], value)
    return value


def in_kernel(
    place, wall, ngain, taps, bias, dtb, avec, mask, halo, expand, tri, *refs
):
    hid = refs[:-14]
    normed, cin, cpre, dtp, cum, dtv, xdt, bc, sloc, pref, send, state, thru, prev = refs[-14:]
    step = pl.program_id(0)
    inner = expand.shape[1]

    @pl.when(step == 0)
    def _():
        state[...] = jnp.zeros_like(state)
        thru[...] = jnp.ones_like(thru)
        prev[...] = halo[...]

    h = pick(place, hid, None)
    inv = lax.rsqrt(jnp.mean(h * h, axis=1, keepdims=True) + epsilon)
    low = (h * inv * ngain[...]).astype(bf16)
    normed[...] = low
    rows = mm(low, wall[:, : inner + BC])
    pre_dt = mm(low, wall[:, inner + BC :])
    dtp[...] = pre_dt
    cin[...] = rows
    ext = jnp.concatenate([prev[...], rows], axis=0)
    prev[...] = rows[GROUP - ROWS :]
    total = taps[CONV - 1 : CONV, :] * rows + bias[0:1, :]
    for k in range(CONV - 1):
        first = ROWS - CONV + 1 + k
        total = total + taps[k : k + 1, :] * ext[first : first + GROUP] * mask[:, k : k + 1]
    cpre[...] = total
    act = total * jax.nn.sigmoid(total)
    x = act[:, :inner]
    low_bc = act[:, inner:].astype(bf16)
    bc[...] = low_bc
    dt = softplus(pre_dt + dtb[0:1, :])
    dtv[...] = dt
    run = mm(tri[...], dt * avec[0:1, :], precision=highest)
    cum[...] = run
    last = run[GROUP - 1 : GROUP]
    xdt[...] = (x * spread(dt, expand[...])).astype(bf16)
    tail = jnp.exp(last - run) * mask[:, 4:5] * dt
    contrib = mm(low_bc[:, :STATE], (x * spread(tail, expand[...])).astype(bf16), ((0,), (0,)))
    through = jnp.broadcast_to(jnp.exp(last) * mask[GROUP - 1 : GROUP, 3:4], (ROWS, LANES))
    through = spread(through, expand[...])
    sloc[0] = state[...]
    pref[0] = thru[...]
    state[...] = through[0:1] * state[...] + contrib
    thru[...] = thru[...] * through

    @pl.when(step == pl.num_programs(0) - 1)
    def _():
        send[:STATE] = state[...]
        send[STATE:] = thru[...]


def pair_lanes(value, which):
    lane = lax.broadcasted_iota(jnp.int32, value.shape, 1)
    keep = lane < HEADDIM if which == 0 else lane >= HEADDIM
    return jnp.where(keep, value, jnp.zeros_like(value))


def intra_kernel(cum, xdt, bc, seg, segrow, y):
    inner = xdt.shape[1]
    run = cum[...]
    run_t = run.T
    base = mm(bc[:, STATE:], bc[:, :STATE], ((1,), (1,)))
    t_at = lax.broadcasted_iota(jnp.int32, (GROUP, GROUP), 0)
    s_at = lax.broadcasted_iota(jnp.int32, (GROUP, GROUP), 1)
    same = (seg[:, 0:1] == segrow[0:1, :]) & (t_at >= s_at)
    closed = jnp.where(same, 0.0, -1e30)
    for pair in range(inner // LANES):
        cols = slice(pair * LANES, (pair + 1) * LANES)
        xs = xdt[:, cols]
        parts = []
        for which in range(2):
            head = 2 * pair + which
            decay = jnp.exp(run[:, head : head + 1] - run_t[head : head + 1, :] + closed)
            parts.append(mm((decay * base).astype(bf16), xs))
        lane = lax.broadcasted_iota(jnp.int32, (GROUP, LANES), 1)
        y[:, cols] = jnp.where(lane < HEADDIM, parts[0], parts[1])


def out_kernel(
    yin, cpre, cum, bc, mask, zval, sloc, pref, entry, dskip, ggain, wout, expand, *refs
):
    cot, (y, gate_in, proj, sums) = refs[:-4], refs[-4:]
    inner = expand.shape[1]
    pre = cpre[...]
    x = pre * jax.nn.sigmoid(pre)
    full = sloc[0] + pref[0][0:1] * entry[...]
    reach = spread(jnp.exp(cum[...]) * mask[:, 3:4], expand[...])
    value = yin[...] + reach * mm(bc[:, STATE:], full.astype(bf16)) + dskip[0:1, :] * x
    y[...] = value
    z = zval[...]
    gated = value * (z * jax.nn.sigmoid(z))
    low = (gated * ggain[0:1, :]).astype(bf16)
    gate_in[...] = low
    proj[...] = mm(low, wout[...], ((1,), (1,)))
    ones = jnp.ones((ROWS, inner), f32)
    squares = mm(ones, gated * gated, ((1,), (1,)), precision=highest)
    if cot:
        back = mm(cot[0][...].astype(bf16), wout[...])
        dots = mm(ones, low.astype(f32) * back, ((1,), (1,)), precision=highest)
        row = lax.broadcasted_iota(jnp.int32, squares.shape, 0)
        squares = jnp.where(row == 0, squares, dots)
    sums[...] = squares


def gate_kernel(
    place, scale, gsq, y, zval, ggain, wout, cum, bc, mask, expand, *refs
):
    gh = refs[:-9]
    gproj, dy, dz, gloc, suf, send, acc, carry, thru = refs[-9:]
    step = pl.program_id(0)

    @pl.when(step == 0)
    def _():
        carry[...] = jnp.zeros_like(carry)
        thru[...] = jnp.ones_like(thru)
        acc[...] = jnp.zeros_like(acc)

    gp = (scale[...] * pick(place, gh, pl.num_programs(0) - 1 - step)).astype(bf16)
    gproj[...] = gp
    ggi = mm(gp, wout[...])
    z = zval[...]
    sigma = jax.nn.sigmoid(z)
    silu = z * sigma
    value = y[...]
    gated = value * silu
    ggated = ggi * ggain[0:1, :] + gated * gsq[...]
    acc[0:1, :] += jnp.sum(ggi * gated, axis=0, keepdims=True)
    low = (ggated * silu).astype(bf16)
    dy[...] = low
    dz[...] = (ggated * value * silu_slope(z, sigma)).astype(bf16)
    run = cum[...]
    last = run[GROUP - 1 : GROUP]
    reach = spread(jnp.exp(run) * mask[:, 3:4], expand[...])
    back = mm(bc[:, STATE:], (reach * low.astype(f32)).astype(bf16), ((0,), (0,)))
    through = jnp.broadcast_to(jnp.exp(last) * mask[GROUP - 1 : GROUP, 3:4], (ROWS, LANES))
    through = spread(through, expand[...])
    gloc[0] = carry[...]
    suf[0] = thru[...]
    carry[...] = back + through[0:1] * carry[...]
    thru[...] = thru[...] * through

    @pl.when(step == pl.num_programs(0) - 1)
    def _():
        send[:STATE] = carry[...]
        send[STATE:] = thru[...]


def intra_back_kernel(cum, xdt, bc, seg, segrow, dy, dz, wz, u, dbc, part):
    inner = xdt.shape[1]
    run = cum[...]
    run_t = run.T
    base = mm(bc[:, :STATE], bc[:, STATE:], ((1,), (1,)))
    s_at = lax.broadcasted_iota(jnp.int32, (GROUP, GROUP), 0)
    t_at = lax.broadcasted_iota(jnp.int32, (GROUP, GROUP), 1)
    same = (seg[:, 0:1] == segrow[0:1, :]) & (t_at >= s_at)
    closed = jnp.where(same, 0.0, -1e30)
    grad_base = jnp.zeros((GROUP, GROUP), f32)
    for pair in range(inner // LANES):
        cols = slice(pair * LANES, (pair + 1) * LANES)
        xs = xdt[:, cols]
        ds = dy[:, cols]
        parts = []
        for which in range(2):
            head = 2 * pair + which
            decay = jnp.exp(run_t[head : head + 1, :] - run[:, head : head + 1] + closed)
            parts.append(mm((decay * base).astype(bf16), ds))
            grad_base = grad_base + decay * mm(xs, pair_lanes(ds, which), ((1,), (1,)))
        lane = lax.broadcasted_iota(jnp.int32, (GROUP, LANES), 1)
        u[:, cols] = jnp.where(lane < HEADDIM, parts[0], parts[1])
    part[...] = mm(dz[...], wz[...], ((1,), (1,)))
    low = grad_base.astype(bf16)
    dbc[:, :STATE] = mm(low, bc[:, STATE:])
    dbc[:, STATE:] = mm(low, bc[:, :STATE], ((0,), (0,)))


def in_back_kernel(
    uin, dbc, dy, y, cpre, cin, dtp, dtv, cum, xdt, bc, mask, sloc, pref, entry, gloc, suf,
    gout, halo, taps, dtb, avec, dskip, expand, triback,
    gall, last8, rim, gtaps, vecs, dsk,
    nexts,
):
    step = pl.program_id(0)
    inner = expand.shape[1]

    @pl.when(step == 0)
    def _():
        nexts[...] = jnp.zeros_like(nexts)
        gtaps[...] = jnp.zeros_like(gtaps)
        vecs[...] = jnp.zeros_like(vecs)
        dsk[...] = jnp.zeros_like(dsk)

    e = expand[...]
    pre = cpre[...]
    sigma = jax.nn.sigmoid(pre)
    x = (pre * sigma)[:, :inner]
    full = sloc[0] + pref[0][0:1] * entry[...]
    nxt = gloc[0] + suf[0][0:1] * gout[...]
    nxt_low = nxt.astype(bf16)
    run = cum[...]
    last = run[GROUP - 1 : GROUP]
    dt = dtv[...]
    low_dy = dy[...].astype(f32)
    xw = xdt[...].astype(f32)
    tail = spread(jnp.exp(last - run) * mask[:, 4:5], e)
    reach = spread(jnp.exp(run) * mask[:, 3:4], e)
    u_inter = tail * mm(bc[:, :STATE], nxt_low)
    u = uin[...] + u_inter
    dx = spread(dt, e) * u + dskip[0:1, :] * low_dy
    dsk[0:1, :] += jnp.sum(low_dy * x, axis=0, keepdims=True)
    db = dbc[:, :STATE] + mm((tail * xw).astype(bf16), nxt_low, ((1,), (1,)))
    dc = dbc[:, STATE:] + mm((reach * low_dy).astype(bf16), full.astype(bf16), ((1,), (1,)))
    grad_dt = gather_heads(x * u, e)
    y_plain = y[...] - dskip[0:1, :] * x
    grad_cum = gather_heads(low_dy * y_plain - xw * u, e)
    flow = jnp.sum(nxt * full, axis=0, keepdims=True)
    flow = gather_heads(jnp.broadcast_to(flow, (ROWS, inner)), e)[0:1]
    ends = jnp.sum(xw * u_inter, axis=0, keepdims=True)
    ends = gather_heads(jnp.broadcast_to(ends, (ROWS, inner)), e)[0:1]
    grad_tot = mask[GROUP - 1 : GROUP, 3:4] * jnp.exp(last) * flow + ends
    grad_da = mm(triback[...], grad_cum, precision=highest) + grad_tot
    a = avec[0:1, :]
    grad_dtv = grad_dt + grad_da * a
    grad_dtpre = grad_dtv * jax.nn.sigmoid(dtp[...] + dtb[0:1, :])
    vecs[0:1, :] += jnp.sum(grad_da * dt, axis=0, keepdims=True) * a
    vecs[1:2, :] += jnp.sum(grad_dtpre, axis=0, keepdims=True)
    slope = silu_slope(pre, sigma)
    grad_pre = jnp.concatenate([dx, db, dc], axis=1) * slope
    gtaps[4:5, :] += jnp.sum(grad_pre, axis=0, keepdims=True)
    rows = cin[...]
    grad_rows = taps[CONV - 1 : CONV, :] * grad_pre
    gtaps[3:4, :] += jnp.sum(rows * grad_pre, axis=0, keepdims=True)
    masked = []
    for k in range(CONV - 1):
        m = grad_pre * mask[:, k : k + 1]
        masked.append(m[:ROWS])
        ahead = CONV - 1 - k
        shifted = jnp.concatenate([m, nexts[k]], axis=0)[ahead : ahead + GROUP]
        grad_rows = grad_rows + taps[k : k + 1, :] * shifted
        gtaps[k : k + 1, :] += jnp.sum(rows * shifted, axis=0, keepdims=True)
    for k in range(CONV - 1):
        nexts[k] = masked[k]
    gall[:, : inner + BC] = grad_rows.astype(bf16)
    gall[:, inner + BC :] = grad_dtpre.astype(bf16)

    @pl.when(step == 0)
    def _():
        last8[...] = grad_rows[GROUP - ROWS :]

    @pl.when(step == pl.num_programs(0) - 1)
    def _():
        spill = jnp.zeros((ROWS, inner + BC), f32)
        edge = halo[...]
        for k in range(CONV - 1):
            down = ROWS - CONV + 1 + k
            moved = jnp.concatenate([jnp.zeros((ROWS, inner + BC), f32), masked[k]], axis=0)
            moved = moved[ROWS - down : 2 * ROWS - down]
            spill = spill + taps[k : k + 1, :] * moved
            gtaps[k : k + 1, :] += jnp.sum(edge * moved, axis=0, keepdims=True)
        rim[...] = spill


def whole(shape):
    return pl.BlockSpec(shape, lambda c: (0,) * len(shape))


def by_rows(cols, count, reverse=False):
    if reverse:
        return pl.BlockSpec((GROUP, cols), lambda c: (count - 1 - c, 0))
    return pl.BlockSpec((GROUP, cols), lambda c: (c, 0))


def by_group(shape, count, reverse=False):
    if reverse:
        return pl.BlockSpec((1,) + shape, lambda c: (count - 1 - c, 0, 0))
    return pl.BlockSpec((1,) + shape, lambda c: (c, 0, 0))


def by_piece(pieces, count, reverse=False):
    if len(pieces) == 1:
        return [(by_rows(pieces[0].shape[1], count, reverse), pieces[0])]
    return [(whole(piece.shape), piece) for piece in pieces]


def by_cols(count):
    return pl.BlockSpec((ROWS, GROUP), lambda c: (0, c))


def call(kernel, count, ins, outs, scratch, micros, name):
    return pl.pallas_call(
        kernel,
        grid=(count,),
        in_specs=[spec for spec, _ in ins],
        out_specs=[spec for spec, _ in outs],
        out_shape=[shape for _, shape in outs],
        scratch_shapes=scratch,
        compiler_params=pltpu.CompilerParams(
            dimension_semantics=("arbitrary",), vmem_limit_bytes=56 * 1024 * 1024
        ),
        cost_estimate=pl.CostEstimate(
            flops=micros * 1_150_000_000, bytes_accessed=1024 * 1024, transcendentals=0
        ),
        name=name,
    )(*[value for _, value in ins])


def shape(*dims, dtype=f32):
    return jax.ShapeDtypeStruct(dims, dtype)


SWAP = ((0, 1), (1, 0))
CROSS = ((0, 1), (3, 2))
CROSS_BACK = ((1, 0), (2, 3))
CORE_OUT = ((0, 2), (3, 1))
CORE_IN = ((2, 0), (1, 3))
DIAGONAL = ((2, 1), (1, 2))
BOTH = ("core", "zh")
BLOCKS = ("chip", "zh")


def shifted(value, steps):
    count = lax.axis_size(BLOCKS)
    leading, last = (max(0, -steps), min(count, count - steps))
    return lax.ppermute(value, BLOCKS, [(source, source + steps) for source in range(leading, last)])


def chain(part, reverse, stages):
    count = lax.axis_size(BLOCKS)
    place = lax.axis_index(BLOCKS)
    state, decay = part[:STATE], part[STATE : STATE + 1]
    entry, reach = jnp.zeros_like(state), jnp.ones_like(decay)
    step = 1
    while step < count:
        got = lax.ppermute(part, BLOCKS, [(i, i ^ step) for i in range(count)])
        got_state, got_decay = got[:STATE], got[STATE : STATE + 1]
        later = ((place & step) == 0) if reverse else ((place & step) != 0)
        stages.append(got)
        entry = jnp.where(later, entry + reach * got_state, entry)
        reach = jnp.where(later, reach * got_decay, reach)
        state = jnp.where(later, state + decay * got_state, got_state + got_decay * state)
        decay = decay * got_decay
        part = jnp.concatenate([state, jnp.broadcast_to(decay, (ROWS, decay.shape[1]))])
        step *= 2
    return entry


def swap(value, axis):
    return lax.ppermute(value, axis, SWAP)


def total(value, axes):
    for axis in axes:
        count = lax.axis_size(axis)
        step = 1
        while step < count:
            value = value + lax.ppermute(value, axis, [(i, i ^ step) for i in range(count)])
            step *= 2
    return value


def take(value, index, count):
    size = value.shape[0] // count
    return lax.dynamic_slice_in_dim(value, index * size, size)


def ordered(place, mine, theirs):
    return jnp.where(
        place == 0, jnp.concatenate([mine, theirs]), jnp.concatenate([theirs, mine])
    )


def behind(value, *marks):
    return lax.optimization_barrier((value, *marks))[0]


def scatter_sum(part, mark=()):
    core, near = lax.axis_index("core"), lax.axis_index("zl")
    half = take(part, core, 2) + behind(swap(take(part, 1 - core, 2), "core"), *mark)
    if lax.axis_size("zl") == 2:
        return take(half, near, 2) + swap(take(half, 1 - near, 2), "zl")
    return lax.psum_scatter(half, "zl", scatter_dimension=0, tiled=True)


def own_rows(value):
    core, near = lax.axis_index("core"), lax.axis_index("zl")
    return take(take(value, core, 2), near, lax.axis_size("zl"))


def gather_near(value):
    if lax.axis_size("zl") == 2:
        return ordered(lax.axis_index("zl"), value, swap(value, "zl"))
    return lax.all_gather(value, "zl", tiled=True)


def gather_rows(value):
    half = gather_near(value)
    return ordered(lax.axis_index("core"), half, swap(half, "core"))


def own_place():
    return 2 * lax.axis_index("core") + lax.axis_index("zl")


def gather_pieces(value):
    if lax.axis_size("zl") != 2 or value.shape[0] != GROUP:
        return [gather_rows(value)]
    near = swap(value, "zl")
    return [value, near, swap(value, "core"), swap(near, "core")]


def place_kernel(place, value, mine, near, theirs, value_s, mine_s, near_s, theirs_s, out):
    away = lax.bitwise_xor(pl.program_id(0), place[0])
    pairs = ((value, mine), (value_s, mine_s), (near, theirs), (near_s, theirs_s))
    for number, (here, there) in enumerate(pairs):

        @pl.when((away == number) & (place[1] == 1))
        def _():
            out[...] = here[...].astype(out.dtype)

        @pl.when((away == number) & (place[1] == 0))
        def _():
            out[...] = there[...].astype(out.dtype)


def cross_over(value):
    return [lax.ppermute(value, BOTH, pairs) for pairs in (CROSS, DIAGONAL, CORE_IN)]


def near_swap(value):
    if lax.axis_size("zl") != 2 or value.shape[0] != GROUP:
        return None
    here = [(2 * kind + i, 2 * kind + 1 - i) for kind in (0, 3) for i in range(2)]
    return lax.ppermute(value, ("core", "zh", "zl"), here)


def near_swaps(value, mine, theirs, near, value_s=None, near_s=None):
    if lax.axis_size("zl") != 2 or value.shape[0] != GROUP:
        return None
    axes = ("core", "zh", "zl")
    there = [(2 * kind + i, 2 * kind + 1 - i) for kind in (1, 2) for i in range(2)]
    return (
        near_swap(value) if value_s is None else value_s,
        lax.ppermute(mine, axes, there),
        lax.ppermute(theirs, axes, there),
        near_swap(near) if near_s is None else near_s,
    )


def deliver(value, mine, theirs, near, dtype, swaps=None, mark=()):
    core, far = lax.axis_index("core"), lax.axis_index("zh")
    held = core == far
    if lax.axis_size("zl") != 2 or value.shape[0] != GROUP:
        mine = gather_near(jnp.where(held, value, mine))
        theirs = gather_near(jnp.where(held, near, theirs))
        full = ordered(core, mine, theirs)
        return narrowed(full) if dtype == bf16 else full
    if swaps is None:
        swaps = near_swaps(value, mine, theirs, near)
    value_s, mine_s, theirs_s, near_s = swaps
    place = jnp.stack([own_place(), held.astype(jnp.int32)]).astype(jnp.int32)
    width = value.shape[1]
    parts = behind((value, mine, near, theirs, value_s, mine_s, near_s, theirs_s), *mark)
    return pl.pallas_call(
        place_kernel,
        grid=(4,),
        in_specs=[pl.BlockSpec(memory_space=pltpu.SMEM)] + [whole((GROUP, width))] * 8,
        out_specs=by_rows(width, 4),
        out_shape=shape(4 * GROUP, width, dtype=dtype),
        compiler_params=pltpu.CompilerParams(
            dimension_semantics=("arbitrary",), vmem_limit_bytes=40 * 1024 * 1024
        ),
        name="place",
    )(place, *parts)


def to_block(value):
    got = lax.ppermute(value, BOTH, CORE_OUT)
    return jnp.where(lax.axis_index("core") == lax.axis_index("zh"), value, got)


def eight(row):
    return jnp.broadcast_to(row[None, :], (ROWS, row.shape[0]))


def pad_lanes(value):
    return jnp.pad(value, [(0, 0)] * (value.ndim - 1) + [(0, LANES - value.shape[-1])])


def weight_kernel(count, extra, place, *refs):
    own, rest = refs[:count], refs[count:]
    outs, rest = rest[-count:], rest[:-count]
    parts, more = (rest[:-2], rest[-2:]) if extra else (rest, ())
    block = pl.program_id(0)
    at = 0
    for source, out in zip(own, outs):
        cols = source.shape[1]

        @pl.when(place[1] == 1)
        def _():
            out[:, :cols] = source[...]

        for away, part in enumerate(parts):

            @pl.when((place[1] == 0) & (lax.bitwise_xor(place[0], block) == away))
            def _():
                out[:, :cols] = part[:, at : at + cols].astype(bf16)

        at += cols
    if more:
        cols = own[0].shape[1]
        outs[0][:, cols : cols + BC] = more[0][...]
        outs[0][:, cols + BC :] = more[1][...].astype(bf16)


def narrow_kernel(wide, narrow):
    narrow[...] = wide[...].astype(bf16)


def narrowed(value):
    rows, cols = value.shape
    return pl.pallas_call(
        narrow_kernel,
        grid=(rows // GROUP,),
        in_specs=[by_rows(cols, 0)],
        out_specs=by_rows(cols, 0),
        out_shape=shape(rows, cols, dtype=bf16),
        name="narrowed",
    )(value)


def weights_over(own, *marks):
    chips = lax.axis_size("chip")
    piece = jnp.concatenate(
        [take(value, lax.axis_index("chip"), chips).astype(f32) for value in behind(own, *marks)],
        axis=1,
    )
    return lax.ppermute(piece, BOTH, CROSS)


def gather_weights(piece, own, more=(), third=()):
    width = own[0].shape[0]
    chips = lax.axis_size("chip")
    chip = lax.axis_index("chip")
    held = (lax.axis_index("core") == lax.axis_index("zh")).astype(jnp.int32)
    size = width // chips
    if chips == 4:
        parts = [piece]
        for away in range(1, chips):
            pairs = [
                (4 * c + kind, 4 * (c ^ away) + kind) for c in range(chips) for kind in (1, 2)
            ]
            parts.append(lax.ppermute(piece, ("chip", "core", "zh"), pairs))
        place = jnp.stack([chip, held]).astype(jnp.int32)
        blocks = chips
    else:
        parts = [lax.all_gather(piece, "chip", tiled=True)]
        place = jnp.stack([0, held]).astype(jnp.int32)
        blocks, size = 1, width
    parts = behind(parts, *third)
    out_cols = [value.shape[1] for value in own]
    out_cols[0] += sum(value.shape[1] for value in more)

    def rows(cols):
        return pl.BlockSpec((size, cols), lambda c: (c, 0))

    return pl.pallas_call(
        functools.partial(weight_kernel, len(own), bool(more)),
        grid=(blocks,),
        in_specs=[pl.BlockSpec(memory_space=pltpu.SMEM)]
        + [rows(value.shape[1]) for value in own]
        + [whole(piece.shape if chips == 4 else parts[0].shape)] * len(parts)
        + [rows(value.shape[1]) for value in more],
        out_specs=[rows(cols) for cols in out_cols],
        out_shape=[shape(width, cols, dtype=bf16) for cols in out_cols],
        compiler_params=pltpu.CompilerParams(
            dimension_semantics=("arbitrary",), vmem_limit_bytes=40 * 1024 * 1024
        ),
        name="weights",
    )(place, *own, *parts, *more)


def shards(
    x_input,
    seg_ids,
    cotangent,
    norm_gain,
    w_z,
    w_x,
    w_bc,
    w_dt,
    conv_x,
    conv_bc,
    bias_x,
    bias_bc,
    dt_bias,
    a_log,
    d_skip,
    gate_gain,
    w_out,
):
    tok, width = x_input.shape
    inner = w_z.shape[2]
    core, far = lax.axis_index("core"), lax.axis_index("zh")
    held = core == far
    heads = w_dt.shape[2]
    count = tok // GROUP
    conv_cols = inner + BC
    all_cols = inner + BC + LANES

    dt_own = w_dt.astype(f32).reshape(LAYERS, width * heads // LANES, LANES)
    dt_sent = lax.ppermute(dt_own, BOTH, CROSS)
    dt_all = pad_lanes(jnp.where(held, dt_own, dt_sent).reshape(LAYERS, width, heads))
    first_x = weights_over([w_x[0]])
    hidden = to_block(x_input.astype(f32))
    first_rest = weights_over([w_z[0], w_out[0]], first_x)
    (wall,) = gather_weights(first_x, [w_x[0]], (w_bc[0], dt_all[0]), (first_rest,))
    seg = to_block(seg_ids.astype(f32))
    small = jnp.concatenate(
        [
            value.reshape(LAYERS, -1)
            for value in (conv_x, bias_x, dt_bias, a_log, d_skip, gate_gain)
        ],
        axis=1,
    )
    small = jnp.where(held, small, lax.ppermute(small, BOTH, CROSS))
    sizes = (CONV * inner, inner, heads, heads, heads, inner)
    pieces, at = [], 0
    for size in sizes:
        pieces.append(small[:, at : at + size])
        at += size
    conv_x, bias_x, dt_bias, a_log, d_skip, gate_gain = pieces
    conv_x = conv_x.reshape(LAYERS, CONV, inner)
    hidden_own = own_rows(hidden)
    hidden_block = hidden
    hidden = [hidden]
    place = jnp.stack([own_place(), own_place()]).astype(jnp.int32)
    smem = pl.BlockSpec(memory_space=pltpu.SMEM)
    edge_seg = shifted(seg[tok - ROWS :], 1)
    seg_ext = jnp.concatenate([edge_seg, seg])
    before = jnp.concatenate([edge_seg[ROWS - 1 :], seg[GROUP - 1 : tok - 1 : GROUP]])
    after = seg[GROUP - 1 :: GROUP]
    mask = jnp.stack(
        [
            (seg_ext[ROWS - CONV + 1 + k : ROWS - CONV + 1 + k + tok] == seg).astype(f32)
            for k in range(CONV - 1)
        ]
        + [
            (seg == jnp.repeat(before, GROUP)).astype(f32),
            (seg == jnp.repeat(after, GROUP)).astype(f32),
            seg,
            seg,
            seg,
        ],
        axis=1,
    )
    seg_col = seg[:, None]
    seg_row = eight(seg)
    expand = (jnp.arange(LANES)[:, None] == jnp.arange(inner)[None, :] // HEADDIM).astype(f32)
    position = jnp.arange(GROUP)
    tri = (position[:, None] >= position[None, :]).astype(f32)
    triback = (position[:, None] <= position[None, :]).astype(f32)

    stored = []
    for layer in range(LAYERS):
        if layer > 0:
            wall = next_wall
        taps = jnp.concatenate([conv_x[layer], conv_bc[layer]], axis=1)
        bias = eight(jnp.concatenate([bias_x[layer], bias_bc[layer]]))
        dtb = eight(pad_lanes(dt_bias[layer]))
        avec = eight(pad_lanes(-jnp.exp(a_log[layer])))
        dskip = eight(jnp.repeat(d_skip[layer], HEADDIM))
        ggain = eight(gate_gain[layer])
        ngain = norm_gain[layer][None, :]
        if len(hidden) == 1:
            end = hidden[0][tok - 16 :]
        else:
            ends = jnp.stack([piece[GROUP - 16 :] for piece in hidden])
            end = lax.dynamic_index_in_dim(ends, 3 ^ own_place(), 0, False)
        end = end * lax.rsqrt(jnp.mean(end * end, axis=1, keepdims=True) + epsilon) * ngain
        end = mm(end.astype(bf16), wall[:, : inner + BC])[ROWS:]
        halo = shifted(end, 1)
        normed, cin, cpre, dtp, cum, dtv, xdt, bc, sloc, pref, send = call(
            in_kernel,
            count,
            [
                (smem, place),
                (whole((width, all_cols)), wall),
                (whole((1, width)), ngain),
                (whole((CONV, conv_cols)), taps),
                (whole((ROWS, conv_cols)), bias),
                (whole((ROWS, LANES)), dtb),
                (whole((ROWS, LANES)), avec),
                (by_rows(ROWS, count), mask),
                (whole((ROWS, conv_cols)), halo),
                (whole((LANES, inner)), expand),
                (whole((GROUP, GROUP)), tri),
            ]
            + by_piece(hidden, count),
            [
                (by_rows(width, count), shape(tok, width, dtype=bf16)),
                (by_rows(conv_cols, count), shape(tok, conv_cols)),
                (by_rows(conv_cols, count), shape(tok, conv_cols)),
                (by_rows(LANES, count), shape(tok, LANES)),
                (by_rows(LANES, count), shape(tok, LANES)),
                (by_rows(LANES, count), shape(tok, LANES)),
                (by_rows(inner, count), shape(tok, inner, dtype=bf16)),
                (by_rows(BC, count), shape(tok, BC, dtype=bf16)),
                (by_group((STATE, inner), count), shape(count, STATE, inner)),
                (by_group((ROWS, inner), count), shape(count, ROWS, inner)),
                (whole((STATE + ROWS, inner)), shape(STATE + ROWS, inner)),
            ],
            [
                pltpu.VMEM((STATE, inner), f32),
                pltpu.VMEM((ROWS, inner), f32),
                pltpu.VMEM((ROWS, conv_cols), f32),
            ],
            16,
            "in_proj_conv",
        )
        if layer == 0:
            wz, wout = gather_weights(
                behind(first_rest, wall), [w_z[0], w_out[0]], third=(send,)
            )
            cotangent = behind(cotangent, send).astype(f32)
            cot_sent = lax.ppermute(cotangent, BOTH, CORE_OUT)
        else:
            wz, wout = next_wz, next_wout
        zval = mm(normed, wz)
        (yin,) = call(
            intra_kernel,
            count,
            [
                (by_rows(LANES, count), cum),
                (by_rows(inner, count), xdt),
                (by_rows(BC, count), bc),
                (by_rows(1, count), seg_col),
                (by_cols(count), seg_row),
            ],
            [(by_rows(inner, count), shape(tok, inner))],
            [],
            6,
            "ssd_within",
        )
        stages = []
        entry = chain(send, False, stages)
        if layer == 0:
            second_all = weights_over([w_x[1], w_z[1], w_out[1]], stages[0])
            entry = behind(entry, second_all, cot_sent)
            cotangent = jnp.where(held, cotangent, cot_sent)
        y, gate_in, proj, sums = call(
            out_kernel,
            count,
            [
                (by_rows(inner, count), yin),
                (by_rows(inner, count), cpre),
                (by_rows(LANES, count), cum),
                (by_rows(BC, count), bc),
                (by_rows(ROWS, count), mask),
                (by_rows(inner, count), zval),
                (by_group((STATE, inner), count), sloc),
                (by_group((ROWS, inner), count), pref),
                (whole((STATE, inner)), entry),
                (whole((ROWS, inner)), dskip),
                (whole((ROWS, inner)), ggain),
                (whole((width, inner)), wout),
                (whole((LANES, inner)), expand),
            ]
            + ([(by_rows(width, count), cotangent)] if layer == LAYERS - 1 else []),
            [
                (by_rows(inner, count), shape(tok, inner)),
                (by_rows(inner, count), shape(tok, inner, dtype=bf16)),
                (by_rows(width, count), shape(tok, width)),
                (by_cols(count), shape(ROWS, tok)),
            ],
            [],
            12,
            "gate_out_proj",
        )
        sums = total(sums, ("core", "zl"))
        gate_scale = lax.rsqrt(sums[0] / INNER + epsilon)
        stored.append(
            dict(
                hidden=hidden_own, normed=normed, zval=zval, cin=cin, cpre=cpre, dtp=dtp, cum=cum,
                dtv=dtv, xdt=xdt, bc=bc, sloc=sloc, pref=pref, entry=entry, y=y, gate_in=gate_in,
                proj=proj, gate_scale=gate_scale, dots=sums[1], halo=halo, wall=wall, wz=wz, wout=wout,
                taps=taps, dtb=dtb, avec=avec, dskip=dskip, ggain=ggain,
            )
        )
        if layer < LAYERS - 1:
            proj_sum = scatter_sum(proj)
            stored[layer]["proj_sum"] = proj_sum
            hidden_own = hidden_own + own_rows(gate_scale)[:, None] * proj_sum
            next_wall, next_wz, next_wout = gather_weights(
                behind(second_all, proj),
                [w_x[1], w_z[1], w_out[1]],
                (w_bc[1], dt_all[1]),
                third=(hidden_own,),
            )
            hidden = gather_pieces(hidden_own)

    grad_h = [cotangent]
    grad_own = own_rows(cotangent)
    matrices = [None] * LAYERS
    vectors = [None] * LAYERS
    shared = [None] * LAYERS
    for layer in reversed(range(LAYERS)):
        kept = stored[layer]
        gate_scale = kept["gate_scale"]
        if layer == LAYERS - 1:
            grad_scale = kept["dots"]
        else:
            grad_scale = gather_rows(jnp.sum(grad_own * kept["proj_sum"], axis=1))
        gsq = -grad_scale * gate_scale**3 / INNER
        rev = functools.partial(by_rows, count=count, reverse=True)
        rev_group = functools.partial(by_group, count=count, reverse=True)
        gproj, dy, dz, gloc, suf, gsend, acc = call(
            gate_kernel,
            count,
            [
                (smem, place),
                (rev(1), gate_scale[:, None]),
                (rev(1), gsq[:, None]),
                (rev(inner), kept["y"]),
                (rev(inner), kept["zval"]),
                (whole((ROWS, inner)), kept["ggain"]),
                (whole((width, inner)), kept["wout"]),
                (rev(LANES), kept["cum"]),
                (rev(BC), kept["bc"]),
                (rev(ROWS), mask),
                (whole((LANES, inner)), expand),
            ]
            + by_piece(grad_h, count, True),
            [
                (rev(width), shape(tok, width, dtype=bf16)),
                (rev(inner), shape(tok, inner, dtype=bf16)),
                (rev(inner), shape(tok, inner, dtype=bf16)),
                (rev_group((STATE, inner)), shape(count, STATE, inner)),
                (rev_group((ROWS, inner)), shape(count, ROWS, inner)),
                (whole((STATE + ROWS, inner)), shape(STATE + ROWS, inner)),
                (whole((ROWS, inner)), shape(ROWS, inner)),
            ],
            [pltpu.VMEM((STATE, inner), f32), pltpu.VMEM((ROWS, inner), f32)],
            10,
            "gate_back",
        )
        if layer == LAYERS - 1:
            last_sum = scatter_sum(kept["proj"], (gate_scale,))
            hidden_own = hidden_own + own_rows(gate_scale)[:, None] * last_sum
            dy = behind(dy, hidden_own)
            gsend = behind(gsend, hidden_own)
            out_parts = cross_over(hidden_own)
            out_held = (near_swap(hidden_own), near_swap(out_parts[2]))
        u, dbc, partial_z = call(
            intra_back_kernel,
            count,
            [
                (by_rows(LANES, count), kept["cum"]),
                (by_rows(inner, count), kept["xdt"]),
                (by_rows(BC, count), kept["bc"]),
                (by_rows(1, count), seg_col),
                (by_cols(count), seg_row),
                (by_rows(inner, count), dy),
                (by_rows(inner, count), dz),
                (whole((width, inner)), kept["wz"]),
            ],
            [
                (by_rows(inner, count), shape(tok, inner)),
                (by_rows(BC, count), shape(tok, BC)),
                (by_rows(width, count), shape(tok, width)),
            ],
            [],
            8,
            "ssd_within_back",
        )
        stages = []
        gout = chain(gsend, True, stages)
        round_one = stages[0]
        if layer == 0:
            out_swaps = near_swaps(hidden_own, *behind(out_parts, round_one), *out_held)
        grad_wout = mm(gproj, kept["gate_in"], ((0,), (0,)))
        grad_wz = mm(kept["normed"], dz, ((0,), (0,)))
        u = behind(u, grad_wout, grad_wz)
        gall, last8, rim, gtaps, vecs, dsk = call(
            in_back_kernel,
            count,
            [
                (rev(inner), u),
                (rev(BC), dbc),
                (rev(inner), dy),
                (rev(inner), kept["y"]),
                (rev(conv_cols), kept["cpre"]),
                (rev(conv_cols), kept["cin"]),
                (rev(LANES), kept["dtp"]),
                (rev(LANES), kept["dtv"]),
                (rev(LANES), kept["cum"]),
                (rev(inner), kept["xdt"]),
                (rev(BC), kept["bc"]),
                (rev(ROWS), mask),
                (rev_group((STATE, inner)), kept["sloc"]),
                (rev_group((ROWS, inner)), kept["pref"]),
                (whole((STATE, inner)), kept["entry"]),
                (rev_group((STATE, inner)), gloc),
                (rev_group((ROWS, inner)), suf),
                (whole((STATE, inner)), gout),
                (whole((ROWS, conv_cols)), kept["halo"]),
                (whole((CONV, conv_cols)), kept["taps"]),
                (whole((ROWS, LANES)), kept["dtb"]),
                (whole((ROWS, LANES)), kept["avec"]),
                (whole((ROWS, inner)), kept["dskip"]),
                (whole((LANES, inner)), expand),
                (whole((GROUP, GROUP)), triback),
            ],
            [
                (rev(all_cols), shape(tok, all_cols, dtype=bf16)),
                (whole((ROWS, conv_cols)), shape(ROWS, conv_cols)),
                (whole((ROWS, conv_cols)), shape(ROWS, conv_cols)),
                (whole((ROWS, conv_cols)), shape(ROWS, conv_cols)),
                (whole((ROWS, LANES)), shape(ROWS, LANES)),
                (whole((ROWS, inner)), shape(ROWS, inner)),
            ],
            [pltpu.VMEM((CONV - 1, ROWS, conv_cols), f32)],
            20,
            "in_proj_conv_back",
        )
        rim_back = shifted(rim, -1)
        if layer == 0:
            last8 = behind(last8, matrices[1], *(out_swaps or ()))
        else:
            last8 = behind(last8, *out_parts, *(out_held if out_held[0] is not None else ()))
        gall = lax.dynamic_update_slice(
            gall, (last8 + rim_back).astype(bf16), (tok - ROWS, 0)
        )
        partial = partial_z + mm(gall, kept["wall"], ((1,), (1,)))
        grad_normed = scatter_sum(partial)
        late = behind(gall, partial)
        grad_wbc = mm(kept["normed"], late[:, inner : inner + BC], ((0,), (0,)))
        grad_win = mm(kept["normed"], behind(late, grad_wbc)[:, :inner], ((0,), (0,)))
        if layer == 0:
            grad_own = input_gradient(grad_own, grad_normed, kept["hidden"], norm_gain[layer])
            grad_parts = cross_over(grad_own)
            own_s = near_swap(grad_own)
            late, partial = behind((gall, partial), grad_parts[2])
            grad_parts, own_s, _ = behind((grad_parts, own_s, grad_win))
            mark = grad_parts[0]
            grad_swaps = near_swaps(grad_own, *grad_parts, own_s)
        grad_wdt = mm(kept["normed"], late[:, inner + BC :], ((0,), (0,)))
        hidden_in = kept["hidden"]
        inv = lax.rsqrt(jnp.mean(hidden_in * hidden_in, axis=1, keepdims=True) + epsilon)
        if layer == 0:
            full = hidden_block
            grad_ngain = jnp.sum(
                partial
                * (full * lax.rsqrt(jnp.mean(full * full, axis=1, keepdims=True) + epsilon)),
                axis=0,
            )
        else:
            grad_ngain = jnp.sum(grad_normed * hidden_in * inv, axis=0)
        if layer > 0:
            grad_own = input_gradient(grad_own, grad_normed, hidden_in, norm_gain[layer])
            grad_h = gather_pieces(grad_own)
        matrices[layer] = lax.psum_scatter(
            jnp.concatenate([grad_wout, grad_wz, grad_win, grad_wbc], axis=1),
            "chip",
            scatter_dimension=0,
            tiled=True,
        )
        vectors[layer] = jnp.concatenate(
            [
                gtaps[: CONV + 1, :inner].reshape(-1),
                acc[0],
                vecs[0, :heads],
                vecs[1, :heads],
                dsk[0],
                grad_wdt[:, :heads].reshape(-1),
                gtaps[: CONV + 1, inner:].reshape(-1),
                grad_ngain,
            ]
        )
    vector = total(behind(jnp.stack(vectors), mark), ("zh",))
    first_sums = join_halves(behind(matrices[1][:, : 3 * inner], vector))
    vector = total(vector, ("chip",))
    other = swap(vector, "core")
    common = (CONV + 1) * BC + width
    shared = total((vector + other)[:, -common:], ("zl",))
    grad_swaps, first_sums, g_last, vector, other, shared = behind(
        (grad_swaps, first_sums, matrices[0], vector, other, shared)
    )
    input_grad = deliver(grad_own, *grad_parts, f32, grad_swaps)
    final_out = deliver(hidden_own, *out_parts, bf16, out_swaps, (first_sums,))
    last_sums = join_halves(g_last[:, : 3 * inner])
    grad_wbc = jnp.stack([g_last[:, 3 * inner :], matrices[1][:, 3 * inner :]], axis=1)
    grad_wbc = total(half_rows(grad_wbc), ("zh",))
    g_cols = [place_rows(last_sums), place_rows(first_sums)]
    by_head = jnp.where(held, vector, other)[:, :-common]
    g_bc = shared[:, :-width].reshape(LAYERS, CONV + 1, BC)
    g_ngain = shared[:, -width:]
    at = 0
    pieces = []
    for size in (CONV * inner, inner, inner, heads, heads, inner, width * heads):
        pieces.append(by_head[:, at : at + size])
        at += size
    g_conv, g_bias, g_ggain, g_alog, g_dtb, g_dsk, g_wdt = pieces
    g_wdt = g_wdt.reshape(LAYERS, width, heads)
    rows = width // lax.axis_size(("chip", "core"))
    g_wdt = lax.dynamic_slice_in_dim(g_wdt, lax.axis_index(("chip", "core")) * rows, rows, axis=1)
    return (
        final_out,
        input_grad,
        g_ngain,
        jnp.stack([g[:, inner : 2 * inner] for g in g_cols]),
        jnp.stack([g[:, 2 * inner :] for g in g_cols]),
        jnp.stack([grad_wbc[:, layer] for layer in range(LAYERS)]),
        g_wdt,
        g_conv.reshape(LAYERS, CONV, inner),
        g_bc[:, :CONV],
        g_bias,
        g_bc[:, CONV],
        g_dtb,
        g_alog,
        jnp.sum(g_dsk.reshape(LAYERS, heads, HEADDIM), axis=2),
        g_ggain,
        jnp.stack([g[:, :inner] for g in g_cols]),
    )


def join_halves(part):
    return part + lax.ppermute(part, BOTH, CROSS_BACK)


def input_gradient(grad_out, grad_normed, hidden, gain):
    inv = lax.rsqrt(jnp.mean(hidden * hidden, axis=1, keepdims=True) + epsilon)
    back = grad_normed * gain[None, :]
    return grad_out + inv * (
        back - hidden * inv * inv * jnp.mean(back * hidden, axis=1, keepdims=True)
    )


def place_rows(full):
    core, far = lax.axis_index("core"), lax.axis_index("zh")
    sent = lax.ppermute(take(full, 1 - core, 2), BOTH, CORE_OUT)
    return jnp.where(core == far, take(full, core, 2), sent)


def half_rows(part):
    core = lax.axis_index("core")
    part = take(part, core, 2) + swap(take(part, 1 - core, 2), "core")
    return total(part, ("zl",))


def solution(mesh):
    seq, head = mesh.devices.shape
    mesh = jax.sharding.Mesh(
        mesh.devices.reshape(seq // 2, 2, 2, head // 2), ("chip", "core", "zh", "zl")
    )
    tokens, columns = ("chip", "core"), ("zh", "zl")
    by_col = P(None, None, columns)
    by_head = P(None, columns)
    both = P(None, tokens, columns)
    placed = (
        P(tokens, None),
        P(tokens),
        P(tokens, None),
        P(),
        by_col,
        by_col,
        P(),
        by_col,
        by_col,
        P(),
        by_head,
        P(),
        by_head,
        by_head,
        by_head,
        by_head,
        by_col,
    )
    return jax.shard_map(
        shards,
        mesh=mesh,
        in_specs=placed,
        out_specs=(
            P(tokens, None),
            P(tokens, None),
            P(),
            both,
            both,
            P(None, tokens, None),
            both,
            by_col,
            P(),
            by_head,
            P(),
            by_head,
            by_head,
            by_head,
            by_head,
            both,
        ),
        check_vma=False,
    )
```

```python
import functools

import jax
import jax.numpy as jnp
from jax import lax
from jax.experimental import pallas as pl
from jax.experimental.pallas import tpu as pltpu
from jax.sharding import PartitionSpec as P

HEADDIM = 64
STATE = 128
CONV = 4
GROUP = 256
LAYERS = 2
INNER = 2048
LANES = 128
ROWS = 8
BC = 2 * STATE

epsilon = 1e-05
highest = lax.Precision.HIGHEST
f32 = jnp.float32
bf16 = jnp.bfloat16


def mm(left, right, dims=((1,), (0,)), precision=None):
    return lax.dot_general(
        left, right, (dims, ((), ())), preferred_element_type=f32, precision=precision
    )


def softplus(value):
    small = jnp.exp(-jnp.abs(value))
    series = small * (1.0 - small * (0.5 - small * (1.0 / 3.0 - small * (0.25 - small * 0.2))))
    return jnp.maximum(value, 0.0) + jnp.where(small < 0.03, series, jnp.log(1.0 + small))


def silu_slope(value, sigma):
    return sigma * (1.0 + value * (1.0 - sigma))


def spread(heads, expand):
    return mm(heads, expand, precision=highest)


def gather_heads(lanes, expand):
    return mm(lanes, expand, ((1,), (1,)), precision=highest)


def pick(place, pieces, held):
    if len(pieces) == 1:
        return pieces[0][...]
    away = lax.bitwise_xor(pl.program_id(0) if held is None else held, place[0])
    value = pieces[3][...]
    for number in range(3):
        value = jnp.where(away == number, pieces[number][...], value)
    return value


def in_kernel(
    place, wall, ngain, taps, bias, dtb, avec, mask, halo, expand, tri, *refs
):
    hid = refs[:-14]
    normed, cin, cpre, dtp, cum, dtv, xdt, bc, sloc, pref, send, state, thru, prev = refs[-14:]
    step = pl.program_id(0)
    inner = expand.shape[1]

    @pl.when(step == 0)
    def _():
        state[...] = jnp.zeros_like(state)
        thru[...] = jnp.ones_like(thru)
        prev[...] = halo[...]

    h = pick(place, hid, None)
    inv = lax.rsqrt(jnp.mean(h * h, axis=1, keepdims=True) + epsilon)
    low = (h * inv * ngain[...]).astype(bf16)
    normed[...] = low
    rows = mm(low, wall[:, : inner + BC])
    pre_dt = mm(low, wall[:, inner + BC :])
    dtp[...] = pre_dt
    cin[...] = rows
    ext = jnp.concatenate([prev[...], rows], axis=0)
    prev[...] = rows[GROUP - ROWS :]
    total = taps[CONV - 1 : CONV, :] * rows + bias[0:1, :]
    for k in range(CONV - 1):
        first = ROWS - CONV + 1 + k
        total = total + taps[k : k + 1, :] * ext[first : first + GROUP] * mask[:, k : k + 1]
    cpre[...] = total
    act = total * jax.nn.sigmoid(total)
    x = act[:, :inner]
    low_bc = act[:, inner:].astype(bf16)
    bc[...] = low_bc
    dt = softplus(pre_dt + dtb[0:1, :])
    dtv[...] = dt
    run = mm(tri[...], dt * avec[0:1, :], precision=highest)
    cum[...] = run
    last = run[GROUP - 1 : GROUP]
    xdt[...] = (x * spread(dt, expand[...])).astype(bf16)
    tail = jnp.exp(last - run) * mask[:, 4:5] * dt
    contrib = mm(low_bc[:, :STATE], (x * spread(tail, expand[...])).astype(bf16), ((0,), (0,)))
    through = jnp.broadcast_to(jnp.exp(last) * mask[GROUP - 1 : GROUP, 3:4], (ROWS, LANES))
    through = spread(through, expand[...])
    sloc[0] = state[...]
    pref[0] = thru[...]
    state[...] = through[0:1] * state[...] + contrib
    thru[...] = thru[...] * through

    @pl.when(step == pl.num_programs(0) - 1)
    def _():
        send[:STATE] = state[...]
        send[STATE:] = thru[...]


def pair_lanes(value, which):
    lane = lax.broadcasted_iota(jnp.int32, value.shape, 1)
    keep = lane < HEADDIM if which == 0 else lane >= HEADDIM
    return jnp.where(keep, value, jnp.zeros_like(value))


def intra_kernel(cum, xdt, bc, seg, segrow, y):
    inner = xdt.shape[1]
    run = cum[...]
    run_t = run.T
    base = mm(bc[:, STATE:], bc[:, :STATE], ((1,), (1,)))
    t_at = lax.broadcasted_iota(jnp.int32, (GROUP, GROUP), 0)
    s_at = lax.broadcasted_iota(jnp.int32, (GROUP, GROUP), 1)
    same = (seg[:, 0:1] == segrow[0:1, :]) & (t_at >= s_at)
    closed = jnp.where(same, 0.0, -1e30)
    for pair in range(inner // LANES):
        cols = slice(pair * LANES, (pair + 1) * LANES)
        xs = xdt[:, cols]
        parts = []
        for which in range(2):
            head = 2 * pair + which
            decay = jnp.exp(run[:, head : head + 1] - run_t[head : head + 1, :] + closed)
            parts.append(mm((decay * base).astype(bf16), xs))
        lane = lax.broadcasted_iota(jnp.int32, (GROUP, LANES), 1)
        y[:, cols] = jnp.where(lane < HEADDIM, parts[0], parts[1])


def out_kernel(
    yin, cpre, cum, bc, mask, zval, sloc, pref, entry, dskip, ggain, wout, expand, *refs
):
    cot, (y, gate_in, proj, sums) = refs[:-4], refs[-4:]
    inner = expand.shape[1]
    pre = cpre[...]
    x = pre * jax.nn.sigmoid(pre)
    full = sloc[0] + pref[0][0:1] * entry[...]
    reach = spread(jnp.exp(cum[...]) * mask[:, 3:4], expand[...])
    value = yin[...] + reach * mm(bc[:, STATE:], full.astype(bf16)) + dskip[0:1, :] * x
    y[...] = value
    z = zval[...]
    gated = value * (z * jax.nn.sigmoid(z))
    low = (gated * ggain[0:1, :]).astype(bf16)
    gate_in[...] = low
    proj[...] = mm(low, wout[...], ((1,), (1,)))
    ones = jnp.ones((ROWS, inner), f32)
    squares = mm(ones, gated * gated, ((1,), (1,)), precision=highest)
    if cot:
        back = mm(cot[0][...].astype(bf16), wout[...])
        dots = mm(ones, low.astype(f32) * back, ((1,), (1,)), precision=highest)
        row = lax.broadcasted_iota(jnp.int32, squares.shape, 0)
        squares = jnp.where(row == 0, squares, dots)
    sums[...] = squares


def gate_kernel(
    place, scale, gsq, y, zval, ggain, wout, cum, bc, mask, expand, *refs
):
    gh = refs[:-9]
    gproj, dy, dz, gloc, suf, send, acc, carry, thru = refs[-9:]
    step = pl.program_id(0)

    @pl.when(step == 0)
    def _():
        carry[...] = jnp.zeros_like(carry)
        thru[...] = jnp.ones_like(thru)
        acc[...] = jnp.zeros_like(acc)

    gp = (scale[...] * pick(place, gh, pl.num_programs(0) - 1 - step)).astype(bf16)
    gproj[...] = gp
    ggi = mm(gp, wout[...])
    z = zval[...]
    sigma = jax.nn.sigmoid(z)
    silu = z * sigma
    value = y[...]
    gated = value * silu
    ggated = ggi * ggain[0:1, :] + gated * gsq[...]
    acc[0:1, :] += jnp.sum(ggi * gated, axis=0, keepdims=True)
    low = (ggated * silu).astype(bf16)
    dy[...] = low
    dz[...] = (ggated * value * silu_slope(z, sigma)).astype(bf16)
    run = cum[...]
    last = run[GROUP - 1 : GROUP]
    reach = spread(jnp.exp(run) * mask[:, 3:4], expand[...])
    back = mm(bc[:, STATE:], (reach * low.astype(f32)).astype(bf16), ((0,), (0,)))
    through = jnp.broadcast_to(jnp.exp(last) * mask[GROUP - 1 : GROUP, 3:4], (ROWS, LANES))
    through = spread(through, expand[...])
    gloc[0] = carry[...]
    suf[0] = thru[...]
    carry[...] = back + through[0:1] * carry[...]
    thru[...] = thru[...] * through

    @pl.when(step == pl.num_programs(0) - 1)
    def _():
        send[:STATE] = carry[...]
        send[STATE:] = thru[...]


def intra_back_kernel(cum, xdt, bc, seg, segrow, dy, dz, wz, u, dbc, part):
    inner = xdt.shape[1]
    run = cum[...]
    run_t = run.T
    base = mm(bc[:, :STATE], bc[:, STATE:], ((1,), (1,)))
    s_at = lax.broadcasted_iota(jnp.int32, (GROUP, GROUP), 0)
    t_at = lax.broadcasted_iota(jnp.int32, (GROUP, GROUP), 1)
    same = (seg[:, 0:1] == segrow[0:1, :]) & (t_at >= s_at)
    closed = jnp.where(same, 0.0, -1e30)
    grad_base = jnp.zeros((GROUP, GROUP), f32)
    for pair in range(inner // LANES):
        cols = slice(pair * LANES, (pair + 1) * LANES)
        xs = xdt[:, cols]
        ds = dy[:, cols]
        parts = []
        for which in range(2):
            head = 2 * pair + which
            decay = jnp.exp(run_t[head : head + 1, :] - run[:, head : head + 1] + closed)
            parts.append(mm((decay * base).astype(bf16), ds))
            grad_base = grad_base + decay * mm(xs, pair_lanes(ds, which), ((1,), (1,)))
        lane = lax.broadcasted_iota(jnp.int32, (GROUP, LANES), 1)
        u[:, cols] = jnp.where(lane < HEADDIM, parts[0], parts[1])
    part[...] = mm(dz[...], wz[...], ((1,), (1,)))
    low = grad_base.astype(bf16)
    dbc[:, :STATE] = mm(low, bc[:, STATE:])
    dbc[:, STATE:] = mm(low, bc[:, :STATE], ((0,), (0,)))


def in_back_kernel(
    uin, dbc, dy, y, cpre, cin, dtp, dtv, cum, xdt, bc, mask, sloc, pref, entry, gloc, suf,
    gout, halo, taps, dtb, avec, dskip, expand, triback,
    gall, last8, rim, gtaps, vecs, dsk,
    nexts,
):
    step = pl.program_id(0)
    inner = expand.shape[1]

    @pl.when(step == 0)
    def _():
        nexts[...] = jnp.zeros_like(nexts)
        gtaps[...] = jnp.zeros_like(gtaps)
        vecs[...] = jnp.zeros_like(vecs)
        dsk[...] = jnp.zeros_like(dsk)

    e = expand[...]
    pre = cpre[...]
    sigma = jax.nn.sigmoid(pre)
    x = (pre * sigma)[:, :inner]
    full = sloc[0] + pref[0][0:1] * entry[...]
    nxt = gloc[0] + suf[0][0:1] * gout[...]
    nxt_low = nxt.astype(bf16)
    run = cum[...]
    last = run[GROUP - 1 : GROUP]
    dt = dtv[...]
    low_dy = dy[...].astype(f32)
    xw = xdt[...].astype(f32)
    tail = spread(jnp.exp(last - run) * mask[:, 4:5], e)
    reach = spread(jnp.exp(run) * mask[:, 3:4], e)
    u_inter = tail * mm(bc[:, :STATE], nxt_low)
    u = uin[...] + u_inter
    dx = spread(dt, e) * u + dskip[0:1, :] * low_dy
    dsk[0:1, :] += jnp.sum(low_dy * x, axis=0, keepdims=True)
    db = dbc[:, :STATE] + mm((tail * xw).astype(bf16), nxt_low, ((1,), (1,)))
    dc = dbc[:, STATE:] + mm((reach * low_dy).astype(bf16), full.astype(bf16), ((1,), (1,)))
    grad_dt = gather_heads(x * u, e)
    y_plain = y[...] - dskip[0:1, :] * x
    grad_cum = gather_heads(low_dy * y_plain - xw * u, e)
    flow = jnp.sum(nxt * full, axis=0, keepdims=True)
    flow = gather_heads(jnp.broadcast_to(flow, (ROWS, inner)), e)[0:1]
    ends = jnp.sum(xw * u_inter, axis=0, keepdims=True)
    ends = gather_heads(jnp.broadcast_to(ends, (ROWS, inner)), e)[0:1]
    grad_tot = mask[GROUP - 1 : GROUP, 3:4] * jnp.exp(last) * flow + ends
    grad_da = mm(triback[...], grad_cum, precision=highest) + grad_tot
    a = avec[0:1, :]
    grad_dtv = grad_dt + grad_da * a
    grad_dtpre = grad_dtv * jax.nn.sigmoid(dtp[...] + dtb[0:1, :])
    vecs[0:1, :] += jnp.sum(grad_da * dt, axis=0, keepdims=True) * a
    vecs[1:2, :] += jnp.sum(grad_dtpre, axis=0, keepdims=True)
    slope = silu_slope(pre, sigma)
    grad_pre = jnp.concatenate([dx, db, dc], axis=1) * slope
    gtaps[4:5, :] += jnp.sum(grad_pre, axis=0, keepdims=True)
    rows = cin[...]
    grad_rows = taps[CONV - 1 : CONV, :] * grad_pre
    gtaps[3:4, :] += jnp.sum(rows * grad_pre, axis=0, keepdims=True)
    masked = []
    for k in range(CONV - 1):
        m = grad_pre * mask[:, k : k + 1]
        masked.append(m[:ROWS])
        ahead = CONV - 1 - k
        shifted = jnp.concatenate([m, nexts[k]], axis=0)[ahead : ahead + GROUP]
        grad_rows = grad_rows + taps[k : k + 1, :] * shifted
        gtaps[k : k + 1, :] += jnp.sum(rows * shifted, axis=0, keepdims=True)
    for k in range(CONV - 1):
        nexts[k] = masked[k]
    gall[:, : inner + BC] = grad_rows.astype(bf16)
    gall[:, inner + BC :] = grad_dtpre.astype(bf16)

    @pl.when(step == 0)
    def _():
        last8[...] = grad_rows[GROUP - ROWS :]

    @pl.when(step == pl.num_programs(0) - 1)
    def _():
        spill = jnp.zeros((ROWS, inner + BC), f32)
        edge = halo[...]
        for k in range(CONV - 1):
            down = ROWS - CONV + 1 + k
            moved = jnp.concatenate([jnp.zeros((ROWS, inner + BC), f32), masked[k]], axis=0)
            moved = moved[ROWS - down : 2 * ROWS - down]
            spill = spill + taps[k : k + 1, :] * moved
            gtaps[k : k + 1, :] += jnp.sum(edge * moved, axis=0, keepdims=True)
        rim[...] = spill


def whole(shape):
    return pl.BlockSpec(shape, lambda c: (0,) * len(shape))


def by_rows(cols, count, reverse=False):
    if reverse:
        return pl.BlockSpec((GROUP, cols), lambda c: (count - 1 - c, 0))
    return pl.BlockSpec((GROUP, cols), lambda c: (c, 0))


def by_group(shape, count, reverse=False):
    if reverse:
        return pl.BlockSpec((1,) + shape, lambda c: (count - 1 - c, 0, 0))
    return pl.BlockSpec((1,) + shape, lambda c: (c, 0, 0))


def by_piece(pieces, count, reverse=False):
    if len(pieces) == 1:
        return [(by_rows(pieces[0].shape[1], count, reverse), pieces[0])]
    return [(whole(piece.shape), piece) for piece in pieces]


def by_cols(count):
    return pl.BlockSpec((ROWS, GROUP), lambda c: (0, c))


def call(kernel, count, ins, outs, scratch, micros, name):
    return pl.pallas_call(
        kernel,
        grid=(count,),
        in_specs=[spec for spec, _ in ins],
        out_specs=[spec for spec, _ in outs],
        out_shape=[shape for _, shape in outs],
        scratch_shapes=scratch,
        compiler_params=pltpu.CompilerParams(
            dimension_semantics=("arbitrary",), vmem_limit_bytes=56 * 1024 * 1024
        ),
        cost_estimate=pl.CostEstimate(
            flops=micros * 1_150_000_000, bytes_accessed=1024 * 1024, transcendentals=0
        ),
        name=name,
    )(*[value for _, value in ins])


def shape(*dims, dtype=f32):
    return jax.ShapeDtypeStruct(dims, dtype)


SWAP = ((0, 1), (1, 0))
CROSS = ((0, 1), (3, 2))
CROSS_BACK = ((1, 0), (2, 3))
CORE_OUT = ((0, 2), (3, 1))
CORE_IN = ((2, 0), (1, 3))
DIAGONAL = ((2, 1), (1, 2))
BOTH = ("core", "zh")
BLOCKS = ("chip", "zh")


def shifted(value, steps):
    count = lax.axis_size(BLOCKS)
    leading, last = (max(0, -steps), min(count, count - steps))
    return lax.ppermute(value, BLOCKS, [(source, source + steps) for source in range(leading, last)])


def chain(part, reverse, stages):
    count = lax.axis_size(BLOCKS)
    place = lax.axis_index(BLOCKS)
    state, decay = part[:STATE], part[STATE : STATE + 1]
    entry, reach = jnp.zeros_like(state), jnp.ones_like(decay)
    step = 1
    while step < count:
        got = lax.ppermute(part, BLOCKS, [(i, i ^ step) for i in range(count)])
        got_state, got_decay = got[:STATE], got[STATE : STATE + 1]
        later = ((place & step) == 0) if reverse else ((place & step) != 0)
        stages.append(got)
        entry = jnp.where(later, entry + reach * got_state, entry)
        reach = jnp.where(later, reach * got_decay, reach)
        state = jnp.where(later, state + decay * got_state, got_state + got_decay * state)
        decay = decay * got_decay
        part = jnp.concatenate([state, jnp.broadcast_to(decay, (ROWS, decay.shape[1]))])
        step *= 2
    return entry


def swap(value, axis):
    return lax.ppermute(value, axis, SWAP)


def total(value, axes):
    for axis in axes:
        count = lax.axis_size(axis)
        step = 1
        while step < count:
            value = value + lax.ppermute(value, axis, [(i, i ^ step) for i in range(count)])
            step *= 2
    return value


def take(value, index, count):
    size = value.shape[0] // count
    return lax.dynamic_slice_in_dim(value, index * size, size)


def ordered(place, mine, theirs):
    return jnp.where(
        place == 0, jnp.concatenate([mine, theirs]), jnp.concatenate([theirs, mine])
    )


def behind(value, *marks):
    return lax.optimization_barrier((value, *marks))[0]


def scatter_sum(part, mark=()):
    core, near = lax.axis_index("core"), lax.axis_index("zl")
    half = take(part, core, 2) + behind(swap(take(part, 1 - core, 2), "core"), *mark)
    if lax.axis_size("zl") == 2:
        return take(half, near, 2) + swap(take(half, 1 - near, 2), "zl")
    return lax.psum_scatter(half, "zl", scatter_dimension=0, tiled=True)


def own_rows(value):
    core, near = lax.axis_index("core"), lax.axis_index("zl")
    return take(take(value, core, 2), near, lax.axis_size("zl"))


def gather_near(value):
    if lax.axis_size("zl") == 2:
        return ordered(lax.axis_index("zl"), value, swap(value, "zl"))
    return lax.all_gather(value, "zl", tiled=True)


def gather_rows(value):
    half = gather_near(value)
    return ordered(lax.axis_index("core"), half, swap(half, "core"))


def own_place():
    return 2 * lax.axis_index("core") + lax.axis_index("zl")


def gather_pieces(value):
    if lax.axis_size("zl") != 2 or value.shape[0] != GROUP:
        return [gather_rows(value)]
    near = swap(value, "zl")
    return [value, near, swap(value, "core"), swap(near, "core")]


def place_kernel(place, value, mine, near, theirs, value_s, mine_s, near_s, theirs_s, out):
    away = lax.bitwise_xor(pl.program_id(0), place[0])
    pairs = ((value, mine), (value_s, mine_s), (near, theirs), (near_s, theirs_s))
    for number, (here, there) in enumerate(pairs):

        @pl.when((away == number) & (place[1] == 1))
        def _():
            out[...] = here[...].astype(out.dtype)

        @pl.when((away == number) & (place[1] == 0))
        def _():
            out[...] = there[...].astype(out.dtype)


def cross_over(value):
    return [lax.ppermute(value, BOTH, pairs) for pairs in (CROSS, DIAGONAL, CORE_IN)]


def near_swap(value):
    if lax.axis_size("zl") != 2 or value.shape[0] != GROUP:
        return None
    here = [(2 * kind + i, 2 * kind + 1 - i) for kind in (0, 3) for i in range(2)]
    return lax.ppermute(value, ("core", "zh", "zl"), here)


def near_swaps(value, mine, theirs, near, value_s=None, near_s=None):
    if lax.axis_size("zl") != 2 or value.shape[0] != GROUP:
        return None
    axes = ("core", "zh", "zl")
    there = [(2 * kind + i, 2 * kind + 1 - i) for kind in (1, 2) for i in range(2)]
    return (
        near_swap(value) if value_s is None else value_s,
        lax.ppermute(mine, axes, there),
        lax.ppermute(theirs, axes, there),
        near_swap(near) if near_s is None else near_s,
    )


def deliver(value, mine, theirs, near, dtype, swaps=None, mark=()):
    core, far = lax.axis_index("core"), lax.axis_index("zh")
    held = core == far
    if lax.axis_size("zl") != 2 or value.shape[0] != GROUP:
        mine = gather_near(jnp.where(held, value, mine))
        theirs = gather_near(jnp.where(held, near, theirs))
        full = ordered(core, mine, theirs)
        return narrowed(full) if dtype == bf16 else full
    if swaps is None:
        swaps = near_swaps(value, mine, theirs, near)
    value_s, mine_s, theirs_s, near_s = swaps
    place = jnp.stack([own_place(), held.astype(jnp.int32)]).astype(jnp.int32)
    width = value.shape[1]
    parts = behind((value, mine, near, theirs, value_s, mine_s, near_s, theirs_s), *mark)
    return pl.pallas_call(
        place_kernel,
        grid=(4,),
        in_specs=[pl.BlockSpec(memory_space=pltpu.SMEM)] + [whole((GROUP, width))] * 8,
        out_specs=by_rows(width, 4),
        out_shape=shape(4 * GROUP, width, dtype=dtype),
        compiler_params=pltpu.CompilerParams(
            dimension_semantics=("arbitrary",), vmem_limit_bytes=40 * 1024 * 1024
        ),
        name="place",
    )(place, *parts)


def to_block(value):
    got = lax.ppermute(value, BOTH, CORE_OUT)
    return jnp.where(lax.axis_index("core") == lax.axis_index("zh"), value, got)


def eight(row):
    return jnp.broadcast_to(row[None, :], (ROWS, row.shape[0]))


def pad_lanes(value):
    return jnp.pad(value, [(0, 0)] * (value.ndim - 1) + [(0, LANES - value.shape[-1])])


def weight_kernel(count, extra, place, *refs):
    own, rest = refs[:count], refs[count:]
    outs, rest = rest[-count:], rest[:-count]
    parts, more = (rest[:-2], rest[-2:]) if extra else (rest, ())
    block = pl.program_id(0)
    at = 0
    for source, out in zip(own, outs):
        cols = source.shape[1]

        @pl.when(place[1] == 1)
        def _():
            out[:, :cols] = source[...]

        for away, part in enumerate(parts):

            @pl.when((place[1] == 0) & (lax.bitwise_xor(place[0], block) == away))
            def _():
                out[:, :cols] = part[:, at : at + cols].astype(bf16)

        at += cols
    if more:
        cols = own[0].shape[1]
        outs[0][:, cols : cols + BC] = more[0][...]
        outs[0][:, cols + BC :] = more[1][...].astype(bf16)


def narrow_kernel(wide, narrow):
    narrow[...] = wide[...].astype(bf16)


def narrowed(value):
    rows, cols = value.shape
    return pl.pallas_call(
        narrow_kernel,
        grid=(rows // GROUP,),
        in_specs=[by_rows(cols, 0)],
        out_specs=by_rows(cols, 0),
        out_shape=shape(rows, cols, dtype=bf16),
        name="narrowed",
    )(value)


def weights_over(own, *marks):
    chips = lax.axis_size("chip")
    piece = jnp.concatenate(
        [take(value, lax.axis_index("chip"), chips).astype(f32) for value in behind(own, *marks)],
        axis=1,
    )
    return lax.ppermute(piece, BOTH, CROSS)


def gather_weights(piece, own, more=(), third=()):
    width = own[0].shape[0]
    chips = lax.axis_size("chip")
    chip = lax.axis_index("chip")
    held = (lax.axis_index("core") == lax.axis_index("zh")).astype(jnp.int32)
    size = width // chips
    if chips == 4:
        parts = [piece]
        for away in range(1, chips):
            pairs = [
                (4 * c + kind, 4 * (c ^ away) + kind) for c in range(chips) for kind in (1, 2)
            ]
            parts.append(lax.ppermute(piece, ("chip", "core", "zh"), pairs))
        place = jnp.stack([chip, held]).astype(jnp.int32)
        blocks = chips
    else:
        parts = [lax.all_gather(piece, "chip", tiled=True)]
        place = jnp.stack([0, held]).astype(jnp.int32)
        blocks, size = 1, width
    parts = behind(parts, *third)
    out_cols = [value.shape[1] for value in own]
    out_cols[0] += sum(value.shape[1] for value in more)

    def rows(cols):
        return pl.BlockSpec((size, cols), lambda c: (c, 0))

    return pl.pallas_call(
        functools.partial(weight_kernel, len(own), bool(more)),
        grid=(blocks,),
        in_specs=[pl.BlockSpec(memory_space=pltpu.SMEM)]
        + [rows(value.shape[1]) for value in own]
        + [whole(piece.shape if chips == 4 else parts[0].shape)] * len(parts)
        + [rows(value.shape[1]) for value in more],
        out_specs=[rows(cols) for cols in out_cols],
        out_shape=[shape(width, cols, dtype=bf16) for cols in out_cols],
        compiler_params=pltpu.CompilerParams(
            dimension_semantics=("arbitrary",), vmem_limit_bytes=40 * 1024 * 1024
        ),
        name="weights",
    )(place, *own, *parts, *more)


def shards(
    x_input,
    seg_ids,
    cotangent,
    norm_gain,
    w_z,
    w_x,
    w_bc,
    w_dt,
    conv_x,
    conv_bc,
    bias_x,
    bias_bc,
    dt_bias,
    a_log,
    d_skip,
    gate_gain,
    w_out,
):
    tok, width = x_input.shape
    inner = w_z.shape[2]
    core, far = lax.axis_index("core"), lax.axis_index("zh")
    held = core == far
    heads = w_dt.shape[2]
    count = tok // GROUP
    conv_cols = inner + BC
    all_cols = inner + BC + LANES

    dt_own = w_dt.astype(f32).reshape(LAYERS, width * heads // LANES, LANES)
    dt_sent = lax.ppermute(dt_own, BOTH, CROSS)
    dt_all = pad_lanes(jnp.where(held, dt_own, dt_sent).reshape(LAYERS, width, heads))
    first_x = weights_over([w_x[0]])
    hidden = to_block(x_input.astype(f32))
    first_rest = weights_over([w_z[0], w_out[0]], first_x)
    (wall,) = gather_weights(first_x, [w_x[0]], (w_bc[0], dt_all[0]), (first_rest,))
    seg = to_block(seg_ids.astype(f32))
    small = jnp.concatenate(
        [
            value.reshape(LAYERS, -1)
            for value in (conv_x, bias_x, dt_bias, a_log, d_skip, gate_gain)
        ],
        axis=1,
    )
    small = jnp.where(held, small, lax.ppermute(small, BOTH, CROSS))
    sizes = (CONV * inner, inner, heads, heads, heads, inner)
    pieces, at = [], 0
    for size in sizes:
        pieces.append(small[:, at : at + size])
        at += size
    conv_x, bias_x, dt_bias, a_log, d_skip, gate_gain = pieces
    conv_x = conv_x.reshape(LAYERS, CONV, inner)
    hidden_own = own_rows(hidden)
    hidden_block = hidden
    hidden = [hidden]
    place = jnp.stack([own_place(), own_place()]).astype(jnp.int32)
    smem = pl.BlockSpec(memory_space=pltpu.SMEM)
    edge_seg = shifted(seg[tok - ROWS :], 1)
    seg_ext = jnp.concatenate([edge_seg, seg])
    before = jnp.concatenate([edge_seg[ROWS - 1 :], seg[GROUP - 1 : tok - 1 : GROUP]])
    after = seg[GROUP - 1 :: GROUP]
    mask = jnp.stack(
        [
            (seg_ext[ROWS - CONV + 1 + k : ROWS - CONV + 1 + k + tok] == seg).astype(f32)
            for k in range(CONV - 1)
        ]
        + [
            (seg == jnp.repeat(before, GROUP)).astype(f32),
            (seg == jnp.repeat(after, GROUP)).astype(f32),
            seg,
            seg,
            seg,
        ],
        axis=1,
    )
    seg_col = seg[:, None]
    seg_row = eight(seg)
    expand = (jnp.arange(LANES)[:, None] == jnp.arange(inner)[None, :] // HEADDIM).astype(f32)
    position = jnp.arange(GROUP)
    tri = (position[:, None] >= position[None, :]).astype(f32)
    triback = (position[:, None] <= position[None, :]).astype(f32)

    stored = []
    for layer in range(LAYERS):
        if layer > 0:
            wall = next_wall
        taps = jnp.concatenate([conv_x[layer], conv_bc[layer]], axis=1)
        bias = eight(jnp.concatenate([bias_x[layer], bias_bc[layer]]))
        dtb = eight(pad_lanes(dt_bias[layer]))
        avec = eight(pad_lanes(-jnp.exp(a_log[layer])))
        dskip = eight(jnp.repeat(d_skip[layer], HEADDIM))
        ggain = eight(gate_gain[layer])
        ngain = norm_gain[layer][None, :]
        if len(hidden) == 1:
            end = hidden[0][tok - 16 :]
        else:
            ends = jnp.stack([piece[GROUP - 16 :] for piece in hidden])
            end = lax.dynamic_index_in_dim(ends, 3 ^ own_place(), 0, False)
        end = end * lax.rsqrt(jnp.mean(end * end, axis=1, keepdims=True) + epsilon) * ngain
        end = mm(end.astype(bf16), wall[:, : inner + BC])[ROWS:]
        halo = shifted(end, 1)
        normed, cin, cpre, dtp, cum, dtv, xdt, bc, sloc, pref, send = call(
            in_kernel,
            count,
            [
                (smem, place),
                (whole((width, all_cols)), wall),
                (whole((1, width)), ngain),
                (whole((CONV, conv_cols)), taps),
                (whole((ROWS, conv_cols)), bias),
                (whole((ROWS, LANES)), dtb),
                (whole((ROWS, LANES)), avec),
                (by_rows(ROWS, count), mask),
                (whole((ROWS, conv_cols)), halo),
                (whole((LANES, inner)), expand),
                (whole((GROUP, GROUP)), tri),
            ]
            + by_piece(hidden, count),
            [
                (by_rows(width, count), shape(tok, width, dtype=bf16)),
                (by_rows(conv_cols, count), shape(tok, conv_cols)),
                (by_rows(conv_cols, count), shape(tok, conv_cols)),
                (by_rows(LANES, count), shape(tok, LANES)),
                (by_rows(LANES, count), shape(tok, LANES)),
                (by_rows(LANES, count), shape(tok, LANES)),
                (by_rows(inner, count), shape(tok, inner, dtype=bf16)),
                (by_rows(BC, count), shape(tok, BC, dtype=bf16)),
                (by_group((STATE, inner), count), shape(count, STATE, inner)),
                (by_group((ROWS, inner), count), shape(count, ROWS, inner)),
                (whole((STATE + ROWS, inner)), shape(STATE + ROWS, inner)),
            ],
            [
                pltpu.VMEM((STATE, inner), f32),
                pltpu.VMEM((ROWS, inner), f32),
                pltpu.VMEM((ROWS, conv_cols), f32),
            ],
            16,
            "in_proj_conv",
        )
        if layer == 0:
            wz, wout = gather_weights(
                behind(first_rest, wall), [w_z[0], w_out[0]], third=(send,)
            )
        else:
            wz, wout = next_wz, next_wout
        zval = mm(normed, wz)
        (yin,) = call(
            intra_kernel,
            count,
            [
                (by_rows(LANES, count), cum),
                (by_rows(inner, count), xdt),
                (by_rows(BC, count), bc),
                (by_rows(1, count), seg_col),
                (by_cols(count), seg_row),
            ],
            [(by_rows(inner, count), shape(tok, inner))],
            [],
            6,
            "ssd_within",
        )
        stages = []
        entry = chain(send, False, stages)
        if layer == 0:
            second_all = weights_over([w_x[1], w_z[1], w_out[1]], stages[0])
            cotangent = behind(cotangent, stages[0]).astype(f32)
            cot_sent = lax.ppermute(cotangent, BOTH, CORE_OUT)
            entry = behind(entry, second_all, cot_sent)
            cotangent = jnp.where(held, cotangent, cot_sent)
        y, gate_in, proj, sums = call(
            out_kernel,
            count,
            [
                (by_rows(inner, count), yin),
                (by_rows(inner, count), cpre),
                (by_rows(LANES, count), cum),
                (by_rows(BC, count), bc),
                (by_rows(ROWS, count), mask),
                (by_rows(inner, count), zval),
                (by_group((STATE, inner), count), sloc),
                (by_group((ROWS, inner), count), pref),
                (whole((STATE, inner)), entry),
                (whole((ROWS, inner)), dskip),
                (whole((ROWS, inner)), ggain),
                (whole((width, inner)), wout),
                (whole((LANES, inner)), expand),
            ]
            + ([(by_rows(width, count), cotangent)] if layer == LAYERS - 1 else []),
            [
                (by_rows(inner, count), shape(tok, inner)),
                (by_rows(inner, count), shape(tok, inner, dtype=bf16)),
                (by_rows(width, count), shape(tok, width)),
                (by_cols(count), shape(ROWS, tok)),
            ],
            [],
            12,
            "gate_out_proj",
        )
        sums = total(sums, ("core", "zl"))
        gate_scale = lax.rsqrt(sums[0] / INNER + epsilon)
        stored.append(
            dict(
                hidden=hidden_own, normed=normed, zval=zval, cin=cin, cpre=cpre, dtp=dtp, cum=cum,
                dtv=dtv, xdt=xdt, bc=bc, sloc=sloc, pref=pref, entry=entry, y=y, gate_in=gate_in,
                proj=proj, gate_scale=gate_scale, dots=sums[1], halo=halo, wall=wall, wz=wz, wout=wout,
                taps=taps, dtb=dtb, avec=avec, dskip=dskip, ggain=ggain,
            )
        )
        if layer < LAYERS - 1:
            proj_sum = scatter_sum(proj)
            stored[layer]["proj_sum"] = proj_sum
            hidden_own = hidden_own + own_rows(gate_scale)[:, None] * proj_sum
            next_wall, next_wz, next_wout = gather_weights(
                behind(second_all, proj),
                [w_x[1], w_z[1], w_out[1]],
                (w_bc[1], dt_all[1]),
                third=(hidden_own,),
            )
            hidden = gather_pieces(hidden_own)

    grad_h = [cotangent]
    grad_own = own_rows(cotangent)
    matrices = [None] * LAYERS
    vectors = [None] * LAYERS
    shared = [None] * LAYERS
    for layer in reversed(range(LAYERS)):
        kept = stored[layer]
        gate_scale = kept["gate_scale"]
        if layer == LAYERS - 1:
            grad_scale = kept["dots"]
        else:
            grad_scale = gather_rows(jnp.sum(grad_own * kept["proj_sum"], axis=1))
        gsq = -grad_scale * gate_scale**3 / INNER
        rev = functools.partial(by_rows, count=count, reverse=True)
        rev_group = functools.partial(by_group, count=count, reverse=True)
        gproj, dy, dz, gloc, suf, gsend, acc = call(
            gate_kernel,
            count,
            [
                (smem, place),
                (rev(1), gate_scale[:, None]),
                (rev(1), gsq[:, None]),
                (rev(inner), kept["y"]),
                (rev(inner), kept["zval"]),
                (whole((ROWS, inner)), kept["ggain"]),
                (whole((width, inner)), kept["wout"]),
                (rev(LANES), kept["cum"]),
                (rev(BC), kept["bc"]),
                (rev(ROWS), mask),
                (whole((LANES, inner)), expand),
            ]
            + by_piece(grad_h, count, True),
            [
                (rev(width), shape(tok, width, dtype=bf16)),
                (rev(inner), shape(tok, inner, dtype=bf16)),
                (rev(inner), shape(tok, inner, dtype=bf16)),
                (rev_group((STATE, inner)), shape(count, STATE, inner)),
                (rev_group((ROWS, inner)), shape(count, ROWS, inner)),
                (whole((STATE + ROWS, inner)), shape(STATE + ROWS, inner)),
                (whole((ROWS, inner)), shape(ROWS, inner)),
            ],
            [pltpu.VMEM((STATE, inner), f32), pltpu.VMEM((ROWS, inner), f32)],
            10,
            "gate_back",
        )
        if layer == LAYERS - 1:
            last_sum = scatter_sum(kept["proj"], (gate_scale,))
            hidden_own = hidden_own + own_rows(gate_scale)[:, None] * last_sum
            dy = behind(dy, hidden_own)
            gsend = behind(gsend, hidden_own)
            out_parts = cross_over(hidden_own)
            out_held = (near_swap(hidden_own), near_swap(out_parts[2]))
        u, dbc, partial_z = call(
            intra_back_kernel,
            count,
            [
                (by_rows(LANES, count), kept["cum"]),
                (by_rows(inner, count), kept["xdt"]),
                (by_rows(BC, count), kept["bc"]),
                (by_rows(1, count), seg_col),
                (by_cols(count), seg_row),
                (by_rows(inner, count), dy),
                (by_rows(inner, count), dz),
                (whole((width, inner)), kept["wz"]),
            ],
            [
                (by_rows(inner, count), shape(tok, inner)),
                (by_rows(BC, count), shape(tok, BC)),
                (by_rows(width, count), shape(tok, width)),
            ],
            [],
            8,
            "ssd_within_back",
        )
        stages = []
        gout = chain(gsend, True, stages)
        round_one = stages[0]
        if layer == 0:
            out_swaps = near_swaps(hidden_own, *behind(out_parts, round_one), *out_held)
        grad_wout = mm(gproj, kept["gate_in"], ((0,), (0,)))
        grad_wz = mm(kept["normed"], dz, ((0,), (0,)))
        u = behind(u, grad_wout, grad_wz)
        gall, last8, rim, gtaps, vecs, dsk = call(
            in_back_kernel,
            count,
            [
                (rev(inner), u),
                (rev(BC), dbc),
                (rev(inner), dy),
                (rev(inner), kept["y"]),
                (rev(conv_cols), kept["cpre"]),
                (rev(conv_cols), kept["cin"]),
                (rev(LANES), kept["dtp"]),
                (rev(LANES), kept["dtv"]),
                (rev(LANES), kept["cum"]),
                (rev(inner), kept["xdt"]),
                (rev(BC), kept["bc"]),
                (rev(ROWS), mask),
                (rev_group((STATE, inner)), kept["sloc"]),
                (rev_group((ROWS, inner)), kept["pref"]),
                (whole((STATE, inner)), kept["entry"]),
                (rev_group((STATE, inner)), gloc),
                (rev_group((ROWS, inner)), suf),
                (whole((STATE, inner)), gout),
                (whole((ROWS, conv_cols)), kept["halo"]),
                (whole((CONV, conv_cols)), kept["taps"]),
                (whole((ROWS, LANES)), kept["dtb"]),
                (whole((ROWS, LANES)), kept["avec"]),
                (whole((ROWS, inner)), kept["dskip"]),
                (whole((LANES, inner)), expand),
                (whole((GROUP, GROUP)), triback),
            ],
            [
                (rev(all_cols), shape(tok, all_cols, dtype=bf16)),
                (whole((ROWS, conv_cols)), shape(ROWS, conv_cols)),
                (whole((ROWS, conv_cols)), shape(ROWS, conv_cols)),
                (whole((ROWS, conv_cols)), shape(ROWS, conv_cols)),
                (whole((ROWS, LANES)), shape(ROWS, LANES)),
                (whole((ROWS, inner)), shape(ROWS, inner)),
            ],
            [pltpu.VMEM((CONV - 1, ROWS, conv_cols), f32)],
            20,
            "in_proj_conv_back",
        )
        rim_back = shifted(rim, -1)
        if layer == 0:
            last8 = behind(last8, matrices[1], *(out_swaps or ()))
        else:
            last8 = behind(last8, *out_parts, *(out_held if out_held[0] is not None else ()))
        gall = lax.dynamic_update_slice(
            gall, (last8 + rim_back).astype(bf16), (tok - ROWS, 0)
        )
        partial = partial_z + mm(gall, kept["wall"], ((1,), (1,)))
        late = behind(gall, partial)
        grad_wbc = mm(kept["normed"], late[:, inner : inner + BC], ((0,), (0,)))
        grad_win = mm(kept["normed"], behind(late, grad_wbc)[:, :inner], ((0,), (0,)))
        grad_normed = scatter_sum(partial, (grad_win,) if layer == 0 else ())
        if layer == 0:
            grad_own = input_gradient(grad_own, grad_normed, kept["hidden"], norm_gain[layer])
            grad_parts = cross_over(grad_own)
            own_s = near_swap(grad_own)
            late, partial = behind((gall, partial), grad_parts[2])
            grad_parts, own_s, _ = behind((grad_parts, own_s, grad_win))
            mark = grad_parts[0]
            grad_swaps = near_swaps(grad_own, *grad_parts, own_s)
        grad_wdt = mm(kept["normed"], late[:, inner + BC :], ((0,), (0,)))
        hidden_in = kept["hidden"]
        inv = lax.rsqrt(jnp.mean(hidden_in * hidden_in, axis=1, keepdims=True) + epsilon)
        if layer == 0:
            full = hidden_block
            grad_ngain = jnp.sum(
                partial
                * (full * lax.rsqrt(jnp.mean(full * full, axis=1, keepdims=True) + epsilon)),
                axis=0,
            )
        else:
            grad_ngain = jnp.sum(grad_normed * hidden_in * inv, axis=0)
        if layer > 0:
            grad_own = input_gradient(grad_own, grad_normed, hidden_in, norm_gain[layer])
            grad_h = gather_pieces(grad_own)
        matrices[layer] = lax.psum_scatter(
            jnp.concatenate([grad_wout, grad_wz, grad_win, grad_wbc], axis=1),
            "chip",
            scatter_dimension=0,
            tiled=True,
        )
        vectors[layer] = jnp.concatenate(
            [
                gtaps[: CONV + 1, :inner].reshape(-1),
                acc[0],
                vecs[0, :heads],
                vecs[1, :heads],
                dsk[0],
                grad_wdt[:, :heads].reshape(-1),
                gtaps[: CONV + 1, inner:].reshape(-1),
                grad_ngain,
            ]
        )
    vector = total(behind(jnp.stack(vectors), mark), ("zh",))
    common = (CONV + 1) * BC + width
    vector = jnp.concatenate(
        [vector[:, :-common], total(vector[:, -common:], ("zl",))], axis=1
    )
    first_sums = join_halves(behind(matrices[1][:, : 3 * inner], vector))
    vector = total(vector, ("chip",))
    other = swap(vector, "core")
    shared = (vector + other)[:, -common:]
    grad_swaps, first_sums, g_last, vector, other, shared = behind(
        (grad_swaps, first_sums, matrices[0], vector, other, shared)
    )
    input_grad = deliver(grad_own, *grad_parts, f32, grad_swaps)
    final_out = deliver(hidden_own, *out_parts, bf16, out_swaps, (first_sums,))
    last_sums = join_halves(g_last[:, : 3 * inner])
    grad_wbc = jnp.stack([g_last[:, 3 * inner :], matrices[1][:, 3 * inner :]], axis=1)
    grad_wbc = total(half_rows(grad_wbc), ("zh",))
    g_cols = [place_rows(last_sums), place_rows(first_sums)]
    by_head = jnp.where(held, vector, other)[:, :-common]
    g_bc = shared[:, :-width].reshape(LAYERS, CONV + 1, BC)
    g_ngain = shared[:, -width:]
    at = 0
    pieces = []
    for size in (CONV * inner, inner, inner, heads, heads, inner, width * heads):
        pieces.append(by_head[:, at : at + size])
        at += size
    g_conv, g_bias, g_ggain, g_alog, g_dtb, g_dsk, g_wdt = pieces
    g_wdt = g_wdt.reshape(LAYERS, width, heads)
    rows = width // lax.axis_size(("chip", "core"))
    g_wdt = lax.dynamic_slice_in_dim(g_wdt, lax.axis_index(("chip", "core")) * rows, rows, axis=1)
    return (
        final_out,
        input_grad,
        g_ngain,
        jnp.stack([g[:, inner : 2 * inner] for g in g_cols]),
        jnp.stack([g[:, 2 * inner :] for g in g_cols]),
        jnp.stack([grad_wbc[:, layer] for layer in range(LAYERS)]),
        g_wdt,
        g_conv.reshape(LAYERS, CONV, inner),
        g_bc[:, :CONV],
        g_bias,
        g_bc[:, CONV],
        g_dtb,
        g_alog,
        jnp.sum(g_dsk.reshape(LAYERS, heads, HEADDIM), axis=2),
        g_ggain,
        jnp.stack([g[:, :inner] for g in g_cols]),
    )


def join_halves(part):
    return part + lax.ppermute(part, BOTH, CROSS_BACK)


def input_gradient(grad_out, grad_normed, hidden, gain):
    inv = lax.rsqrt(jnp.mean(hidden * hidden, axis=1, keepdims=True) + epsilon)
    back = grad_normed * gain[None, :]
    return grad_out + inv * (
        back - hidden * inv * inv * jnp.mean(back * hidden, axis=1, keepdims=True)
    )


def place_rows(full):
    core, far = lax.axis_index("core"), lax.axis_index("zh")
    sent = lax.ppermute(take(full, 1 - core, 2), BOTH, CORE_OUT)
    return jnp.where(core == far, take(full, core, 2), sent)


def half_rows(part):
    core = lax.axis_index("core")
    part = take(part, core, 2) + swap(take(part, 1 - core, 2), "core")
    return total(part, ("zl",))


def solution(mesh):
    seq, head = mesh.devices.shape
    mesh = jax.sharding.Mesh(
        mesh.devices.reshape(seq // 2, 2, 2, head // 2), ("chip", "core", "zh", "zl")
    )
    tokens, columns = ("chip", "core"), ("zh", "zl")
    by_col = P(None, None, columns)
    by_head = P(None, columns)
    both = P(None, tokens, columns)
    placed = (
        P(tokens, None),
        P(tokens),
        P(tokens, None),
        P(),
        by_col,
        by_col,
        P(),
        by_col,
        by_col,
        P(),
        by_head,
        P(),
        by_head,
        by_head,
        by_head,
        by_head,
        by_col,
    )
    return jax.shard_map(
        shards,
        mesh=mesh,
        in_specs=placed,
        out_specs=(
            P(tokens, None),
            P(tokens, None),
            P(),
            both,
            both,
            P(None, tokens, None),
            both,
            by_col,
            P(),
            by_head,
            P(),
            by_head,
            by_head,
            by_head,
            by_head,
            both,
        ),
        check_vma=False,
    )
```

```python
import functools

import jax
import jax.numpy as jnp
from jax import lax
from jax.experimental import pallas as pl
from jax.experimental.pallas import tpu as pltpu
from jax.sharding import PartitionSpec as P

HEADDIM = 64
STATE = 128
CONV = 4
GROUP = 256
LAYERS = 2
INNER = 2048
LANES = 128
ROWS = 8
BC = 2 * STATE

epsilon = 1e-05
highest = lax.Precision.HIGHEST
f32 = jnp.float32
bf16 = jnp.bfloat16


def mm(left, right, dims=((1,), (0,)), precision=None):
    return lax.dot_general(
        left, right, (dims, ((), ())), preferred_element_type=f32, precision=precision
    )


def softplus(value):
    small = jnp.exp(-jnp.abs(value))
    series = small * (1.0 - small * (0.5 - small * (1.0 / 3.0 - small * (0.25 - small * 0.2))))
    return jnp.maximum(value, 0.0) + jnp.where(small < 0.03, series, jnp.log(1.0 + small))


def silu_slope(value, sigma):
    return sigma * (1.0 + value * (1.0 - sigma))


def spread(heads, expand):
    return mm(heads, expand, precision=highest)


def gather_heads(lanes, expand):
    return mm(lanes, expand, ((1,), (1,)), precision=highest)


def pick(place, pieces, held):
    if len(pieces) == 1:
        return pieces[0][...]
    away = lax.bitwise_xor(pl.program_id(0) if held is None else held, place[0])
    value = pieces[3][...]
    for number in range(3):
        value = jnp.where(away == number, pieces[number][...], value)
    return value


def in_kernel(
    place, wall, ngain, taps, bias, dtb, avec, mask, halo, expand, tri, *refs
):
    hid = refs[:-14]
    normed, cin, cpre, dtp, cum, dtv, xdt, bc, sloc, pref, send, state, thru, prev = refs[-14:]
    step = pl.program_id(0)
    inner = expand.shape[1]

    @pl.when(step == 0)
    def _():
        state[...] = jnp.zeros_like(state)
        thru[...] = jnp.ones_like(thru)
        prev[...] = halo[...]

    h = pick(place, hid, None)
    inv = lax.rsqrt(jnp.mean(h * h, axis=1, keepdims=True) + epsilon)
    low = (h * inv * ngain[...]).astype(bf16)
    normed[...] = low
    rows = mm(low, wall[:, : inner + BC])
    pre_dt = mm(low, wall[:, inner + BC :])
    dtp[...] = pre_dt
    cin[...] = rows
    ext = jnp.concatenate([prev[...], rows], axis=0)
    prev[...] = rows[GROUP - ROWS :]
    total = taps[CONV - 1 : CONV, :] * rows + bias[0:1, :]
    for k in range(CONV - 1):
        first = ROWS - CONV + 1 + k
        total = total + taps[k : k + 1, :] * ext[first : first + GROUP] * mask[:, k : k + 1]
    cpre[...] = total
    act = total * jax.nn.sigmoid(total)
    x = act[:, :inner]
    low_bc = act[:, inner:].astype(bf16)
    bc[...] = low_bc
    dt = softplus(pre_dt + dtb[0:1, :])
    dtv[...] = dt
    run = mm(tri[...], dt * avec[0:1, :], precision=highest)
    cum[...] = run
    last = run[GROUP - 1 : GROUP]
    xdt[...] = (x * spread(dt, expand[...])).astype(bf16)
    tail = jnp.exp(last - run) * mask[:, 4:5] * dt
    contrib = mm(low_bc[:, :STATE], (x * spread(tail, expand[...])).astype(bf16), ((0,), (0,)))
    through = jnp.broadcast_to(jnp.exp(last) * mask[GROUP - 1 : GROUP, 3:4], (ROWS, LANES))
    through = spread(through, expand[...])
    sloc[0] = state[...]
    pref[0] = thru[...]
    state[...] = through[0:1] * state[...] + contrib
    thru[...] = thru[...] * through

    @pl.when(step == pl.num_programs(0) - 1)
    def _():
        send[:STATE] = state[...]
        send[STATE:] = thru[...]


def pair_lanes(value, which):
    lane = lax.broadcasted_iota(jnp.int32, value.shape, 1)
    keep = lane < HEADDIM if which == 0 else lane >= HEADDIM
    return jnp.where(keep, value, jnp.zeros_like(value))


def intra_kernel(cum, xdt, bc, seg, segrow, y):
    inner = xdt.shape[1]
    run = cum[...]
    run_t = run.T
    base = mm(bc[:, STATE:], bc[:, :STATE], ((1,), (1,)))
    t_at = lax.broadcasted_iota(jnp.int32, (GROUP, GROUP), 0)
    s_at = lax.broadcasted_iota(jnp.int32, (GROUP, GROUP), 1)
    same = (seg[:, 0:1] == segrow[0:1, :]) & (t_at >= s_at)
    closed = jnp.where(same, 0.0, -1e30)
    for pair in range(inner // LANES):
        cols = slice(pair * LANES, (pair + 1) * LANES)
        xs = xdt[:, cols]
        parts = []
        for which in range(2):
            head = 2 * pair + which
            decay = jnp.exp(run[:, head : head + 1] - run_t[head : head + 1, :] + closed)
            parts.append(mm((decay * base).astype(bf16), xs))
        lane = lax.broadcasted_iota(jnp.int32, (GROUP, LANES), 1)
        y[:, cols] = jnp.where(lane < HEADDIM, parts[0], parts[1])


def out_kernel(
    yin, cpre, cum, bc, mask, zval, sloc, pref, entry, dskip, ggain, wout, expand, *refs
):
    cot, (y, gate_in, proj, sums) = refs[:-4], refs[-4:]
    inner = expand.shape[1]
    pre = cpre[...]
    x = pre * jax.nn.sigmoid(pre)
    full = sloc[0] + pref[0][0:1] * entry[...]
    reach = spread(jnp.exp(cum[...]) * mask[:, 3:4], expand[...])
    value = yin[...] + reach * mm(bc[:, STATE:], full.astype(bf16)) + dskip[0:1, :] * x
    y[...] = value
    z = zval[...]
    gated = value * (z * jax.nn.sigmoid(z))
    low = (gated * ggain[0:1, :]).astype(bf16)
    gate_in[...] = low
    proj[...] = mm(low, wout[...], ((1,), (1,)))
    ones = jnp.ones((ROWS, inner), f32)
    squares = mm(ones, gated * gated, ((1,), (1,)), precision=highest)
    if cot:
        back = mm(cot[0][...].astype(bf16), wout[...])
        dots = mm(ones, low.astype(f32) * back, ((1,), (1,)), precision=highest)
        row = lax.broadcasted_iota(jnp.int32, squares.shape, 0)
        squares = jnp.where(row == 0, squares, dots)
    sums[...] = squares


def gate_kernel(
    place, scale, gsq, y, zval, ggain, wout, cum, bc, mask, expand, *refs
):
    gh = refs[:-9]
    gproj, dy, dz, gloc, suf, send, acc, carry, thru = refs[-9:]
    step = pl.program_id(0)

    @pl.when(step == 0)
    def _():
        carry[...] = jnp.zeros_like(carry)
        thru[...] = jnp.ones_like(thru)
        acc[...] = jnp.zeros_like(acc)

    gp = (scale[...] * pick(place, gh, pl.num_programs(0) - 1 - step)).astype(bf16)
    gproj[...] = gp
    ggi = mm(gp, wout[...])
    z = zval[...]
    sigma = jax.nn.sigmoid(z)
    silu = z * sigma
    value = y[...]
    gated = value * silu
    ggated = ggi * ggain[0:1, :] + gated * gsq[...]
    acc[0:1, :] += jnp.sum(ggi * gated, axis=0, keepdims=True)
    low = (ggated * silu).astype(bf16)
    dy[...] = low
    dz[...] = (ggated * value * silu_slope(z, sigma)).astype(bf16)
    run = cum[...]
    last = run[GROUP - 1 : GROUP]
    reach = spread(jnp.exp(run) * mask[:, 3:4], expand[...])
    back = mm(bc[:, STATE:], (reach * low.astype(f32)).astype(bf16), ((0,), (0,)))
    through = jnp.broadcast_to(jnp.exp(last) * mask[GROUP - 1 : GROUP, 3:4], (ROWS, LANES))
    through = spread(through, expand[...])
    gloc[0] = carry[...]
    suf[0] = thru[...]
    carry[...] = back + through[0:1] * carry[...]
    thru[...] = thru[...] * through

    @pl.when(step == pl.num_programs(0) - 1)
    def _():
        send[:STATE] = carry[...]
        send[STATE:] = thru[...]


def intra_back_kernel(cum, xdt, bc, seg, segrow, dy, dz, wz, u, dbc, part):
    inner = xdt.shape[1]
    run = cum[...]
    run_t = run.T
    base = mm(bc[:, :STATE], bc[:, STATE:], ((1,), (1,)))
    s_at = lax.broadcasted_iota(jnp.int32, (GROUP, GROUP), 0)
    t_at = lax.broadcasted_iota(jnp.int32, (GROUP, GROUP), 1)
    same = (seg[:, 0:1] == segrow[0:1, :]) & (t_at >= s_at)
    closed = jnp.where(same, 0.0, -1e30)
    grad_base = jnp.zeros((GROUP, GROUP), f32)
    for pair in range(inner // LANES):
        cols = slice(pair * LANES, (pair + 1) * LANES)
        xs = xdt[:, cols]
        ds = dy[:, cols]
        parts = []
        for which in range(2):
            head = 2 * pair + which
            decay = jnp.exp(run_t[head : head + 1, :] - run[:, head : head + 1] + closed)
            parts.append(mm((decay * base).astype(bf16), ds))
            grad_base = grad_base + decay * mm(xs, pair_lanes(ds, which), ((1,), (1,)))
        lane = lax.broadcasted_iota(jnp.int32, (GROUP, LANES), 1)
        u[:, cols] = jnp.where(lane < HEADDIM, parts[0], parts[1])
    part[...] = mm(dz[...], wz[...], ((1,), (1,)))
    low = grad_base.astype(bf16)
    dbc[:, :STATE] = mm(low, bc[:, STATE:])
    dbc[:, STATE:] = mm(low, bc[:, :STATE], ((0,), (0,)))


def in_back_kernel(
    uin, dbc, dy, y, cpre, cin, dtp, dtv, cum, xdt, bc, mask, sloc, pref, entry, gloc, suf,
    gout, halo, taps, dtb, avec, dskip, expand, triback,
    gall, last8, rim, gtaps, vecs, dsk,
    nexts,
):
    step = pl.program_id(0)
    inner = expand.shape[1]

    @pl.when(step == 0)
    def _():
        nexts[...] = jnp.zeros_like(nexts)
        gtaps[...] = jnp.zeros_like(gtaps)
        vecs[...] = jnp.zeros_like(vecs)
        dsk[...] = jnp.zeros_like(dsk)

    e = expand[...]
    pre = cpre[...]
    sigma = jax.nn.sigmoid(pre)
    x = (pre * sigma)[:, :inner]
    full = sloc[0] + pref[0][0:1] * entry[...]
    nxt = gloc[0] + suf[0][0:1] * gout[...]
    nxt_low = nxt.astype(bf16)
    run = cum[...]
    last = run[GROUP - 1 : GROUP]
    dt = dtv[...]
    low_dy = dy[...].astype(f32)
    xw = xdt[...].astype(f32)
    tail = spread(jnp.exp(last - run) * mask[:, 4:5], e)
    reach = spread(jnp.exp(run) * mask[:, 3:4], e)
    u_inter = tail * mm(bc[:, :STATE], nxt_low)
    u = uin[...] + u_inter
    dx = spread(dt, e) * u + dskip[0:1, :] * low_dy
    dsk[0:1, :] += jnp.sum(low_dy * x, axis=0, keepdims=True)
    db = dbc[:, :STATE] + mm((tail * xw).astype(bf16), nxt_low, ((1,), (1,)))
    dc = dbc[:, STATE:] + mm((reach * low_dy).astype(bf16), full.astype(bf16), ((1,), (1,)))
    grad_dt = gather_heads(x * u, e)
    y_plain = y[...] - dskip[0:1, :] * x
    grad_cum = gather_heads(low_dy * y_plain - xw * u, e)
    flow = jnp.sum(nxt * full, axis=0, keepdims=True)
    flow = gather_heads(jnp.broadcast_to(flow, (ROWS, inner)), e)[0:1]
    ends = jnp.sum(xw * u_inter, axis=0, keepdims=True)
    ends = gather_heads(jnp.broadcast_to(ends, (ROWS, inner)), e)[0:1]
    grad_tot = mask[GROUP - 1 : GROUP, 3:4] * jnp.exp(last) * flow + ends
    grad_da = mm(triback[...], grad_cum, precision=highest) + grad_tot
    a = avec[0:1, :]
    grad_dtv = grad_dt + grad_da * a
    grad_dtpre = grad_dtv * jax.nn.sigmoid(dtp[...] + dtb[0:1, :])
    vecs[0:1, :] += jnp.sum(grad_da * dt, axis=0, keepdims=True) * a
    vecs[1:2, :] += jnp.sum(grad_dtpre, axis=0, keepdims=True)
    slope = silu_slope(pre, sigma)
    grad_pre = jnp.concatenate([dx, db, dc], axis=1) * slope
    gtaps[4:5, :] += jnp.sum(grad_pre, axis=0, keepdims=True)
    rows = cin[...]
    grad_rows = taps[CONV - 1 : CONV, :] * grad_pre
    gtaps[3:4, :] += jnp.sum(rows * grad_pre, axis=0, keepdims=True)
    masked = []
    for k in range(CONV - 1):
        m = grad_pre * mask[:, k : k + 1]
        masked.append(m[:ROWS])
        ahead = CONV - 1 - k
        shifted = jnp.concatenate([m, nexts[k]], axis=0)[ahead : ahead + GROUP]
        grad_rows = grad_rows + taps[k : k + 1, :] * shifted
        gtaps[k : k + 1, :] += jnp.sum(rows * shifted, axis=0, keepdims=True)
    for k in range(CONV - 1):
        nexts[k] = masked[k]
    gall[:, : inner + BC] = grad_rows.astype(bf16)
    gall[:, inner + BC :] = grad_dtpre.astype(bf16)

    @pl.when(step == 0)
    def _():
        last8[...] = grad_rows[GROUP - ROWS :]

    @pl.when(step == pl.num_programs(0) - 1)
    def _():
        spill = jnp.zeros((ROWS, inner + BC), f32)
        edge = halo[...]
        for k in range(CONV - 1):
            down = ROWS - CONV + 1 + k
            moved = jnp.concatenate([jnp.zeros((ROWS, inner + BC), f32), masked[k]], axis=0)
            moved = moved[ROWS - down : 2 * ROWS - down]
            spill = spill + taps[k : k + 1, :] * moved
            gtaps[k : k + 1, :] += jnp.sum(edge * moved, axis=0, keepdims=True)
        rim[...] = spill


def whole(shape):
    return pl.BlockSpec(shape, lambda c: (0,) * len(shape))


def by_rows(cols, count, reverse=False):
    if reverse:
        return pl.BlockSpec((GROUP, cols), lambda c: (count - 1 - c, 0))
    return pl.BlockSpec((GROUP, cols), lambda c: (c, 0))


def by_group(shape, count, reverse=False):
    if reverse:
        return pl.BlockSpec((1,) + shape, lambda c: (count - 1 - c, 0, 0))
    return pl.BlockSpec((1,) + shape, lambda c: (c, 0, 0))


def by_piece(pieces, count, reverse=False):
    if len(pieces) == 1:
        return [(by_rows(pieces[0].shape[1], count, reverse), pieces[0])]
    return [(whole(piece.shape), piece) for piece in pieces]


def by_cols(count):
    return pl.BlockSpec((ROWS, GROUP), lambda c: (0, c))


def call(kernel, count, ins, outs, scratch, micros, name):
    return pl.pallas_call(
        kernel,
        grid=(count,),
        in_specs=[spec for spec, _ in ins],
        out_specs=[spec for spec, _ in outs],
        out_shape=[shape for _, shape in outs],
        scratch_shapes=scratch,
        compiler_params=pltpu.CompilerParams(
            dimension_semantics=("arbitrary",), vmem_limit_bytes=56 * 1024 * 1024
        ),
        cost_estimate=pl.CostEstimate(
            flops=micros * 1_150_000_000, bytes_accessed=1024 * 1024, transcendentals=0
        ),
        name=name,
    )(*[value for _, value in ins])


def shape(*dims, dtype=f32):
    return jax.ShapeDtypeStruct(dims, dtype)


SWAP = ((0, 1), (1, 0))
CROSS = ((0, 1), (3, 2))
CROSS_BACK = ((1, 0), (2, 3))
CORE_OUT = ((0, 2), (3, 1))
CORE_IN = ((2, 0), (1, 3))
DIAGONAL = ((2, 1), (1, 2))
BOTH = ("core", "zh")
BLOCKS = ("chip", "zh")


def shifted(value, steps):
    count = lax.axis_size(BLOCKS)
    leading, last = (max(0, -steps), min(count, count - steps))
    return lax.ppermute(value, BLOCKS, [(source, source + steps) for source in range(leading, last)])


def chain(part, reverse, stages):
    count = lax.axis_size(BLOCKS)
    place = lax.axis_index(BLOCKS)
    state, decay = part[:STATE], part[STATE : STATE + 1]
    entry, reach = jnp.zeros_like(state), jnp.ones_like(decay)
    step = 1
    while step < count:
        got = lax.ppermute(part, BLOCKS, [(i, i ^ step) for i in range(count)])
        got_state, got_decay = got[:STATE], got[STATE : STATE + 1]
        later = ((place & step) == 0) if reverse else ((place & step) != 0)
        stages.append(got)
        entry = jnp.where(later, entry + reach * got_state, entry)
        reach = jnp.where(later, reach * got_decay, reach)
        state = jnp.where(later, state + decay * got_state, got_state + got_decay * state)
        decay = decay * got_decay
        part = jnp.concatenate([state, jnp.broadcast_to(decay, (ROWS, decay.shape[1]))])
        step *= 2
    return entry


def swap(value, axis):
    return lax.ppermute(value, axis, SWAP)


def total(value, axes):
    for axis in axes:
        count = lax.axis_size(axis)
        step = 1
        while step < count:
            value = value + lax.ppermute(value, axis, [(i, i ^ step) for i in range(count)])
            step *= 2
    return value


def take(value, index, count):
    size = value.shape[0] // count
    return lax.dynamic_slice_in_dim(value, index * size, size)


def ordered(place, mine, theirs):
    return jnp.where(
        place == 0, jnp.concatenate([mine, theirs]), jnp.concatenate([theirs, mine])
    )


def behind(value, *marks):
    return lax.optimization_barrier((value, *marks))[0]


def scatter_sum(part, mark=()):
    core, near = lax.axis_index("core"), lax.axis_index("zl")
    half = take(part, core, 2) + behind(swap(take(part, 1 - core, 2), "core"), *mark)
    if lax.axis_size("zl") == 2:
        return take(half, near, 2) + swap(take(half, 1 - near, 2), "zl")
    return lax.psum_scatter(half, "zl", scatter_dimension=0, tiled=True)


def own_rows(value):
    core, near = lax.axis_index("core"), lax.axis_index("zl")
    return take(take(value, core, 2), near, lax.axis_size("zl"))


def gather_near(value):
    if lax.axis_size("zl") == 2:
        return ordered(lax.axis_index("zl"), value, swap(value, "zl"))
    return lax.all_gather(value, "zl", tiled=True)


def gather_rows(value):
    half = gather_near(value)
    return ordered(lax.axis_index("core"), half, swap(half, "core"))


def own_place():
    return 2 * lax.axis_index("core") + lax.axis_index("zl")


def gather_pieces(value):
    if lax.axis_size("zl") != 2 or value.shape[0] != GROUP:
        return [gather_rows(value)]
    near = swap(value, "zl")
    return [value, near, swap(value, "core"), swap(near, "core")]


def place_kernel(place, value, mine, near, theirs, value_s, mine_s, near_s, theirs_s, out):
    away = lax.bitwise_xor(pl.program_id(0), place[0])
    pairs = ((value, mine), (value_s, mine_s), (near, theirs), (near_s, theirs_s))
    for number, (here, there) in enumerate(pairs):

        @pl.when((away == number) & (place[1] == 1))
        def _():
            out[...] = here[...].astype(out.dtype)

        @pl.when((away == number) & (place[1] == 0))
        def _():
            out[...] = there[...].astype(out.dtype)


def cross_over(value):
    return [lax.ppermute(value, BOTH, pairs) for pairs in (CROSS, DIAGONAL, CORE_IN)]


def near_swap(value):
    if lax.axis_size("zl") != 2 or value.shape[0] != GROUP:
        return None
    here = [(2 * kind + i, 2 * kind + 1 - i) for kind in (0, 3) for i in range(2)]
    return lax.ppermute(value, ("core", "zh", "zl"), here)


def near_swaps(value, mine, theirs, near, value_s=None, near_s=None):
    if lax.axis_size("zl") != 2 or value.shape[0] != GROUP:
        return None
    axes = ("core", "zh", "zl")
    there = [(2 * kind + i, 2 * kind + 1 - i) for kind in (1, 2) for i in range(2)]
    return (
        near_swap(value) if value_s is None else value_s,
        lax.ppermute(mine, axes, there),
        lax.ppermute(theirs, axes, there),
        near_swap(near) if near_s is None else near_s,
    )


def deliver(value, mine, theirs, near, dtype, swaps=None, mark=()):
    core, far = lax.axis_index("core"), lax.axis_index("zh")
    held = core == far
    if lax.axis_size("zl") != 2 or value.shape[0] != GROUP:
        mine = gather_near(jnp.where(held, value, mine))
        theirs = gather_near(jnp.where(held, near, theirs))
        full = ordered(core, mine, theirs)
        return narrowed(full) if dtype == bf16 else full
    if swaps is None:
        swaps = near_swaps(value, mine, theirs, near)
    value_s, mine_s, theirs_s, near_s = swaps
    place = jnp.stack([own_place(), held.astype(jnp.int32)]).astype(jnp.int32)
    width = value.shape[1]
    parts = behind((value, mine, near, theirs, value_s, mine_s, near_s, theirs_s), *mark)
    return pl.pallas_call(
        place_kernel,
        grid=(4,),
        in_specs=[pl.BlockSpec(memory_space=pltpu.SMEM)] + [whole((GROUP, width))] * 8,
        out_specs=by_rows(width, 4),
        out_shape=shape(4 * GROUP, width, dtype=dtype),
        compiler_params=pltpu.CompilerParams(
            dimension_semantics=("arbitrary",), vmem_limit_bytes=40 * 1024 * 1024
        ),
        name="place",
    )(place, *parts)


def to_block(value):
    got = lax.ppermute(value, BOTH, CORE_OUT)
    return jnp.where(lax.axis_index("core") == lax.axis_index("zh"), value, got)


def eight(row):
    return jnp.broadcast_to(row[None, :], (ROWS, row.shape[0]))


def pad_lanes(value):
    return jnp.pad(value, [(0, 0)] * (value.ndim - 1) + [(0, LANES - value.shape[-1])])


def weight_kernel(count, extra, place, *refs):
    own, rest = refs[:count], refs[count:]
    outs, rest = rest[-count:], rest[:-count]
    parts, more = (rest[:-2], rest[-2:]) if extra else (rest, ())
    block = pl.program_id(0)
    at = 0
    for source, out in zip(own, outs):
        cols = source.shape[1]

        @pl.when(place[1] == 1)
        def _():
            out[:, :cols] = source[...]

        for away, part in enumerate(parts):

            @pl.when((place[1] == 0) & (lax.bitwise_xor(place[0], block) == away))
            def _():
                out[:, :cols] = part[:, at : at + cols].astype(bf16)

        at += cols
    if more:
        cols = own[0].shape[1]
        outs[0][:, cols : cols + BC] = more[0][...]
        outs[0][:, cols + BC :] = more[1][...].astype(bf16)


def narrow_kernel(wide, narrow):
    narrow[...] = wide[...].astype(bf16)


def narrowed(value):
    rows, cols = value.shape
    return pl.pallas_call(
        narrow_kernel,
        grid=(rows // GROUP,),
        in_specs=[by_rows(cols, 0)],
        out_specs=by_rows(cols, 0),
        out_shape=shape(rows, cols, dtype=bf16),
        name="narrowed",
    )(value)


def weights_over(own, *marks):
    chips = lax.axis_size("chip")
    piece = jnp.concatenate(
        [take(value, lax.axis_index("chip"), chips).astype(f32) for value in behind(own, *marks)],
        axis=1,
    )
    return lax.ppermute(piece, BOTH, CROSS)


def gather_weights(piece, own, more=(), third=()):
    width = own[0].shape[0]
    chips = lax.axis_size("chip")
    chip = lax.axis_index("chip")
    held = (lax.axis_index("core") == lax.axis_index("zh")).astype(jnp.int32)
    size = width // chips
    if chips == 4:
        parts = [piece]
        for away in range(1, chips):
            pairs = [
                (4 * c + kind, 4 * (c ^ away) + kind) for c in range(chips) for kind in (1, 2)
            ]
            parts.append(lax.ppermute(piece, ("chip", "core", "zh"), pairs))
        place = jnp.stack([chip, held]).astype(jnp.int32)
        blocks = chips
    else:
        parts = [lax.all_gather(piece, "chip", tiled=True)]
        place = jnp.stack([0, held]).astype(jnp.int32)
        blocks, size = 1, width
    parts = behind(parts, *third)
    out_cols = [value.shape[1] for value in own]
    out_cols[0] += sum(value.shape[1] for value in more)

    def rows(cols):
        return pl.BlockSpec((size, cols), lambda c: (c, 0))

    return pl.pallas_call(
        functools.partial(weight_kernel, len(own), bool(more)),
        grid=(blocks,),
        in_specs=[pl.BlockSpec(memory_space=pltpu.SMEM)]
        + [rows(value.shape[1]) for value in own]
        + [whole(piece.shape if chips == 4 else parts[0].shape)] * len(parts)
        + [rows(value.shape[1]) for value in more],
        out_specs=[rows(cols) for cols in out_cols],
        out_shape=[shape(width, cols, dtype=bf16) for cols in out_cols],
        compiler_params=pltpu.CompilerParams(
            dimension_semantics=("arbitrary",), vmem_limit_bytes=40 * 1024 * 1024
        ),
        name="weights",
    )(place, *own, *parts, *more)


def shards(
    x_input,
    seg_ids,
    cotangent,
    norm_gain,
    w_z,
    w_x,
    w_bc,
    w_dt,
    conv_x,
    conv_bc,
    bias_x,
    bias_bc,
    dt_bias,
    a_log,
    d_skip,
    gate_gain,
    w_out,
):
    tok, width = x_input.shape
    inner = w_z.shape[2]
    core, far = lax.axis_index("core"), lax.axis_index("zh")
    held = core == far
    heads = w_dt.shape[2]
    count = tok // GROUP
    conv_cols = inner + BC
    all_cols = inner + BC + LANES

    dt_own = w_dt.astype(f32).reshape(LAYERS, width * heads // LANES, LANES)
    dt_sent = lax.ppermute(dt_own, BOTH, CROSS)
    dt_all = pad_lanes(jnp.where(held, dt_own, dt_sent).reshape(LAYERS, width, heads))
    first_x = weights_over([w_x[0]])
    hidden = to_block(x_input.astype(f32))
    first_rest = weights_over([w_z[0], w_out[0]], first_x)
    (wall,) = gather_weights(first_x, [w_x[0]], (w_bc[0], dt_all[0]), (first_rest,))
    seg = to_block(seg_ids.astype(f32))
    small = jnp.concatenate(
        [
            value.reshape(LAYERS, -1)
            for value in (conv_x, bias_x, dt_bias, a_log, d_skip, gate_gain)
        ],
        axis=1,
    )
    small = jnp.where(held, small, lax.ppermute(small, BOTH, CROSS))
    sizes = (CONV * inner, inner, heads, heads, heads, inner)
    pieces, at = [], 0
    for size in sizes:
        pieces.append(small[:, at : at + size])
        at += size
    conv_x, bias_x, dt_bias, a_log, d_skip, gate_gain = pieces
    conv_x = conv_x.reshape(LAYERS, CONV, inner)
    hidden_own = own_rows(hidden)
    hidden_block = hidden
    hidden = [hidden]
    place = jnp.stack([own_place(), own_place()]).astype(jnp.int32)
    smem = pl.BlockSpec(memory_space=pltpu.SMEM)
    edge_seg = shifted(seg[tok - ROWS :], 1)
    seg_ext = jnp.concatenate([edge_seg, seg])
    before = jnp.concatenate([edge_seg[ROWS - 1 :], seg[GROUP - 1 : tok - 1 : GROUP]])
    after = seg[GROUP - 1 :: GROUP]
    mask = jnp.stack(
        [
            (seg_ext[ROWS - CONV + 1 + k : ROWS - CONV + 1 + k + tok] == seg).astype(f32)
            for k in range(CONV - 1)
        ]
        + [
            (seg == jnp.repeat(before, GROUP)).astype(f32),
            (seg == jnp.repeat(after, GROUP)).astype(f32),
            seg,
            seg,
            seg,
        ],
        axis=1,
    )
    seg_col = seg[:, None]
    seg_row = eight(seg)
    expand = (jnp.arange(LANES)[:, None] == jnp.arange(inner)[None, :] // HEADDIM).astype(f32)
    position = jnp.arange(GROUP)
    tri = (position[:, None] >= position[None, :]).astype(f32)
    triback = (position[:, None] <= position[None, :]).astype(f32)

    stored = []
    for layer in range(LAYERS):
        if layer > 0:
            wall = next_wall
        taps = jnp.concatenate([conv_x[layer], conv_bc[layer]], axis=1)
        bias = eight(jnp.concatenate([bias_x[layer], bias_bc[layer]]))
        dtb = eight(pad_lanes(dt_bias[layer]))
        avec = eight(pad_lanes(-jnp.exp(a_log[layer])))
        dskip = eight(jnp.repeat(d_skip[layer], HEADDIM))
        ggain = eight(gate_gain[layer])
        ngain = norm_gain[layer][None, :]
        if len(hidden) == 1:
            end = hidden[0][tok - 16 :]
        else:
            ends = jnp.stack([piece[GROUP - 16 :] for piece in hidden])
            end = lax.dynamic_index_in_dim(ends, 3 ^ own_place(), 0, False)
        end = end * lax.rsqrt(jnp.mean(end * end, axis=1, keepdims=True) + epsilon) * ngain
        end = mm(end.astype(bf16), wall[:, : inner + BC])[ROWS:]
        halo = shifted(end, 1)
        normed, cin, cpre, dtp, cum, dtv, xdt, bc, sloc, pref, send = call(
            in_kernel,
            count,
            [
                (smem, place),
                (whole((width, all_cols)), wall),
                (whole((1, width)), ngain),
                (whole((CONV, conv_cols)), taps),
                (whole((ROWS, conv_cols)), bias),
                (whole((ROWS, LANES)), dtb),
                (whole((ROWS, LANES)), avec),
                (by_rows(ROWS, count), mask),
                (whole((ROWS, conv_cols)), halo),
                (whole((LANES, inner)), expand),
                (whole((GROUP, GROUP)), tri),
            ]
            + by_piece(hidden, count),
            [
                (by_rows(width, count), shape(tok, width, dtype=bf16)),
                (by_rows(conv_cols, count), shape(tok, conv_cols)),
                (by_rows(conv_cols, count), shape(tok, conv_cols)),
                (by_rows(LANES, count), shape(tok, LANES)),
                (by_rows(LANES, count), shape(tok, LANES)),
                (by_rows(LANES, count), shape(tok, LANES)),
                (by_rows(inner, count), shape(tok, inner, dtype=bf16)),
                (by_rows(BC, count), shape(tok, BC, dtype=bf16)),
                (by_group((STATE, inner), count), shape(count, STATE, inner)),
                (by_group((ROWS, inner), count), shape(count, ROWS, inner)),
                (whole((STATE + ROWS, inner)), shape(STATE + ROWS, inner)),
            ],
            [
                pltpu.VMEM((STATE, inner), f32),
                pltpu.VMEM((ROWS, inner), f32),
                pltpu.VMEM((ROWS, conv_cols), f32),
            ],
            16,
            "in_proj_conv",
        )
        if layer == 0:
            wz, wout = gather_weights(
                behind(first_rest, wall), [w_z[0], w_out[0]], third=(send,)
            )
            cotangent = behind(cotangent, send).astype(f32)
            cot_sent = lax.ppermute(cotangent, BOTH, CORE_OUT)
        else:
            wz, wout = next_wz, next_wout
        zval = mm(normed, wz)
        (yin,) = call(
            intra_kernel,
            count,
            [
                (by_rows(LANES, count), cum),
                (by_rows(inner, count), xdt),
                (by_rows(BC, count), bc),
                (by_rows(1, count), seg_col),
                (by_cols(count), seg_row),
            ],
            [(by_rows(inner, count), shape(tok, inner))],
            [],
            6,
            "ssd_within",
        )
        stages = []
        entry = chain(send, False, stages)
        if layer == 0:
            second_all = weights_over([w_x[1], w_z[1], w_out[1]], stages[0])
            entry = behind(entry, second_all, cot_sent)
            cotangent = jnp.where(held, cotangent, cot_sent)
        y, gate_in, proj, sums = call(
            out_kernel,
            count,
            [
                (by_rows(inner, count), yin),
                (by_rows(inner, count), cpre),
                (by_rows(LANES, count), cum),
                (by_rows(BC, count), bc),
                (by_rows(ROWS, count), mask),
                (by_rows(inner, count), zval),
                (by_group((STATE, inner), count), sloc),
                (by_group((ROWS, inner), count), pref),
                (whole((STATE, inner)), entry),
                (whole((ROWS, inner)), dskip),
                (whole((ROWS, inner)), ggain),
                (whole((width, inner)), wout),
                (whole((LANES, inner)), expand),
            ]
            + ([(by_rows(width, count), cotangent)] if layer == LAYERS - 1 else []),
            [
                (by_rows(inner, count), shape(tok, inner)),
                (by_rows(inner, count), shape(tok, inner, dtype=bf16)),
                (by_rows(width, count), shape(tok, width)),
                (by_cols(count), shape(ROWS, tok)),
            ],
            [],
            12,
            "gate_out_proj",
        )
        sums = total(sums, ("core", "zl"))
        gate_scale = lax.rsqrt(sums[0] / INNER + epsilon)
        stored.append(
            dict(
                hidden=hidden_own, normed=normed, zval=zval, cin=cin, cpre=cpre, dtp=dtp, cum=cum,
                dtv=dtv, xdt=xdt, bc=bc, sloc=sloc, pref=pref, entry=entry, y=y, gate_in=gate_in,
                proj=proj, gate_scale=gate_scale, dots=sums[1], halo=halo, wall=wall, wz=wz, wout=wout,
                taps=taps, dtb=dtb, avec=avec, dskip=dskip, ggain=ggain,
            )
        )
        if layer < LAYERS - 1:
            proj_sum = scatter_sum(proj)
            stored[layer]["proj_sum"] = proj_sum
            hidden_own = hidden_own + own_rows(gate_scale)[:, None] * proj_sum
            next_wall, next_wz, next_wout = gather_weights(
                behind(second_all, proj),
                [w_x[1], w_z[1], w_out[1]],
                (w_bc[1], dt_all[1]),
                third=(hidden_own,),
            )
            hidden = gather_pieces(hidden_own)

    grad_h = [cotangent]
    grad_own = own_rows(cotangent)
    matrices = [None] * LAYERS
    vectors = [None] * LAYERS
    shared = [None] * LAYERS
    for layer in reversed(range(LAYERS)):
        kept = stored[layer]
        gate_scale = kept["gate_scale"]
        if layer == LAYERS - 1:
            grad_scale = kept["dots"]
        else:
            grad_scale = gather_rows(jnp.sum(grad_own * kept["proj_sum"], axis=1))
        gsq = -grad_scale * gate_scale**3 / INNER
        rev = functools.partial(by_rows, count=count, reverse=True)
        rev_group = functools.partial(by_group, count=count, reverse=True)
        gproj, dy, dz, gloc, suf, gsend, acc = call(
            gate_kernel,
            count,
            [
                (smem, place),
                (rev(1), gate_scale[:, None]),
                (rev(1), gsq[:, None]),
                (rev(inner), kept["y"]),
                (rev(inner), kept["zval"]),
                (whole((ROWS, inner)), kept["ggain"]),
                (whole((width, inner)), kept["wout"]),
                (rev(LANES), kept["cum"]),
                (rev(BC), kept["bc"]),
                (rev(ROWS), mask),
                (whole((LANES, inner)), expand),
            ]
            + by_piece(grad_h, count, True),
            [
                (rev(width), shape(tok, width, dtype=bf16)),
                (rev(inner), shape(tok, inner, dtype=bf16)),
                (rev(inner), shape(tok, inner, dtype=bf16)),
                (rev_group((STATE, inner)), shape(count, STATE, inner)),
                (rev_group((ROWS, inner)), shape(count, ROWS, inner)),
                (whole((STATE + ROWS, inner)), shape(STATE + ROWS, inner)),
                (whole((ROWS, inner)), shape(ROWS, inner)),
            ],
            [pltpu.VMEM((STATE, inner), f32), pltpu.VMEM((ROWS, inner), f32)],
            10,
            "gate_back",
        )
        if layer == LAYERS - 1:
            last_sum = scatter_sum(kept["proj"], (gate_scale,))
            hidden_own = hidden_own + own_rows(gate_scale)[:, None] * last_sum
            dy = behind(dy, hidden_own)
            gsend = behind(gsend, hidden_own)
            out_parts = cross_over(hidden_own)
            out_held = (near_swap(hidden_own), near_swap(out_parts[2]))
        u, dbc, partial_z = call(
            intra_back_kernel,
            count,
            [
                (by_rows(LANES, count), kept["cum"]),
                (by_rows(inner, count), kept["xdt"]),
                (by_rows(BC, count), kept["bc"]),
                (by_rows(1, count), seg_col),
                (by_cols(count), seg_row),
                (by_rows(inner, count), dy),
                (by_rows(inner, count), dz),
                (whole((width, inner)), kept["wz"]),
            ],
            [
                (by_rows(inner, count), shape(tok, inner)),
                (by_rows(BC, count), shape(tok, BC)),
                (by_rows(width, count), shape(tok, width)),
            ],
            [],
            8,
            "ssd_within_back",
        )
        stages = []
        gout = chain(gsend, True, stages)
        round_one = stages[0]
        if layer == 0:
            out_swaps = near_swaps(hidden_own, *behind(out_parts, round_one), *out_held)
        grad_wout = mm(gproj, kept["gate_in"], ((0,), (0,)))
        grad_wz = mm(kept["normed"], dz, ((0,), (0,)))
        u = behind(u, grad_wout, grad_wz)
        gall, last8, rim, gtaps, vecs, dsk = call(
            in_back_kernel,
            count,
            [
                (rev(inner), u),
                (rev(BC), dbc),
                (rev(inner), dy),
                (rev(inner), kept["y"]),
                (rev(conv_cols), kept["cpre"]),
                (rev(conv_cols), kept["cin"]),
                (rev(LANES), kept["dtp"]),
                (rev(LANES), kept["dtv"]),
                (rev(LANES), kept["cum"]),
                (rev(inner), kept["xdt"]),
                (rev(BC), kept["bc"]),
                (rev(ROWS), mask),
                (rev_group((STATE, inner)), kept["sloc"]),
                (rev_group((ROWS, inner)), kept["pref"]),
                (whole((STATE, inner)), kept["entry"]),
                (rev_group((STATE, inner)), gloc),
                (rev_group((ROWS, inner)), suf),
                (whole((STATE, inner)), gout),
                (whole((ROWS, conv_cols)), kept["halo"]),
                (whole((CONV, conv_cols)), kept["taps"]),
                (whole((ROWS, LANES)), kept["dtb"]),
                (whole((ROWS, LANES)), kept["avec"]),
                (whole((ROWS, inner)), kept["dskip"]),
                (whole((LANES, inner)), expand),
                (whole((GROUP, GROUP)), triback),
            ],
            [
                (rev(all_cols), shape(tok, all_cols, dtype=bf16)),
                (whole((ROWS, conv_cols)), shape(ROWS, conv_cols)),
                (whole((ROWS, conv_cols)), shape(ROWS, conv_cols)),
                (whole((ROWS, conv_cols)), shape(ROWS, conv_cols)),
                (whole((ROWS, LANES)), shape(ROWS, LANES)),
                (whole((ROWS, inner)), shape(ROWS, inner)),
            ],
            [pltpu.VMEM((CONV - 1, ROWS, conv_cols), f32)],
            20,
            "in_proj_conv_back",
        )
        rim_back = shifted(rim, -1)
        if layer == 0:
            last8 = behind(last8, matrices[1], *(out_swaps or ()))
        else:
            last8 = behind(last8, *out_parts, *(out_held if out_held[0] is not None else ()))
        gall = lax.dynamic_update_slice(
            gall, (last8 + rim_back).astype(bf16), (tok - ROWS, 0)
        )
        partial = partial_z + mm(gall, kept["wall"], ((1,), (1,)))
        late = behind(gall, partial)
        grad_wbc = mm(kept["normed"], late[:, inner : inner + BC], ((0,), (0,)))
        grad_win = mm(kept["normed"], behind(late, grad_wbc)[:, :inner], ((0,), (0,)))
        grad_normed = scatter_sum(partial, (grad_win,) if layer == 0 else ())
        if layer == 0:
            first_part = behind(matrices[1][:, : 3 * inner], partial)
            first_got = lax.ppermute(first_part, BOTH, CROSS_BACK)
            grad_normed = behind(grad_normed, first_got)
            grad_own = input_gradient(grad_own, grad_normed, kept["hidden"], norm_gain[layer])
            grad_parts = cross_over(grad_own)
            own_s = near_swap(grad_own)
            late, partial = behind((gall, partial), grad_parts[2])
            grad_parts, own_s, _ = behind((grad_parts, own_s, grad_win))
            mark = grad_parts[0]
            grad_swaps = near_swaps(grad_own, *grad_parts, own_s)
        grad_wdt = mm(kept["normed"], late[:, inner + BC :], ((0,), (0,)))
        hidden_in = kept["hidden"]
        inv = lax.rsqrt(jnp.mean(hidden_in * hidden_in, axis=1, keepdims=True) + epsilon)
        if layer == 0:
            full = hidden_block
            grad_ngain = jnp.sum(
                partial
                * (full * lax.rsqrt(jnp.mean(full * full, axis=1, keepdims=True) + epsilon)),
                axis=0,
            )
        else:
            grad_ngain = jnp.sum(grad_normed * hidden_in * inv, axis=0)
        if layer > 0:
            grad_own = input_gradient(grad_own, grad_normed, hidden_in, norm_gain[layer])
            grad_h = gather_pieces(grad_own)
        matrices[layer] = lax.psum_scatter(
            jnp.concatenate([grad_wout, grad_wz, grad_win, grad_wbc], axis=1),
            "chip",
            scatter_dimension=0,
            tiled=True,
        )
        vectors[layer] = jnp.concatenate(
            [
                gtaps[: CONV + 1, :inner].reshape(-1),
                acc[0],
                vecs[0, :heads],
                vecs[1, :heads],
                dsk[0],
                grad_wdt[:, :heads].reshape(-1),
                gtaps[: CONV + 1, inner:].reshape(-1),
                grad_ngain,
            ]
        )
    vector = total(behind(jnp.stack(vectors), mark), ("zh",))
    common = (CONV + 1) * BC + width
    vector = jnp.concatenate(
        [vector[:, :-common], total(vector[:, -common:], ("zl",))], axis=1
    )
    first_sums = first_part + first_got
    vector = total(vector, ("chip",))
    other = swap(vector, "core")
    shared = (vector + other)[:, -common:]
    grad_swaps, first_sums, g_last, vector, other, shared = behind(
        (grad_swaps, first_sums, matrices[0], vector, other, shared)
    )
    input_grad = deliver(grad_own, *grad_parts, f32, grad_swaps)
    final_out = deliver(hidden_own, *out_parts, bf16, out_swaps, (first_sums,))
    last_sums = join_halves(g_last[:, : 3 * inner])
    grad_wbc = jnp.stack([g_last[:, 3 * inner :], matrices[1][:, 3 * inner :]], axis=1)
    grad_wbc = total(half_rows(grad_wbc), ("zh",))
    g_cols = [place_rows(last_sums), place_rows(first_sums)]
    by_head = jnp.where(held, vector, other)[:, :-common]
    g_bc = shared[:, :-width].reshape(LAYERS, CONV + 1, BC)
    g_ngain = shared[:, -width:]
    at = 0
    pieces = []
    for size in (CONV * inner, inner, inner, heads, heads, inner, width * heads):
        pieces.append(by_head[:, at : at + size])
        at += size
    g_conv, g_bias, g_ggain, g_alog, g_dtb, g_dsk, g_wdt = pieces
    g_wdt = g_wdt.reshape(LAYERS, width, heads)
    rows = width // lax.axis_size(("chip", "core"))
    g_wdt = lax.dynamic_slice_in_dim(g_wdt, lax.axis_index(("chip", "core")) * rows, rows, axis=1)
    return (
        final_out,
        input_grad,
        g_ngain,
        jnp.stack([g[:, inner : 2 * inner] for g in g_cols]),
        jnp.stack([g[:, 2 * inner :] for g in g_cols]),
        jnp.stack([grad_wbc[:, layer] for layer in range(LAYERS)]),
        g_wdt,
        g_conv.reshape(LAYERS, CONV, inner),
        g_bc[:, :CONV],
        g_bias,
        g_bc[:, CONV],
        g_dtb,
        g_alog,
        jnp.sum(g_dsk.reshape(LAYERS, heads, HEADDIM), axis=2),
        g_ggain,
        jnp.stack([g[:, :inner] for g in g_cols]),
    )


def join_halves(part):
    return part + lax.ppermute(part, BOTH, CROSS_BACK)


def input_gradient(grad_out, grad_normed, hidden, gain):
    inv = lax.rsqrt(jnp.mean(hidden * hidden, axis=1, keepdims=True) + epsilon)
    back = grad_normed * gain[None, :]
    return grad_out + inv * (
        back - hidden * inv * inv * jnp.mean(back * hidden, axis=1, keepdims=True)
    )


def place_rows(full):
    core, far = lax.axis_index("core"), lax.axis_index("zh")
    sent = lax.ppermute(take(full, 1 - core, 2), BOTH, CORE_OUT)
    return jnp.where(core == far, take(full, core, 2), sent)


def half_rows(part):
    core = lax.axis_index("core")
    part = take(part, core, 2) + swap(take(part, 1 - core, 2), "core")
    return total(part, ("zl",))


def solution(mesh):
    seq, head = mesh.devices.shape
    mesh = jax.sharding.Mesh(
        mesh.devices.reshape(seq // 2, 2, 2, head // 2), ("chip", "core", "zh", "zl")
    )
    tokens, columns = ("chip", "core"), ("zh", "zl")
    by_col = P(None, None, columns)
    by_head = P(None, columns)
    both = P(None, tokens, columns)
    placed = (
        P(tokens, None),
        P(tokens),
        P(tokens, None),
        P(),
        by_col,
        by_col,
        P(),
        by_col,
        by_col,
        P(),
        by_head,
        P(),
        by_head,
        by_head,
        by_head,
        by_head,
        by_col,
    )
    return jax.shard_map(
        shards,
        mesh=mesh,
        in_specs=placed,
        out_specs=(
            P(tokens, None),
            P(tokens, None),
            P(),
            both,
            both,
            P(None, tokens, None),
            both,
            by_col,
            P(),
            by_head,
            P(),
            by_head,
            by_head,
            by_head,
            by_head,
            both,
        ),
        check_vma=False,
    )
```
